32 devices in a mesh: dp: 8 (over z, x), seq: 4 (over y, core).
Axes of the slice: x: 2, y: 2, z: 4, core: 2. Of those that a mesh axis runs over, the one named last changes fastest.
Arguments:
- tokens: bfloat16 [16, 2048, 512], P('dp', 'seq'), may hold values from -6 to 6
- feature_matrix: bfloat16 [64, 256], replicated, may hold values from -6 to 6
- input_weight: bfloat16 [512, 1536], P(('dp', 'seq')), may hold values from -0.125 to 0.125
- output_weight: bfloat16 [512, 512], P(('dp', 'seq')), may hold values from -3 to 3
- output_bias: bfloat16 [512], P(('dp', 'seq')), may hold values from -1.75 to 1.75
- up_weight: bfloat16 [512, 2048], P(('dp', 'seq')), may hold values from -0.25 to 0.25
- up_bias: bfloat16 [2048], P(('dp', 'seq')), may hold values from -1.75 to 1.75
- down_weight: bfloat16 [2048, 512], P(('dp', 'seq')), may hold values from -0.125 to 0.125
- down_bias: bfloat16 [512], P(('dp', 'seq')), may hold values from -1.75 to 1.75
- first_gain: bfloat16 [512], P(('dp', 'seq')), may hold values from 0.5 to 1.5
- first_shift: bfloat16 [512], P(('dp', 'seq')), may hold values from -1.25 to 1.25
- second_gain: bfloat16 [512], P(('dp', 'seq')), may hold values from 0.5 to 1.5
- second_shift: bfloat16 [512], P(('dp', 'seq')), may hold values from -1.25 to 1.25
- cotangent: bfloat16 [16, 2048, 512], P('dp', 'seq'), may hold values from -6 to 6
Outputs:
- result: float32 [16, 2048, 512], P('dp', 'seq')
- tokens_grad: float32 [16, 2048, 512], P('dp', 'seq')
- input_weight_grad: float32 [512, 1536], P(('dp', 'seq'))
- output_weight_grad: float32 [512, 512], P(('dp', 'seq'))
- output_bias_grad: float32 [512], P(('dp', 'seq'))
- up_weight_grad: float32 [512, 2048], P(('dp', 'seq'))
- up_bias_grad: float32 [2048], P(('dp', 'seq'))
- down_weight_grad: float32 [2048, 512], P(('dp', 'seq'))
- down_bias_grad: float32 [512], P(('dp', 'seq'))
- first_gain_grad: float32 [512], P(('dp', 'seq'))
- first_shift_grad: float32 [512], P(('dp', 'seq'))
- second_gain_grad: float32 [512], P(('dp', 'seq'))
- second_shift_grad: float32 [512], P(('dp', 'seq'))
The draws below stay inside these ranges and needn't reach their ends.
All inputs are finite; a program needn't handle non-finite values.
Results may differ from the reference program's by a relative error of at most 0.015.
Values may be sent and summed in bfloat16 or wider, within the bound.
A program may use at most 192 MiB of HBM per device.

```python
import math
import jax
import jax.numpy as jnp
from jax import lax

D = 512
H = 8
DH = 64
M = 256
FF = 2048
BLOCK = 512
SEQUENCES = 16
SEQ_LEN = 2048
N_SEQ = 4


def steps_of(rng, shape, pieces, low, largest):
    def one(position, shards_of):
        heights = jax.random.uniform(jax.random.fold_in(jax.random.fold_in(rng, 6), position), (shards_of,), jnp.float32, low / len(pieces), largest / len(pieces))
        return jnp.repeat(jnp.exp(heights), shape[position] // shards_of).reshape((-1,) + (1,) * (len(shape) - position - 1))

    gain = one(*pieces[0])
    for cut in pieces[1:]:
        gain = gain * one(*cut)
    return gain


def normal_values(key, dims, scale, limit, cuts=(), kind=jnp.bfloat16):
    level = steps_of(key, dims, cuts, -0.22, 0.18) if cuts else 1.0
    entries = jax.random.normal(key, dims, jnp.float32) * scale * level
    return jnp.minimum(jnp.maximum(entries, -limit), limit).astype(kind)


def setup_inputs(seed: int = 0) -> dict:
    key_of = jax.random.split(jax.random.key(seed), 15)
    return {
        "tokens": normal_values(key_of[0], (SEQUENCES, SEQ_LEN, D), 1.0, 6.0, ((0, 8), (1, 4))),
        "feature_matrix": normal_values(key_of[1], (DH, M), 1.0, 6.0),
        "input_weight": normal_values(key_of[2], (D, 3 * D), (4 * D) ** -0.5, 0.125, ((0, 32),)),
        "output_weight": normal_values(key_of[3], (D, D), (D // 128) ** -0.5, 3.0, ((0, 32),)),
        "output_bias": normal_values(key_of[4], (D,), 0.3, 1.75, ((0, 32),)),
        "up_weight": normal_values(key_of[5], (D, FF), D ** -0.5, 0.25, ((0, 32),)),
        "up_bias": normal_values(key_of[6], (FF,), 0.3, 1.75, ((0, 32),)),
        "down_weight": normal_values(key_of[7], (FF, D), FF ** -0.5, 0.125, ((0, 32),)),
        "down_bias": normal_values(key_of[8], (D,), 0.3, 1.75, ((0, 32),)),
        "first_gain": jnp.clip(1.0 + 0.1 * jax.random.normal(key_of[9], (D,), jnp.float32), 0.5, 1.5).astype(jnp.bfloat16),
        "first_shift": normal_values(key_of[10], (D,), 0.2, 1.25, ((0, 32),)),
        "second_gain": jnp.clip(1.0 + 0.1 * jax.random.normal(key_of[11], (D,), jnp.float32), 0.5, 1.5).astype(jnp.bfloat16),
        "second_shift": normal_values(key_of[12], (D,), 0.2, 1.25, ((0, 32),)),
        "cotangent": normal_values(key_of[13], (SEQUENCES, SEQ_LEN, D), 1.0, 6.0, ((0, 8), (1, 4))),
    }


@jax.custom_vjp
def reduced_precision(v):
    return lax.optimization_barrier(v.astype(jnp.bfloat16)).astype(jnp.float32)

@jax.custom_vjp
def reduced_backward(v):
    return v

def low_keep(v):
    return (reduced_precision(v), None)

def low_pass(kept, grad):
    return (grad,)

def back_keep(v):
    return (v, None)

def back_low(kept, grad):
    return (reduced_precision(grad),)
reduced_precision.defvjp(low_keep, low_pass)
reduced_backward.defvjp(back_keep, back_low)
finest_precision = lax.Precision.HIGHEST
epsilon = 1e-05

def layer_norm(value_rows, norm_gain, norm_shift):
    center = lax.optimization_barrier(jnp.mean(value_rows, axis=-1, keepdims=True))
    centred = value_rows - center
    spread = lax.optimization_barrier(jnp.mean(centred * centred, axis=-1, keepdims=True))
    return centred * lax.rsqrt(spread + epsilon) * norm_gain + norm_shift

def features(projection, matrix, feature_scale):
    raw_proj = reduced_backward(jnp.einsum('rhd,dm->rhm', projection, matrix, precision=finest_precision))
    half_norm = 0.5 * feature_scale * feature_scale * lax.optimization_barrier(jnp.sum(projection * projection, axis=-1, keepdims=True))
    return reduced_precision(jnp.exp(feature_scale * raw_proj - half_norm) / math.sqrt(M))

def block_step(block_carry, block_inputs):
    running_prefix_state, norm_sum = block_carry
    query_features, key_features, value_rows = block_inputs
    length = query_features.shape[0]
    positions = jnp.arange(length)
    causal = (positions[:, None] >= positions[None, :]).astype(jnp.float32)
    scores = reduced_backward(jnp.einsum('ihm,jhm->hij', query_features, key_features, precision=finest_precision) * causal[None])
    denominator = lax.optimization_barrier(jnp.sum(scores, axis=-1)) + jnp.einsum('ihm,hm->hi', query_features, norm_sum, precision=finest_precision)
    attention_numerator = jnp.einsum('hij,jhd->ihd', reduced_precision(scores), value_rows, precision=finest_precision)
    attention_numerator = reduced_backward(attention_numerator + jnp.einsum('plq,lqu->plu', query_features, reduced_precision(running_prefix_state), precision=finest_precision))
    block_out = attention_numerator / jnp.transpose(denominator)[:, :, None]
    block_local_state = reduced_backward(jnp.einsum('nqo,nqi->qoi', key_features, value_rows, precision=finest_precision))
    return ((running_prefix_state + block_local_state, norm_sum + lax.optimization_barrier(jnp.sum(key_features, axis=0))), block_out)

def by_block(value_rows):
    return value_rows.reshape((N_SEQ, BLOCK) + value_rows.shape[1:])

def forward(inputs, matrix, weights):
    input_weight, output_weight, output_bias, up_weight, up_bias, down_weight, down_bias, first_gain, first_shift, second_gain, second_shift = weights
    length = inputs.shape[0]
    normed = reduced_precision(layer_norm(inputs, first_gain, first_shift))
    mixed = reduced_precision(reduced_backward(jnp.dot(normed, input_weight, precision=finest_precision)))
    head_parts = mixed.reshape(length, 3, H, DH)
    feature_scale = DH ** (-0.25)
    query_features = features(head_parts[:, 0], matrix, feature_scale)
    key_features = features(head_parts[:, 1], matrix, feature_scale)
    value_rows = head_parts[:, 2]
    start_carry = (jnp.zeros((H, M, DH), jnp.float32), jnp.zeros((H, M), jnp.float32))
    _, block_outputs = lax.scan(jax.checkpoint(block_step), start_carry, (by_block(query_features), by_block(key_features), by_block(value_rows)))
    attended = reduced_precision(block_outputs.reshape(length, D))
    middle = inputs + reduced_backward(jnp.dot(attended, output_weight, precision=finest_precision)) + output_bias
    normed_two = reduced_precision(layer_norm(middle, second_gain, second_shift))
    hidden = reduced_backward(jnp.dot(normed_two, up_weight, precision=finest_precision)) + up_bias
    active = reduced_precision(jax.nn.gelu(hidden, approximate=True))
    return middle + reduced_backward(jnp.dot(active, down_weight, precision=finest_precision)) + down_bias

def reference(tokens, feature_matrix, input_weight, output_weight, output_bias, up_weight, up_bias, down_weight, down_bias, first_gain, first_shift, second_gain, second_shift, cotangent):
    weights = (input_weight.astype(jnp.float32), output_weight.astype(jnp.float32), output_bias.astype(jnp.float32), up_weight.astype(jnp.float32), up_bias.astype(jnp.float32), down_weight.astype(jnp.float32), down_bias.astype(jnp.float32), first_gain.astype(jnp.float32), first_shift.astype(jnp.float32), second_gain.astype(jnp.float32), second_shift.astype(jnp.float32))
    matrix = feature_matrix.astype(jnp.float32)
    token_values = tokens.astype(jnp.float32)
    cot_values = cotangent.astype(jnp.float32)

    def sequence_step(totals, seq_pair):
        seq_tokens, seq_cot = seq_pair

        def forward_only(inputs, params):
            return forward(inputs, matrix, params)
        seq_result, pullback = jax.vjp(forward_only, seq_tokens, weights)
        input_grad, weight_grads = pullback(seq_cot)
        totals = jax.tree.map(jnp.add, totals, weight_grads)
        return (totals, (seq_result, input_grad))
    zero_grads = jax.tree.map(jnp.zeros_like, weights)
    totals, (results, input_grads) = lax.scan(sequence_step, zero_grads, (token_values, cot_values))
    return (results, input_grads, totals[0], totals[1], totals[2], totals[3], totals[4], totals[5], totals[6], totals[7], totals[8], totals[9], totals[10])
```

```python
import math

import jax
import jax.numpy as jnp
from jax import lax
from jax.sharding import PartitionSpec as P

H = 8
DH = 64

from jax.experimental import pallas as pl
from jax.experimental.pallas import tpu as pltpu

MESH = pl.DeviceIdType.MESH


class Geometry:
    def __init__(self, mesh):
        dp, seq = mesh.shape["dp"], mesh.shape["seq"]
        self.C = 2
        self.Y = seq // 2
        self.X = 1 << ((dp.bit_length() - 1) // 2)
        self.Z = dp // self.X

    def me(self):
        dp, seq = lax.axis_index("dp"), lax.axis_index("seq")
        return dp // self.X, dp % self.X, seq // 2, seq % 2

    def device(self, z, x, y, c):
        return (z * self.X + x, y * 2 + c)

    def barrier(self):
        z, x, y, c = self.me()
        peers = [self.device(z, x, y, 1 - c)]
        peers += [self.device((z + k) % self.Z, x, y, c) for k in range(1, self.Z)]
        peers += [self.device(z, (x + k) % self.X, y, c) for k in range(1, self.X)]
        peers += [self.device(z, x, (y + k) % self.Y, c) for k in range(1, self.Y)]
        semaphore = pltpu.get_barrier_semaphore()
        for peer in peers:
            pl.semaphore_signal(semaphore, inc=1, device_id=peer, device_id_type=MESH)
        pl.semaphore_wait(semaphore, len(peers))


class Lane:
    def __init__(self):
        self.count = 0
        self.send = self.recv = None

    def take(self, n=1):
        first = self.count
        self.count += n
        return first


def remote(lane, index, src, dst, device):
    return pltpu.make_async_remote_copy(
        src_ref=src, dst_ref=dst, send_sem=lane.send.at[index], recv_sem=lane.recv.at[index],
        device_id=device, device_id_type=MESH)


class Gather:
    def __init__(self, geo, lane):
        self.geo, self.lane = geo, lane
        self.zs = lane.take(geo.Z - 1)
        self.second = lane.take(max(geo.X, geo.Y) - 1)
        self.third = lane.take(max(geo.X, geo.Y) - 1)
        self.core = lane.take()

    def bind(self, own, full):
        self.own, self.full = own, full

    def z_copies(self, incoming):
        g = self.geo
        z, x, y, c = g.me()
        for k in range(1, g.Z):
            if incoming:
                slot = self.full.at[(z + g.Z - k) % g.Z, x, y, c]
                yield remote(self.lane, self.zs + k - 1, slot, slot, g.device((z + k) % g.Z, x, y, c))
            else:
                yield remote(self.lane, self.zs + k - 1, self.own, self.full.at[z, x, y, c],
                             g.device((z + k) % g.Z, x, y, c))

    def axis_copies(self, phase, order, incoming):
        g = self.geo
        z, x, y, c = g.me()
        base = self.second if phase == 2 else self.third
        along_x = (phase == 2) == (order == 0)
        size = g.X if along_x else g.Y
        for k in range(1, size):
            if along_x:
                source = (x + g.X - k) % g.X if incoming else x
                device = g.device(z, (x + k) % g.X, y, c)
                slot = self.full.at[:, source, y, c] if phase == 2 else self.full.at[:, source, :, c]
            else:
                source = (y + g.Y - k) % g.Y if incoming else y
                device = g.device(z, x, (y + k) % g.Y, c)
                slot = self.full.at[:, x, source, c] if phase == 2 else self.full.at[:, :, source, c]
            yield remote(self.lane, base + k - 1, slot, slot, device)

    def both(self, action):
        c = self.geo.me()[3]
        for order in range(2):
            @pl.when(c == order)
            def _():
                action(order)

    def step(self, n):
        g = self.geo
        z, x, y, c = g.me()
        if n == 0:
            for copy in self.z_copies(False):
                copy.start()
            self.full[z, x, y, c] = self.own[...]
        elif n == 1:
            for copy in self.z_copies(True):
                copy.wait_recv()
            self.both(lambda order: [copy.start() for copy in self.axis_copies(2, order, False)])
        elif n == 2:
            def go(order):
                for copy in self.axis_copies(2, order, True):
                    copy.wait_recv()
                for copy in self.axis_copies(3, order, False):
                    copy.start()
            self.both(go)
        elif n == 3:
            def go(order):
                for copy in self.axis_copies(3, order, True):
                    copy.wait_recv()
            self.both(go)
            slot = self.full.at[:, :, :, c]
            remote(self.lane, self.core, slot, slot, g.device(z, x, y, 1 - c)).start()
        else:
            slot = self.full.at[:, :, :, 1 - c]
            remote(self.lane, self.core, slot, slot, g.device(z, x, y, 1 - c)).wait_recv()

    def drain(self):
        g = self.geo
        z, x, y, c = g.me()
        for copy in self.z_copies(False):
            copy.wait_send()

        def go(order):
            for phase in (2, 3):
                for copy in self.axis_copies(phase, order, False):
                    copy.wait_send()
        self.both(go)
        slot = self.full.at[:, :, :, c]
        remote(self.lane, self.core, slot, slot, g.device(z, x, y, 1 - c)).wait_send()


class Scatter:
    def __init__(self, geo, lane):
        self.geo, self.lane = geo, lane
        self.core = lane.take()
        self.first = lane.take(max(geo.X, geo.Y) - 1)
        self.second = lane.take(max(geo.X, geo.Y) - 1)
        self.zs = lane.take(geo.Z - 1)

    @staticmethod
    def scratch(geo, rows, width):
        wide = max(geo.X, geo.Y)
        kind = jnp.bfloat16
        return [
            pltpu.VMEM((geo.Z, geo.X, geo.Y, rows, width), kind),
            pltpu.VMEM((wide - 1, geo.Z, wide, rows, width), kind),
            pltpu.VMEM((wide - 1, geo.Z, rows, width), kind),
            pltpu.VMEM((geo.Z - 1, rows, width), kind),
        ]

    def bind(self, part, out, buffers):
        self.part, self.out = part, out
        self.rc, self.ra, self.rb, self.rz = buffers

    def both(self, action):
        c = self.geo.me()[3]
        for order in range(2):
            @pl.when(c == order)
            def _():
                action(order)

    def core_copy(self):
        z, x, y, c = self.geo.me()
        return remote(self.lane, self.core, self.part.at[:, :, :, 1 - c], self.rc,
                      self.geo.device(z, x, y, 1 - c))

    def axis_copies(self, phase, order):
        g = self.geo
        z, x, y, c = g.me()
        base = self.first if phase == 1 else self.second
        along_x = (phase == 1) == (order == 1)
        for k in range(1, g.X if along_x else g.Y):
            if along_x:
                far = (x + k) % g.X
                device = g.device(z, far, y, c)
                src = self.part.at[:, far, :, c] if phase == 1 else self.part.at[:, far, y, c]
                dst = self.ra.at[k - 1, :, pl.ds(0, g.Y)] if phase == 1 else self.rb.at[k - 1]
            else:
                far = (y + k) % g.Y
                device = g.device(z, x, far, c)
                src = self.part.at[:, :, far, c] if phase == 1 else self.part.at[:, x, far, c]
                dst = self.ra.at[k - 1, :, pl.ds(0, g.X)] if phase == 1 else self.rb.at[k - 1]
            yield remote(self.lane, base + k - 1, src, dst, device)

    def z_copies(self):
        g = self.geo
        z, x, y, c = g.me()
        for k in range(1, g.Z):
            far = (z + k) % g.Z
            yield remote(self.lane, self.zs + k - 1, self.part.at[far, x, y, c], self.rz.at[k - 1],
                         g.device(far, x, y, c))

    def step(self, n):
        g = self.geo
        z, x, y, c = g.me()
        wide = lambda ref: ref.astype(jnp.float32)
        if n == 0:
            self.core_copy().start()
        elif n == 1:
            self.core_copy().wait_recv()

            def add(i, _):
                total = wide(self.part[i, :, :, c]) + wide(self.rc[i])
                self.part[i, :, :, c] = total.astype(jnp.bfloat16)
                return 0
            lax.fori_loop(0, g.Z, add, 0)
            self.both(lambda order: [copy.start() for copy in self.axis_copies(1, order)])
        elif n == 2:
            def go(order):
                copies = list(self.axis_copies(1, order))
                for copy in copies:
                    copy.wait_recv()
                count = len(copies)
                if order == 0:
                    def add(i, _):
                        total = wide(self.part[i, :, y, c])
                        for k in range(count):
                            total += wide(self.ra[k, i, : g.X])
                        self.part[i, :, y, c] = total.astype(jnp.bfloat16)
                        return 0
                else:
                    def add(i, _):
                        total = wide(self.part[i, x, :, c])
                        for k in range(count):
                            total += wide(self.ra[k, i, : g.Y])
                        self.part[i, x, :, c] = total.astype(jnp.bfloat16)
                        return 0
                lax.fori_loop(0, g.Z, add, 0)
                for copy in self.axis_copies(2, order):
                    copy.start()
            self.both(go)
        elif n == 3:
            def go(order):
                copies = list(self.axis_copies(2, order))
                for copy in copies:
                    copy.wait_recv()

                def add(i, _):
                    total = wide(self.part[i, x, y, c])
                    for k in range(len(copies)):
                        total += wide(self.rb[k, i])
                    self.part[i, x, y, c] = total.astype(jnp.bfloat16)
                    return 0
                lax.fori_loop(0, g.Z, add, 0)
            self.both(go)
            for copy in self.z_copies():
                copy.start()
        else:
            total = wide(self.part[z, x, y, c])
            for k, copy in enumerate(self.z_copies()):
                copy.wait_recv()
                total += wide(self.rz[k])
            self.out[...] = total

    def drain(self):
        self.core_copy().wait_send()

        def go(order):
            for phase in (1, 2):
                for copy in self.axis_copies(phase, order):
                    copy.wait_send()
        self.both(go)
        for copy in self.z_copies():
            copy.wait_send()


def run_steps(tasks):
    for n in range(5 + len(tasks) - 1):
        for i, task in enumerate(tasks):
            if 0 <= n - i < 5:
                task.step(n - i)
    for task in tasks:
        task.drain()


def gather_all(geo, shards):
    lane = Lane()
    tasks = [Gather(geo, lane) for _ in shards]
    n = len(shards)

    def body(*refs):
        own, full = refs[:n], refs[n:2 * n]
        lane.send, lane.recv = refs[2 * n], refs[2 * n + 1]
        for task, a, b in zip(tasks, own, full):
            task.bind(a, b)
        geo.barrier()
        run_steps(tasks)

    vmem = pl.BlockSpec(memory_space=pltpu.VMEM)
    return pl.pallas_call(
        body,
        out_shape=[jax.ShapeDtypeStruct((geo.Z, geo.X, geo.Y, 2) + s.shape, s.dtype) for s in shards],
        in_specs=[vmem] * n, out_specs=[vmem] * n,
        scratch_shapes=[pltpu.SemaphoreType.DMA((lane.count,)), pltpu.SemaphoreType.DMA((lane.count,))],
        compiler_params=pltpu.CompilerParams(collective_id=0, has_side_effects=True, vmem_limit_bytes=56 << 20),
    )(*shards)


def scatter_all(geo, parts):
    lane = Lane()
    tasks = [Scatter(geo, lane) for _ in parts]
    n = len(parts)

    def body(*refs):
        part, out = refs[:n], refs[n:2 * n]
        held = refs[2 * n:3 * n]
        buffers = refs[3 * n:7 * n]
        lane.send, lane.recv = refs[7 * n], refs[7 * n + 1]
        for i, task in enumerate(tasks):
            held[i][...] = part[i][...]
            task.bind(held[i], out[i], buffers[4 * i:4 * i + 4])
        geo.barrier()
        run_steps(tasks)

    vmem = pl.BlockSpec(memory_space=pltpu.VMEM)
    scratch = [pltpu.VMEM(p.shape, p.dtype) for p in parts]
    for p in parts:
        scratch += Scatter.scratch(geo, p.shape[-2], p.shape[-1])
    scratch += [pltpu.SemaphoreType.DMA((lane.count,)), pltpu.SemaphoreType.DMA((lane.count,))]
    return pl.pallas_call(
        body,
        out_shape=[jax.ShapeDtypeStruct(p.shape[-2:], jnp.float32) for p in parts],
        in_specs=[vmem] * n, out_specs=[vmem] * n,
        scratch_shapes=scratch,
        compiler_params=pltpu.CompilerParams(collective_id=1, has_side_effects=True, vmem_limit_bytes=56 << 20),
    )(*parts)


epsilon = 1e-05
finest_precision = lax.Precision.HIGHEST


def prefix(array, axis, combine, identity):
    count, here = (lax.axis_size(axis), lax.axis_index(axis))
    everything = jax.tree.map(
        lambda part, kind: lax.all_gather(part.astype(kind), axis),
        array,
        (jnp.bfloat16, jnp.bfloat16),
    )
    start = jax.tree.map(
        lambda part, zero: jnp.broadcast_to(jnp.asarray(zero, part.dtype), part.shape),
        array,
        identity,
    )

    def hop(k, before):
        reached = k < here
        new = combine(
            before, jax.tree.map(lambda part, own: part[k].astype(own.dtype), everything, array)
        )
        return jax.tree.map(lambda a, b: jnp.where(reached, a, b), new, before)

    return lax.fori_loop(0, count, hop, start)


def prefix_2(array, axis, join, neutral):
    count = lax.axis_size(axis)
    place = lax.axis_index(axis)
    ahead = count - 1 - place
    gathered = jax.tree.map(
        lambda a, kind: lax.all_gather(a.astype(kind), axis),
        array,
        jax.tree.map(lambda a: jnp.bfloat16 if a.dtype == jnp.float32 else a.dtype, array),
    )
    state = jax.tree.map(lambda a, e: jnp.zeros_like(a) + jnp.asarray(e, a.dtype), array, neutral)

    def one(hop, state):
        source = count - 1 - hop
        return join(
            state,
            jax.tree.map(
                lambda a, own: lax.dynamic_index_in_dim(a, source, 0, False).astype(own.dtype),
                gathered,
                array,
            ),
        )

    return lax.fori_loop(0, ahead, one, state)


def layer_norm(value_rows, norm_gain, norm_shift):
    center = jnp.mean(value_rows, axis=-1, keepdims=True)
    centred = value_rows - center
    spread = jnp.mean(centred * centred, axis=-1, keepdims=True)
    return centred * lax.rsqrt(spread + epsilon) * norm_gain + norm_shift


def gelu_tanh(value_rows):
    return jax.nn.gelu(value_rows, approximate=True)


def add_pair(earlier, later_term):
    return (earlier[0] + later_term[0], earlier[1] + later_term[1])


def causal_mask(length):
    positions = jnp.arange(length)
    return (positions[:, None] >= positions[None, :]).astype(jnp.float32)


def favor_map(proj_low, matrix, feature_scale):
    raw_proj = jnp.einsum("rhd,dm->rhm", proj_low, matrix, preferred_element_type=jnp.float32)
    projection = proj_low.astype(jnp.float32)
    half_norm = (
        0.5
        * feature_scale
        * feature_scale
        * jnp.sum(projection * projection, axis=-1, keepdims=True)
    )
    return jnp.exp(feature_scale * raw_proj - half_norm) / math.sqrt(matrix.shape[1])


def favor_back(map_grad, favor_value, proj_low, matrix, feature_scale):
    log_grad = map_grad * favor_value
    raw_grad = (feature_scale * log_grad).astype(jnp.bfloat16)
    projection = proj_low.astype(jnp.float32)
    through = jnp.einsum("rhm,dm->rhd", raw_grad, matrix, preferred_element_type=jnp.float32)
    return (
        through
        - feature_scale * feature_scale * jnp.sum(log_grad, axis=-1, keepdims=True) * projection
    )


def front(token_block, matrix, params):
    inputs = token_block.astype(jnp.float32)
    length = inputs.shape[0]
    normed = layer_norm(
        inputs, params[7].astype(jnp.float32), params[8].astype(jnp.float32)
    ).astype(jnp.bfloat16)
    mixed = jnp.dot(normed, params[0], preferred_element_type=jnp.float32).astype(jnp.bfloat16)
    head_parts = mixed.reshape(length, 3, H, DH)
    feature_scale = DH ** (-0.25)
    query_features = favor_map(head_parts[:, 0], matrix, feature_scale)
    key_features = favor_map(head_parts[:, 1], matrix, feature_scale)
    query_reduced = query_features.astype(jnp.bfloat16)
    key_reduced = key_features.astype(jnp.bfloat16)
    value_rows = head_parts[:, 2]
    block_local_state = jnp.einsum(
        "nqo,nqi->qoi", key_reduced, value_rows, preferred_element_type=jnp.float32
    )
    local_sum = jnp.sum(key_reduced.astype(jnp.float32), axis=0)
    return (
        inputs,
        normed,
        head_parts,
        query_features,
        key_features,
        query_reduced,
        key_reduced,
        value_rows,
        block_local_state,
        local_sum,
    )


def attend(query_reduced, key_reduced, value_rows, running_prefix_state, norm_sum):
    causal = causal_mask(query_reduced.shape[0])
    scores = (
        jnp.einsum("ihm,jhm->hij", query_reduced, key_reduced, preferred_element_type=jnp.float32)
        * causal[None]
    )
    denominator = jnp.sum(scores, axis=-1).T + jnp.einsum(
        "ihm,hm->ih", query_reduced.astype(jnp.float32), norm_sum, precision=finest_precision
    )
    attention_numerator = jnp.einsum(
        "hij,jhd->ihd", scores.astype(jnp.bfloat16), value_rows, preferred_element_type=jnp.float32
    )
    attention_numerator = attention_numerator + jnp.einsum(
        "plq,lqu->plu",
        query_reduced,
        running_prefix_state.astype(jnp.bfloat16),
        preferred_element_type=jnp.float32,
    )
    return (attention_numerator / denominator[:, :, None], attention_numerator, denominator)


def upper(inputs, output, params):
    length = output.shape[0]
    attended = output.reshape(length, -1).astype(jnp.bfloat16)
    middle = (
        inputs
        + jnp.dot(attended, params[1], preferred_element_type=jnp.float32)
        + params[2].astype(jnp.float32)
    )
    return (attended, middle)


def feed(middle, params):
    normed_two = layer_norm(
        middle, params[9].astype(jnp.float32), params[10].astype(jnp.float32)
    ).astype(jnp.bfloat16)
    hidden = jnp.dot(normed_two, params[3], preferred_element_type=jnp.float32) + params[4].astype(
        jnp.float32
    )
    active = gelu_tanh(hidden).astype(jnp.bfloat16)
    return (
        middle
        + jnp.dot(active, params[5], preferred_element_type=jnp.float32)
        + params[6].astype(jnp.float32)
    )


def upper_back(token_block, upstream, matrix, params, block_carry):
    pieces = front(token_block, matrix, params)
    (
        inputs,
        normed,
        head_parts,
        query_features,
        key_features,
        query_reduced,
        key_reduced,
        value_rows,
        block_local_state,
        local_sum,
    ) = pieces
    running_prefix_state, norm_sum = block_carry
    output, attention_numerator, denominator = attend(
        query_reduced, key_reduced, value_rows, running_prefix_state, norm_sum
    )
    attended, middle = upper(inputs, output, params)
    normed_float, second_pull = jax.vjp(
        layer_norm, middle, params[9].astype(jnp.float32), params[10].astype(jnp.float32)
    )
    normed_two = normed_float.astype(jnp.bfloat16)
    hidden = jnp.dot(normed_two, params[3], preferred_element_type=jnp.float32) + params[4].astype(
        jnp.float32
    )
    active_float, gelu_pull = jax.vjp(gelu_tanh, hidden)
    active = active_float.astype(jnp.bfloat16)
    stored = {"front": pieces, "carry": block_carry, "middle": middle}
    down_term = upstream.astype(jnp.bfloat16)
    stored["down"] = jnp.einsum("rf,rd->fd", active, down_term, preferred_element_type=jnp.float32)
    stored["down_bias"] = jnp.sum(upstream, axis=0)
    active_grad = jnp.einsum("rd,fd->rf", down_term, params[5], preferred_element_type=jnp.float32)
    (hidden_grad,) = gelu_pull(active_grad)
    up_term = hidden_grad.astype(jnp.bfloat16)
    stored["up"] = jnp.einsum("rd,rf->df", normed_two, up_term, preferred_element_type=jnp.float32)
    stored["up_bias"] = jnp.sum(hidden_grad, axis=0)
    normed_two_grad = jnp.einsum(
        "rf,df->rd", up_term, params[3], preferred_element_type=jnp.float32
    )
    middle_part, gain_two_grad, shift_two_grad = second_pull(normed_two_grad)
    stored["gain_two"] = gain_two_grad
    stored["shift_two"] = shift_two_grad
    middle_grad = upstream + middle_part
    stored["middle_grad"] = middle_grad
    out_term = middle_grad.astype(jnp.bfloat16)
    stored["out"] = jnp.einsum("re,rd->ed", attended, out_term, preferred_element_type=jnp.float32)
    stored["out_bias"] = jnp.sum(middle_grad, axis=0)
    attended_grad = jnp.einsum(
        "rd,ed->re", out_term, params[1], preferred_element_type=jnp.float32
    ).reshape(output.shape)
    numerator_grad = (attended_grad / denominator[:, :, None]).astype(jnp.bfloat16)
    denom_grad = -jnp.sum(attended_grad * attention_numerator, axis=-1) / (
        denominator * denominator
    )
    stored["numer_grad"] = numerator_grad
    stored["denom_grad"] = denom_grad
    stored["state_grad"] = jnp.einsum(
        "jfp,jfl->fpl", query_reduced, numerator_grad, preferred_element_type=jnp.float32
    )
    stored["sum_grad"] = jnp.einsum(
        "ih,ihm->hm", denom_grad, query_reduced.astype(jnp.float32), precision=finest_precision
    )
    return stored


def lower_back(stored, later_part, matrix, params):
    (
        inputs,
        normed,
        head_parts,
        query_features,
        key_features,
        query_reduced,
        key_reduced,
        value_rows,
        block_local_state,
        local_sum,
    ) = stored["front"]
    running_prefix_state, norm_sum = stored["carry"]
    state_later, sum_later = later_part
    numerator_grad = stored["numer_grad"]
    denom_grad = stored["denom_grad"]
    length = inputs.shape[0]
    causal = causal_mask(length)
    scores = (
        jnp.einsum("ihm,jhm->hij", query_reduced, key_reduced, preferred_element_type=jnp.float32)
        * causal[None]
    )
    scores_grad = jnp.einsum(
        "ihd,jhd->hij", numerator_grad, value_rows, preferred_element_type=jnp.float32
    )
    score_term = ((scores_grad + denom_grad.T[:, :, None]) * causal[None]).astype(jnp.bfloat16)
    later_reduced = state_later.astype(jnp.bfloat16)
    query_grad = jnp.einsum(
        "hij,jhm->ihm", score_term, key_reduced, preferred_element_type=jnp.float32
    )
    query_grad = query_grad + jnp.einsum(
        "gvw,vcw->gvc",
        numerator_grad,
        running_prefix_state.astype(jnp.bfloat16),
        preferred_element_type=jnp.float32,
    )
    query_grad = query_grad + denom_grad[:, :, None] * norm_sum[None]
    key_grad = jnp.einsum(
        "hij,ihm->jhm", score_term, query_reduced, preferred_element_type=jnp.float32
    )
    key_grad = key_grad + jnp.einsum(
        "prc,rqc->prq", value_rows, later_reduced, preferred_element_type=jnp.float32
    )
    key_grad = key_grad + sum_later[None]
    value_grad = jnp.einsum(
        "hij,ihd->jhd",
        scores.astype(jnp.bfloat16),
        numerator_grad,
        preferred_element_type=jnp.float32,
    )
    value_grad = value_grad + jnp.einsum(
        "qsa,saw->qsw", key_reduced, later_reduced, preferred_element_type=jnp.float32
    )
    feature_scale = DH ** (-0.25)
    query_proj = favor_back(query_grad, query_features, head_parts[:, 0], matrix, feature_scale)
    key_proj = favor_back(key_grad, key_features, head_parts[:, 1], matrix, feature_scale)
    mixed_grad = (
        jnp.stack([query_proj, key_proj, value_grad], axis=1)
        .reshape(length, -1)
        .astype(jnp.bfloat16)
    )
    input_part = jnp.einsum("rd,re->de", normed, mixed_grad, preferred_element_type=jnp.float32)
    normed_grad = jnp.einsum("re,de->rd", mixed_grad, params[0], preferred_element_type=jnp.float32)
    _, first_pull = jax.vjp(
        layer_norm, inputs, params[7].astype(jnp.float32), params[8].astype(jnp.float32)
    )
    inputs_part, gain_one_grad, shift_one_grad = first_pull(normed_grad)
    return (stored["middle_grad"] + inputs_part, input_part, gain_one_grad, shift_one_grad)


def fused(geo, args):
    (tokens, feature_matrix, input_weight, output_weight, output_bias, up_weight, up_bias, down_weight,
     down_bias, first_gain, first_shift, second_gain, second_shift, cotangent) = args
    small = jnp.stack([output_bias, down_bias, first_gain, first_shift, second_gain, second_shift], axis=1)
    small = jnp.concatenate([small, up_bias.reshape(-1, 4), jnp.zeros((small.shape[0], 118), small.dtype)], axis=1)
    full = gather_all(geo, [small, input_weight, output_weight, up_weight, down_weight])
    small, wi, wo, wu, wd = [f.reshape(-1, f.shape[-1]) for f in full]
    params = (wi, wo, small[:, 0], wu, small[:, 6:10].reshape(-1), wd, small[:, 1], small[:, 2], small[:, 3],
              small[:, 4], small[:, 5])
    micros = tokens.shape[0]
    carries, results, stored_list, later_list = [], [], [], []
    for m in range(micros):
        pieces = front(tokens[m], feature_matrix, params)
        carry = prefix((pieces[8], pieces[9]), "seq", add_pair, (jnp.zeros_like(pieces[8]), jnp.zeros_like(pieces[9])))
        stored = upper_back(tokens[m], cotangent[m].astype(jnp.float32), feature_matrix, params, carry)
        results.append(feed(stored["middle"], params))
        stored_list.append(stored)
        later_list.append(prefix_2((stored["state_grad"], stored["sum_grad"]), "seq", add_pair,
                                   (jnp.zeros_like(stored["state_grad"]), jnp.zeros_like(stored["sum_grad"]))))
    names = ["out", "out_bias", "up", "up_bias", "down", "down_bias", "gain_two", "shift_two"]
    upper = [sum(s[name] for s in stored_list) for name in names]
    token_grads, lower = [], None
    for m in range(micros):
        tg, *parts = lower_back(stored_list[m], later_list[m], feature_matrix, params)
        token_grads.append(tg)
        lower = parts if lower is None else [a + b for a, b in zip(lower, parts)]
    shape = (geo.Z, geo.X, geo.Y, 2)
    cut = lambda a: a.astype(jnp.bfloat16).reshape(shape + (-1, a.shape[-1]))
    vec = jnp.stack([upper[1], upper[5], lower[1], lower[2], upper[6], upper[7]], axis=1)
    vec = jnp.concatenate([vec, upper[3].reshape(-1, 4), jnp.zeros((vec.shape[0], 118), jnp.float32)], axis=1)
    down, up, out, inp, vec = scatter_all(geo, [cut(upper[4]), cut(upper[2]), cut(upper[0]), cut(lower[0]), cut(vec)])
    return (jnp.stack(results), jnp.stack(token_grads), inp, out, vec[:, 0], up, vec[:, 6:10].reshape(-1), down,
            vec[:, 1], vec[:, 2], vec[:, 3], vec[:, 4], vec[:, 5])


def local(
    tokens,
    feature_matrix,
    input_weight,
    output_weight,
    output_bias,
    up_weight,
    up_bias,
    down_weight,
    down_bias,
    first_gain,
    first_shift,
    second_gain,
    second_shift,
    cotangent,
):
    params = (
        lax.all_gather(input_weight, ("dp", "seq"), axis=0, tiled=True),
        lax.all_gather(output_weight, ("dp", "seq"), axis=0, tiled=True),
        lax.all_gather(output_bias, ("dp", "seq"), axis=0, tiled=True),
        lax.all_gather(up_weight, ("dp", "seq"), axis=0, tiled=True),
        lax.all_gather(up_bias, ("dp", "seq"), axis=0, tiled=True),
        lax.all_gather(down_weight, ("dp", "seq"), axis=0, tiled=True),
        lax.all_gather(down_bias, ("dp", "seq"), axis=0, tiled=True),
        lax.all_gather(first_gain, ("dp", "seq"), axis=0, tiled=True),
        lax.all_gather(first_shift, ("dp", "seq"), axis=0, tiled=True),
        lax.all_gather(second_gain, ("dp", "seq"), axis=0, tiled=True),
        lax.all_gather(second_shift, ("dp", "seq"), axis=0, tiled=True),
    )
    micros = tokens.shape[0]
    fronts = []
    carries = []
    for micro_step in range(micros):
        pieces = front(tokens[micro_step], feature_matrix, params)
        fronts.append(pieces)
        carries.append(
            prefix(
                (pieces[8], pieces[9]),
                "seq",
                add_pair,
                (jnp.zeros_like(pieces[8]), jnp.zeros_like(pieces[9])),
            )
        )
    results = []
    for micro_step in range(micros):
        pieces = fronts[micro_step]
        running_prefix_state, norm_sum = carries[micro_step]
        output = attend(pieces[5], pieces[6], pieces[7], running_prefix_state, norm_sum)[0]
        attended, middle = upper(pieces[0], output, params)
        results.append(feed(middle, params))
    result = jnp.stack(results)
    back_params = (
        lax.all_gather(input_weight, ("dp", "seq"), axis=0, tiled=True),
        lax.all_gather(output_weight, ("dp", "seq"), axis=0, tiled=True),
        lax.all_gather(output_bias, ("dp", "seq"), axis=0, tiled=True),
        lax.all_gather(up_weight, ("dp", "seq"), axis=0, tiled=True),
        lax.all_gather(up_bias, ("dp", "seq"), axis=0, tiled=True),
        lax.all_gather(down_weight, ("dp", "seq"), axis=0, tiled=True),
        lax.all_gather(down_bias, ("dp", "seq"), axis=0, tiled=True),
        lax.all_gather(first_gain, ("dp", "seq"), axis=0, tiled=True),
        lax.all_gather(first_shift, ("dp", "seq"), axis=0, tiled=True),
        lax.all_gather(second_gain, ("dp", "seq"), axis=0, tiled=True),
        lax.all_gather(second_shift, ("dp", "seq"), axis=0, tiled=True),
    )
    stored_list = []
    later_list = []
    for micro_step in range(micros):
        stored = upper_back(
            tokens[micro_step],
            cotangent[micro_step].astype(jnp.float32),
            feature_matrix,
            back_params,
            carries[micro_step],
        )
        stored_list.append(stored)
        later_list.append(
            prefix_2(
                (stored["state_grad"], stored["sum_grad"]),
                "seq",
                add_pair,
                (jnp.zeros_like(stored["state_grad"]), jnp.zeros_like(stored["sum_grad"])),
            )
        )
    upper_names = ["out", "out_bias", "up", "up_bias", "down", "down_bias", "gain_two", "shift_two"]
    upper_totals = [stored_list[0][name] for name in upper_names]
    micro_step = 1
    upper_totals = [
        total + stored_list[micro_step][name] for total, name in zip(upper_totals, upper_names)
    ]
    token_grads = []
    lower_totals = None
    for micro_step in range(micros):
        stored = stored_list[micro_step]
        tokens_part, input_part, gain_part, shift_part = lower_back(
            stored, later_list[micro_step], feature_matrix, back_params
        )
        token_grads.append(tokens_part)
        lower_parts = (input_part, gain_part, shift_part)
        if micro_step == 0:
            lower_totals = lower_parts
        else:
            lower_totals = jax.tree.map(jnp.add, lower_totals, lower_parts)
    shares = (
        lax.psum_scatter(lower_totals[0], ("dp", "seq"), scatter_dimension=0, tiled=True),
        lax.psum_scatter(upper_totals[0], ("dp", "seq"), scatter_dimension=0, tiled=True),
        lax.psum_scatter(upper_totals[1], ("dp", "seq"), scatter_dimension=0, tiled=True),
        lax.psum_scatter(upper_totals[2], ("dp", "seq"), scatter_dimension=0, tiled=True),
        lax.psum_scatter(upper_totals[3], ("dp", "seq"), scatter_dimension=0, tiled=True),
        lax.psum_scatter(upper_totals[4], ("dp", "seq"), scatter_dimension=0, tiled=True),
        lax.psum_scatter(upper_totals[5], ("dp", "seq"), scatter_dimension=0, tiled=True),
        lax.psum_scatter(lower_totals[1], ("dp", "seq"), scatter_dimension=0, tiled=True),
        lax.psum_scatter(lower_totals[2], ("dp", "seq"), scatter_dimension=0, tiled=True),
        lax.psum_scatter(upper_totals[6], ("dp", "seq"), scatter_dimension=0, tiled=True),
        lax.psum_scatter(upper_totals[7], ("dp", "seq"), scatter_dimension=0, tiled=True),
    )
    return (
        result,
        jnp.stack(token_grads),
        shares[0],
        shares[1],
        shares[2],
        shares[3],
        shares[4],
        shares[5],
        shares[6],
        shares[7],
        shares[8],
        shares[9],
        shares[10],
    )


def solution(mesh):
    in_specs = (
        P("dp", "seq", None),
        P(),
        P(("dp", "seq"), None),
        P(("dp", "seq"), None),
        P(("dp", "seq")),
        P(("dp", "seq"), None),
        P(("dp", "seq")),
        P(("dp", "seq"), None),
        P(("dp", "seq")),
        P(("dp", "seq")),
        P(("dp", "seq")),
        P(("dp", "seq")),
        P(("dp", "seq")),
        P("dp", "seq", None),
    )
    out_specs = (
        P("dp", "seq", None),
        P("dp", "seq", None),
        P(("dp", "seq"), None),
        P(("dp", "seq"), None),
        P(("dp", "seq")),
        P(("dp", "seq"), None),
        P(("dp", "seq")),
        P(("dp", "seq"), None),
        P(("dp", "seq")),
        P(("dp", "seq")),
        P(("dp", "seq")),
        P(("dp", "seq")),
        P(("dp", "seq")),
    )
    geo = Geometry(mesh)
    rows = 512 // (mesh.shape["dp"] * mesh.shape["seq"])
    if rows % 16 == 0:
        def body(*args):
            return fused(geo, args)
    else:
        body = local
    return jax.shard_map(body, mesh=mesh, in_specs=in_specs, out_specs=out_specs, check_vma=False)
```

```python
import functools
import math

import jax
import jax.numpy as jnp
from jax import lax
from jax.sharding import PartitionSpec as P

H = 8
DH = 64

from jax.experimental import pallas as pl
from jax.experimental.pallas import tpu as pltpu

MESH = pl.DeviceIdType.MESH


class Geometry:
    def __init__(self, mesh):
        dp, seq = mesh.shape["dp"], mesh.shape["seq"]
        self.C = 2
        self.Y = seq // 2
        self.X = 1 << ((dp.bit_length() - 1) // 2)
        self.Z = dp // self.X

    def me(self):
        dp, seq = lax.axis_index("dp"), lax.axis_index("seq")
        return dp // self.X, dp % self.X, seq // 2, seq % 2

    def device(self, z, x, y, c):
        return (z * self.X + x, y * 2 + c)

    def barrier(self):
        z, x, y, c = self.me()
        peers = [self.device(z, x, y, 1 - c)]
        peers += [self.device((z + k) % self.Z, x, y, c) for k in range(1, self.Z)]
        peers += [self.device(z, (x + k) % self.X, y, c) for k in range(1, self.X)]
        peers += [self.device(z, x, (y + k) % self.Y, c) for k in range(1, self.Y)]
        semaphore = pltpu.get_barrier_semaphore()
        for peer in peers:
            pl.semaphore_signal(semaphore, inc=1, device_id=peer, device_id_type=MESH)
        pl.semaphore_wait(semaphore, len(peers))


class Lane:
    def __init__(self):
        self.count = 0
        self.send = self.recv = None

    def take(self, n=1):
        first = self.count
        self.count += n
        return first


def remote(lane, index, src, dst, device):
    return pltpu.make_async_remote_copy(
        src_ref=src, dst_ref=dst, send_sem=lane.send.at[index], recv_sem=lane.recv.at[index],
        device_id=device, device_id_type=MESH)


class Gather:
    def __init__(self, geo, lane):
        self.geo, self.lane = geo, lane
        self.begin = lane.count
        self.zs = lane.take(geo.Z - 1)
        self.second = lane.take(max(geo.X, geo.Y) - 1)
        self.third = lane.take(max(geo.X, geo.Y) - 1)
        self.core = lane.take()

    indices = ("zs", "second", "third", "core")

    def shifted(self, by):
        other = object.__new__(type(self))
        other.geo, other.lane = self.geo, self.lane
        for name in self.indices:
            setattr(other, name, getattr(self, name) + by)
        return other

    def bind(self, own, full):
        self.own, self.full = own, full

    def z_copies(self, incoming):
        g = self.geo
        z, x, y, c = g.me()
        for k in range(1, g.Z):
            if incoming:
                slot = self.full.at[(z + g.Z - k) % g.Z, x, y, c]
                yield remote(self.lane, self.zs + k - 1, slot, slot, g.device((z + k) % g.Z, x, y, c))
            else:
                yield remote(self.lane, self.zs + k - 1, self.own, self.full.at[z, x, y, c],
                             g.device((z + k) % g.Z, x, y, c))

    def axis_copies(self, phase, order, incoming):
        g = self.geo
        z, x, y, c = g.me()
        base = self.second if phase == 2 else self.third
        along_x = (phase == 2) == (order == 0)
        size = g.X if along_x else g.Y
        for k in range(1, size):
            if along_x:
                source = (x + g.X - k) % g.X if incoming else x
                device = g.device(z, (x + k) % g.X, y, c)
                slot = self.full.at[:, source, y, c] if phase == 2 else self.full.at[:, source, :, c]
            else:
                source = (y + g.Y - k) % g.Y if incoming else y
                device = g.device(z, x, (y + k) % g.Y, c)
                slot = self.full.at[:, x, source, c] if phase == 2 else self.full.at[:, :, source, c]
            yield remote(self.lane, base + k - 1, slot, slot, device)

    def both(self, action):
        c = self.geo.me()[3]
        for order in range(2):
            @pl.when(c == order)
            def _():
                action(order)

    def step(self, n):
        g = self.geo
        z, x, y, c = g.me()
        if n == 0:
            for copy in self.z_copies(False):
                copy.start()
            self.full[z, x, y, c] = self.own[...]
        elif n == 1:
            for copy in self.z_copies(True):
                copy.wait_recv()
            self.both(lambda order: [copy.start() for copy in self.axis_copies(2, order, False)])
        elif n == 2:
            def go(order):
                for copy in self.axis_copies(2, order, True):
                    copy.wait_recv()
                for copy in self.axis_copies(3, order, False):
                    copy.start()
            self.both(go)
        elif n == 3:
            def go(order):
                for copy in self.axis_copies(3, order, True):
                    copy.wait_recv()
            self.both(go)
            slot = self.full.at[:, :, :, c]
            remote(self.lane, self.core, slot, slot, g.device(z, x, y, 1 - c)).start()
        else:
            slot = self.full.at[:, :, :, 1 - c]
            remote(self.lane, self.core, slot, slot, g.device(z, x, y, 1 - c)).wait_recv()

    def drain(self):
        g = self.geo
        z, x, y, c = g.me()
        for copy in self.z_copies(False):
            copy.wait_send()

        def go(order):
            for phase in (2, 3):
                for copy in self.axis_copies(phase, order, False):
                    copy.wait_send()
        self.both(go)
        slot = self.full.at[:, :, :, c]
        remote(self.lane, self.core, slot, slot, g.device(z, x, y, 1 - c)).wait_send()


class Scatter:
    def __init__(self, geo, lane):
        self.geo, self.lane = geo, lane
        self.begin = lane.count
        self.core = lane.take()
        self.first = lane.take(max(geo.X, geo.Y) - 1)
        self.second = lane.take(max(geo.X, geo.Y) - 1)
        self.zs = lane.take(geo.Z - 1)

    @staticmethod
    def scratch(geo, rows, width):
        wide = max(geo.X, geo.Y)
        kind = jnp.bfloat16
        return [
            pltpu.VMEM((geo.Z, geo.X, geo.Y, rows, width), kind),
            pltpu.VMEM((wide - 1, geo.Z, wide, rows, width), kind),
            pltpu.VMEM((wide - 1, geo.Z, rows, width), kind),
            pltpu.VMEM((geo.Z - 1, rows, width), kind),
        ]

    indices = ("core", "first", "second", "zs")

    def shifted(self, by):
        other = object.__new__(type(self))
        other.geo, other.lane = self.geo, self.lane
        for name in self.indices:
            setattr(other, name, getattr(self, name) + by)
        return other

    def bind(self, part, out, buffers):
        self.part, self.out = part, out
        self.rc, self.ra, self.rb, self.rz = buffers

    def both(self, action):
        c = self.geo.me()[3]
        for order in range(2):
            @pl.when(c == order)
            def _():
                action(order)

    def core_copy(self):
        z, x, y, c = self.geo.me()
        return remote(self.lane, self.core, self.part.at[:, :, :, 1 - c], self.rc,
                      self.geo.device(z, x, y, 1 - c))

    def axis_copies(self, phase, order):
        g = self.geo
        z, x, y, c = g.me()
        base = self.first if phase == 1 else self.second
        along_x = (phase == 1) == (order == 1)
        for k in range(1, g.X if along_x else g.Y):
            if along_x:
                far = (x + k) % g.X
                device = g.device(z, far, y, c)
                src = self.part.at[:, far, :, c] if phase == 1 else self.part.at[:, far, y, c]
                dst = self.ra.at[k - 1, :, pl.ds(0, g.Y)] if phase == 1 else self.rb.at[k - 1]
            else:
                far = (y + k) % g.Y
                device = g.device(z, x, far, c)
                src = self.part.at[:, :, far, c] if phase == 1 else self.part.at[:, x, far, c]
                dst = self.ra.at[k - 1, :, pl.ds(0, g.X)] if phase == 1 else self.rb.at[k - 1]
            yield remote(self.lane, base + k - 1, src, dst, device)

    def z_copies(self):
        g = self.geo
        z, x, y, c = g.me()
        for k in range(1, g.Z):
            far = (z + k) % g.Z
            yield remote(self.lane, self.zs + k - 1, self.part.at[far, x, y, c], self.rz.at[k - 1],
                         g.device(far, x, y, c))

    def step(self, n):
        g = self.geo
        z, x, y, c = g.me()
        wide = lambda ref: ref.astype(jnp.float32)
        if n == 0:
            self.core_copy().start()
        elif n == 1:
            self.core_copy().wait_recv()

            def add(i, _):
                total = wide(self.part[i, :, :, c]) + wide(self.rc[i])
                self.part[i, :, :, c] = total.astype(jnp.bfloat16)
                return 0
            lax.fori_loop(0, g.Z, add, 0)
            self.both(lambda order: [copy.start() for copy in self.axis_copies(1, order)])
        elif n == 2:
            def go(order):
                copies = list(self.axis_copies(1, order))
                for copy in copies:
                    copy.wait_recv()
                count = len(copies)
                if order == 0:
                    def add(i, _):
                        total = wide(self.part[i, :, y, c])
                        for k in range(count):
                            total += wide(self.ra[k, i, : g.X])
                        self.part[i, :, y, c] = total.astype(jnp.bfloat16)
                        return 0
                else:
                    def add(i, _):
                        total = wide(self.part[i, x, :, c])
                        for k in range(count):
                            total += wide(self.ra[k, i, : g.Y])
                        self.part[i, x, :, c] = total.astype(jnp.bfloat16)
                        return 0
                lax.fori_loop(0, g.Z, add, 0)
                for copy in self.axis_copies(2, order):
                    copy.start()
            self.both(go)
        elif n == 3:
            def go(order):
                copies = list(self.axis_copies(2, order))
                for copy in copies:
                    copy.wait_recv()

                def add(i, _):
                    total = wide(self.part[i, x, y, c])
                    for k in range(len(copies)):
                        total += wide(self.rb[k, i])
                    self.part[i, x, y, c] = total.astype(jnp.bfloat16)
                    return 0
                lax.fori_loop(0, g.Z, add, 0)
            self.both(go)
            for copy in self.z_copies():
                copy.start()
        else:
            total = wide(self.part[z, x, y, c])
            for k, copy in enumerate(self.z_copies()):
                copy.wait_recv()
                total += wide(self.rz[k])
            self.out[...] = total

    def drain(self):
        self.core_copy().wait_send()

        def go(order):
            for phase in (1, 2):
                for copy in self.axis_copies(phase, order):
                    copy.wait_send()
        self.both(go)
        for copy in self.z_copies():
            copy.wait_send()


epsilon = 1e-05
finest_precision = lax.Precision.HIGHEST


def prefix(array, axis, combine, identity):
    count, here = (lax.axis_size(axis), lax.axis_index(axis))
    everything = jax.tree.map(
        lambda part, kind: lax.all_gather(part.astype(kind), axis),
        array,
        (jnp.bfloat16, jnp.bfloat16),
    )
    start = jax.tree.map(
        lambda part, zero: jnp.broadcast_to(jnp.asarray(zero, part.dtype), part.shape),
        array,
        identity,
    )

    def hop(k, before):
        reached = k < here
        new = combine(
            before, jax.tree.map(lambda part, own: part[k].astype(own.dtype), everything, array)
        )
        return jax.tree.map(lambda a, b: jnp.where(reached, a, b), new, before)

    return lax.fori_loop(0, count, hop, start)


def prefix_2(array, axis, join, neutral):
    count = lax.axis_size(axis)
    place = lax.axis_index(axis)
    ahead = count - 1 - place
    gathered = jax.tree.map(
        lambda a, kind: lax.all_gather(a.astype(kind), axis),
        array,
        jax.tree.map(lambda a: jnp.bfloat16 if a.dtype == jnp.float32 else a.dtype, array),
    )
    state = jax.tree.map(lambda a, e: jnp.zeros_like(a) + jnp.asarray(e, a.dtype), array, neutral)

    def one(hop, state):
        source = count - 1 - hop
        return join(
            state,
            jax.tree.map(
                lambda a, own: lax.dynamic_index_in_dim(a, source, 0, False).astype(own.dtype),
                gathered,
                array,
            ),
        )

    return lax.fori_loop(0, ahead, one, state)


def layer_norm(value_rows, norm_gain, norm_shift):
    center = jnp.mean(value_rows, axis=-1, keepdims=True)
    centred = value_rows - center
    spread = jnp.mean(centred * centred, axis=-1, keepdims=True)
    return centred * lax.rsqrt(spread + epsilon) * norm_gain + norm_shift


def gelu_tanh(value_rows):
    return jax.nn.gelu(value_rows, approximate=True)


def add_pair(earlier, later_term):
    return (earlier[0] + later_term[0], earlier[1] + later_term[1])


def causal_mask(length):
    positions = jnp.arange(length)
    return (positions[:, None] >= positions[None, :]).astype(jnp.float32)


def favor_map(proj_low, matrix, feature_scale):
    raw_proj = jnp.einsum("rhd,dm->rhm", proj_low, matrix, preferred_element_type=jnp.float32)
    projection = proj_low.astype(jnp.float32)
    half_norm = (
        0.5
        * feature_scale
        * feature_scale
        * jnp.sum(projection * projection, axis=-1, keepdims=True)
    )
    return jnp.exp(feature_scale * raw_proj - half_norm) / math.sqrt(matrix.shape[1])


def favor_back(map_grad, favor_value, proj_low, matrix, feature_scale):
    log_grad = map_grad * favor_value
    raw_grad = (feature_scale * log_grad).astype(jnp.bfloat16)
    projection = proj_low.astype(jnp.float32)
    through = jnp.einsum("rhm,dm->rhd", raw_grad, matrix, preferred_element_type=jnp.float32)
    return (
        through
        - feature_scale * feature_scale * jnp.sum(log_grad, axis=-1, keepdims=True) * projection
    )


def front(token_block, matrix, params):
    inputs = token_block.astype(jnp.float32)
    length = inputs.shape[0]
    normed = layer_norm(
        inputs, params[7].astype(jnp.float32), params[8].astype(jnp.float32)
    ).astype(jnp.bfloat16)
    mixed = jnp.dot(normed, params[0], preferred_element_type=jnp.float32).astype(jnp.bfloat16)
    head_parts = mixed.reshape(length, 3, H, DH)
    feature_scale = DH ** (-0.25)
    query_features = favor_map(head_parts[:, 0], matrix, feature_scale)
    key_features = favor_map(head_parts[:, 1], matrix, feature_scale)
    query_reduced = query_features.astype(jnp.bfloat16)
    key_reduced = key_features.astype(jnp.bfloat16)
    value_rows = head_parts[:, 2]
    block_local_state = jnp.einsum(
        "nqo,nqi->qoi", key_reduced, value_rows, preferred_element_type=jnp.float32
    )
    local_sum = jnp.sum(key_reduced.astype(jnp.float32), axis=0)
    return (
        inputs,
        normed,
        head_parts,
        query_features,
        key_features,
        query_reduced,
        key_reduced,
        value_rows,
        block_local_state,
        local_sum,
    )


def attend(query_reduced, key_reduced, value_rows, running_prefix_state, norm_sum):
    causal = causal_mask(query_reduced.shape[0])
    scores = (
        jnp.einsum("ihm,jhm->hij", query_reduced, key_reduced, preferred_element_type=jnp.float32)
        * causal[None]
    )
    denominator = jnp.sum(scores, axis=-1).T + jnp.einsum(
        "ihm,hm->ih", query_reduced.astype(jnp.float32), norm_sum, precision=finest_precision
    )
    attention_numerator = jnp.einsum(
        "hij,jhd->ihd", scores.astype(jnp.bfloat16), value_rows, preferred_element_type=jnp.float32
    )
    attention_numerator = attention_numerator + jnp.einsum(
        "plq,lqu->plu",
        query_reduced,
        running_prefix_state.astype(jnp.bfloat16),
        preferred_element_type=jnp.float32,
    )
    return (attention_numerator / denominator[:, :, None], attention_numerator, denominator)


def upper(inputs, output, params):
    length = output.shape[0]
    attended = output.reshape(length, -1).astype(jnp.bfloat16)
    middle = (
        inputs
        + jnp.dot(attended, params[1], preferred_element_type=jnp.float32)
        + params[2].astype(jnp.float32)
    )
    return (attended, middle)


def feed(middle, params):
    normed_two = layer_norm(
        middle, params[9].astype(jnp.float32), params[10].astype(jnp.float32)
    ).astype(jnp.bfloat16)
    hidden = jnp.dot(normed_two, params[3], preferred_element_type=jnp.float32) + params[4].astype(
        jnp.float32
    )
    active = gelu_tanh(hidden).astype(jnp.bfloat16)
    return (
        middle
        + jnp.dot(active, params[5], preferred_element_type=jnp.float32)
        + params[6].astype(jnp.float32)
    )


def upper_back(token_block, upstream, matrix, params, block_carry):
    pieces = front(token_block, matrix, params)
    (
        inputs,
        normed,
        head_parts,
        query_features,
        key_features,
        query_reduced,
        key_reduced,
        value_rows,
        block_local_state,
        local_sum,
    ) = pieces
    running_prefix_state, norm_sum = block_carry
    output, attention_numerator, denominator = attend(
        query_reduced, key_reduced, value_rows, running_prefix_state, norm_sum
    )
    attended, middle = upper(inputs, output, params)
    normed_float, second_pull = jax.vjp(
        layer_norm, middle, params[9].astype(jnp.float32), params[10].astype(jnp.float32)
    )
    normed_two = normed_float.astype(jnp.bfloat16)
    hidden = jnp.dot(normed_two, params[3], preferred_element_type=jnp.float32) + params[4].astype(
        jnp.float32
    )
    active_float, gelu_pull = jax.vjp(gelu_tanh, hidden)
    active = active_float.astype(jnp.bfloat16)
    stored = {"front": pieces, "carry": block_carry}
    down_term = upstream.astype(jnp.bfloat16)
    stored["down"] = jnp.einsum("rf,rd->fd", active, down_term, preferred_element_type=jnp.float32)
    stored["down_bias"] = jnp.sum(upstream, axis=0)
    active_grad = jnp.einsum("rd,fd->rf", down_term, params[5], preferred_element_type=jnp.float32)
    (hidden_grad,) = gelu_pull(active_grad)
    up_term = hidden_grad.astype(jnp.bfloat16)
    stored["up"] = jnp.einsum("rd,rf->df", normed_two, up_term, preferred_element_type=jnp.float32)
    stored["up_bias"] = jnp.sum(hidden_grad, axis=0)
    normed_two_grad = jnp.einsum(
        "rf,df->rd", up_term, params[3], preferred_element_type=jnp.float32
    )
    middle_part, gain_two_grad, shift_two_grad = second_pull(normed_two_grad)
    stored["gain_two"] = gain_two_grad
    stored["shift_two"] = shift_two_grad
    middle_grad = upstream + middle_part
    stored["middle_grad"] = middle_grad
    out_term = middle_grad.astype(jnp.bfloat16)
    stored["out"] = jnp.einsum("re,rd->ed", attended, out_term, preferred_element_type=jnp.float32)
    stored["out_bias"] = jnp.sum(middle_grad, axis=0)
    attended_grad = jnp.einsum(
        "rd,ed->re", out_term, params[1], preferred_element_type=jnp.float32
    ).reshape(output.shape)
    numerator_grad = (attended_grad / denominator[:, :, None]).astype(jnp.bfloat16)
    denom_grad = -jnp.sum(attended_grad * attention_numerator, axis=-1) / (
        denominator * denominator
    )
    stored["numer_grad"] = numerator_grad
    stored["denom_grad"] = denom_grad
    stored["state_grad"] = jnp.einsum(
        "jfp,jfl->fpl", query_reduced, numerator_grad, preferred_element_type=jnp.float32
    )
    stored["sum_grad"] = jnp.einsum(
        "ih,ihm->hm", denom_grad, query_reduced.astype(jnp.float32), precision=finest_precision
    )
    return stored


def lower_back(stored, later_part, matrix, params):
    (
        inputs,
        normed,
        head_parts,
        query_features,
        key_features,
        query_reduced,
        key_reduced,
        value_rows,
        block_local_state,
        local_sum,
    ) = stored["front"]
    running_prefix_state, norm_sum = stored["carry"]
    state_later, sum_later = later_part
    numerator_grad = stored["numer_grad"]
    denom_grad = stored["denom_grad"]
    length = inputs.shape[0]
    causal = causal_mask(length)
    scores = (
        jnp.einsum("ihm,jhm->hij", query_reduced, key_reduced, preferred_element_type=jnp.float32)
        * causal[None]
    )
    scores_grad = jnp.einsum(
        "ihd,jhd->hij", numerator_grad, value_rows, preferred_element_type=jnp.float32
    )
    score_term = ((scores_grad + denom_grad.T[:, :, None]) * causal[None]).astype(jnp.bfloat16)
    later_reduced = state_later.astype(jnp.bfloat16)
    query_grad = jnp.einsum(
        "hij,jhm->ihm", score_term, key_reduced, preferred_element_type=jnp.float32
    )
    query_grad = query_grad + jnp.einsum(
        "gvw,vcw->gvc",
        numerator_grad,
        running_prefix_state.astype(jnp.bfloat16),
        preferred_element_type=jnp.float32,
    )
    query_grad = query_grad + denom_grad[:, :, None] * norm_sum[None]
    key_grad = jnp.einsum(
        "hij,ihm->jhm", score_term, query_reduced, preferred_element_type=jnp.float32
    )
    key_grad = key_grad + jnp.einsum(
        "prc,rqc->prq", value_rows, later_reduced, preferred_element_type=jnp.float32
    )
    key_grad = key_grad + sum_later[None]
    value_grad = jnp.einsum(
        "hij,ihd->jhd",
        scores.astype(jnp.bfloat16),
        numerator_grad,
        preferred_element_type=jnp.float32,
    )
    value_grad = value_grad + jnp.einsum(
        "qsa,saw->qsw", key_reduced, later_reduced, preferred_element_type=jnp.float32
    )
    feature_scale = DH ** (-0.25)
    query_proj = favor_back(query_grad, query_features, head_parts[:, 0], matrix, feature_scale)
    key_proj = favor_back(key_grad, key_features, head_parts[:, 1], matrix, feature_scale)
    mixed_grad = (
        jnp.stack([query_proj, key_proj, value_grad], axis=1)
        .reshape(length, -1)
        .astype(jnp.bfloat16)
    )
    input_part = jnp.einsum("rd,re->de", normed, mixed_grad, preferred_element_type=jnp.float32)
    normed_grad = jnp.einsum("re,de->rd", mixed_grad, params[0], preferred_element_type=jnp.float32)
    _, first_pull = jax.vjp(
        layer_norm, inputs, params[7].astype(jnp.float32), params[8].astype(jnp.float32)
    )
    inputs_part, gain_one_grad, shift_one_grad = first_pull(normed_grad)
    return (stored["middle_grad"] + inputs_part, input_part, gain_one_grad, shift_one_grad)


BF = jnp.bfloat16
F32 = jnp.float32
M = 256
SCALE = DH ** (-0.25)
LOG2E = math.log2(math.e)
PAIRS = H // 2
STATE_ROWS = 160


def dot(a, b):
    return jnp.dot(a, b, preferred_element_type=F32)


def dot_nt(a, b):
    return lax.dot_general(a, b, (((1,), (1,)), ((), ())), preferred_element_type=F32)


class States:
    def __init__(self, geo, lane, earlier):
        self.geo, self.lane, self.earlier = geo, lane, earlier
        self.per = geo.Y + 1
        self.first = lane.take(self.per * PAIRS)

    @staticmethod
    def scratch(geo):
        one = (PAIRS, STATE_ROWS, M)
        two = (PAIRS, 2, STATE_ROWS, M)
        return [pltpu.VMEM(two, BF), pltpu.VMEM(two, BF), pltpu.VMEM(one, BF),
                pltpu.VMEM((PAIRS, max(geo.Y - 1, 1), STATE_ROWS, M), BF), pltpu.VMEM(one, BF),
                pltpu.VMEM(one, BF), pltpu.VMEM(two, BF)]

    def bind(self, buffers):
        self.own, self.sibling, self.chip, self.chips, self.base, self.base_sibling, self.total = buffers

    def copies(self, p, phase):
        g = self.geo
        z, x, y, c = g.me()
        index = self.first + p * self.per
        other = g.device(z, x, y, 1 - c)
        if phase == 0:
            return [remote(self.lane, index, self.own.at[p], self.sibling.at[p], other)]
        if phase == 1:
            return [remote(self.lane, index + k, self.chip.at[p], self.chips.at[p, k - 1],
                           g.device(z, x, (y + k) % g.Y, c)) for k in range(1, g.Y)]
        return [remote(self.lane, index + g.Y, self.base.at[p], self.base_sibling.at[p], other)]

    def step(self, n, p):
        g = self.geo
        z, x, y, c = g.me()
        if n > 0:
            for copy in self.copies(p, n - 1):
                copy.wait_recv()
        if n == 1:
            self.chip[p] = (self.own[p, c].astype(F32) + self.sibling[p, c].astype(F32)).astype(BF)
        elif n == 2:
            total = jnp.zeros((STATE_ROWS, M), F32)
            for k in range(1, g.Y):
                source = (y + g.Y - k) % g.Y
                counts = source < y if self.earlier else source > y
                total += jnp.where(counts, 1.0, 0.0) * self.chips[p, k - 1].astype(F32)
            self.base[p] = total.astype(BF)
        elif n == 3:
            near = jnp.where(c == (1 if self.earlier else 0), 1.0, 0.0)
            self.total[p, c] = (self.base[p].astype(F32) + near * self.sibling[p, c].astype(F32)).astype(BF)
            self.total[p, 1 - c] = (self.base_sibling[p].astype(F32)
                                    + near * self.sibling[p, 1 - c].astype(F32)).astype(BF)
        if n < 3:
            for copy in self.copies(p, n):
                copy.start()

    def drain(self):
        for p in range(PAIRS):
            for phase in range(3):
                for copy in self.copies(p, phase):
                    copy.wait_send()


class Many:
    def __init__(self, kind, geo, lane, count):
        self.tasks = [kind(geo, lane) for _ in range(count)]
        self.per = (lane.count - self.tasks[0].begin) // count

    def bind(self, chunk):
        self.chunk = chunk

    def step(self, n, p):
        task = self.tasks[0].shifted(p * self.per)
        task.bind(*self.chunk(p))
        task.step(n)

    def drain(self):
        for p in range(len(self.tasks)):
            task = self.tasks[0].shifted(p * self.per)
            task.bind(*self.chunk(p))
            task.drain()


def layer_kernel(geo, lane, plan, *refs):
    (tokens, cot, feat, small_own, wi_in, wo_in, wu_in, wd_own,
     result, tokens_grad, inp_out, ou_out, down_out, vec_out,
     small, wi_own, wi, wou_own, wou, wd, normed, normed_t, mixed, pq, pk, den, attended, middle, n2_t,
     act, hg, vecs, ub, ubg, grads, fa, ft,
     part_i, part_u, part_d, part_v) = refs[:41]
    rest = list(refs[41:])
    fwd, bwd, gs, gi, gu, gd, ri, ru, rd, rv = plan
    take = lambda n: [rest.pop(0) for _ in range(n)]
    fwd.bind(take(7))
    bwd.bind(take(7))
    bi, bu, bd, bv = take(4), take(4), take(4), take(4)
    lane.send, lane.recv = take(2)
    gs.bind(small_own, small)
    gi.bind(lambda p: (wi_own.at[p], wi.at[p]))
    gu.bind(wou_own, wou)
    gd.bind(wd_own, wd)
    inp_parts = inp_out
    ri.bind(lambda p: (part_i.at[p], inp_parts.at[p], [b.at[p] for b in bi]))
    ru.bind(part_u, ou_out, bu)
    rd.bind(part_d, down_out, bd)
    rv.bind(part_v, vec_out, bv)
    n2 = normed
    D = tokens.shape[-1]
    L = tokens.shape[1]
    FF = wd.shape[0] * wd.shape[1] * wd.shape[2] * 2 * wd.shape[4]
    HALF = L // 2
    lead = (geo.Z, geo.X, geo.Y, 2)

    def loop(n, body):
        def step(i, _):
            body(i)
            return 0
        lax.fori_loop(0, n, step, 0)

    for p in range(PAIRS):
        wi_own[p] = jnp.concatenate([wi_in[:, k * D + p * 128: k * D + (p + 1) * 128] for k in range(3)], axis=1)
    wou_own[:, :D] = wo_in[...]
    wou_own[:, D:] = wu_in[...]
    geo.barrier()
    gs.step(0)
    for p in range(PAIRS):
        gi.step(0, p)
    gu.step(0)
    gd.step(0)

    f = feat[...]
    zero = jnp.zeros((DH, M), BF)
    one = jnp.ones((DH, M), BF)
    fa[0] = jnp.concatenate([f, zero, -one, zero], axis=0)
    fa[1] = jnp.concatenate([zero, f, zero, -one], axis=0)
    ft[...] = jnp.concatenate([jnp.concatenate([f, zero], axis=1), jnp.concatenate([zero, f], axis=1),
                               jnp.concatenate([one, zero], axis=1), jnp.concatenate([zero, one], axis=1)], axis=0)
    low_lane = lax.broadcasted_iota(jnp.int32, (1, 128), 1) < DH
    m0f = jnp.where(low_lane, 1.0, 0.0)
    m0 = m0f.astype(BF)
    m1 = (1.0 - m0f).astype(BF)
    tri_r = lax.broadcasted_iota(jnp.int32, (HALF, HALF), 0)
    tri_c = lax.broadcasted_iota(jnp.int32, (HALF, HALF), 1)

    gs.step(1)
    gi.step(1, 0)
    gs.step(2)
    gi.step(1, 1)
    gi.step(2, 0)
    gs.step(3)
    gi.step(1, 2)
    gi.step(2, 1)
    gs.step(4)

    flat = lambda v: v.reshape(-1, v.shape[-1])
    sm = small[...]
    vecs[...] = flat(sm[..., :128]).astype(F32).T[:8]
    ub[...] = jnp.sum(sm[..., 128:].astype(F32).reshape(-1, 2 * sm.shape[-2], 128), axis=1)
    out_bias, down_bias = lambda: vecs[0:1], lambda: vecs[1:2]

    def norm_parts(rows):
        center = jnp.mean(rows, axis=-1, keepdims=True)
        centred = rows - center
        spread = jnp.mean(centred * centred, axis=-1, keepdims=True)
        inv = lax.rsqrt(spread + epsilon)
        return centred * inv, inv

    def first_norm(s):
        hat, _ = norm_parts(tokens[s].astype(F32))
        value = (hat * vecs[2:3] + vecs[3:4]).astype(BF)
        normed[s] = value
        normed_t[s] = value.T
    gi.step(3, 0)
    loop(2, first_norm)
    gi.step(1, 3)
    gi.step(2, 2)
    gi.step(3, 1)

    def vx(s, p):
        v = mixed[s, p, :, 2 * 128:]
        ones = jnp.ones(v.shape, BF)
        return (jnp.concatenate([v * m0, ones * m0], axis=1), jnp.concatenate([v * m1, ones * m1], axis=1))

    def project(p):
        gi.step(4, p)
        w = flat(wi[p])

        def seq(s):
            mixed[s, p] = dot(normed[s], w).astype(BF)
            for part, target in ((0, pq), (1, pk)):
                rows = mixed[s, p, :, part * 128:(part + 1) * 128]
                wide = rows.astype(F32)
                lhs = jnp.concatenate([rows, (wide * wide * (0.5 * SCALE)).astype(BF)], axis=1)
                for h in range(2):
                    power = dot(lhs, fa[h]) * (SCALE * LOG2E) - 0.5 * math.log2(M)
                    target[s, 2 * p + h] = jnp.exp2(power).astype(BF)
            v = mixed[s, p, :, 2 * 128:]
            lhs = jnp.concatenate([v.T, jnp.ones((16, L), BF)], axis=0)
            r0 = dot(lhs, pk[s, 2 * p])
            r1 = dot(lhs, pk[s, 2 * p + 1])
            fwd.own[p, s] = jnp.concatenate([r0[:64], r1[64:128], r0[128:], r1[128:]], axis=0).astype(BF)
        loop(2, seq)
        fwd.step(0, p)

        @pl.when(p == 0)
        def _():
            gi.step(2, 3)
            gi.step(3, 2)
            gu.step(1)

        @pl.when(p == 1)
        def _():
            gi.step(3, 3)
            gd.step(1)

        @pl.when(p == 2)
        def _():
            gu.step(2)

        for n in range(1, 4):
            @pl.when(p >= n)
            def _():
                fwd.step(n, p - n)
    loop(PAIRS, project)
    gd.step(2)
    fwd.step(1, 3)
    fwd.step(2, 2)
    fwd.step(3, 1)

    def state_cols(total, p, s, h, copies):
        state = total[p, s, h * 64:(h + 1) * 64]
        extra = total[p, s, 128 + 16 * h:144 + 16 * h]
        zeros = jnp.zeros((DH, M), BF)
        if copies:
            extra = jnp.concatenate([extra] * 4, axis=0)
        else:
            extra = jnp.concatenate([extra, jnp.zeros((48, M), BF)], axis=0)
        parts = [state, zeros, extra, zeros] if h == 0 else [zeros, state, zeros, extra]
        return jnp.concatenate(parts, axis=0)

    lower = tri_r >= tri_c
    upper = tri_r <= tri_c

    def attend_pair(p):
        def seq(s):
            v0, v1 = vx(s, p)
            states = jnp.concatenate([state_cols(fwd.total, p, s, h, True) for h in range(2)], axis=1)
            lanes = pl.ds(pl.multiple_of(p * 128, 128), 128)
            for b in range(2):
                rows = slice(b * HALF, (b + 1) * HALF)
                scores = []
                for h in range(2):
                    q = pq[s, 2 * p + h, rows]
                    if b == 1:
                        scores.append(dot_nt(q, pk[s, 2 * p + h, :HALF]).astype(BF))
                    scores.append(jnp.where(lower, dot_nt(q, pk[s, 2 * p + h, rows]), 0.0).astype(BF))
                rhs = jnp.concatenate([v0[:(b + 1) * HALF], v1[:(b + 1) * HALF]], axis=0)
                ext = dot(jnp.concatenate(scores, axis=1), rhs)
                ext += dot_nt(jnp.concatenate([pq[s, 2 * p, rows], pq[s, 2 * p + 1, rows]], axis=1), states)
                n_, d_ = ext[:, :128], ext[:, 128:]
                inv = 1.0 / d_
                den[s, rows, lanes] = inv
                attended[s, rows, lanes] = (n_ * inv).astype(BF)
        loop(2, seq)

        @pl.when(p == 0)
        def _():
            fwd.step(2, 3)
            fwd.step(3, 2)
            gu.step(3)

        @pl.when(p == 1)
        def _():
            fwd.step(3, 3)
            gd.step(3)
    loop(PAIRS, attend_pair)
    gu.step(4)
    gd.step(4)

    def wo():
        return flat(wou[..., :D])

    def to_middle(s):
        value = tokens[s].astype(F32) + dot(attended[s], wo()) + out_bias()
        middle[s] = value
        hat, _ = norm_parts(value)
        low = (hat * vecs[4:5] + vecs[5:6]).astype(BF)
        n2[s] = low
        n2_t[s] = low.T
        result[s] = value + down_bias()
        tokens_grad[s] = jnp.zeros((L, D), F32)
    loop(2, to_middle)
    ubg[...] = jnp.zeros(ubg.shape, F32)
    grads[...] = jnp.zeros(grads.shape, F32)

    k0 = math.sqrt(2.0 / math.pi)

    def feed_tile(t):
        lanes = pl.ds(pl.multiple_of(D + t * 512, 512), 512)
        bias = jnp.concatenate([ub[pl.ds(4 * t + i, 1)] for i in range(4)], axis=1)
        wut = lambda: flat(wou[:, :, :, :, :, lanes])
        wdt = lambda: flat(wd[t])

        def seq(s):
            for b in range(2):
                rows = slice(b * HALF, (b + 1) * HALF)
                u = dot(n2[s, rows], wut()) + bias
                uu = u * u
                th = jnp.tanh(u * (k0 + (k0 * 0.044715) * uu))
                half = 0.5 + 0.5 * th
                a = (u * half).astype(BF)
                act[s, rows] = a
                slope = half + (0.5 * u) * (1.0 - th * th) * (k0 + (3.0 * 0.044715 * k0) * uu)
                back = dot_nt(cot[s, rows], wdt()) * slope
                total = jnp.sum(back, axis=0, keepdims=True)
                for i in range(4):
                    ubg[pl.ds(4 * t + i, 1)] += total[:, i * 128:(i + 1) * 128]
                low = back.astype(BF)
                hg[s, rows] = low
                result[s, rows] += dot(a, wdt())
                tokens_grad[s, rows] += dot_nt(low, wut())
        loop(2, seq)
        dwd = dot(act[0].T, cot[0]) + dot(act[1].T, cot[1])
        part_d[t] = dwd.astype(BF).reshape(part_d.shape[1:])
        dwu = dot(n2_t[0], hg[0]) + dot(n2_t[1], hg[1])
        part_u[:, :, :, :, :, lanes] = dwu.astype(BF).reshape(lead + (-1, 512))
    loop(FF // 512, feed_tile)
    rd.step(0)

    ones_block = jnp.concatenate([jnp.concatenate([jnp.ones((64, 64), F32), jnp.zeros((64, 64), F32)], axis=1),
                                  jnp.concatenate([jnp.zeros((64, 64), F32), jnp.ones((64, 64), F32)], axis=1)],
                                 axis=0).astype(BF)
    ones_two = jnp.concatenate([ones_block, ones_block], axis=0)
    lane_id = lax.broadcasted_iota(jnp.int32, (1, 128), 1)
    hi_lane = jnp.where((lane_id % DH) == 0, 1.0, 0.0)
    lo_lane = jnp.where((lane_id % DH) == 1, 1.0, 0.0)

    def norm_back(rows, dy, gain):
        hat, inv = norm_parts(rows)
        dg = dy * gain
        m_a = jnp.mean(dg, axis=-1, keepdims=True)
        m_b = jnp.mean(dg * hat, axis=-1, keepdims=True)
        return (inv * (dg - m_a - hat * m_b), jnp.sum(dy * hat, axis=0, keepdims=True),
                jnp.sum(dy, axis=0, keepdims=True))

    def out_back(s):
        dx, dgain, dshift = norm_back(middle[s], tokens_grad[s], vecs[4:5])
        up = cot[s].astype(F32)
        mg = up + dx
        middle[s] = mg
        low = mg.astype(BF)
        act[s] = low
        grads[0:1] += jnp.sum(mg, axis=0, keepdims=True)
        grads[1:2] += jnp.sum(up, axis=0, keepdims=True)
        grads[4:5] += dgain
        grads[5:6] += dshift
        ag = dot_nt(low, wo())
        inv = den[s]
        ng = ag * inv
        prod = ng * attended[s].astype(F32)
        n2[s] = ng.astype(BF)
        for p in range(PAIRS):
            cols = slice(p * 128, (p + 1) * 128)
            pr = prod[:, cols]
            hi = pr.astype(BF)
            lo = (pr - hi.astype(F32)).astype(BF)
            dgr = -dot(jnp.concatenate([hi, lo], axis=1), ones_two)
            dhi = dgr.astype(BF).astype(F32)
            dlo = dgr - dhi
            hg[s, :, cols] = (dhi * hi_lane + dlo * lo_lane).astype(BF)
    loop(2, out_back)
    dwo = dot(attended[0].T, act[0]) + dot(attended[1].T, act[1])
    part_u[:, :, :, :, :, :D] = dwo.astype(BF).reshape(lead + (-1, D))
    ru.step(0)

    def ngx(s, p):
        lanes = pl.ds(pl.multiple_of(p * 128, 128), 128)
        return jnp.concatenate([n2[s, :, lanes], hg[s, :, lanes]], axis=1)

    def state_back(p):
        def seq(s):
            lhs = ngx(s, p).T
            r0 = dot(lhs, pq[s, 2 * p])
            r1 = dot(lhs, pq[s, 2 * p + 1])
            bwd.own[p, s] = jnp.concatenate([r0[:64], r1[64:128], r0[128:144], r1[192:208]], axis=0).astype(BF)
        loop(2, seq)
        bwd.step(0, p)

        @pl.when(p == 1)
        def _():
            rd.step(1)

        @pl.when(p == 3)
        def _():
            ru.step(1)
        for n in range(1, 4):
            @pl.when(p >= n)
            def _():
                bwd.step(n, p - n)
    loop(PAIRS, state_back)
    bwd.step(1, 3)
    bwd.step(2, 2)
    bwd.step(3, 1)

    def pair_back(i):
        p, s = i // 2, i % 2
        v0, v1 = vx(s, p)
        x = ngx(s, p)
        ng = x[:, :128]
        logs_q, logs_k, at = [], [], []
        for h, v in ((0, v0), (1, v1)):
            q, k = pq[s, 2 * p + h], pk[s, 2 * p + h]
            sx = state_cols(fwd.total, p, s, h, True)
            sg = state_cols(bwd.total, p, s, h, False)
            lo, hi = slice(0, HALF), slice(HALF, L)

            def masked(keep, value):
                return jnp.where(keep, value, 0.0).astype(BF)
            g00 = masked(lower, dot_nt(x[lo], v[lo]))
            g10 = dot_nt(x[hi], v[lo]).astype(BF)
            g11 = masked(lower, dot_nt(x[hi], v[hi]))
            qg0 = dot(jnp.concatenate([g00, x[lo]], axis=1), jnp.concatenate([k[lo], sx], axis=0))
            qg1 = dot(jnp.concatenate([g10, g11, x[hi]], axis=1), jnp.concatenate([k, sx], axis=0))
            logs_q.append((jnp.concatenate([qg0, qg1], axis=0) * q.astype(F32)).astype(BF))
            t00 = masked(upper, dot_nt(v[lo], x[lo]))
            t01 = dot_nt(v[lo], x[hi]).astype(BF)
            t11 = masked(upper, dot_nt(v[hi], x[hi]))
            kg0 = dot(jnp.concatenate([t00, t01, v[lo]], axis=1), jnp.concatenate([q, sg], axis=0))
            kg1 = dot(jnp.concatenate([t11, v[hi]], axis=1), jnp.concatenate([q[hi], sg], axis=0))
            logs_k.append((jnp.concatenate([kg0, kg1], axis=0) * k.astype(F32)).astype(BF))
            a00 = masked(upper, dot_nt(k[lo], q[lo]))
            a01 = dot_nt(k[lo], q[hi]).astype(BF)
            a11 = masked(upper, dot_nt(k[hi], q[hi]))
            at.append((a00, a01, a11))
        n0, n1 = ng * m0, ng * m1
        vg0 = dot(jnp.concatenate([at[0][0], at[0][1], at[1][0], at[1][1]], axis=1),
                  jnp.concatenate([n0, n1], axis=0))
        vg1 = dot(jnp.concatenate([at[0][2], at[1][2]], axis=1), jnp.concatenate([n0[HALF:], n1[HALF:]], axis=0))
        zeros = jnp.zeros((DH, M), BF)
        sgt = jnp.concatenate([jnp.concatenate([bwd.total[p, s, :64], zeros], axis=0),
                               jnp.concatenate([zeros, bwd.total[p, s, 64:128]], axis=0)], axis=1)
        vg = jnp.concatenate([vg0, vg1], axis=0)
        vg += dot_nt(jnp.concatenate([pk[s, 2 * p], pk[s, 2 * p + 1]], axis=1), sgt)
        out = []
        for part, logs in ((0, logs_q), (1, logs_k)):
            through = dot_nt(jnp.concatenate(logs, axis=1), ft[...])
            rows = mixed[s, p, :, part * 128:(part + 1) * 128].astype(F32)
            out.append((SCALE * through[:, :128] - SCALE * SCALE * through[:, 128:] * rows).astype(BF))
        mg = jnp.concatenate(out + [vg.astype(BF)], axis=1)
        act[s, :, :384] = mg
        back = dot_nt(mg, flat(wi[p]))

        @pl.when(p == 0)
        def _():
            tokens_grad[s] = back

        @pl.when(p > 0)
        def _():
            tokens_grad[s] += back

        @pl.when(s == 1)
        def _():
            dwi = dot(normed_t[0], act[0, :, :384]) + dot(normed_t[1], act[1, :, :384])
            part_i[p] = dwi.astype(BF).reshape(lead + (-1, 384))
            ri.step(0, p)
        schedule = {0: [lambda: bwd.step(2, 3), lambda: bwd.step(3, 2)], 1: [lambda: bwd.step(3, 3)],
                    2: [lambda: rd.step(2), lambda: ri.step(1, 0)],
                    3: [lambda: ru.step(2)],
                    4: [lambda: rd.step(3), lambda: ri.step(2, 0), lambda: ri.step(1, 1)],
                    5: [lambda: ru.step(3)],
                    6: [lambda: rd.step(4), lambda: ri.step(3, 0), lambda: ri.step(2, 1), lambda: ri.step(1, 2)],
                    7: [lambda: ru.step(4), lambda: ri.step(4, 0), lambda: ri.step(3, 1), lambda: ri.step(2, 2)]}
        for at_step, actions in schedule.items():
            @pl.when(i == at_step)
            def _():
                for action in actions:
                    action()
    loop(2 * PAIRS, pair_back)
    ri.step(1, 3)

    def first_back(s):
        dx, dgain, dshift = norm_back(tokens[s].astype(F32), tokens_grad[s], vecs[2:3])
        tokens_grad[s] = middle[s] + dx
        grads[2:3] += dgain
        grads[3:4] += dshift
    loop(2, first_back)
    part_v[..., :128] = jnp.concatenate([grads[...], jnp.zeros((120, D), F32)], axis=0).T.astype(BF).reshape(lead + (-1, 128))
    first_row = lax.broadcasted_iota(jnp.int32, (16, 128), 0) == 0
    for z in range(geo.Z):
        for x in range(geo.X):
            for y in range(geo.Y):
                chip = (z * geo.X + x) * geo.Y + y
                tile = jnp.where(first_row, ubg[chip:chip + 1], 0.0).astype(BF)
                for c in range(2):
                    part_v[z, x, y, c, :, 128:] = tile
    rv.step(0)
    ri.step(4, 1)
    ri.step(3, 2)
    ri.step(2, 3)
    rv.step(1)
    ri.step(4, 2)
    ri.step(3, 3)
    rv.step(2)
    ri.step(4, 3)
    rv.step(3)
    rv.step(4)
    for task in (gs, gi, gu, gd, fwd, bwd, ri, ru, rd, rv):
        task.drain()


def fused(geo, args):
    (tokens, feature_matrix, input_weight, output_weight, output_bias, up_weight, up_bias, down_weight,
     down_bias, first_gain, first_shift, second_gain, second_shift, cotangent) = args
    rows, D = input_weight.shape[0], tokens.shape[-1]
    L = tokens.shape[1]
    FF = up_weight.shape[1]
    core = geo.me()[3]
    cols = jnp.stack([output_bias, down_bias, first_gain, first_shift, second_gain, second_shift], axis=1)
    width = up_bias.shape[0]
    placed = jnp.where(jnp.arange(128) // width == core, jnp.tile(up_bias, 128 // width), 0)
    small = jnp.concatenate([jnp.pad(cols, ((0, 0), (0, 122))),
                             jnp.pad(placed[None], ((0, rows - 1), (0, 0)))], axis=1)
    lane = Lane()
    fwd, bwd = States(geo, lane, True), States(geo, lane, False)
    gs, gi, gu, gd = Gather(geo, lane), Many(Gather, geo, lane, PAIRS), Gather(geo, lane), Gather(geo, lane)
    ri = Many(Scatter, geo, lane, PAIRS)
    ru, rd, rv = Scatter(geo, lane), Scatter(geo, lane), Scatter(geo, lane)
    plan = (fwd, bwd, gs, gi, gu, gd, ri, ru, rd, rv)
    lead = (geo.Z, geo.X, geo.Y, 2)
    down_rows = down_weight.shape[0]
    wide = D + FF
    V = pltpu.VMEM
    scratch = [
        V(lead + (rows, 256), BF), V((PAIRS, rows, 384), BF), V((PAIRS,) + lead + (rows, 384), BF),
        V((rows, wide), BF), V(lead + (rows, wide), BF), V(lead + (down_rows, D), BF),
        V((2, L, D), BF), V((2, D, L), BF), V((2, PAIRS, L, 384), BF), V((2, H, L, M), BF), V((2, H, L, M), BF),
        V((2, L, D), F32), V((2, L, D), BF), V((2, L, D), F32), V((2, D, L), BF),
        V((2, L, 512), BF), V((2, L, 512), BF),
        V((8, D), F32), V((FF // 128, 128), F32), V((FF // 128, 128), F32), V((8, D), F32),
        V((2, M, M), BF), V((M, 2 * M), BF),
        V((PAIRS,) + lead + (rows, 384), BF), V(lead + (rows, wide), BF), V(lead + (down_rows, D), BF),
        V(lead + (rows, 256), BF),
    ]
    scratch += States.scratch(geo) + States.scratch(geo)
    scratch += [V((PAIRS,) + s.shape, s.dtype) for s in Scatter.scratch(geo, rows, 384)]
    scratch += Scatter.scratch(geo, rows, wide) + Scatter.scratch(geo, down_rows, D) + Scatter.scratch(geo, rows, 256)
    scratch += [pltpu.SemaphoreType.DMA((lane.count,)), pltpu.SemaphoreType.DMA((lane.count,))]
    vmem = pl.BlockSpec(memory_space=pltpu.VMEM)
    shape = jax.ShapeDtypeStruct
    outs = [shape(tokens.shape, F32), shape(tokens.shape, F32), shape((PAIRS, rows, 384), F32),
            shape((rows, wide), F32), shape((down_rows, D), F32), shape((rows, 256), F32)]
    result, tokens_grad, inp, ou, down, vec = pl.pallas_call(
        functools.partial(layer_kernel, geo, lane, plan),
        out_shape=outs, in_specs=[vmem] * 8, out_specs=[vmem] * 6, scratch_shapes=scratch,
        compiler_params=pltpu.CompilerParams(collective_id=0, has_side_effects=True, vmem_limit_bytes=60 << 20),
    )(tokens, cotangent, feature_matrix, small, input_weight, output_weight, up_weight, down_weight)
    inp = inp.reshape(PAIRS, rows, 3, 128).transpose(1, 2, 0, 3).reshape(rows, 3 * D)
    up_bias_grad = lax.dynamic_slice(vec[0], (128 + core * width,), (width,))
    return (result, tokens_grad, inp, ou[:, :D], vec[:, 0], ou[:, D:], up_bias_grad, down,
            vec[:, 1], vec[:, 2], vec[:, 3], vec[:, 4], vec[:, 5])


def local(
    tokens,
    feature_matrix,
    input_weight,
    output_weight,
    output_bias,
    up_weight,
    up_bias,
    down_weight,
    down_bias,
    first_gain,
    first_shift,
    second_gain,
    second_shift,
    cotangent,
):
    params = (
        lax.all_gather(input_weight, ("dp", "seq"), axis=0, tiled=True),
        lax.all_gather(output_weight, ("dp", "seq"), axis=0, tiled=True),
        lax.all_gather(output_bias, ("dp", "seq"), axis=0, tiled=True),
        lax.all_gather(up_weight, ("dp", "seq"), axis=0, tiled=True),
        lax.all_gather(up_bias, ("dp", "seq"), axis=0, tiled=True),
        lax.all_gather(down_weight, ("dp", "seq"), axis=0, tiled=True),
        lax.all_gather(down_bias, ("dp", "seq"), axis=0, tiled=True),
        lax.all_gather(first_gain, ("dp", "seq"), axis=0, tiled=True),
        lax.all_gather(first_shift, ("dp", "seq"), axis=0, tiled=True),
        lax.all_gather(second_gain, ("dp", "seq"), axis=0, tiled=True),
        lax.all_gather(second_shift, ("dp", "seq"), axis=0, tiled=True),
    )
    micros = tokens.shape[0]
    fronts = []
    carries = []
    for micro_step in range(micros):
        pieces = front(tokens[micro_step], feature_matrix, params)
        fronts.append(pieces)
        carries.append(
            prefix(
                (pieces[8], pieces[9]),
                "seq",
                add_pair,
                (jnp.zeros_like(pieces[8]), jnp.zeros_like(pieces[9])),
            )
        )
    results = []
    for micro_step in range(micros):
        pieces = fronts[micro_step]
        running_prefix_state, norm_sum = carries[micro_step]
        output = attend(pieces[5], pieces[6], pieces[7], running_prefix_state, norm_sum)[0]
        attended, middle = upper(pieces[0], output, params)
        results.append(feed(middle, params))
    result = jnp.stack(results)
    back_params = (
        lax.all_gather(input_weight, ("dp", "seq"), axis=0, tiled=True),
        lax.all_gather(output_weight, ("dp", "seq"), axis=0, tiled=True),
        lax.all_gather(output_bias, ("dp", "seq"), axis=0, tiled=True),
        lax.all_gather(up_weight, ("dp", "seq"), axis=0, tiled=True),
        lax.all_gather(up_bias, ("dp", "seq"), axis=0, tiled=True),
        lax.all_gather(down_weight, ("dp", "seq"), axis=0, tiled=True),
        lax.all_gather(down_bias, ("dp", "seq"), axis=0, tiled=True),
        lax.all_gather(first_gain, ("dp", "seq"), axis=0, tiled=True),
        lax.all_gather(first_shift, ("dp", "seq"), axis=0, tiled=True),
        lax.all_gather(second_gain, ("dp", "seq"), axis=0, tiled=True),
        lax.all_gather(second_shift, ("dp", "seq"), axis=0, tiled=True),
    )
    stored_list = []
    later_list = []
    for micro_step in range(micros):
        stored = upper_back(
            tokens[micro_step],
            cotangent[micro_step].astype(jnp.float32),
            feature_matrix,
            back_params,
            carries[micro_step],
        )
        stored_list.append(stored)
        later_list.append(
            prefix_2(
                (stored["state_grad"], stored["sum_grad"]),
                "seq",
                add_pair,
                (jnp.zeros_like(stored["state_grad"]), jnp.zeros_like(stored["sum_grad"])),
            )
        )
    upper_names = ["out", "out_bias", "up", "up_bias", "down", "down_bias", "gain_two", "shift_two"]
    upper_totals = [stored_list[0][name] for name in upper_names]
    micro_step = 1
    upper_totals = [
        total + stored_list[micro_step][name] for total, name in zip(upper_totals, upper_names)
    ]
    token_grads = []
    lower_totals = None
    for micro_step in range(micros):
        stored = stored_list[micro_step]
        tokens_part, input_part, gain_part, shift_part = lower_back(
            stored, later_list[micro_step], feature_matrix, back_params
        )
        token_grads.append(tokens_part)
        lower_parts = (input_part, gain_part, shift_part)
        if micro_step == 0:
            lower_totals = lower_parts
        else:
            lower_totals = jax.tree.map(jnp.add, lower_totals, lower_parts)
    shares = (
        lax.psum_scatter(lower_totals[0], ("dp", "seq"), scatter_dimension=0, tiled=True),
        lax.psum_scatter(upper_totals[0], ("dp", "seq"), scatter_dimension=0, tiled=True),
        lax.psum_scatter(upper_totals[1], ("dp", "seq"), scatter_dimension=0, tiled=True),
        lax.psum_scatter(upper_totals[2], ("dp", "seq"), scatter_dimension=0, tiled=True),
        lax.psum_scatter(upper_totals[3], ("dp", "seq"), scatter_dimension=0, tiled=True),
        lax.psum_scatter(upper_totals[4], ("dp", "seq"), scatter_dimension=0, tiled=True),
        lax.psum_scatter(upper_totals[5], ("dp", "seq"), scatter_dimension=0, tiled=True),
        lax.psum_scatter(lower_totals[1], ("dp", "seq"), scatter_dimension=0, tiled=True),
        lax.psum_scatter(lower_totals[2], ("dp", "seq"), scatter_dimension=0, tiled=True),
        lax.psum_scatter(upper_totals[6], ("dp", "seq"), scatter_dimension=0, tiled=True),
        lax.psum_scatter(upper_totals[7], ("dp", "seq"), scatter_dimension=0, tiled=True),
    )
    return (
        result,
        jnp.stack(token_grads),
        shares[0],
        shares[1],
        shares[2],
        shares[3],
        shares[4],
        shares[5],
        shares[6],
        shares[7],
        shares[8],
        shares[9],
        shares[10],
    )


def solution(mesh):
    in_specs = (
        P("dp", "seq", None),
        P(),
        P(("dp", "seq"), None),
        P(("dp", "seq"), None),
        P(("dp", "seq")),
        P(("dp", "seq"), None),
        P(("dp", "seq")),
        P(("dp", "seq"), None),
        P(("dp", "seq")),
        P(("dp", "seq")),
        P(("dp", "seq")),
        P(("dp", "seq")),
        P(("dp", "seq")),
        P("dp", "seq", None),
    )
    out_specs = (
        P("dp", "seq", None),
        P("dp", "seq", None),
        P(("dp", "seq"), None),
        P(("dp", "seq"), None),
        P(("dp", "seq")),
        P(("dp", "seq"), None),
        P(("dp", "seq")),
        P(("dp", "seq"), None),
        P(("dp", "seq")),
        P(("dp", "seq")),
        P(("dp", "seq")),
        P(("dp", "seq")),
        P(("dp", "seq")),
    )
    geo = Geometry(mesh)
    rows = 512 // (mesh.shape["dp"] * mesh.shape["seq"])
    if rows % 16 == 0:
        def body(*args):
            return fused(geo, args)
    else:
        body = local
    return jax.shard_map(body, mesh=mesh, in_specs=in_specs, out_specs=out_specs, check_vma=False)
```

```python
import functools
import math

import jax
import jax.numpy as jnp
from jax import lax
from jax.sharding import PartitionSpec as P

H = 8
DH = 64

from jax.experimental import pallas as pl
from jax.experimental.pallas import tpu as pltpu

MESH = pl.DeviceIdType.MESH


class Geometry:
    def __init__(self, mesh):
        dp, seq = mesh.shape["dp"], mesh.shape["seq"]
        self.C = 2
        self.Y = seq // 2
        self.X = 1 << ((dp.bit_length() - 1) // 2)
        self.Z = dp // self.X

    def me(self):
        dp, seq = lax.axis_index("dp"), lax.axis_index("seq")
        return dp // self.X, dp % self.X, seq // 2, seq % 2

    def device(self, z, x, y, c):
        return (z * self.X + x, y * 2 + c)

    def barrier(self):
        z, x, y, c = self.me()
        peers = [self.device(z, x, y, 1 - c)]
        peers += [self.device((z + i) % self.Z, (x + j) % self.X, (y + k) % self.Y, c)
                  for i in range(self.Z) for j in range(self.X) for k in range(self.Y)][1:]
        semaphore = pltpu.get_barrier_semaphore()
        for peer in peers:
            pl.semaphore_signal(semaphore, inc=1, device_id=peer, device_id_type=MESH)
        pl.semaphore_wait(semaphore, len(peers))


class Lane:
    def __init__(self):
        self.count = 0
        self.send = self.recv = None

    def take(self, n=1):
        first = self.count
        self.count += n
        return first


def remote(lane, index, src, dst, device):
    return pltpu.make_async_remote_copy(
        src_ref=src, dst_ref=dst, send_sem=lane.send.at[index], recv_sem=lane.recv.at[index],
        device_id=device, device_id_type=MESH)


class Gather:
    def __init__(self, geo, lane):
        self.geo, self.lane = geo, lane
        self.zs = lane.take(geo.Z - 1)
        self.second = lane.take(max(geo.X, geo.Y) - 1)
        self.third = lane.take(max(geo.X, geo.Y) - 1)
        self.core = lane.take()

    def bind(self, own, full):
        self.own, self.full = own, full

    def z_copies(self, incoming):
        g = self.geo
        z, x, y, c = g.me()
        for k in range(1, g.Z):
            if incoming:
                slot = self.full.at[(z + g.Z - k) % g.Z, x, y, c]
                yield remote(self.lane, self.zs + k - 1, slot, slot, g.device((z + k) % g.Z, x, y, c))
            else:
                yield remote(self.lane, self.zs + k - 1, self.own, self.full.at[z, x, y, c],
                             g.device((z + k) % g.Z, x, y, c))

    def axis_copies(self, phase, order, incoming):
        g = self.geo
        z, x, y, c = g.me()
        base = self.second if phase == 2 else self.third
        along_x = (phase == 2) == (order == 0)
        size = g.X if along_x else g.Y
        for k in range(1, size):
            if along_x:
                source = (x + g.X - k) % g.X if incoming else x
                device = g.device(z, (x + k) % g.X, y, c)
                slot = self.full.at[:, source, y, c] if phase == 2 else self.full.at[:, source, :, c]
            else:
                source = (y + g.Y - k) % g.Y if incoming else y
                device = g.device(z, x, (y + k) % g.Y, c)
                slot = self.full.at[:, x, source, c] if phase == 2 else self.full.at[:, :, source, c]
            yield remote(self.lane, base + k - 1, slot, slot, device)

    def both(self, action):
        c = self.geo.me()[3]
        for order in range(2):
            @pl.when(c == order)
            def _():
                action(order)

    def step(self, n):
        g = self.geo
        z, x, y, c = g.me()
        if n == 0:
            for copy in self.z_copies(False):
                copy.start()
            self.full[z, x, y, c] = self.own[...]
        elif n == 1:
            for copy in self.z_copies(True):
                copy.wait_recv()
            self.both(lambda order: [copy.start() for copy in self.axis_copies(2, order, False)])
        elif n == 2:
            def go(order):
                for copy in self.axis_copies(2, order, True):
                    copy.wait_recv()
                for copy in self.axis_copies(3, order, False):
                    copy.start()
            self.both(go)
        elif n == 3:
            def go(order):
                for copy in self.axis_copies(3, order, True):
                    copy.wait_recv()
            self.both(go)
            slot = self.full.at[:, :, :, c]
            remote(self.lane, self.core, slot, slot, g.device(z, x, y, 1 - c)).start()
        else:
            slot = self.full.at[:, :, :, 1 - c]
            remote(self.lane, self.core, slot, slot, g.device(z, x, y, 1 - c)).wait_recv()

    def drain(self):
        g = self.geo
        z, x, y, c = g.me()
        for copy in self.z_copies(False):
            copy.wait_send()

        def go(order):
            for phase in (2, 3):
                for copy in self.axis_copies(phase, order, False):
                    copy.wait_send()
        self.both(go)
        slot = self.full.at[:, :, :, c]
        remote(self.lane, self.core, slot, slot, g.device(z, x, y, 1 - c)).wait_send()


class Scatter:
    def __init__(self, geo, lane):
        self.geo, self.lane = geo, lane
        self.core = lane.take()
        self.first = lane.take(max(geo.X, geo.Y) - 1)
        self.second = lane.take(max(geo.X, geo.Y) - 1)
        self.zs = lane.take(geo.Z - 1)

    @staticmethod
    def scratch(geo, rows, width):
        wide = max(geo.X, geo.Y)
        kind = jnp.bfloat16
        return [
            pltpu.VMEM((geo.Z, geo.X, geo.Y, rows, width), kind),
            pltpu.VMEM((wide - 1, geo.Z, wide, rows, width), kind),
            pltpu.VMEM((wide - 1, geo.Z, rows, width), kind),
            pltpu.VMEM((geo.Z - 1, rows, width), kind),
        ]

    def bind(self, part, out, buffers):
        self.part, self.out = part, out
        self.rc, self.ra, self.rb, self.rz = buffers

    def both(self, action):
        c = self.geo.me()[3]
        for order in range(2):
            @pl.when(c == order)
            def _():
                action(order)

    def core_copy(self):
        z, x, y, c = self.geo.me()
        return remote(self.lane, self.core, self.part.at[:, :, :, 1 - c], self.rc,
                      self.geo.device(z, x, y, 1 - c))

    def axis_copies(self, phase, order):
        g = self.geo
        z, x, y, c = g.me()
        base = self.first if phase == 1 else self.second
        along_x = (phase == 1) == (order == 1)
        for k in range(1, g.X if along_x else g.Y):
            if along_x:
                far = (x + k) % g.X
                device = g.device(z, far, y, c)
                src = self.part.at[:, far, :, c] if phase == 1 else self.part.at[:, far, y, c]
                dst = self.ra.at[k - 1, :, pl.ds(0, g.Y)] if phase == 1 else self.rb.at[k - 1]
            else:
                far = (y + k) % g.Y
                device = g.device(z, x, far, c)
                src = self.part.at[:, :, far, c] if phase == 1 else self.part.at[:, x, far, c]
                dst = self.ra.at[k - 1, :, pl.ds(0, g.X)] if phase == 1 else self.rb.at[k - 1]
            yield remote(self.lane, base + k - 1, src, dst, device)

    def z_copies(self):
        g = self.geo
        z, x, y, c = g.me()
        for k in range(1, g.Z):
            far = (z + k) % g.Z
            yield remote(self.lane, self.zs + k - 1, self.part.at[far, x, y, c], self.rz.at[k - 1],
                         g.device(far, x, y, c))

    def step(self, n):
        g = self.geo
        z, x, y, c = g.me()
        wide = lambda ref: ref.astype(jnp.float32)
        if n == 0:
            self.core_copy().start()
        elif n == 1:
            self.core_copy().wait_recv()

            def add(i, _):
                total = wide(self.part[i, :, :, c]) + wide(self.rc[i])
                self.part[i, :, :, c] = total.astype(jnp.bfloat16)
                return 0
            lax.fori_loop(0, g.Z, add, 0)
            self.both(lambda order: [copy.start() for copy in self.axis_copies(1, order)])
        elif n == 2:
            def go(order):
                copies = list(self.axis_copies(1, order))
                for copy in copies:
                    copy.wait_recv()
                count = len(copies)
                if order == 0:
                    def add(i, _):
                        total = wide(self.part[i, :, y, c])
                        for k in range(count):
                            total += wide(self.ra[k, i, : g.X])
                        self.part[i, :, y, c] = total.astype(jnp.bfloat16)
                        return 0
                else:
                    def add(i, _):
                        total = wide(self.part[i, x, :, c])
                        for k in range(count):
                            total += wide(self.ra[k, i, : g.Y])
                        self.part[i, x, :, c] = total.astype(jnp.bfloat16)
                        return 0
                lax.fori_loop(0, g.Z, add, 0)
                for copy in self.axis_copies(2, order):
                    copy.start()
            self.both(go)
        elif n == 3:
            def go(order):
                copies = list(self.axis_copies(2, order))
                for copy in copies:
                    copy.wait_recv()

                def add(i, _):
                    total = wide(self.part[i, x, y, c])
                    for k in range(len(copies)):
                        total += wide(self.rb[k, i])
                    self.part[i, x, y, c] = total.astype(jnp.bfloat16)
                    return 0
                lax.fori_loop(0, g.Z, add, 0)
            self.both(go)
            for copy in self.z_copies():
                copy.start()
        else:
            total = wide(self.part[z, x, y, c])
            for k, copy in enumerate(self.z_copies()):
                copy.wait_recv()
                total += wide(self.rz[k])
            self.out[...] = total

    def drain(self):
        self.core_copy().wait_send()

        def go(order):
            for phase in (1, 2):
                for copy in self.axis_copies(phase, order):
                    copy.wait_send()
        self.both(go)
        for copy in self.z_copies():
            copy.wait_send()


epsilon = 1e-05
finest_precision = lax.Precision.HIGHEST


def prefix(array, axis, combine, identity):
    count, here = (lax.axis_size(axis), lax.axis_index(axis))
    everything = jax.tree.map(
        lambda part, kind: lax.all_gather(part.astype(kind), axis),
        array,
        (jnp.bfloat16, jnp.bfloat16),
    )
    start = jax.tree.map(
        lambda part, zero: jnp.broadcast_to(jnp.asarray(zero, part.dtype), part.shape),
        array,
        identity,
    )

    def hop(k, before):
        reached = k < here
        new = combine(
            before, jax.tree.map(lambda part, own: part[k].astype(own.dtype), everything, array)
        )
        return jax.tree.map(lambda a, b: jnp.where(reached, a, b), new, before)

    return lax.fori_loop(0, count, hop, start)


def prefix_2(array, axis, join, neutral):
    count = lax.axis_size(axis)
    place = lax.axis_index(axis)
    ahead = count - 1 - place
    gathered = jax.tree.map(
        lambda a, kind: lax.all_gather(a.astype(kind), axis),
        array,
        jax.tree.map(lambda a: jnp.bfloat16 if a.dtype == jnp.float32 else a.dtype, array),
    )
    state = jax.tree.map(lambda a, e: jnp.zeros_like(a) + jnp.asarray(e, a.dtype), array, neutral)

    def one(hop, state):
        source = count - 1 - hop
        return join(
            state,
            jax.tree.map(
                lambda a, own: lax.dynamic_index_in_dim(a, source, 0, False).astype(own.dtype),
                gathered,
                array,
            ),
        )

    return lax.fori_loop(0, ahead, one, state)


def layer_norm(value_rows, norm_gain, norm_shift):
    center = jnp.mean(value_rows, axis=-1, keepdims=True)
    centred = value_rows - center
    spread = jnp.mean(centred * centred, axis=-1, keepdims=True)
    return centred * lax.rsqrt(spread + epsilon) * norm_gain + norm_shift


def gelu_tanh(value_rows):
    return jax.nn.gelu(value_rows, approximate=True)


def add_pair(earlier, later_term):
    return (earlier[0] + later_term[0], earlier[1] + later_term[1])


def causal_mask(length):
    positions = jnp.arange(length)
    return (positions[:, None] >= positions[None, :]).astype(jnp.float32)


def favor_map(proj_low, matrix, feature_scale):
    raw_proj = jnp.einsum("rhd,dm->rhm", proj_low, matrix, preferred_element_type=jnp.float32)
    projection = proj_low.astype(jnp.float32)
    half_norm = (
        0.5
        * feature_scale
        * feature_scale
        * jnp.sum(projection * projection, axis=-1, keepdims=True)
    )
    return jnp.exp(feature_scale * raw_proj - half_norm) / math.sqrt(matrix.shape[1])


def favor_back(map_grad, favor_value, proj_low, matrix, feature_scale):
    log_grad = map_grad * favor_value
    raw_grad = (feature_scale * log_grad).astype(jnp.bfloat16)
    projection = proj_low.astype(jnp.float32)
    through = jnp.einsum("rhm,dm->rhd", raw_grad, matrix, preferred_element_type=jnp.float32)
    return (
        through
        - feature_scale * feature_scale * jnp.sum(log_grad, axis=-1, keepdims=True) * projection
    )


def front(token_block, matrix, params):
    inputs = token_block.astype(jnp.float32)
    length = inputs.shape[0]
    normed = layer_norm(
        inputs, params[7].astype(jnp.float32), params[8].astype(jnp.float32)
    ).astype(jnp.bfloat16)
    mixed = jnp.dot(normed, params[0], preferred_element_type=jnp.float32).astype(jnp.bfloat16)
    head_parts = mixed.reshape(length, 3, H, DH)
    feature_scale = DH ** (-0.25)
    query_features = favor_map(head_parts[:, 0], matrix, feature_scale)
    key_features = favor_map(head_parts[:, 1], matrix, feature_scale)
    query_reduced = query_features.astype(jnp.bfloat16)
    key_reduced = key_features.astype(jnp.bfloat16)
    value_rows = head_parts[:, 2]
    block_local_state = jnp.einsum(
        "nqo,nqi->qoi", key_reduced, value_rows, preferred_element_type=jnp.float32
    )
    local_sum = jnp.sum(key_reduced.astype(jnp.float32), axis=0)
    return (
        inputs,
        normed,
        head_parts,
        query_features,
        key_features,
        query_reduced,
        key_reduced,
        value_rows,
        block_local_state,
        local_sum,
    )


def attend(query_reduced, key_reduced, value_rows, running_prefix_state, norm_sum):
    causal = causal_mask(query_reduced.shape[0])
    scores = (
        jnp.einsum("ihm,jhm->hij", query_reduced, key_reduced, preferred_element_type=jnp.float32)
        * causal[None]
    )
    denominator = jnp.sum(scores, axis=-1).T + jnp.einsum(
        "ihm,hm->ih", query_reduced.astype(jnp.float32), norm_sum, precision=finest_precision
    )
    attention_numerator = jnp.einsum(
        "hij,jhd->ihd", scores.astype(jnp.bfloat16), value_rows, preferred_element_type=jnp.float32
    )
    attention_numerator = attention_numerator + jnp.einsum(
        "plq,lqu->plu",
        query_reduced,
        running_prefix_state.astype(jnp.bfloat16),
        preferred_element_type=jnp.float32,
    )
    return (attention_numerator / denominator[:, :, None], attention_numerator, denominator)


def upper(inputs, output, params):
    length = output.shape[0]
    attended = output.reshape(length, -1).astype(jnp.bfloat16)
    middle = (
        inputs
        + jnp.dot(attended, params[1], preferred_element_type=jnp.float32)
        + params[2].astype(jnp.float32)
    )
    return (attended, middle)


def feed(middle, params):
    normed_two = layer_norm(
        middle, params[9].astype(jnp.float32), params[10].astype(jnp.float32)
    ).astype(jnp.bfloat16)
    hidden = jnp.dot(normed_two, params[3], preferred_element_type=jnp.float32) + params[4].astype(
        jnp.float32
    )
    active = gelu_tanh(hidden).astype(jnp.bfloat16)
    return (
        middle
        + jnp.dot(active, params[5], preferred_element_type=jnp.float32)
        + params[6].astype(jnp.float32)
    )


def upper_back(token_block, upstream, matrix, params, block_carry):
    pieces = front(token_block, matrix, params)
    (
        inputs,
        normed,
        head_parts,
        query_features,
        key_features,
        query_reduced,
        key_reduced,
        value_rows,
        block_local_state,
        local_sum,
    ) = pieces
    running_prefix_state, norm_sum = block_carry
    output, attention_numerator, denominator = attend(
        query_reduced, key_reduced, value_rows, running_prefix_state, norm_sum
    )
    attended, middle = upper(inputs, output, params)
    normed_float, second_pull = jax.vjp(
        layer_norm, middle, params[9].astype(jnp.float32), params[10].astype(jnp.float32)
    )
    normed_two = normed_float.astype(jnp.bfloat16)
    hidden = jnp.dot(normed_two, params[3], preferred_element_type=jnp.float32) + params[4].astype(
        jnp.float32
    )
    active_float, gelu_pull = jax.vjp(gelu_tanh, hidden)
    active = active_float.astype(jnp.bfloat16)
    stored = {"front": pieces, "carry": block_carry}
    down_term = upstream.astype(jnp.bfloat16)
    stored["down"] = jnp.einsum("rf,rd->fd", active, down_term, preferred_element_type=jnp.float32)
    stored["down_bias"] = jnp.sum(upstream, axis=0)
    active_grad = jnp.einsum("rd,fd->rf", down_term, params[5], preferred_element_type=jnp.float32)
    (hidden_grad,) = gelu_pull(active_grad)
    up_term = hidden_grad.astype(jnp.bfloat16)
    stored["up"] = jnp.einsum("rd,rf->df", normed_two, up_term, preferred_element_type=jnp.float32)
    stored["up_bias"] = jnp.sum(hidden_grad, axis=0)
    normed_two_grad = jnp.einsum(
        "rf,df->rd", up_term, params[3], preferred_element_type=jnp.float32
    )
    middle_part, gain_two_grad, shift_two_grad = second_pull(normed_two_grad)
    stored["gain_two"] = gain_two_grad
    stored["shift_two"] = shift_two_grad
    middle_grad = upstream + middle_part
    stored["middle_grad"] = middle_grad
    out_term = middle_grad.astype(jnp.bfloat16)
    stored["out"] = jnp.einsum("re,rd->ed", attended, out_term, preferred_element_type=jnp.float32)
    stored["out_bias"] = jnp.sum(middle_grad, axis=0)
    attended_grad = jnp.einsum(
        "rd,ed->re", out_term, params[1], preferred_element_type=jnp.float32
    ).reshape(output.shape)
    numerator_grad = (attended_grad / denominator[:, :, None]).astype(jnp.bfloat16)
    denom_grad = -jnp.sum(attended_grad * attention_numerator, axis=-1) / (
        denominator * denominator
    )
    stored["numer_grad"] = numerator_grad
    stored["denom_grad"] = denom_grad
    stored["state_grad"] = jnp.einsum(
        "jfp,jfl->fpl", query_reduced, numerator_grad, preferred_element_type=jnp.float32
    )
    stored["sum_grad"] = jnp.einsum(
        "ih,ihm->hm", denom_grad, query_reduced.astype(jnp.float32), precision=finest_precision
    )
    return stored


def lower_back(stored, later_part, matrix, params):
    (
        inputs,
        normed,
        head_parts,
        query_features,
        key_features,
        query_reduced,
        key_reduced,
        value_rows,
        block_local_state,
        local_sum,
    ) = stored["front"]
    running_prefix_state, norm_sum = stored["carry"]
    state_later, sum_later = later_part
    numerator_grad = stored["numer_grad"]
    denom_grad = stored["denom_grad"]
    length = inputs.shape[0]
    causal = causal_mask(length)
    scores = (
        jnp.einsum("ihm,jhm->hij", query_reduced, key_reduced, preferred_element_type=jnp.float32)
        * causal[None]
    )
    scores_grad = jnp.einsum(
        "ihd,jhd->hij", numerator_grad, value_rows, preferred_element_type=jnp.float32
    )
    score_term = ((scores_grad + denom_grad.T[:, :, None]) * causal[None]).astype(jnp.bfloat16)
    later_reduced = state_later.astype(jnp.bfloat16)
    query_grad = jnp.einsum(
        "hij,jhm->ihm", score_term, key_reduced, preferred_element_type=jnp.float32
    )
    query_grad = query_grad + jnp.einsum(
        "gvw,vcw->gvc",
        numerator_grad,
        running_prefix_state.astype(jnp.bfloat16),
        preferred_element_type=jnp.float32,
    )
    query_grad = query_grad + denom_grad[:, :, None] * norm_sum[None]
    key_grad = jnp.einsum(
        "hij,ihm->jhm", score_term, query_reduced, preferred_element_type=jnp.float32
    )
    key_grad = key_grad + jnp.einsum(
        "prc,rqc->prq", value_rows, later_reduced, preferred_element_type=jnp.float32
    )
    key_grad = key_grad + sum_later[None]
    value_grad = jnp.einsum(
        "hij,ihd->jhd",
        scores.astype(jnp.bfloat16),
        numerator_grad,
        preferred_element_type=jnp.float32,
    )
    value_grad = value_grad + jnp.einsum(
        "qsa,saw->qsw", key_reduced, later_reduced, preferred_element_type=jnp.float32
    )
    feature_scale = DH ** (-0.25)
    query_proj = favor_back(query_grad, query_features, head_parts[:, 0], matrix, feature_scale)
    key_proj = favor_back(key_grad, key_features, head_parts[:, 1], matrix, feature_scale)
    mixed_grad = (
        jnp.stack([query_proj, key_proj, value_grad], axis=1)
        .reshape(length, -1)
        .astype(jnp.bfloat16)
    )
    input_part = jnp.einsum("rd,re->de", normed, mixed_grad, preferred_element_type=jnp.float32)
    normed_grad = jnp.einsum("re,de->rd", mixed_grad, params[0], preferred_element_type=jnp.float32)
    _, first_pull = jax.vjp(
        layer_norm, inputs, params[7].astype(jnp.float32), params[8].astype(jnp.float32)
    )
    inputs_part, gain_one_grad, shift_one_grad = first_pull(normed_grad)
    return (stored["middle_grad"] + inputs_part, input_part, gain_one_grad, shift_one_grad)


BF = jnp.bfloat16
F32 = jnp.float32
M = 256
SCALE = DH ** (-0.25)
LOG2E = math.log2(math.e)
PAIRS = H // 2
STATE_ROWS = 160


def dot(a, b):
    return jnp.dot(a, b, preferred_element_type=F32)


def dot_nt(a, b):
    return lax.dot_general(a, b, (((1,), (1,)), ((), ())), preferred_element_type=F32)


class States:
    def __init__(self, geo, lane, earlier):
        self.geo, self.lane, self.earlier = geo, lane, earlier
        self.per = geo.Y + 1
        self.first = lane.take(self.per * PAIRS)

    @staticmethod
    def scratch(geo):
        one = (PAIRS, STATE_ROWS, M)
        two = (PAIRS, 2, STATE_ROWS, M)
        return [pltpu.VMEM(two, BF), pltpu.VMEM(two, BF), pltpu.VMEM(one, BF),
                pltpu.VMEM((PAIRS, max(geo.Y - 1, 1), STATE_ROWS, M), BF), pltpu.VMEM(one, BF),
                pltpu.VMEM(one, BF), pltpu.VMEM(two, BF)]

    def bind(self, buffers):
        self.own, self.sibling, self.chip, self.chips, self.base, self.base_sibling, self.total = buffers

    def copies(self, p, phase):
        g = self.geo
        z, x, y, c = g.me()
        index = self.first + p * self.per
        other = g.device(z, x, y, 1 - c)
        if phase == 0:
            return [remote(self.lane, index, self.own.at[p], self.sibling.at[p], other)]
        if phase == 1:
            return [remote(self.lane, index + k, self.chip.at[p], self.chips.at[p, k - 1],
                           g.device(z, x, (y + k) % g.Y, c)) for k in range(1, g.Y)]
        return [remote(self.lane, index + g.Y, self.base.at[p], self.base_sibling.at[p], other)]

    def step(self, n, p):
        g = self.geo
        z, x, y, c = g.me()
        if n > 0:
            for copy in self.copies(p, n - 1):
                copy.wait_recv()
        if n == 1:
            self.chip[p] = (self.own[p, c].astype(F32) + self.sibling[p, c].astype(F32)).astype(BF)
        elif n == 2:
            total = jnp.zeros((STATE_ROWS, M), F32)
            for k in range(1, g.Y):
                source = (y + g.Y - k) % g.Y
                counts = source < y if self.earlier else source > y
                total += jnp.where(counts, 1.0, 0.0) * self.chips[p, k - 1].astype(F32)
            self.base[p] = total.astype(BF)
        elif n == 3:
            near = jnp.where(c == (1 if self.earlier else 0), 1.0, 0.0)
            self.total[p, c] = (self.base[p].astype(F32) + near * self.sibling[p, c].astype(F32)).astype(BF)
            self.total[p, 1 - c] = (self.base_sibling[p].astype(F32)
                                    + near * self.sibling[p, 1 - c].astype(F32)).astype(BF)
        if n < 3:
            for copy in self.copies(p, n):
                copy.start()

    def drain(self):
        for p in range(PAIRS):
            for phase in range(3):
                for copy in self.copies(p, phase):
                    copy.wait_send()


class PairStates:
    def __init__(self, states, p):
        self.states, self.p = states, p

    def step(self, n):
        self.states.step(n, self.p)


class ScatterDirect:
    def __init__(self, geo, lane):
        self.geo, self.lane = geo, lane
        self.far = [(i, j, k) for i in range(geo.Z) for j in range(geo.X) for k in range(geo.Y)][1:]
        self.core = lane.take()
        self.first = lane.take(len(self.far))

    @staticmethod
    def scratch(geo, rows, width):
        return [pltpu.VMEM((geo.Z, geo.X, geo.Y, rows, width), jnp.bfloat16),
                pltpu.VMEM((geo.Z * geo.X * geo.Y - 1, rows, width), jnp.bfloat16)]

    def bind(self, part, out, buffers):
        self.part, self.out = part, out
        self.rc, self.rz = buffers

    def core_copy(self):
        z, x, y, c = self.geo.me()
        return remote(self.lane, self.core, self.part.at[:, :, :, 1 - c], self.rc, self.geo.device(z, x, y, 1 - c))

    def copies(self):
        g = self.geo
        z, x, y, c = g.me()
        for n, (i, j, k) in enumerate(self.far):
            to = ((z + i) % g.Z, (x + j) % g.X, (y + k) % g.Y, c)
            yield remote(self.lane, self.first + n, self.part.at[to], self.rz.at[n], g.device(*to))

    def step(self, n):
        g = self.geo
        z, x, y, c = g.me()
        if n == 0:
            self.core_copy().start()
        elif n == 1:
            self.core_copy().wait_recv()

            def add(i, _):
                total = self.part[i, :, :, c].astype(F32) + self.rc[i].astype(F32)
                self.part[i, :, :, c] = total.astype(BF)
                return 0
            lax.fori_loop(0, g.Z, add, 0)
            for copy in self.copies():
                copy.start()
        else:
            total = self.part[z, x, y, c].astype(F32)
            for n, copy in enumerate(self.copies()):
                copy.wait_recv()
                total += self.rz[n].astype(F32)
            self.out[...] = total

    def drain(self):
        self.core_copy().wait_send()
        for copy in self.copies():
            copy.wait_send()


DIRECT = ("rI3", "rV",)
PLAN = {
    "start": (("S", 0), ("I0", 0), ("I1", 0), ("I2", 0), ("I3", 0),),
    "first": (("O", 0), ("F0", 0), ("F1", 0), ("S", 1), ("I0", 1), ("I1", 1), ("S", 2), ("I2", 1), ("I0", 2),
        ("I3", 1), ("I1", 2), ("S", 3), ("O", 1), ("I2", 2), ("S", 4),),
    "norm1": (("I0", 3), ("I3", 2),),
    "proj0.pre": (("F0", 1), ("I1", 3), ("O", 2), ("I0", 4),),
    "proj0.1": (("f0", 0), ("I2", 3), ("F1", 1), ("I3", 3),),
    "proj1.pre": (("I1", 4),),
    "proj1.1": (("f1", 0), ("f0", 1),),
    "proj2.pre": (("I2", 4),),
    "proj2.0": (("I3", 4), ("O", 3),),
    "proj2.1": (("f2", 0), ("f1", 1),),
    "proj3.1": (("f3", 0), ("f2", 1), ("O", 4), ("F2", 0),),
    "att0.pre": (("f0", 2), ("f3", 1), ("f0", 3),),
    "att0.0": (("f1", 2), ("F0", 2),),
    "att0.1": (("F3", 0),),
    "att1.pre": (("f2", 2), ("f1", 3),),
    "att1.1": (("f2", 3), ("F2", 1), ("f3", 2),),
    "att2.0": (("F1", 2),),
    "att2.1": (("f3", 3),),
    "att3.0": (("F0", 3),),
    "att3.1": (("F3", 1),),
    "mid.0": (("F2", 2),),
    "feed0.pre": (("F0", 4),),
    "feed0.0": (("F1", 3),),
    "feed0.1": (("F3", 2),),
    "feed0.end": (("rF0", 0), ("F1", 4),),
    "feed1.0": (("F2", 3),),
    "feed1.1": (("rF0", 1), ("F3", 3),),
    "feed2.pre": (("F2", 4),),
    "feed2.0": (("F3", 4),),
    "feed2.end": (("rF2", 0), ("rF0", 2),),
    "feed3.1": (("rF2", 1),),
    "feed3.end": (("rF0", 3),),
    "out.end": (("rO", 0),),
    "st0": (("b0", 0), ("rF2", 2),),
    "st1": (("b1", 0), ("rF1", 0),),
    "st2": (("b2", 0), ("rF0", 4), ("b0", 1), ("rO", 1),),
    "st3": (("b3", 0), ("b1", 1),),
    "pb0.pre": (("rF3", 0), ("rF2", 3), ("rF1", 1), ("b2", 1), ("b3", 1), ("b0", 2), ("rF3", 1), ("b0", 3),),
    "pb0.m": (("rF2", 4), ("b1", 2), ("rO", 2),),
    "pb1.m": (("b1", 3),),
    "pb1": (("rI0", 0), ("rF1", 2),),
    "pb2.m": (("b2", 2), ("rI0", 1),),
    "pb3.m": (("b2", 3),),
    "pb3": (("rI1", 0),),
    "pb4.m": (("b3", 2), ("rI0", 2), ("rI1", 1), ("rF1", 3),),
    "pb5.m": (("b3", 3), ("rF3", 2),),
    "pb5": (("rI2", 0), ("rI1", 2),),
    "pb6": (("rF3", 3),),
    "pb7.m": (("rI2", 1), ("rI1", 3), ("rO", 3),),
    "pb7": (("rI3", 0), ("rI0", 3),),
    "nb1": (("rI3", 1), ("rI2", 2), ("rI1", 4), ("rF3", 4),),
    "fb1": (("rV", 0), ("rF1", 4), ("rO", 4),),
    "end": (("rI0", 4), ("rV", 1), ("rI2", 3), ("rI3", 2), ("rV", 2), ("rI2", 4),),
}


def layer_kernel(geo, lane, plan, *refs):
    (tokens_hbm, cot_hbm, feat, out_bias_in, down_bias_in, first_gain_in, first_shift_in, second_gain_in,
     second_shift_in, up_bias_in, wi_in, wo_own, wu_in, wd_in,
     result_hbm, tokens_grad_hbm, inp_out, out_out, up_out, down_out, vec_out,
     tokens, cot, result, tokens_grad, small_own, small, wi_own, wi, wo_all, wf_own, wf,
     normed, normed_t, mixed, pq, pk, den, attended, middle, n2_t,
     act, hg, vecs, grads, fa, ft, perm, part_i, part_o, part_f, part_v, up_parts, vec_sum) = refs[:54]
    rest = list(refs[54:])
    fwd, bwd, tasks = plan
    take = lambda n: [rest.pop(0) for _ in range(n)]
    fwd.bind(take(7))
    bwd.bind(take(7))
    scatter_buffers = {name: take(2 if type(task) is ScatterDirect else 4)
                       for name, task in tasks.items() if name[0] == "r"}
    lane.send, lane.recv = take(2)
    local_sem = rest.pop(0)
    tasks["S"].bind(small_own, small)
    tasks["O"].bind(wo_own, wo_all)
    tasks["rO"].bind(part_o, out_out, scatter_buffers["rO"])
    tasks["rV"].bind(part_v, vec_sum, scatter_buffers["rV"])
    for p in range(PAIRS):
        tasks[f"I{p}"].bind(wi_own.at[p], wi.at[p])
        tasks[f"rI{p}"].bind(part_i.at[p], inp_out.at[p], scatter_buffers[f"rI{p}"])
    for t in range(wf.shape[0]):
        tasks[f"F{t}"].bind(wf_own.at[t], wf.at[t])
        tasks[f"rF{t}"].bind(part_f.at[t], up_parts.at[t], scatter_buffers[f"rF{t}"])
    n2 = normed
    D = tokens.shape[-1]
    L = tokens.shape[1]
    TILES = wf.shape[0]
    HALF = L // 2
    lead = (geo.Z, geo.X, geo.Y, 2)
    z, x, y, c = geo.me()
    place = (((z * geo.X + x) * geo.Y + y) * 2 + c) % 8

    def loop(n, body):
        def step(i, _):
            body(i)
            return 0
        lax.fori_loop(0, n, step, 0)

    def pump(point):
        for name, n in PLAN.get(point, ()):
            tasks[name].step(n)

    def pump_at(now, points):
        for when, point in enumerate(points):
            if point in PLAN:
                @pl.when(now == when)
                def _():
                    pump(point)

    def local(i, src, dst):
        return pltpu.make_async_copy(src, dst, local_sem.at[i])

    local(0, tokens_hbm, tokens).start()
    local(1, cot_hbm, cot).start()
    vec_sum[...] = jnp.zeros((16, 128), F32)
    for v, ref in enumerate((out_bias_in, down_bias_in, first_gain_in, first_shift_in, second_gain_in,
                             second_shift_in)):
        vec_sum[v, :16] = ref[...].astype(F32)
    up_bias_row = up_bias_in[...].astype(F32)
    for t in range(TILES):
        vec_sum[6 + t, :16] = up_bias_row[t * 16:(t + 1) * 16]
    small_own[...] = pltpu.roll(vec_sum[...], place * 16, 1).astype(BF)
    for p in range(PAIRS):
        wi_own[p] = jnp.concatenate([wi_in[:, k * D + p * 128: k * D + (p + 1) * 128] for k in range(3)], axis=1)
    geo.barrier()
    pump("start")
    source = lax.broadcasted_iota(jnp.int32, (512, 1), 0)
    target = (source % 64) // 16 * 128 + source // 64 * 16 + source % 16
    perm[...] = jnp.where(lax.broadcasted_iota(jnp.int32, (512, 512), 1) == target, 1.0, 0.0).astype(BF)
    stacked = jnp.concatenate([wu_in[:, g * 512:(g + 1) * 512] for g in range(TILES)], axis=0)
    stacked = dot(stacked, perm[...]).astype(BF)
    for t in range(TILES):
        for g in range(TILES):
            wf_own[t, :, g * 128:(g + 1) * 128] = stacked[g * 16:(g + 1) * 16, t * 128:(t + 1) * 128]
        wf_own[t, :, D:] = wd_in[t * 16:(t + 1) * 16]

    f = feat[...]
    zero = jnp.zeros((DH, M), BF)
    one = jnp.ones((DH, M), BF)
    fa[0] = jnp.concatenate([f, zero, -one, zero], axis=0)
    fa[1] = jnp.concatenate([zero, f, zero, -one], axis=0)
    ft[...] = jnp.concatenate([jnp.concatenate([f, zero], axis=1), jnp.concatenate([zero, f], axis=1),
                               jnp.concatenate([one, zero], axis=1), jnp.concatenate([zero, one], axis=1)], axis=0)
    low_lane = lax.broadcasted_iota(jnp.int32, (1, 128), 1) < DH
    m0f = jnp.where(low_lane, 1.0, 0.0)
    m0 = m0f.astype(BF)
    m1 = (1.0 - m0f).astype(BF)
    tri_r = lax.broadcasted_iota(jnp.int32, (HALF, HALF), 0)
    tri_c = lax.broadcasted_iota(jnp.int32, (HALF, HALF), 1)

    pump("first")

    flat = lambda v: v.reshape(-1, v.shape[-1])
    sums = jnp.sum(small[...].astype(F32).reshape(-1, 8, 16, 128), axis=1)
    vecs[...] = jnp.concatenate([sums[g] for g in range(D // 128)], axis=1)
    out_bias, down_bias = lambda: vecs[0:1], lambda: vecs[1:2]

    def norm_parts(rows):
        center = jnp.mean(rows, axis=-1, keepdims=True)
        centred = rows - center
        spread = jnp.mean(centred * centred, axis=-1, keepdims=True)
        inv = lax.rsqrt(spread + epsilon)
        return centred * inv, inv

    def first_norm(s):
        hat, _ = norm_parts(tokens[s].astype(F32))
        value = (hat * vecs[2:3] + vecs[3:4]).astype(BF)
        normed[s] = value
        normed_t[s] = value.T
    pump("vec")
    local(0, tokens_hbm, tokens).wait()
    first_norm(0)
    pump("norm0")
    first_norm(1)
    pump("norm1")

    def vx(s, p):
        v = mixed[s, p, :, 2 * 128:]
        ones = jnp.ones(v.shape, BF)
        return (jnp.concatenate([v * m0, ones * m0], axis=1), jnp.concatenate([v * m1, ones * m1], axis=1))

    def project(i):
        p, s = i // 2, i % 2
        pump_at(i, [f"proj{n // 2}.pre" if n % 2 == 0 else "" for n in range(2 * PAIRS)])
        mixed[s, p] = dot(normed[s], flat(wi[p])).astype(BF)
        for part, target in ((0, pq), (1, pk)):
            rows = mixed[s, p, :, part * 128:(part + 1) * 128]
            wide = rows.astype(F32)
            lhs = jnp.concatenate([rows, (wide * wide * (0.5 * SCALE)).astype(BF)], axis=1)
            for h in range(2):
                power = dot(lhs, fa[h]) * (SCALE * LOG2E) - 0.5 * math.log2(M)
                target[s, 2 * p + h] = jnp.exp2(power).astype(BF)
        v = mixed[s, p, :, 2 * 128:]
        lhs = jnp.concatenate([v.T, jnp.ones((16, L), BF)], axis=0)
        r0 = dot(lhs, pk[s, 2 * p])
        r1 = dot(lhs, pk[s, 2 * p + 1])
        fwd.own[p, s] = jnp.concatenate([r0[:64], r1[64:128], r0[128:], r1[128:]], axis=0).astype(BF)
        pump_at(i, [f"proj{n // 2}.{n % 2}" for n in range(2 * PAIRS)])
    loop(2 * PAIRS, project)

    def state_cols(total, p, s, h, copies):
        state = total[p, s, h * 64:(h + 1) * 64]
        extra = total[p, s, 128 + 16 * h:144 + 16 * h]
        zeros = jnp.zeros((DH, M), BF)
        if copies:
            extra = jnp.concatenate([extra] * 4, axis=0)
        else:
            extra = jnp.concatenate([extra, jnp.zeros((48, M), BF)], axis=0)
        parts = [state, zeros, extra, zeros] if h == 0 else [zeros, state, zeros, extra]
        return jnp.concatenate(parts, axis=0)

    lower = tri_r >= tri_c
    upper = tri_r <= tri_c

    def attend_pair(i):
        p, s = i // 2, i % 2
        pump_at(i, [f"att{n // 2}.pre" if n % 2 == 0 else "" for n in range(2 * PAIRS)])
        v0, v1 = vx(s, p)
        states = jnp.concatenate([state_cols(fwd.total, p, s, h, True) for h in range(2)], axis=1)
        lanes = pl.ds(pl.multiple_of(p * 128, 128), 128)
        for b in range(2):
            rows = slice(b * HALF, (b + 1) * HALF)
            scores = []
            for h in range(2):
                q = pq[s, 2 * p + h, rows]
                if b == 1:
                    scores.append(dot_nt(q, pk[s, 2 * p + h, :HALF]).astype(BF))
                scores.append(jnp.where(lower, dot_nt(q, pk[s, 2 * p + h, rows]), 0.0).astype(BF))
            rhs = jnp.concatenate([v0[:(b + 1) * HALF], v1[:(b + 1) * HALF]], axis=0)
            ext = dot(jnp.concatenate(scores, axis=1), rhs)
            ext += dot_nt(jnp.concatenate([pq[s, 2 * p, rows], pq[s, 2 * p + 1, rows]], axis=1), states)
            n_, d_ = ext[:, :128], ext[:, 128:]
            inv = 1.0 / d_
            den[s, rows, lanes] = inv
            attended[s, rows, lanes] = (n_ * inv).astype(BF)
        pump_at(i, [f"att{n // 2}.{n % 2}" for n in range(2 * PAIRS)])
    loop(2 * PAIRS, attend_pair)
    pump("mid.pre")
    local(1, cot_hbm, cot).wait()

    def wo():
        return flat(wo_all[...])

    def to_middle(s):
        value = tokens[s].astype(F32) + dot(attended[s], wo()) + out_bias()
        middle[s] = value
        hat, _ = norm_parts(value)
        low = (hat * vecs[4:5] + vecs[5:6]).astype(BF)
        n2[s] = low
        n2_t[s] = low.T
        result[s] = value + down_bias()
        tokens_grad[s] = jnp.zeros((L, D), F32)
        pump_at(s, ["mid.0", "mid.1"])
    loop(2, to_middle)
    grads[...] = jnp.zeros(grads.shape, F32)

    k0 = math.sqrt(2.0 / math.pi)

    def feed_tile(t):
        pump_at(t, [f"feed{n}.pre" for n in range(TILES)])
        bias = vecs[pl.ds(6 + t, 1)]
        wut = lambda: flat(wf[t, :, :, :, :, :, :D])
        wdt = lambda: flat(wf[t, :, :, :, :, :, D:])

        def seq(s):
            for b in range(2):
                rows = slice(b * HALF, (b + 1) * HALF)
                u = dot(n2[s, rows], wut()) + bias
                uu = u * u
                th = jnp.tanh(u * (k0 + (k0 * 0.044715) * uu))
                half = 0.5 + 0.5 * th
                a = (u * half).astype(BF)
                act[s, rows] = a
                slope = half + (0.5 * u) * (1.0 - th * th) * (k0 + (3.0 * 0.044715 * k0) * uu)
                back = dot_nt(cot[s, rows], wdt()) * slope
                grads[pl.ds(6 + t, 1)] += jnp.sum(back, axis=0, keepdims=True)
                low = back.astype(BF)
                hg[s, rows] = low
                result[s, rows] += dot(a, wdt())
                tokens_grad[s, rows] += dot_nt(low, wut())
            pump_at(2 * t + s, [f"feed{n // 2}.{n % 2}" for n in range(2 * TILES)])
        loop(2, seq)
        dwd = dot(act[0].T, cot[0]) + dot(act[1].T, cot[1])
        part_f[t, :, :, :, :, :, D:] = dwd.astype(BF).reshape(lead + (-1, D))
        dwu = dot(n2_t[0], hg[0]) + dot(n2_t[1], hg[1])
        part_f[t, :, :, :, :, :, :D] = dwu.astype(BF).reshape(lead + (-1, 512))
        pump_at(t, [f"feed{n}.end" for n in range(TILES)])
    loop(TILES, feed_tile)
    local(2, result, result_hbm).start()

    ones_block = jnp.concatenate([jnp.concatenate([jnp.ones((64, 64), F32), jnp.zeros((64, 64), F32)], axis=1),
                                  jnp.concatenate([jnp.zeros((64, 64), F32), jnp.ones((64, 64), F32)], axis=1)],
                                 axis=0).astype(BF)
    ones_two = jnp.concatenate([ones_block, ones_block], axis=0)
    lane_id = lax.broadcasted_iota(jnp.int32, (1, 128), 1)
    hi_lane = jnp.where((lane_id % DH) == 0, 1.0, 0.0)
    lo_lane = jnp.where((lane_id % DH) == 1, 1.0, 0.0)

    def norm_back(rows, dy, gain):
        hat, inv = norm_parts(rows)
        dg = dy * gain
        m_a = jnp.mean(dg, axis=-1, keepdims=True)
        m_b = jnp.mean(dg * hat, axis=-1, keepdims=True)
        return (inv * (dg - m_a - hat * m_b), jnp.sum(dy * hat, axis=0, keepdims=True),
                jnp.sum(dy, axis=0, keepdims=True))

    def out_back(s):
        dx, dgain, dshift = norm_back(middle[s], tokens_grad[s], vecs[4:5])
        up = cot[s].astype(F32)
        mg = up + dx
        middle[s] = mg
        low = mg.astype(BF)
        act[s] = low
        grads[0:1] += jnp.sum(mg, axis=0, keepdims=True)
        grads[1:2] += jnp.sum(up, axis=0, keepdims=True)
        grads[4:5] += dgain
        grads[5:6] += dshift
        ag = dot_nt(low, wo())
        inv = den[s]
        ng = ag * inv
        prod = ng * attended[s].astype(F32)
        n2[s] = ng.astype(BF)
        for p in range(PAIRS):
            cols = slice(p * 128, (p + 1) * 128)
            pr = prod[:, cols]
            hi = pr.astype(BF)
            lo = (pr - hi.astype(F32)).astype(BF)
            dgr = -dot(jnp.concatenate([hi, lo], axis=1), ones_two)
            dhi = dgr.astype(BF).astype(F32)
            dlo = dgr - dhi
            hg[s, :, cols] = (dhi * hi_lane + dlo * lo_lane).astype(BF)
        pump_at(s, ["out.0", "out.1"])
    loop(2, out_back)
    dwo = dot(attended[0].T, act[0]) + dot(attended[1].T, act[1])
    part_o[...] = dwo.astype(BF).reshape(lead + (-1, D))
    pump("out.end")

    def ngx(s, p):
        lanes = pl.ds(pl.multiple_of(p * 128, 128), 128)
        return jnp.concatenate([n2[s, :, lanes], hg[s, :, lanes]], axis=1)

    def state_back(p):
        def seq(s):
            lhs = ngx(s, p).T
            r0 = dot(lhs, pq[s, 2 * p])
            r1 = dot(lhs, pq[s, 2 * p + 1])
            bwd.own[p, s] = jnp.concatenate([r0[:64], r1[64:128], r0[128:144], r1[192:208]], axis=0).astype(BF)
        loop(2, seq)
        pump_at(p, [f"st{n}" for n in range(PAIRS)])
    loop(PAIRS, state_back)

    def pair_back(i):
        p, s = i // 2, i % 2
        pump_at(i, [f"pb{n}.pre" for n in range(2 * PAIRS)])
        v0, v1 = vx(s, p)
        x = ngx(s, p)
        ng = x[:, :128]
        logs_q, logs_k, att = [], [], []
        for h, v in ((0, v0), (1, v1)):
            q, k = pq[s, 2 * p + h], pk[s, 2 * p + h]
            sx = state_cols(fwd.total, p, s, h, True)
            sg = state_cols(bwd.total, p, s, h, False)
            lo, hi = slice(0, HALF), slice(HALF, L)

            def masked(keep, value):
                return jnp.where(keep, value, 0.0).astype(BF)
            g00 = masked(lower, dot_nt(x[lo], v[lo]))
            g10 = dot_nt(x[hi], v[lo]).astype(BF)
            g11 = masked(lower, dot_nt(x[hi], v[hi]))
            qg0 = dot(jnp.concatenate([g00, x[lo]], axis=1), jnp.concatenate([k[lo], sx], axis=0))
            qg1 = dot(jnp.concatenate([g10, g11, x[hi]], axis=1), jnp.concatenate([k, sx], axis=0))
            logs_q.append((jnp.concatenate([qg0, qg1], axis=0) * q.astype(F32)).astype(BF))
            t00 = masked(upper, dot_nt(v[lo], x[lo]))
            t01 = dot_nt(v[lo], x[hi]).astype(BF)
            t11 = masked(upper, dot_nt(v[hi], x[hi]))
            kg0 = dot(jnp.concatenate([t00, t01, v[lo]], axis=1), jnp.concatenate([q, sg], axis=0))
            kg1 = dot(jnp.concatenate([t11, v[hi]], axis=1), jnp.concatenate([q[hi], sg], axis=0))
            logs_k.append((jnp.concatenate([kg0, kg1], axis=0) * k.astype(F32)).astype(BF))
            a00 = masked(upper, dot_nt(k[lo], q[lo]))
            a01 = dot_nt(k[lo], q[hi]).astype(BF)
            a11 = masked(upper, dot_nt(k[hi], q[hi]))
            att.append((a00, a01, a11))
        pump_at(i, [f"pb{n}.m" for n in range(2 * PAIRS)])
        n0, n1 = ng * m0, ng * m1
        vg0 = dot(jnp.concatenate([att[0][0], att[0][1], att[1][0], att[1][1]], axis=1),
                  jnp.concatenate([n0, n1], axis=0))
        vg1 = dot(jnp.concatenate([att[0][2], att[1][2]], axis=1), jnp.concatenate([n0[HALF:], n1[HALF:]], axis=0))
        zeros = jnp.zeros((DH, M), BF)
        sgt = jnp.concatenate([jnp.concatenate([bwd.total[p, s, :64], zeros], axis=0),
                               jnp.concatenate([zeros, bwd.total[p, s, 64:128]], axis=0)], axis=1)
        vg = jnp.concatenate([vg0, vg1], axis=0)
        vg += dot_nt(jnp.concatenate([pk[s, 2 * p], pk[s, 2 * p + 1]], axis=1), sgt)
        out = []
        for part, logs in ((0, logs_q), (1, logs_k)):
            through = dot_nt(jnp.concatenate(logs, axis=1), ft[...])
            rows = mixed[s, p, :, part * 128:(part + 1) * 128].astype(F32)
            out.append((SCALE * through[:, :128] - SCALE * SCALE * through[:, 128:] * rows).astype(BF))
        mg = jnp.concatenate(out + [vg.astype(BF)], axis=1)
        act[s, :, :384] = mg
        mixed[s, p] = mg

        @pl.when(s == 1)
        def _():
            dwi = dot(normed_t[0], act[0, :, :384]) + dot(normed_t[1], act[1, :, :384])
            part_i[p] = dwi.astype(BF).reshape(lead + (-1, 384))
        pump_at(i, [f"pb{n}" for n in range(2 * PAIRS)])
    loop(2 * PAIRS, pair_back)

    def normed_back(s):
        for b in range(2):
            rows = slice(b * HALF, (b + 1) * HALF)
            back = dot_nt(mixed[s, 0, rows], flat(wi[0]))
            for p in range(1, PAIRS):
                back += dot_nt(mixed[s, p, rows], flat(wi[p]))
            tokens_grad[s, rows] = back
    normed_back(0)
    pump("nb0")
    normed_back(1)
    pump("nb1")

    def first_back(s):
        dx, dgain, dshift = norm_back(tokens[s].astype(F32), tokens_grad[s], vecs[2:3])
        tokens_grad[s] = middle[s] + dx
        grads[2:3] += dgain
        grads[3:4] += dshift
    first_back(0)
    pump("fb0")
    first_back(1)
    for g in range(D // 128):
        tile = grads[:, g * 128:(g + 1) * 128].astype(BF)
        for k in range(8):
            chip, core = (8 * g + k) // 2, k % 2
            part_v[chip // (geo.X * geo.Y), chip // geo.Y % geo.X, chip % geo.Y, core] = tile
    local(3, tokens_grad, tokens_grad_hbm).start()
    pump("fb1")
    stacked = jnp.concatenate([jnp.concatenate([up_parts[t, :, g * 128:(g + 1) * 128] for t in range(TILES)], axis=1)
                               for g in range(TILES)], axis=0)
    high = stacked.astype(BF)
    low = (stacked - high.astype(F32)).astype(BF)
    stacked = dot_nt(high, perm[...]) + dot_nt(low, perm[...])
    for g in range(TILES):
        up_out[:, g * 512:(g + 1) * 512] = stacked[g * 16:(g + 1) * 16]
    for t in range(TILES):
        down_out[t * 16:(t + 1) * 16] = up_parts[t, :, D:]
    late = {name for name, n in PLAN["end"]}
    drains = [fwd, bwd] + [task for name, task in tasks.items() if name not in late and hasattr(task, "drain")]
    for task in drains:
        task.drain()
    pump("end")
    vec_out[...] = pltpu.roll(vec_sum[...], lax.rem(8 - place, 8) * 16, 1)
    local(2, result, result_hbm).wait()
    local(3, tokens_grad, tokens_grad_hbm).wait()
    for name in sorted(late):
        if hasattr(tasks[name], "drain"):
            tasks[name].drain()


def finish_kernel(result_in, tokens_grad_in, inp, out, up, down, vec, *refs):
    (result, tokens_grad, inp_out, out_out, out_bias, up_out, up_bias, down_out, down_bias,
     first_gain, first_shift, second_gain, second_shift, held, in_sems, out_sems) = refs
    cuts = []
    for a, b, n in ((result_in, result, 0), (tokens_grad_in, tokens_grad, 1)):
        for m in range(a.shape[0]):
            for k in range(2):
                rows = pl.ds(k * (a.shape[1] // 2), a.shape[1] // 2)
                i = len(cuts)
                slot = held.at[n, m, rows]
                cuts.append((pltpu.make_async_copy(a.at[m, rows], slot, in_sems.at[i]),
                             pltpu.make_async_copy(slot, b.at[m, rows], out_sems.at[i])))
    for first, _ in cuts:
        first.start()
    D = out.shape[-1]
    for p in range(PAIRS):
        for k in range(3):
            inp_out[:, k * D + p * 128: k * D + (p + 1) * 128] = inp[p, :, k * 128:(k + 1) * 128]
    out_out[...] = out[...]
    up_out[...] = up[...]
    down_out[...] = down[...]
    n = out_bias.shape[-1]
    for v, ref in enumerate((out_bias, down_bias, first_gain, first_shift, second_gain, second_shift)):
        ref[...] = vec[v, :n]
    for t in range(4):
        up_bias[pl.ds(t * n, n)] = vec[6 + t, :n]
    for first, second in cuts:
        first.wait()
        second.start()
    for _, second in cuts:
        second.wait()


def fused(geo, args):
    (tokens, feature_matrix, input_weight, output_weight, output_bias, up_weight, up_bias, down_weight,
     down_bias, first_gain, first_shift, second_gain, second_shift, cotangent) = args
    rows, D = input_weight.shape[0], tokens.shape[-1]
    L = tokens.shape[1]
    FF = up_weight.shape[1]
    tiles = FF // 512
    lane = Lane()
    fwd, bwd = States(geo, lane, True), States(geo, lane, False)
    tasks = {name: Gather(geo, lane) for name in ["S", "O"] + [f"I{p}" for p in range(PAIRS)]
             + [f"F{t}" for t in range(tiles)]}
    scatters = {"rO": D, "rV": 128}
    scatters.update({f"rI{p}": 384 for p in range(PAIRS)})
    scatters.update({f"rF{t}": 2 * D for t in range(tiles)})
    for name in scatters:
        tasks[name] = (ScatterDirect if name in DIRECT else Scatter)(geo, lane)
    for p in range(PAIRS):
        tasks[f"f{p}"], tasks[f"b{p}"] = PairStates(fwd, p), PairStates(bwd, p)
    plan = (fwd, bwd, tasks)
    lead = (geo.Z, geo.X, geo.Y, 2)
    V = pltpu.VMEM
    scratch = [
        V((2, L, D), BF), V((2, L, D), BF), V((2, L, D), F32), V((2, L, D), F32),
        V((rows, 128), BF), V(lead + (rows, 128), BF), V((PAIRS, rows, 384), BF), V((PAIRS,) + lead + (rows, 384), BF),
        V(lead + (rows, D), BF), V((tiles, rows, 2 * D), BF), V((tiles,) + lead + (rows, 2 * D), BF),
        V((2, L, D), BF), V((2, D, L), BF), V((2, PAIRS, L, 384), BF), V((2, H, L, M), BF), V((2, H, L, M), BF),
        V((2, L, D), F32), V((2, L, D), BF), V((2, L, D), F32), V((2, D, L), BF),
        V((2, L, 512), BF), V((2, L, 512), BF), V((16, D), F32), V((16, D), F32),
        V((2, M, M), BF), V((M, 2 * M), BF), V((512, 512), BF),
        V((PAIRS,) + lead + (rows, 384), BF), V(lead + (rows, D), BF), V((tiles,) + lead + (rows, 2 * D), BF),
        V(lead + (rows, 128), BF), V((tiles, rows, 2 * D), F32), V((rows, 128), F32),
    ]
    scratch += States.scratch(geo) + States.scratch(geo)
    for name, width in scatters.items():
        scratch += type(tasks[name]).scratch(geo, rows, width)
    scratch += [pltpu.SemaphoreType.DMA((lane.count,)), pltpu.SemaphoreType.DMA((lane.count,)),
                pltpu.SemaphoreType.DMA((4,))]
    vmem = pl.BlockSpec(memory_space=pltpu.VMEM)
    hbm = pl.BlockSpec(memory_space=pl.ANY)
    shape = jax.ShapeDtypeStruct
    outs = [shape(tokens.shape, F32), shape(tokens.shape, F32), shape((PAIRS, rows, 384), F32),
            shape((rows, D), F32), shape((rows, FF), F32), shape(down_weight.shape, F32), shape((rows, 128), F32)]
    parts = pl.pallas_call(
        functools.partial(layer_kernel, geo, lane, plan),
        out_shape=outs, in_specs=[hbm] * 2 + [vmem] * 12, out_specs=[hbm] * 2 + [vmem] * 5, scratch_shapes=scratch,
        compiler_params=pltpu.CompilerParams(collective_id=0, has_side_effects=True, vmem_limit_bytes=60 << 20),
    )(tokens, cotangent, feature_matrix, output_bias, down_bias, first_gain, first_shift, second_gain, second_shift,
      up_bias, input_weight, output_weight, up_weight, down_weight)
    vector = shape((rows,), F32)
    return pl.pallas_call(
        finish_kernel,
        out_shape=[outs[0], outs[1], shape(input_weight.shape, F32), outs[3], vector, outs[4],
                   shape(up_bias.shape, F32), outs[5]] + [vector] * 5,
        in_specs=[hbm] * 2 + [vmem] * 5, out_specs=[hbm] * 2 + [vmem] * 11,
        scratch_shapes=[V((2,) + tokens.shape, F32), pltpu.SemaphoreType.DMA((8,)), pltpu.SemaphoreType.DMA((8,))],
        compiler_params=pltpu.CompilerParams(vmem_limit_bytes=60 << 20),
    )(*parts)

def local(
    tokens,
    feature_matrix,
    input_weight,
    output_weight,
    output_bias,
    up_weight,
    up_bias,
    down_weight,
    down_bias,
    first_gain,
    first_shift,
    second_gain,
    second_shift,
    cotangent,
):
    params = (
        lax.all_gather(input_weight, ("dp", "seq"), axis=0, tiled=True),
        lax.all_gather(output_weight, ("dp", "seq"), axis=0, tiled=True),
        lax.all_gather(output_bias, ("dp", "seq"), axis=0, tiled=True),
        lax.all_gather(up_weight, ("dp", "seq"), axis=0, tiled=True),
        lax.all_gather(up_bias, ("dp", "seq"), axis=0, tiled=True),
        lax.all_gather(down_weight, ("dp", "seq"), axis=0, tiled=True),
        lax.all_gather(down_bias, ("dp", "seq"), axis=0, tiled=True),
        lax.all_gather(first_gain, ("dp", "seq"), axis=0, tiled=True),
        lax.all_gather(first_shift, ("dp", "seq"), axis=0, tiled=True),
        lax.all_gather(second_gain, ("dp", "seq"), axis=0, tiled=True),
        lax.all_gather(second_shift, ("dp", "seq"), axis=0, tiled=True),
    )
    micros = tokens.shape[0]
    fronts = []
    carries = []
    for micro_step in range(micros):
        pieces = front(tokens[micro_step], feature_matrix, params)
        fronts.append(pieces)
        carries.append(
            prefix(
                (pieces[8], pieces[9]),
                "seq",
                add_pair,
                (jnp.zeros_like(pieces[8]), jnp.zeros_like(pieces[9])),
            )
        )
    results = []
    for micro_step in range(micros):
        pieces = fronts[micro_step]
        running_prefix_state, norm_sum = carries[micro_step]
        output = attend(pieces[5], pieces[6], pieces[7], running_prefix_state, norm_sum)[0]
        attended, middle = upper(pieces[0], output, params)
        results.append(feed(middle, params))
    result = jnp.stack(results)
    back_params = (
        lax.all_gather(input_weight, ("dp", "seq"), axis=0, tiled=True),
        lax.all_gather(output_weight, ("dp", "seq"), axis=0, tiled=True),
        lax.all_gather(output_bias, ("dp", "seq"), axis=0, tiled=True),
        lax.all_gather(up_weight, ("dp", "seq"), axis=0, tiled=True),
        lax.all_gather(up_bias, ("dp", "seq"), axis=0, tiled=True),
        lax.all_gather(down_weight, ("dp", "seq"), axis=0, tiled=True),
        lax.all_gather(down_bias, ("dp", "seq"), axis=0, tiled=True),
        lax.all_gather(first_gain, ("dp", "seq"), axis=0, tiled=True),
        lax.all_gather(first_shift, ("dp", "seq"), axis=0, tiled=True),
        lax.all_gather(second_gain, ("dp", "seq"), axis=0, tiled=True),
        lax.all_gather(second_shift, ("dp", "seq"), axis=0, tiled=True),
    )
    stored_list = []
    later_list = []
    for micro_step in range(micros):
        stored = upper_back(
            tokens[micro_step],
            cotangent[micro_step].astype(jnp.float32),
            feature_matrix,
            back_params,
            carries[micro_step],
        )
        stored_list.append(stored)
        later_list.append(
            prefix_2(
                (stored["state_grad"], stored["sum_grad"]),
                "seq",
                add_pair,
                (jnp.zeros_like(stored["state_grad"]), jnp.zeros_like(stored["sum_grad"])),
            )
        )
    upper_names = ["out", "out_bias", "up", "up_bias", "down", "down_bias", "gain_two", "shift_two"]
    upper_totals = [stored_list[0][name] for name in upper_names]
    micro_step = 1
    upper_totals = [
        total + stored_list[micro_step][name] for total, name in zip(upper_totals, upper_names)
    ]
    token_grads = []
    lower_totals = None
    for micro_step in range(micros):
        stored = stored_list[micro_step]
        tokens_part, input_part, gain_part, shift_part = lower_back(
            stored, later_list[micro_step], feature_matrix, back_params
        )
        token_grads.append(tokens_part)
        lower_parts = (input_part, gain_part, shift_part)
        if micro_step == 0:
            lower_totals = lower_parts
        else:
            lower_totals = jax.tree.map(jnp.add, lower_totals, lower_parts)
    shares = (
        lax.psum_scatter(lower_totals[0], ("dp", "seq"), scatter_dimension=0, tiled=True),
        lax.psum_scatter(upper_totals[0], ("dp", "seq"), scatter_dimension=0, tiled=True),
        lax.psum_scatter(upper_totals[1], ("dp", "seq"), scatter_dimension=0, tiled=True),
        lax.psum_scatter(upper_totals[2], ("dp", "seq"), scatter_dimension=0, tiled=True),
        lax.psum_scatter(upper_totals[3], ("dp", "seq"), scatter_dimension=0, tiled=True),
        lax.psum_scatter(upper_totals[4], ("dp", "seq"), scatter_dimension=0, tiled=True),
        lax.psum_scatter(upper_totals[5], ("dp", "seq"), scatter_dimension=0, tiled=True),
        lax.psum_scatter(lower_totals[1], ("dp", "seq"), scatter_dimension=0, tiled=True),
        lax.psum_scatter(lower_totals[2], ("dp", "seq"), scatter_dimension=0, tiled=True),
        lax.psum_scatter(upper_totals[6], ("dp", "seq"), scatter_dimension=0, tiled=True),
        lax.psum_scatter(upper_totals[7], ("dp", "seq"), scatter_dimension=0, tiled=True),
    )
    return (
        result,
        jnp.stack(token_grads),
        shares[0],
        shares[1],
        shares[2],
        shares[3],
        shares[4],
        shares[5],
        shares[6],
        shares[7],
        shares[8],
        shares[9],
        shares[10],
    )


def solution(mesh):
    in_specs = (
        P("dp", "seq", None),
        P(),
        P(("dp", "seq"), None),
        P(("dp", "seq"), None),
        P(("dp", "seq")),
        P(("dp", "seq"), None),
        P(("dp", "seq")),
        P(("dp", "seq"), None),
        P(("dp", "seq")),
        P(("dp", "seq")),
        P(("dp", "seq")),
        P(("dp", "seq")),
        P(("dp", "seq")),
        P("dp", "seq", None),
    )
    out_specs = (
        P("dp", "seq", None),
        P("dp", "seq", None),
        P(("dp", "seq"), None),
        P(("dp", "seq"), None),
        P(("dp", "seq")),
        P(("dp", "seq"), None),
        P(("dp", "seq")),
        P(("dp", "seq"), None),
        P(("dp", "seq")),
        P(("dp", "seq")),
        P(("dp", "seq")),
        P(("dp", "seq")),
        P(("dp", "seq")),
    )
    geo = Geometry(mesh)
    rows = 512 // (mesh.shape["dp"] * mesh.shape["seq"])
    if rows == 16:
        def body(*args):
            return fused(geo, args)
    else:
        body = local
    return jax.shard_map(body, mesh=mesh, in_specs=in_specs, out_specs=out_specs, check_vma=False)
```

```python
import functools
import math

import jax
import jax.numpy as jnp
from jax import lax
from jax.sharding import PartitionSpec as P

H = 8
DH = 64

from jax.experimental import pallas as pl
from jax.experimental.pallas import tpu as pltpu

MESH = pl.DeviceIdType.MESH


class Geometry:
    def __init__(self, mesh):
        dp, seq = mesh.shape["dp"], mesh.shape["seq"]
        self.C = 2
        self.Y = seq // 2
        self.X = 1 << ((dp.bit_length() - 1) // 2)
        self.Z = dp // self.X

    def me(self):
        dp, seq = lax.axis_index("dp"), lax.axis_index("seq")
        return dp // self.X, dp % self.X, seq // 2, seq % 2

    def device(self, z, x, y, c):
        return (z * self.X + x, y * 2 + c)

    def greet(self):
        z, x, y, c = self.me()
        peers = [self.device(z, x, y, 1 - c)]
        peers += [self.device((z + i) % self.Z, (x + j) % self.X, (y + k) % self.Y, c)
                  for i in range(self.Z) for j in range(self.X) for k in range(self.Y)][1:]
        semaphore = pltpu.get_barrier_semaphore()
        for peer in peers:
            pl.semaphore_signal(semaphore, inc=1, device_id=peer, device_id_type=MESH)

    def barrier(self):
        pl.semaphore_wait(pltpu.get_barrier_semaphore(), self.Z * self.X * self.Y)


class Lane:
    def __init__(self):
        self.count = 0
        self.send = self.recv = None

    def take(self, n=1):
        first = self.count
        self.count += n
        return first


def remote(lane, index, src, dst, device):
    return pltpu.make_async_remote_copy(
        src_ref=src, dst_ref=dst, send_sem=lane.send.at[index], recv_sem=lane.recv.at[index],
        device_id=device, device_id_type=MESH)


class Gather:
    def __init__(self, geo, lane, orders):
        self.geo, self.lane, self.orders = geo, lane, orders
        self.zs = lane.take()
        self.second = lane.take(max(geo.X, geo.Y) - 1)
        self.third = lane.take(max(geo.X, geo.Y) - 1)
        self.core = lane.take()

    def bind(self, own, full):
        self.own, self.full = own, full

    def z_copies(self):
        g = self.geo
        z, x, y, c = g.me()
        for k in range(1, g.Z):
            yield remote(self.lane, self.zs, self.own, self.full.at[z, x, y, c], g.device((z + k) % g.Z, x, y, c))

    def z_whole(self):
        g = self.geo
        z, x, y, c = g.me()
        slots = self.full.at[pl.ds(0, g.Z - 1), x, y, c]
        return remote(self.lane, self.zs, slots, slots, g.device((z + 1) % g.Z, x, y, c))

    def axis_copies(self, phase, order, incoming):
        g = self.geo
        z, x, y, c = g.me()
        base = self.second if phase == 2 else self.third
        along_x = (phase == 2) == (order == 0)
        size = g.X if along_x else g.Y
        for k in range(1, size):
            if along_x:
                source = (x + g.X - k) % g.X if incoming else x
                device = g.device(z, (x + k) % g.X, y, c)
                slot = self.full.at[:, source, y, c] if phase == 2 else self.full.at[:, source, :, c]
            else:
                source = (y + g.Y - k) % g.Y if incoming else y
                device = g.device(z, x, (y + k) % g.Y, c)
                slot = self.full.at[:, x, source, c] if phase == 2 else self.full.at[:, :, source, c]
            yield remote(self.lane, base + k - 1, slot, slot, device)

    def both(self, action):
        c = self.geo.me()[3]
        if self.orders[0] == self.orders[1]:
            action(self.orders[0])
            return
        for core in range(2):
            @pl.when(c == core)
            def _():
                action(self.orders[core])

    def step(self, n):
        g = self.geo
        z, x, y, c = g.me()
        if n == 0:
            for copy in self.z_copies():
                copy.start()
            self.full[z, x, y, c] = self.own[...]
        elif n == 1:
            self.z_whole().wait_recv()
            self.both(lambda order: [copy.start() for copy in self.axis_copies(2, order, False)])
        elif n == 2:
            def go(order):
                for copy in self.axis_copies(2, order, True):
                    copy.wait_recv()
                for copy in self.axis_copies(3, order, False):
                    copy.start()
            self.both(go)
        elif n == 3:
            def go(order):
                for copy in self.axis_copies(3, order, True):
                    copy.wait_recv()
            self.both(go)
            slot = self.full.at[:, :, :, c]
            remote(self.lane, self.core, slot, slot, g.device(z, x, y, 1 - c)).start()
        else:
            slot = self.full.at[:, :, :, 1 - c]
            remote(self.lane, self.core, slot, slot, g.device(z, x, y, 1 - c)).wait_recv()

    def drain(self):
        g = self.geo
        z, x, y, c = g.me()
        self.z_whole().wait_send()

        def go(order):
            for phase in (2, 3):
                for copy in self.axis_copies(phase, order, False):
                    copy.wait_send()
        self.both(go)
        slot = self.full.at[:, :, :, c]
        remote(self.lane, self.core, slot, slot, g.device(z, x, y, 1 - c)).wait_send()


class Scatter:
    def __init__(self, geo, lane, orders):
        self.geo, self.lane, self.orders = geo, lane, orders
        self.core = lane.take()
        self.first = lane.take(max(geo.X, geo.Y) - 1)
        self.second = lane.take(max(geo.X, geo.Y) - 1)
        self.zs = lane.take()

    @staticmethod
    def scratch(geo, rows, width):
        wide = max(geo.X, geo.Y)
        kind = jnp.bfloat16
        return [
            pltpu.VMEM((geo.Z, geo.X, geo.Y, rows, width), kind),
            pltpu.VMEM((wide - 1, geo.Z, wide, rows, width), kind),
            pltpu.VMEM((wide - 1, geo.Z, rows, width), kind),
            pltpu.VMEM((geo.Z - 1, rows, width), kind),
        ]

    def bind(self, part, out, buffers):
        self.part, self.out = part, out
        self.rc, self.ra, self.rb, self.rz = buffers

    def both(self, action):
        c = self.geo.me()[3]
        if self.orders[0] == self.orders[1]:
            action(self.orders[0])
            return
        for core in range(2):
            @pl.when(c == core)
            def _():
                action(self.orders[core])

    def core_copy(self):
        z, x, y, c = self.geo.me()
        return remote(self.lane, self.core, self.part.at[:, :, :, 1 - c], self.rc,
                      self.geo.device(z, x, y, 1 - c))

    def axis_copies(self, phase, order):
        g = self.geo
        z, x, y, c = g.me()
        base = self.first if phase == 1 else self.second
        along_x = (phase == 1) == (order == 1)
        for k in range(1, g.X if along_x else g.Y):
            if along_x:
                far = (x + k) % g.X
                device = g.device(z, far, y, c)
                src = self.part.at[:, far, :, c] if phase == 1 else self.part.at[:, far, y, c]
                dst = self.ra.at[k - 1, :, pl.ds(0, g.Y)] if phase == 1 else self.rb.at[k - 1]
            else:
                far = (y + k) % g.Y
                device = g.device(z, x, far, c)
                src = self.part.at[:, :, far, c] if phase == 1 else self.part.at[:, x, far, c]
                dst = self.ra.at[k - 1, :, pl.ds(0, g.X)] if phase == 1 else self.rb.at[k - 1]
            yield remote(self.lane, base + k - 1, src, dst, device)

    def z_copies(self):
        g = self.geo
        z, x, y, c = g.me()
        for k in range(1, g.Z):
            far = (z + k) % g.Z
            yield remote(self.lane, self.zs, self.part.at[far, x, y, c], self.rz.at[k - 1], g.device(far, x, y, c))

    def z_whole(self):
        g = self.geo
        z, x, y, c = g.me()
        return remote(self.lane, self.zs, self.rz, self.rz, g.device((z + 1) % g.Z, x, y, c))

    def step(self, n):
        g = self.geo
        z, x, y, c = g.me()
        wide = lambda ref: ref.astype(jnp.float32)
        if n == 0:
            self.core_copy().start()
        elif n == 1:
            self.core_copy().wait_recv()

            def add(i, _):
                total = wide(self.part[i, :, :, c]) + wide(self.rc[i])
                self.part[i, :, :, c] = total.astype(jnp.bfloat16)
                return 0
            lax.fori_loop(0, g.Z, add, 0)
            self.both(lambda order: [copy.start() for copy in self.axis_copies(1, order)])
        elif n == 2:
            def go(order):
                copies = list(self.axis_copies(1, order))
                for copy in copies:
                    copy.wait_recv()
                count = len(copies)
                if order == 0:
                    def add(i, _):
                        total = wide(self.part[i, :, y, c])
                        for k in range(count):
                            total += wide(self.ra[k, i, : g.X])
                        self.part[i, :, y, c] = total.astype(jnp.bfloat16)
                        return 0
                else:
                    def add(i, _):
                        total = wide(self.part[i, x, :, c])
                        for k in range(count):
                            total += wide(self.ra[k, i, : g.Y])
                        self.part[i, x, :, c] = total.astype(jnp.bfloat16)
                        return 0
                lax.fori_loop(0, g.Z, add, 0)
                for copy in self.axis_copies(2, order):
                    copy.start()
            self.both(go)
        elif n == 3:
            def go(order):
                copies = list(self.axis_copies(2, order))
                for copy in copies:
                    copy.wait_recv()

                def add(i, _):
                    total = wide(self.part[i, x, y, c])
                    for k in range(len(copies)):
                        total += wide(self.rb[k, i])
                    self.part[i, x, y, c] = total.astype(jnp.bfloat16)
                    return 0
                lax.fori_loop(0, g.Z, add, 0)
            self.both(go)
            for copy in self.z_copies():
                copy.start()
        else:
            total = wide(self.part[z, x, y, c])
            self.z_whole().wait_recv()
            for k in range(g.Z - 1):
                total += wide(self.rz[k])
            self.out[...] = total

    def drain(self):
        self.core_copy().wait_send()

        def go(order):
            for phase in (1, 2):
                for copy in self.axis_copies(phase, order):
                    copy.wait_send()
        self.both(go)
        self.z_whole().wait_send()


epsilon = 1e-05
finest_precision = lax.Precision.HIGHEST


def prefix(array, axis, combine, identity):
    count, here = (lax.axis_size(axis), lax.axis_index(axis))
    everything = jax.tree.map(
        lambda part, kind: lax.all_gather(part.astype(kind), axis),
        array,
        (jnp.bfloat16, jnp.bfloat16),
    )
    start = jax.tree.map(
        lambda part, zero: jnp.broadcast_to(jnp.asarray(zero, part.dtype), part.shape),
        array,
        identity,
    )

    def hop(k, before):
        reached = k < here
        new = combine(
            before, jax.tree.map(lambda part, own: part[k].astype(own.dtype), everything, array)
        )
        return jax.tree.map(lambda a, b: jnp.where(reached, a, b), new, before)

    return lax.fori_loop(0, count, hop, start)


def prefix_2(array, axis, join, neutral):
    count = lax.axis_size(axis)
    place = lax.axis_index(axis)
    ahead = count - 1 - place
    gathered = jax.tree.map(
        lambda a, kind: lax.all_gather(a.astype(kind), axis),
        array,
        jax.tree.map(lambda a: jnp.bfloat16 if a.dtype == jnp.float32 else a.dtype, array),
    )
    state = jax.tree.map(lambda a, e: jnp.zeros_like(a) + jnp.asarray(e, a.dtype), array, neutral)

    def one(hop, state):
        source = count - 1 - hop
        return join(
            state,
            jax.tree.map(
                lambda a, own: lax.dynamic_index_in_dim(a, source, 0, False).astype(own.dtype),
                gathered,
                array,
            ),
        )

    return lax.fori_loop(0, ahead, one, state)


def layer_norm(value_rows, norm_gain, norm_shift):
    center = jnp.mean(value_rows, axis=-1, keepdims=True)
    centred = value_rows - center
    spread = jnp.mean(centred * centred, axis=-1, keepdims=True)
    return centred * lax.rsqrt(spread + epsilon) * norm_gain + norm_shift


def gelu_tanh(value_rows):
    return jax.nn.gelu(value_rows, approximate=True)


def add_pair(earlier, later_term):
    return (earlier[0] + later_term[0], earlier[1] + later_term[1])


def causal_mask(length):
    positions = jnp.arange(length)
    return (positions[:, None] >= positions[None, :]).astype(jnp.float32)


def favor_map(proj_low, matrix, feature_scale):
    raw_proj = jnp.einsum("rhd,dm->rhm", proj_low, matrix, preferred_element_type=jnp.float32)
    projection = proj_low.astype(jnp.float32)
    half_norm = (
        0.5
        * feature_scale
        * feature_scale
        * jnp.sum(projection * projection, axis=-1, keepdims=True)
    )
    return jnp.exp(feature_scale * raw_proj - half_norm) / math.sqrt(matrix.shape[1])


def favor_back(map_grad, favor_value, proj_low, matrix, feature_scale):
    log_grad = map_grad * favor_value
    raw_grad = (feature_scale * log_grad).astype(jnp.bfloat16)
    projection = proj_low.astype(jnp.float32)
    through = jnp.einsum("rhm,dm->rhd", raw_grad, matrix, preferred_element_type=jnp.float32)
    return (
        through
        - feature_scale * feature_scale * jnp.sum(log_grad, axis=-1, keepdims=True) * projection
    )


def front(token_block, matrix, params):
    inputs = token_block.astype(jnp.float32)
    length = inputs.shape[0]
    normed = layer_norm(
        inputs, params[7].astype(jnp.float32), params[8].astype(jnp.float32)
    ).astype(jnp.bfloat16)
    mixed = jnp.dot(normed, params[0], preferred_element_type=jnp.float32).astype(jnp.bfloat16)
    head_parts = mixed.reshape(length, 3, H, DH)
    feature_scale = DH ** (-0.25)
    query_features = favor_map(head_parts[:, 0], matrix, feature_scale)
    key_features = favor_map(head_parts[:, 1], matrix, feature_scale)
    query_reduced = query_features.astype(jnp.bfloat16)
    key_reduced = key_features.astype(jnp.bfloat16)
    value_rows = head_parts[:, 2]
    block_local_state = jnp.einsum(
        "nqo,nqi->qoi", key_reduced, value_rows, preferred_element_type=jnp.float32
    )
    local_sum = jnp.sum(key_reduced.astype(jnp.float32), axis=0)
    return (
        inputs,
        normed,
        head_parts,
        query_features,
        key_features,
        query_reduced,
        key_reduced,
        value_rows,
        block_local_state,
        local_sum,
    )


def attend(query_reduced, key_reduced, value_rows, running_prefix_state, norm_sum):
    causal = causal_mask(query_reduced.shape[0])
    scores = (
        jnp.einsum("ihm,jhm->hij", query_reduced, key_reduced, preferred_element_type=jnp.float32)
        * causal[None]
    )
    denominator = jnp.sum(scores, axis=-1).T + jnp.einsum(
        "ihm,hm->ih", query_reduced.astype(jnp.float32), norm_sum, precision=finest_precision
    )
    attention_numerator = jnp.einsum(
        "hij,jhd->ihd", scores.astype(jnp.bfloat16), value_rows, preferred_element_type=jnp.float32
    )
    attention_numerator = attention_numerator + jnp.einsum(
        "plq,lqu->plu",
        query_reduced,
        running_prefix_state.astype(jnp.bfloat16),
        preferred_element_type=jnp.float32,
    )
    return (attention_numerator / denominator[:, :, None], attention_numerator, denominator)


def upper(inputs, output, params):
    length = output.shape[0]
    attended = output.reshape(length, -1).astype(jnp.bfloat16)
    middle = (
        inputs
        + jnp.dot(attended, params[1], preferred_element_type=jnp.float32)
        + params[2].astype(jnp.float32)
    )
    return (attended, middle)


def feed(middle, params):
    normed_two = layer_norm(
        middle, params[9].astype(jnp.float32), params[10].astype(jnp.float32)
    ).astype(jnp.bfloat16)
    hidden = jnp.dot(normed_two, params[3], preferred_element_type=jnp.float32) + params[4].astype(
        jnp.float32
    )
    active = gelu_tanh(hidden).astype(jnp.bfloat16)
    return (
        middle
        + jnp.dot(active, params[5], preferred_element_type=jnp.float32)
        + params[6].astype(jnp.float32)
    )


def upper_back(token_block, upstream, matrix, params, block_carry):
    pieces = front(token_block, matrix, params)
    (
        inputs,
        normed,
        head_parts,
        query_features,
        key_features,
        query_reduced,
        key_reduced,
        value_rows,
        block_local_state,
        local_sum,
    ) = pieces
    running_prefix_state, norm_sum = block_carry
    output, attention_numerator, denominator = attend(
        query_reduced, key_reduced, value_rows, running_prefix_state, norm_sum
    )
    attended, middle = upper(inputs, output, params)
    normed_float, second_pull = jax.vjp(
        layer_norm, middle, params[9].astype(jnp.float32), params[10].astype(jnp.float32)
    )
    normed_two = normed_float.astype(jnp.bfloat16)
    hidden = jnp.dot(normed_two, params[3], preferred_element_type=jnp.float32) + params[4].astype(
        jnp.float32
    )
    active_float, gelu_pull = jax.vjp(gelu_tanh, hidden)
    active = active_float.astype(jnp.bfloat16)
    stored = {"front": pieces, "carry": block_carry}
    down_term = upstream.astype(jnp.bfloat16)
    stored["down"] = jnp.einsum("rf,rd->fd", active, down_term, preferred_element_type=jnp.float32)
    stored["down_bias"] = jnp.sum(upstream, axis=0)
    active_grad = jnp.einsum("rd,fd->rf", down_term, params[5], preferred_element_type=jnp.float32)
    (hidden_grad,) = gelu_pull(active_grad)
    up_term = hidden_grad.astype(jnp.bfloat16)
    stored["up"] = jnp.einsum("rd,rf->df", normed_two, up_term, preferred_element_type=jnp.float32)
    stored["up_bias"] = jnp.sum(hidden_grad, axis=0)
    normed_two_grad = jnp.einsum(
        "rf,df->rd", up_term, params[3], preferred_element_type=jnp.float32
    )
    middle_part, gain_two_grad, shift_two_grad = second_pull(normed_two_grad)
    stored["gain_two"] = gain_two_grad
    stored["shift_two"] = shift_two_grad
    middle_grad = upstream + middle_part
    stored["middle_grad"] = middle_grad
    out_term = middle_grad.astype(jnp.bfloat16)
    stored["out"] = jnp.einsum("re,rd->ed", attended, out_term, preferred_element_type=jnp.float32)
    stored["out_bias"] = jnp.sum(middle_grad, axis=0)
    attended_grad = jnp.einsum(
        "rd,ed->re", out_term, params[1], preferred_element_type=jnp.float32
    ).reshape(output.shape)
    numerator_grad = (attended_grad / denominator[:, :, None]).astype(jnp.bfloat16)
    denom_grad = -jnp.sum(attended_grad * attention_numerator, axis=-1) / (
        denominator * denominator
    )
    stored["numer_grad"] = numerator_grad
    stored["denom_grad"] = denom_grad
    stored["state_grad"] = jnp.einsum(
        "jfp,jfl->fpl", query_reduced, numerator_grad, preferred_element_type=jnp.float32
    )
    stored["sum_grad"] = jnp.einsum(
        "ih,ihm->hm", denom_grad, query_reduced.astype(jnp.float32), precision=finest_precision
    )
    return stored


def lower_back(stored, later_part, matrix, params):
    (
        inputs,
        normed,
        head_parts,
        query_features,
        key_features,
        query_reduced,
        key_reduced,
        value_rows,
        block_local_state,
        local_sum,
    ) = stored["front"]
    running_prefix_state, norm_sum = stored["carry"]
    state_later, sum_later = later_part
    numerator_grad = stored["numer_grad"]
    denom_grad = stored["denom_grad"]
    length = inputs.shape[0]
    causal = causal_mask(length)
    scores = (
        jnp.einsum("ihm,jhm->hij", query_reduced, key_reduced, preferred_element_type=jnp.float32)
        * causal[None]
    )
    scores_grad = jnp.einsum(
        "ihd,jhd->hij", numerator_grad, value_rows, preferred_element_type=jnp.float32
    )
    score_term = ((scores_grad + denom_grad.T[:, :, None]) * causal[None]).astype(jnp.bfloat16)
    later_reduced = state_later.astype(jnp.bfloat16)
    query_grad = jnp.einsum(
        "hij,jhm->ihm", score_term, key_reduced, preferred_element_type=jnp.float32
    )
    query_grad = query_grad + jnp.einsum(
        "gvw,vcw->gvc",
        numerator_grad,
        running_prefix_state.astype(jnp.bfloat16),
        preferred_element_type=jnp.float32,
    )
    query_grad = query_grad + denom_grad[:, :, None] * norm_sum[None]
    key_grad = jnp.einsum(
        "hij,ihm->jhm", score_term, query_reduced, preferred_element_type=jnp.float32
    )
    key_grad = key_grad + jnp.einsum(
        "prc,rqc->prq", value_rows, later_reduced, preferred_element_type=jnp.float32
    )
    key_grad = key_grad + sum_later[None]
    value_grad = jnp.einsum(
        "hij,ihd->jhd",
        scores.astype(jnp.bfloat16),
        numerator_grad,
        preferred_element_type=jnp.float32,
    )
    value_grad = value_grad + jnp.einsum(
        "qsa,saw->qsw", key_reduced, later_reduced, preferred_element_type=jnp.float32
    )
    feature_scale = DH ** (-0.25)
    query_proj = favor_back(query_grad, query_features, head_parts[:, 0], matrix, feature_scale)
    key_proj = favor_back(key_grad, key_features, head_parts[:, 1], matrix, feature_scale)
    mixed_grad = (
        jnp.stack([query_proj, key_proj, value_grad], axis=1)
        .reshape(length, -1)
        .astype(jnp.bfloat16)
    )
    input_part = jnp.einsum("rd,re->de", normed, mixed_grad, preferred_element_type=jnp.float32)
    normed_grad = jnp.einsum("re,de->rd", mixed_grad, params[0], preferred_element_type=jnp.float32)
    _, first_pull = jax.vjp(
        layer_norm, inputs, params[7].astype(jnp.float32), params[8].astype(jnp.float32)
    )
    inputs_part, gain_one_grad, shift_one_grad = first_pull(normed_grad)
    return (stored["middle_grad"] + inputs_part, input_part, gain_one_grad, shift_one_grad)


BF = jnp.bfloat16
F32 = jnp.float32
M = 256
SCALE = DH ** (-0.25)
LOG2E = math.log2(math.e)
PAIRS = H // 2
STATE_ROWS = 160


def dot(a, b):
    return jnp.dot(a, b, preferred_element_type=F32)


def dot_nt(a, b):
    return lax.dot_general(a, b, (((1,), (1,)), ((), ())), preferred_element_type=F32)


class States:
    def __init__(self, geo, lane, earlier):
        self.geo, self.lane, self.earlier = geo, lane, earlier
        self.per = geo.Y + 1
        self.first = lane.take(self.per * PAIRS)

    @staticmethod
    def scratch(geo):
        one = (PAIRS, STATE_ROWS, M)
        two = (PAIRS, 2, STATE_ROWS, M)
        return [pltpu.VMEM(two, BF), pltpu.VMEM(two, BF), pltpu.VMEM(one, BF),
                pltpu.VMEM((PAIRS, max(geo.Y - 1, 1), STATE_ROWS, M), BF), pltpu.VMEM(one, BF),
                pltpu.VMEM(one, BF), pltpu.VMEM(two, BF)]

    def bind(self, buffers):
        self.own, self.sibling, self.chip, self.chips, self.base, self.base_sibling, self.total = buffers

    def copies(self, p, phase):
        g = self.geo
        z, x, y, c = g.me()
        index = self.first + p * self.per
        other = g.device(z, x, y, 1 - c)
        if phase == 0:
            return [remote(self.lane, index, self.own.at[p], self.sibling.at[p], other)]
        if phase == 1:
            return [remote(self.lane, index + k, self.chip.at[p], self.chips.at[p, k - 1],
                           g.device(z, x, (y + k) % g.Y, c)) for k in range(1, g.Y)]
        return [remote(self.lane, index + g.Y, self.base.at[p], self.base_sibling.at[p], other)]

    def step(self, n, p):
        g = self.geo
        z, x, y, c = g.me()
        if n > 0:
            for copy in self.copies(p, n - 1):
                copy.wait_recv()
        if n == 1:
            self.chip[p] = (self.own[p, c].astype(F32) + self.sibling[p, c].astype(F32)).astype(BF)
        elif n == 2:
            total = jnp.zeros((STATE_ROWS, M), F32)
            for k in range(1, g.Y):
                source = (y + g.Y - k) % g.Y
                counts = source < y if self.earlier else source > y
                total += jnp.where(counts, 1.0, 0.0) * self.chips[p, k - 1].astype(F32)
            self.base[p] = total.astype(BF)
        elif n == 3:
            near = jnp.where(c == (1 if self.earlier else 0), 1.0, 0.0)
            self.total[p, c] = (self.base[p].astype(F32) + near * self.sibling[p, c].astype(F32)).astype(BF)
            self.total[p, 1 - c] = (self.base_sibling[p].astype(F32)
                                    + near * self.sibling[p, 1 - c].astype(F32)).astype(BF)
        if n < 3:
            for copy in self.copies(p, n):
                copy.start()

    def drain(self):
        for p in range(PAIRS):
            for phase in range(3):
                for copy in self.copies(p, phase):
                    copy.wait_send()


class GatherPlane(Gather):
    def __init__(self, geo, lane):
        self.geo, self.lane = geo, lane
        self.far = [(j, k) for j in range(geo.X) for k in range(geo.Y)][1:]
        self.zs, self.plane, self.core = lane.take(), lane.take(len(self.far)), lane.take()

    def plane_copies(self, incoming):
        g = self.geo
        z, x, y, c = g.me()
        for n, (j, k) in enumerate(self.far):
            slot = self.full.at[:, (x + g.X - j) % g.X, (y + g.Y - k) % g.Y, c] if incoming else self.full.at[:, x, y, c]
            yield remote(self.lane, self.plane + n, slot, slot, g.device(z, (x + j) % g.X, (y + k) % g.Y, c))

    def core_copy(self, own):
        z, x, y, c = self.geo.me()
        slot = self.full.at[:, :, :, c if own else 1 - c]
        return remote(self.lane, self.core, slot, slot, self.geo.device(z, x, y, 1 - c))

    def step(self, n):
        if n == 0:
            super().step(0)
        elif n == 1:
            self.z_whole().wait_recv()
            for copy in self.plane_copies(False):
                copy.start()
        elif n == 2:
            for copy in self.plane_copies(True):
                copy.wait_recv()
            self.core_copy(True).start()
        else:
            self.core_copy(False).wait_recv()

    def drain(self):
        self.z_whole().wait_send()
        for copy in self.plane_copies(False):
            copy.wait_send()
        self.core_copy(True).wait_send()


class PairStates:
    def __init__(self, states, p):
        self.states, self.p = states, p

    def step(self, n):
        self.states.step(n, self.p)


class ScatterDirect:
    def __init__(self, geo, lane):
        self.geo, self.lane = geo, lane
        self.far = [(i, j, k) for i in range(geo.Z) for j in range(geo.X) for k in range(geo.Y)][1:]
        self.core = lane.take()
        self.first = lane.take()

    @staticmethod
    def scratch(geo, rows, width):
        return [pltpu.VMEM((geo.Z, geo.X, geo.Y, rows, width), jnp.bfloat16),
                pltpu.VMEM((geo.Z * geo.X * geo.Y - 1, rows, width), jnp.bfloat16)]

    def bind(self, part, out, buffers):
        self.part, self.out = part, out
        self.rc, self.rz = buffers

    def core_copy(self):
        z, x, y, c = self.geo.me()
        return remote(self.lane, self.core, self.part.at[:, :, :, 1 - c], self.rc, self.geo.device(z, x, y, 1 - c))

    def copies(self):
        g = self.geo
        z, x, y, c = g.me()
        for n, (i, j, k) in enumerate(self.far):
            to = ((z + i) % g.Z, (x + j) % g.X, (y + k) % g.Y, c)
            yield remote(self.lane, self.first, self.part.at[to], self.rz.at[n], g.device(*to))

    def whole(self):
        z, x, y, c = self.geo.me()
        return remote(self.lane, self.first, self.rz, self.rz, self.geo.device((z + 1) % self.geo.Z, x, y, c))

    def step(self, n):
        g = self.geo
        z, x, y, c = g.me()
        if n == 0:
            self.core_copy().start()
        elif n == 1:
            self.core_copy().wait_recv()

            def add(i, _):
                total = self.part[i, :, :, c].astype(F32) + self.rc[i].astype(F32)
                self.part[i, :, :, c] = total.astype(BF)
                return 0
            lax.fori_loop(0, g.Z, add, 0)
            for copy in self.copies():
                copy.start()
        else:
            total = self.part[z, x, y, c].astype(F32)
            self.whole().wait_recv()
            for n in range(len(self.far)):
                total += self.rz[n].astype(F32)
            self.out[...] = total

    def drain(self):
        self.core_copy().wait_send()
        self.whole().wait_send()


DIRECT = ("rG", "rV1",)
PLANE = ()
ORDERS = {"F0": (1, 1), "rF3": (1, 1), "rF1": (1, 1), "rO": (1, 1), "rV0": (1, 1)}
PLAN = {
    "start": (("S", 0), ("I0", 0), ("I1", 0), ("I2", 0), ("I3", 0),),
    "first": (("O", 0), ("F0", 0), ("F1", 0), ("F2", 0), ("S", 1), ("I0", 1), ("I1", 1), ("S", 2), ("I2", 1),
        ("I0", 2), ("I3", 1), ("I1", 2), ("S", 3), ("O", 1), ("I2", 2), ("S", 4),),
    "proj.pre0": (("I0", 3), ("I3", 2), ("F0", 1), ("I1", 3), ("O", 2), ("I0", 4),),
    "proj0": (("f0", 0), ("I2", 3), ("F1", 1), ("I3", 3),),
    "proj.pre1": (("I1", 4),),
    "proj1": (("f1", 0), ("f0", 1),),
    "proj.pre2": (("I2", 4),),
    "proj2": (("f2", 0), ("f1", 1), ("O", 3), ("F0", 2), ("F2", 1), ("F3", 0),),
    "proj.pre3": (("I3", 4),),
    "proj3": (("f3", 0), ("f2", 1),),
    "block1": (("f3", 1), ("f1", 2),),
    "block2": (("F3", 1),),
    "att.pre0": (("F1", 2), ("f0", 2), ("f2", 2), ("F0", 3), ("f0", 3),),
    "att.pre1": (("f1", 3), ("F2", 2), ("f3", 2),),
    "att1": (("O", 4),),
    "att.pre2": (("f2", 3),),
    "att2": (("F0", 4), ("F3", 2),),
    "att.pre3": (("f3", 3),),
    "mid": (("F1", 3),),
    "feed0": (("F2", 3),),
    "feed.pre1": (("F1", 4),),
    "feed1": (("rF1", 0), ("F2", 4), ("F3", 3),),
    "feed2": (("rF2", 0), ("rF1", 1), ("F3", 4),),
    "feed3": (("rF3", 0), ("rF2", 1),),
    "out": (("rF3", 1), ("rF1", 2), ("rO", 0),),
    "st0": (("b0", 0),),
    "st1": (("b1", 0),),
    "st2": (("b2", 0),),
    "st3": (("b3", 0), ("rF2", 2), ("rO", 1), ("b0", 1),),
    "q0": (("b1", 1), ("b2", 1), ("b3", 1), ("rF0", 0),),
    "q1": (("rF1", 3),),
    "q2": (("b0", 2), ("rF3", 2),),
    "q3": (("b1", 2),),
    "q.end": (("rQ", 0),),
    "k.pre0": (("b0", 3),),
    "k0": (("b2", 2), ("b1", 3), ("rF0", 1), ("b3", 2), ("rQ", 1), ("rF1", 4), ("rO", 2),),
    "k1": (("b2", 3), ("b3", 3), ("rF3", 3),),
    "k3": (("rF2", 3), ("rF0", 2),),
    "k.end": (("rK", 0), ("rQ", 2),),
    "v0": (("rV0", 0), ("rK", 1), ("rF0", 3), ("rO", 3),),
    "v1": (("rV1", 0), ("rV0", 1), ("rQ", 3), ("rF2", 4),),
    "nb0": (("rK", 2),),
    "nb1": (("rV1", 1), ("rF0", 4),),
    "fb1": (("rG", 0), ("rV0", 2), ("rO", 4),),
    "end0": (("rF3", 4),),
    "end": (("rK", 3), ("rQ", 4), ("rG", 1), ("rV0", 3), ("rV1", 2), ("rK", 4), ("rG", 2), ("rV0", 4),),
}


def layer_kernel(geo, lane, plan, *refs):
    (tokens_hbm, cot_hbm, feat_hbm, out_bias_hbm, down_bias_hbm, first_gain_hbm, first_shift_hbm, second_gain_hbm,
     second_shift_hbm, up_bias_hbm, wi_hbm, wo_hbm, wu_hbm, wd_hbm,
     result_hbm, tokens_grad_hbm, inp_hbm, out_hbm, up_hbm, down_hbm, vec_hbm,
     feat, out_bias_in, down_bias_in, first_gain_in, first_shift_in, second_gain_in, second_shift_in, up_bias_in,
     wi_in, wu_in, wd_in, inp_out, out_out, up_out, down_out, vec_out,
     tokens, cot, result, tokens_grad, small_own, small, wi_own, wi, wo_own, wo_all, wf_own, wf,
     normed, normed_t, mixed, pq, pk, den, attended, middle, n2_t,
     act, hg, vecs, grads, fa, ft, perm, part_q, part_k, part_v, part_o, part_f, part_g, up_parts, vec_sum) = refs[:73]
    rest = list(refs[73:])
    fwd, bwd, tasks = plan
    take = lambda n: [rest.pop(0) for _ in range(n)]
    fwd.bind(take(7))
    bwd.bind(take(7))
    scatter_buffers = {name: take(2 if type(task) is ScatterDirect else 4)
                       for name, task in tasks.items() if name[0] == "r"}
    lane.send, lane.recv = take(2)
    local_sem = rest.pop(0)
    tasks["S"].bind(small_own, small)
    tasks["O"].bind(wo_own, wo_all)
    tasks["rO"].bind(part_o, out_out, scatter_buffers["rO"])
    tasks["rG"].bind(part_g, vec_sum, scatter_buffers["rG"])
    wide = tokens.shape[-1]
    tasks["rQ"].bind(part_q, inp_out.at[:, pl.ds(0, wide)], scatter_buffers["rQ"])
    tasks["rK"].bind(part_k, inp_out.at[:, pl.ds(wide, wide)], scatter_buffers["rK"])
    for n in range(2):
        tasks[f"rV{n}"].bind(part_v.at[n], inp_out.at[:, pl.ds(2 * wide + 256 * n, 256)], scatter_buffers[f"rV{n}"])
    for p in range(PAIRS):
        tasks[f"I{p}"].bind(wi_own.at[p], wi.at[p])
    for t in range(wf.shape[0]):
        tasks[f"F{t}"].bind(wf_own.at[t], wf.at[t])
        tasks[f"rF{t}"].bind(part_f.at[t], up_parts.at[t], scatter_buffers[f"rF{t}"])
    n2 = normed
    D = tokens.shape[-1]
    L = tokens.shape[1]
    TILES = wf.shape[0]
    HALF = L // 2
    lead = (geo.Z, geo.X, geo.Y, 2)
    z, x, y, c = geo.me()
    place = (((z * geo.X + x) * geo.Y + y) * 2 + c) % 8

    def loop(n, body):
        def step(i, _):
            body(i)
            return 0
        lax.fori_loop(0, n, step, 0)

    def pairs(body, before, after):
        def step(p):
            if before:
                pump_at(p, [before + f"{n}" for n in range(PAIRS)])
            body(p, 0)
            body(p, 1)
            pump_at(p, [after + f"{n}" for n in range(PAIRS)])
        loop(PAIRS, step)

    def pump(point):
        for name, n in PLAN.get(point, ()):
            tasks[name].step(n)

    def pump_at(now, points):
        for when, point in enumerate(points):
            if point in PLAN:
                @pl.when(now == when)
                def _():
                    pump(point)

    def local(i, src, dst):
        return pltpu.make_async_copy(src, dst, local_sem.at[i])

    entry = ((feat_hbm, feat), (out_bias_hbm, out_bias_in), (down_bias_hbm, down_bias_in),
             (first_gain_hbm, first_gain_in), (first_shift_hbm, first_shift_in), (second_gain_hbm, second_gain_in),
             (second_shift_hbm, second_shift_in), (up_bias_hbm, up_bias_in), (wi_hbm, wi_in), (wo_hbm, wo_own),
             (wu_hbm, wu_in), (wd_hbm, wd_in))
    entry = [local(9 + i, a, b) for i, (a, b) in enumerate(entry)]
    for copy in entry[1:9] + entry[:1] + entry[9:]:
        copy.start()
    local(0, tokens_hbm, tokens).start()
    local(1, cot_hbm, cot).start()
    geo.greet()
    for copy in entry[1:9]:
        copy.wait()
    vec_sum[...] = jnp.zeros((16, 128), F32)
    for v, ref in enumerate((out_bias_in, down_bias_in, first_gain_in, first_shift_in, second_gain_in,
                             second_shift_in)):
        vec_sum[v, :16] = ref[...].astype(F32)
    up_bias_row = up_bias_in[...].astype(F32)
    for t in range(TILES):
        vec_sum[6 + t, :16] = up_bias_row[t * 16:(t + 1) * 16]
    small_own[...] = pltpu.roll(vec_sum[...], place * 16, 1).astype(BF)
    for p in range(PAIRS):
        wi_own[p] = jnp.concatenate([wi_in[:, k * D + p * 128: k * D + (p + 1) * 128] for k in range(3)], axis=1)
    geo.barrier()
    pump("start")
    for copy in entry[:1] + entry[9:]:
        copy.wait()
    source = lax.broadcasted_iota(jnp.int32, (512, 1), 0)
    target = (source % 64) // 16 * 128 + source // 64 * 16 + source % 16
    perm[...] = jnp.where(lax.broadcasted_iota(jnp.int32, (512, 512), 1) == target, 1.0, 0.0).astype(BF)
    stacked = jnp.concatenate([wu_in[:, g * 512:(g + 1) * 512] for g in range(TILES)], axis=0)
    stacked = dot(stacked, perm[...]).astype(BF)
    for t in range(TILES):
        for g in range(TILES):
            wf_own[t, :, g * 128:(g + 1) * 128] = stacked[g * 16:(g + 1) * 16, t * 128:(t + 1) * 128]
        wf_own[t, :, D:] = wd_in[t * 16:(t + 1) * 16]

    f = feat[...]
    zero = jnp.zeros((DH, M), BF)
    one = jnp.ones((DH, M), BF)
    fa[0] = jnp.concatenate([f, zero, -one, zero], axis=0)
    fa[1] = jnp.concatenate([zero, f, zero, -one], axis=0)
    ft[...] = jnp.concatenate([jnp.concatenate([f, zero], axis=1), jnp.concatenate([zero, f], axis=1),
                               jnp.concatenate([one, zero], axis=1), jnp.concatenate([zero, one], axis=1)], axis=0)
    low_lane = lax.broadcasted_iota(jnp.int32, (1, 128), 1) < DH
    m0f = jnp.where(low_lane, 1.0, 0.0)
    m0 = m0f.astype(BF)
    m1 = (1.0 - m0f).astype(BF)
    tri_r = lax.broadcasted_iota(jnp.int32, (HALF, HALF), 0)
    tri_c = lax.broadcasted_iota(jnp.int32, (HALF, HALF), 1)

    pump("first")

    flat = lambda v: v.reshape(-1, v.shape[-1])
    sums = jnp.sum(small[...].astype(F32).reshape(-1, 8, 16, 128), axis=1)
    vecs[...] = jnp.concatenate([sums[g] for g in range(D // 128)], axis=1)
    out_bias, down_bias = lambda: vecs[0:1], lambda: vecs[1:2]

    def norm_parts(rows):
        center = jnp.mean(rows, axis=-1, keepdims=True)
        centred = rows - center
        spread = jnp.mean(centred * centred, axis=-1, keepdims=True)
        inv = lax.rsqrt(spread + epsilon)
        return centred * inv, inv

    def first_norm(s):
        hat, _ = norm_parts(tokens[s].astype(F32))
        value = (hat * vecs[2:3] + vecs[3:4]).astype(BF)
        normed[s] = value
        normed_t[s] = value.T
    pump("vec")
    local(0, tokens_hbm, tokens).wait()
    first_norm(0)
    pump("norm0")
    first_norm(1)
    pump("norm1")

    def vx(s, p):
        v = mixed[s, p, :, 2 * 128:]
        ones = jnp.ones(v.shape, BF)
        return (jnp.concatenate([v * m0, ones * m0], axis=1), jnp.concatenate([v * m1, ones * m1], axis=1))

    def project(p, s):
        mixed[s, p] = dot(normed[s], flat(wi[p])).astype(BF)
        for part, target in ((0, pq), (1, pk)):
            rows = mixed[s, p, :, part * 128:(part + 1) * 128]
            wide = rows.astype(F32)
            lhs = jnp.concatenate([rows, (wide * wide * (0.5 * SCALE)).astype(BF)], axis=1)
            for h in range(2):
                power = dot(lhs, fa[h]) * (SCALE * LOG2E) - 0.5 * math.log2(M)
                target[s, 2 * p + h] = jnp.exp2(power).astype(BF)
        v = mixed[s, p, :, 2 * 128:]
        lhs = jnp.concatenate([v.T, jnp.ones((16, L), BF)], axis=0)
        r0 = dot(lhs, pk[s, 2 * p])
        r1 = dot(lhs, pk[s, 2 * p + 1])
        fwd.own[p, s] = jnp.concatenate([r0[:64], r1[64:128], r0[128:], r1[128:]], axis=0).astype(BF)
    pairs(project, "proj.pre", "proj")

    def state_cols(total, p, s, h, copies):
        state = total[p, s, h * 64:(h + 1) * 64]
        extra = total[p, s, 128 + 16 * h:144 + 16 * h]
        zeros = jnp.zeros((DH, M), BF)
        if copies:
            extra = jnp.concatenate([extra] * 4, axis=0)
        else:
            extra = jnp.concatenate([extra, jnp.zeros((48, M), BF)], axis=0)
        parts = [state, zeros, extra, zeros] if h == 0 else [zeros, state, zeros, extra]
        return jnp.concatenate(parts, axis=0)

    lower = tri_r >= tri_c
    upper = tri_r <= tri_c

    def attend_block(p, s):
        v0, v1 = vx(s, p)
        lanes = pl.ds(pl.multiple_of(p * 128, 128), 128)
        for b in range(2):
            rows = slice(b * HALF, (b + 1) * HALF)
            scores = []
            for h in range(2):
                q = pq[s, 2 * p + h, rows]
                if b == 1:
                    scores.append(dot_nt(q, pk[s, 2 * p + h, :HALF]).astype(BF))
                scores.append(jnp.where(lower, dot_nt(q, pk[s, 2 * p + h, rows]), 0.0).astype(BF))
            rhs = jnp.concatenate([v0[:(b + 1) * HALF], v1[:(b + 1) * HALF]], axis=0)
            ext = dot(jnp.concatenate(scores, axis=1), rhs)
            result[s, rows, lanes] = ext[:, :128]
            den[s, rows, lanes] = ext[:, 128:]
    pairs(attend_block, None, "block")

    def attend_earlier(p, s):
        lanes = pl.ds(pl.multiple_of(p * 128, 128), 128)
        states = jnp.concatenate([state_cols(fwd.total, p, s, h, True) for h in range(2)], axis=1)
        ext = dot_nt(jnp.concatenate([pq[s, 2 * p], pq[s, 2 * p + 1]], axis=1), states)
        inv = 1.0 / (ext[:, 128:] + den[s, :, lanes])
        den[s, :, lanes] = inv
        attended[s, :, lanes] = ((ext[:, :128] + result[s, :, lanes]) * inv).astype(BF)
    pairs(attend_earlier, "att.pre", "att")
    pump("mid.pre")
    local(1, cot_hbm, cot).wait()

    def wo():
        return flat(wo_all[...])

    def to_middle(s):
        value = tokens[s].astype(F32) + dot(attended[s], wo()) + out_bias()
        middle[s] = value
        hat, _ = norm_parts(value)
        low = (hat * vecs[4:5] + vecs[5:6]).astype(BF)
        n2[s] = low
        n2_t[s] = low.T
        result[s] = value + down_bias()
        tokens_grad[s] = jnp.zeros((L, D), F32)
    to_middle(0)
    to_middle(1)
    pump("mid")
    grads[...] = jnp.zeros(grads.shape, F32)

    k0 = math.sqrt(2.0 / math.pi)

    def feed_tile(t):
        pump_at(t, [f"feed.pre{n}" for n in range(TILES)])
        bias = vecs[pl.ds(6 + t, 1)]
        wut = lambda: flat(wf[t, :, :, :, :, :, :D])
        wdt = lambda: flat(wf[t, :, :, :, :, :, D:])

        def seq(s):
            for b in range(2):
                rows = slice(b * HALF, (b + 1) * HALF)
                u = dot(n2[s, rows], wut()) + bias
                uu = u * u
                th = jnp.tanh(u * (k0 + (k0 * 0.044715) * uu))
                half = 0.5 + 0.5 * th
                a = (u * half).astype(BF)
                act[s, rows] = a
                slope = half + (0.5 * u) * (1.0 - th * th) * (k0 + (3.0 * 0.044715 * k0) * uu)
                back = dot_nt(cot[s, rows], wdt()) * slope
                grads[pl.ds(6 + t, 1)] += jnp.sum(back, axis=0, keepdims=True)
                low = back.astype(BF)
                hg[s, rows] = low
                result[s, rows] += dot(a, wdt())
                tokens_grad[s, rows] += dot_nt(low, wut())
        seq(0)
        seq(1)
        dwd = dot(act[0].T, cot[0]) + dot(act[1].T, cot[1])
        part_f[t, :, :, :, :, :, D:] = dwd.astype(BF).reshape(lead + (-1, D))
        dwu = dot(n2_t[0], hg[0]) + dot(n2_t[1], hg[1])
        part_f[t, :, :, :, :, :, :D] = dwu.astype(BF).reshape(lead + (-1, 512))
        pump_at(t, [f"feed{n}" for n in range(TILES)])
    loop(TILES, feed_tile)
    local(2, result, result_hbm).start()

    ones_block = jnp.concatenate([jnp.concatenate([jnp.ones((64, 64), F32), jnp.zeros((64, 64), F32)], axis=1),
                                  jnp.concatenate([jnp.zeros((64, 64), F32), jnp.ones((64, 64), F32)], axis=1)],
                                 axis=0).astype(BF)
    ones_two = jnp.concatenate([ones_block, ones_block], axis=0)
    lane_id = lax.broadcasted_iota(jnp.int32, (1, 128), 1)
    hi_lane = jnp.where((lane_id % DH) == 0, 1.0, 0.0)
    lo_lane = jnp.where((lane_id % DH) == 1, 1.0, 0.0)

    def norm_back(rows, dy, gain):
        hat, inv = norm_parts(rows)
        dg = dy * gain
        m_a = jnp.mean(dg, axis=-1, keepdims=True)
        m_b = jnp.mean(dg * hat, axis=-1, keepdims=True)
        return (inv * (dg - m_a - hat * m_b), jnp.sum(dy * hat, axis=0, keepdims=True),
                jnp.sum(dy, axis=0, keepdims=True))

    def out_back(s):
        dx, dgain, dshift = norm_back(middle[s], tokens_grad[s], vecs[4:5])
        up = cot[s].astype(F32)
        mg = up + dx
        middle[s] = mg
        low = mg.astype(BF)
        act[s] = low
        grads[0:1] += jnp.sum(mg, axis=0, keepdims=True)
        grads[1:2] += jnp.sum(up, axis=0, keepdims=True)
        grads[4:5] += dgain
        grads[5:6] += dshift
        ag = dot_nt(low, wo())
        inv = den[s]
        ng = ag * inv
        prod = ng * attended[s].astype(F32)
        n2[s] = ng.astype(BF)
        for p in range(PAIRS):
            cols = slice(p * 128, (p + 1) * 128)
            pr = prod[:, cols]
            hi = pr.astype(BF)
            lo = (pr - hi.astype(F32)).astype(BF)
            dgr = -dot(jnp.concatenate([hi, lo], axis=1), ones_two)
            dhi = dgr.astype(BF).astype(F32)
            dlo = dgr - dhi
            hg[s, :, cols] = (dhi * hi_lane + dlo * lo_lane).astype(BF)
    out_back(0)
    out_back(1)
    dwo = dot(attended[0].T, act[0]) + dot(attended[1].T, act[1])
    part_o[...] = dwo.astype(BF).reshape(lead + (-1, D))
    pump("out")

    def ngx(s, p):
        lanes = pl.ds(pl.multiple_of(p * 128, 128), 128)
        return jnp.concatenate([n2[s, :, lanes], hg[s, :, lanes]], axis=1)

    def state_back(p):
        def seq(s):
            lhs = ngx(s, p).T
            r0 = dot(lhs, pq[s, 2 * p])
            r1 = dot(lhs, pq[s, 2 * p + 1])
            bwd.own[p, s] = jnp.concatenate([r0[:64], r1[64:128], r0[128:144], r1[192:208]], axis=0).astype(BF)
        seq(0)
        seq(1)
        pump_at(p, [f"st{n}" for n in range(PAIRS)])
    loop(PAIRS, state_back)

    lo, hi = slice(0, HALF), slice(HALF, L)

    def masked(keep, value):
        return jnp.where(keep, value, 0.0).astype(BF)

    def through_features(s, p, part, logs):
        through = dot_nt(jnp.concatenate(logs, axis=1), ft[...])
        cols = slice(part * 128, (part + 1) * 128)
        rows = mixed[s, p, :, cols].astype(F32)
        mixed[s, p, :, cols] = (SCALE * through[:, :128] - SCALE * SCALE * through[:, 128:] * rows).astype(BF)

    def input_part(part, chosen):
        cols = slice(part * 128, (part + 1) * 128)
        total = sum(dot(normed_t[s], jnp.concatenate([mixed[s, p, :, cols] for p in chosen], axis=1))
                    for s in range(2))
        return total.astype(BF).reshape(lead + (-1, 128 * len(chosen)))

    def query_back(p, s):
        x = ngx(s, p)
        logs = []
        for h, v in enumerate(vx(s, p)):
            q, k = pq[s, 2 * p + h], pk[s, 2 * p + h]
            sx = state_cols(fwd.total, p, s, h, True)
            g00 = masked(lower, dot_nt(x[lo], v[lo]))
            g10 = dot_nt(x[hi], v[lo]).astype(BF)
            g11 = masked(lower, dot_nt(x[hi], v[hi]))
            qg0 = dot(jnp.concatenate([g00, x[lo]], axis=1), jnp.concatenate([k[lo], sx], axis=0))
            qg1 = dot(jnp.concatenate([g10, g11, x[hi]], axis=1), jnp.concatenate([k, sx], axis=0))
            logs.append((jnp.concatenate([qg0, qg1], axis=0) * q.astype(F32)).astype(BF))
        through_features(s, p, 0, logs)
    pairs(query_back, None, "q")
    part_q[...] = input_part(0, range(PAIRS))
    pump("q.end")

    def key_back(p, s):
        x = ngx(s, p)
        logs = []
        for h, v in enumerate(vx(s, p)):
            q, k = pq[s, 2 * p + h], pk[s, 2 * p + h]
            sg = state_cols(bwd.total, p, s, h, False)
            t00 = masked(upper, dot_nt(v[lo], x[lo]))
            t01 = dot_nt(v[lo], x[hi]).astype(BF)
            t11 = masked(upper, dot_nt(v[hi], x[hi]))
            kg0 = dot(jnp.concatenate([t00, t01, v[lo]], axis=1), jnp.concatenate([q, sg], axis=0))
            kg1 = dot(jnp.concatenate([t11, v[hi]], axis=1), jnp.concatenate([q[hi], sg], axis=0))
            logs.append((jnp.concatenate([kg0, kg1], axis=0) * k.astype(F32)).astype(BF))
        through_features(s, p, 1, logs)
    pairs(key_back, "k.pre", "k")
    part_k[...] = input_part(1, range(PAIRS))
    pump("k.end")

    def value_back(p, s):
        lanes = pl.ds(pl.multiple_of(p * 128, 128), 128)
        ng = n2[s, :, lanes]
        parts = []
        for h in range(2):
            q, k = pq[s, 2 * p + h], pk[s, 2 * p + h]
            parts.append((masked(upper, dot_nt(k[lo], q[lo])), dot_nt(k[lo], q[hi]).astype(BF),
                          masked(upper, dot_nt(k[hi], q[hi]))))
        n0, n1 = ng * m0, ng * m1
        vg0 = dot(jnp.concatenate([parts[0][0], parts[0][1], parts[1][0], parts[1][1]], axis=1),
                  jnp.concatenate([n0, n1], axis=0))
        vg1 = dot(jnp.concatenate([parts[0][2], parts[1][2]], axis=1), jnp.concatenate([n0[hi], n1[hi]], axis=0))
        zeros = jnp.zeros((DH, M), BF)
        sgt = jnp.concatenate([jnp.concatenate([bwd.total[p, s, :64], zeros], axis=0),
                               jnp.concatenate([zeros, bwd.total[p, s, 64:128]], axis=0)], axis=1)
        vg = jnp.concatenate([vg0, vg1], axis=0)
        vg += dot_nt(jnp.concatenate([pk[s, 2 * p], pk[s, 2 * p + 1]], axis=1), sgt)
        mixed[s, p, :, 256:] = vg.astype(BF)
    for n in range(2):
        def step(i):
            value_back(2 * n + i, 0)
            value_back(2 * n + i, 1)
        loop(2, step)
        part_v[n] = input_part(2, range(2 * n, 2 * n + 2))
        pump(f"v{n}")

    def normed_back(s):
        for b in range(2):
            rows = slice(b * HALF, (b + 1) * HALF)
            back = dot_nt(mixed[s, 0, rows], flat(wi[0]))
            for p in range(1, PAIRS):
                back += dot_nt(mixed[s, p, rows], flat(wi[p]))
            tokens_grad[s, rows] = back
    normed_back(0)
    pump("nb0")
    normed_back(1)
    pump("nb1")

    def first_back(s):
        dx, dgain, dshift = norm_back(tokens[s].astype(F32), tokens_grad[s], vecs[2:3])
        tokens_grad[s] = middle[s] + dx
        grads[2:3] += dgain
        grads[3:4] += dshift
    first_back(0)
    pump("fb0")
    first_back(1)
    for g in range(D // 128):
        tile = grads[:, g * 128:(g + 1) * 128].astype(BF)
        for k in range(8):
            chip, core = (8 * g + k) // 2, k % 2
            part_g[chip // (geo.X * geo.Y), chip // geo.Y % geo.X, chip % geo.Y, core] = tile
    local(3, tokens_grad, tokens_grad_hbm).start()
    pump("fb1")
    pump("end0")
    local(5, out_out, out_hbm).start()
    stacked = jnp.concatenate([jnp.concatenate([up_parts[t, :, g * 128:(g + 1) * 128] for t in range(TILES)], axis=1)
                               for g in range(TILES)], axis=0)
    high = stacked.astype(BF)
    low = (stacked - high.astype(F32)).astype(BF)
    stacked = dot_nt(high, perm[...]) + dot_nt(low, perm[...])
    for g in range(TILES):
        up_out[:, g * 512:(g + 1) * 512] = stacked[g * 16:(g + 1) * 16]
    for t in range(TILES):
        down_out[t * 16:(t + 1) * 16] = up_parts[t, :, D:]
    local(6, up_out, up_hbm).start()
    local(7, down_out, down_hbm).start()
    late = {name for name, n in PLAN["end"]}
    drains = [fwd, bwd] + [task for name, task in tasks.items() if name not in late and hasattr(task, "drain")]
    for task in drains:
        task.drain()
    pump("end")
    vec_out[...] = pltpu.roll(vec_sum[...], lax.rem(8 - place, 8) * 16, 1)
    local(8, vec_out, vec_hbm).start()
    local(4, inp_out, inp_hbm).start()
    for i, (a, b) in enumerate(((result, result_hbm), (tokens_grad, tokens_grad_hbm), (inp_out, inp_hbm),
                                (out_out, out_hbm), (up_out, up_hbm), (down_out, down_hbm), (vec_out, vec_hbm))):
        local(2 + i, a, b).wait()
    for name in sorted(late):
        if hasattr(tasks[name], "drain"):
            tasks[name].drain()


def finish_kernel(*refs):
    ins, outs = refs[:7], refs[7:20]
    held, (inp, out, up, down, vec), vec_rows = refs[20], refs[21:26], refs[26:33]
    in_sems, out_sems = refs[33:]
    waits = []

    def copy(src, dst, sems, i):
        return pltpu.make_async_copy(src, dst, sems.at[i])
    small_in = [copy(a, b, in_sems, i) for i, (a, b) in enumerate(zip(ins[2:], (inp, out, up, down, vec)))]
    for one in small_in[:1] + small_in[4:]:
        one.start()
    cuts = []
    for n in range(2):
        for m in range(ins[n].shape[0]):
            for k in range(2):
                rows = pl.ds(k * (ins[n].shape[1] // 2), ins[n].shape[1] // 2)
                slot = held.at[n, m, rows]
                cuts.append((copy(ins[n].at[m, rows], slot, in_sems, 5 + len(cuts)),
                             copy(slot, outs[n].at[m, rows], out_sems, 11 + len(cuts))))
    for first, _ in cuts[:4]:
        first.start()
    for one in small_in[1:4]:
        one.start()
    for first, _ in cuts[4:]:
        first.start()
    small_in[0].wait()
    small_in[4].wait()
    n = vec_rows[0].shape[-1]
    for v in range(6):
        vec_rows[v][...] = vec[v, :n]
    for t in range(up.shape[-1] // 512):
        vec_rows[6][pl.ds(t * n, n)] = vec[6 + t, :n]
    final = {2: inp, 4: vec_rows[0], 8: vec_rows[1], 9: vec_rows[2], 10: vec_rows[3], 11: vec_rows[4],
             12: vec_rows[5], 6: vec_rows[6]}
    for i, (place, ref) in enumerate(final.items()):
        waits.append(copy(ref, outs[place], out_sems, i))
        waits[-1].start()
    for first, second in cuts[:4]:
        first.wait()
        second.start()
        waits.append(second)
    for i, (one, ref, place) in enumerate(zip(small_in[1:4], (out, up, down), (3, 5, 7))):
        one.wait()
        waits.append(copy(ref, outs[place], out_sems, 8 + i))
        waits[-1].start()
    for first, second in cuts[4:]:
        first.wait()
        second.start()
        waits.append(second)
    for one in waits:
        one.wait()


def fused(geo, args):
    (tokens, feature_matrix, input_weight, output_weight, output_bias, up_weight, up_bias, down_weight,
     down_bias, first_gain, first_shift, second_gain, second_shift, cotangent) = args
    rows, D = input_weight.shape[0], tokens.shape[-1]
    L = tokens.shape[1]
    FF = up_weight.shape[1]
    tiles = FF // 512
    lane = Lane()
    fwd, bwd = States(geo, lane, True), States(geo, lane, False)
    names = ["S", "O"] + [f"I{p}" for p in range(PAIRS)] + [f"F{t}" for t in range(tiles)]
    tasks = {name: GatherPlane(geo, lane) if name in PLANE else Gather(geo, lane, ORDERS.get(name, (0, 1)))
             for name in names}
    scatters = {"rO": D, "rQ": D, "rK": D, "rV0": 256, "rV1": 256, "rG": 128}
    scatters.update({f"rF{t}": 2 * D for t in range(tiles)})
    for name in scatters:
        tasks[name] = ScatterDirect(geo, lane) if name in DIRECT else Scatter(geo, lane, ORDERS.get(name, (0, 1)))
    for p in range(PAIRS):
        tasks[f"f{p}"], tasks[f"b{p}"] = PairStates(fwd, p), PairStates(bwd, p)
    plan = (fwd, bwd, tasks)
    lead = (geo.Z, geo.X, geo.Y, 2)
    V = pltpu.VMEM
    shape = jax.ShapeDtypeStruct
    outs = [shape(tokens.shape, F32), shape(tokens.shape, F32), shape(input_weight.shape, F32),
            shape((rows, D), F32), shape((rows, FF), F32), shape(down_weight.shape, F32), shape((rows, 128), F32)]
    arrays = (tokens, cotangent, feature_matrix, output_bias, down_bias, first_gain, first_shift, second_gain,
              second_shift, up_bias, input_weight, output_weight, up_weight, down_weight)
    scratch = [V(a.shape, BF) for a in arrays[2:11] + arrays[12:]] + [V(o.shape, F32) for o in outs[2:]]
    scratch += [
        V((2, L, D), BF), V((2, L, D), BF), V((2, L, D), F32), V((2, L, D), F32),
        V((rows, 128), BF), V(lead + (rows, 128), BF), V((PAIRS, rows, 384), BF), V((PAIRS,) + lead + (rows, 384), BF),
        V((rows, D), BF), V(lead + (rows, D), BF), V((tiles, rows, 2 * D), BF),
        V((tiles,) + lead + (rows, 2 * D), BF),
        V((2, L, D), BF), V((2, D, L), BF), V((2, PAIRS, L, 384), BF), V((2, H, L, M), BF), V((2, H, L, M), BF),
        V((2, L, D), F32), V((2, L, D), BF), V((2, L, D), F32), V((2, D, L), BF),
        V((2, L, 512), BF), V((2, L, 512), BF), V((16, D), F32), V((16, D), F32),
        V((2, M, M), BF), V((M, 2 * M), BF), V((512, 512), BF),
        V(lead + (rows, D), BF), V(lead + (rows, D), BF), V((2,) + lead + (rows, 256), BF), V(lead + (rows, D), BF),
        V((tiles,) + lead + (rows, 2 * D), BF), V(lead + (rows, 128), BF), V((tiles, rows, 2 * D), F32), V((rows, 128), F32),
    ]
    scratch += States.scratch(geo) + States.scratch(geo)
    for name, width in scatters.items():
        scratch += type(tasks[name]).scratch(geo, rows, width)
    scratch += [pltpu.SemaphoreType.DMA((lane.count,)), pltpu.SemaphoreType.DMA((lane.count,)),
                pltpu.SemaphoreType.DMA((21,))]
    hbm = pl.BlockSpec(memory_space=pl.ANY)
    parts = pl.pallas_call(
        functools.partial(layer_kernel, geo, lane, plan),
        out_shape=outs, in_specs=[hbm] * 14, out_specs=[hbm] * 7, scratch_shapes=scratch,
        compiler_params=pltpu.CompilerParams(collective_id=0, has_side_effects=True, vmem_limit_bytes=60 << 20),
    )(*arrays)
    vector = shape((rows,), F32)
    final = [outs[0], outs[1], shape(input_weight.shape, F32), outs[3], vector, outs[4],
             shape(up_bias.shape, F32), outs[5]] + [vector] * 5
    return pl.pallas_call(
        finish_kernel,
        out_shape=final, in_specs=[hbm] * 7, out_specs=[hbm] * 13,
        scratch_shapes=[V((2,) + tokens.shape, F32)] + [V(o.shape, F32) for o in outs[2:]]
        + [V((rows,), F32)] * 6 + [V(up_bias.shape, F32)]
        + [pltpu.SemaphoreType.DMA((13,)), pltpu.SemaphoreType.DMA((19,))],
        compiler_params=pltpu.CompilerParams(vmem_limit_bytes=60 << 20),
    )(*parts)

def local(
    tokens,
    feature_matrix,
    input_weight,
    output_weight,
    output_bias,
    up_weight,
    up_bias,
    down_weight,
    down_bias,
    first_gain,
    first_shift,
    second_gain,
    second_shift,
    cotangent,
):
    params = (
        lax.all_gather(input_weight, ("dp", "seq"), axis=0, tiled=True),
        lax.all_gather(output_weight, ("dp", "seq"), axis=0, tiled=True),
        lax.all_gather(output_bias, ("dp", "seq"), axis=0, tiled=True),
        lax.all_gather(up_weight, ("dp", "seq"), axis=0, tiled=True),
        lax.all_gather(up_bias, ("dp", "seq"), axis=0, tiled=True),
        lax.all_gather(down_weight, ("dp", "seq"), axis=0, tiled=True),
        lax.all_gather(down_bias, ("dp", "seq"), axis=0, tiled=True),
        lax.all_gather(first_gain, ("dp", "seq"), axis=0, tiled=True),
        lax.all_gather(first_shift, ("dp", "seq"), axis=0, tiled=True),
        lax.all_gather(second_gain, ("dp", "seq"), axis=0, tiled=True),
        lax.all_gather(second_shift, ("dp", "seq"), axis=0, tiled=True),
    )
    micros = tokens.shape[0]
    fronts = []
    carries = []
    for micro_step in range(micros):
        pieces = front(tokens[micro_step], feature_matrix, params)
        fronts.append(pieces)
        carries.append(
            prefix(
                (pieces[8], pieces[9]),
                "seq",
                add_pair,
                (jnp.zeros_like(pieces[8]), jnp.zeros_like(pieces[9])),
            )
        )
    results = []
    for micro_step in range(micros):
        pieces = fronts[micro_step]
        running_prefix_state, norm_sum = carries[micro_step]
        output = attend(pieces[5], pieces[6], pieces[7], running_prefix_state, norm_sum)[0]
        attended, middle = upper(pieces[0], output, params)
        results.append(feed(middle, params))
    result = jnp.stack(results)
    back_params = (
        lax.all_gather(input_weight, ("dp", "seq"), axis=0, tiled=True),
        lax.all_gather(output_weight, ("dp", "seq"), axis=0, tiled=True),
        lax.all_gather(output_bias, ("dp", "seq"), axis=0, tiled=True),
        lax.all_gather(up_weight, ("dp", "seq"), axis=0, tiled=True),
        lax.all_gather(up_bias, ("dp", "seq"), axis=0, tiled=True),
        lax.all_gather(down_weight, ("dp", "seq"), axis=0, tiled=True),
        lax.all_gather(down_bias, ("dp", "seq"), axis=0, tiled=True),
        lax.all_gather(first_gain, ("dp", "seq"), axis=0, tiled=True),
        lax.all_gather(first_shift, ("dp", "seq"), axis=0, tiled=True),
        lax.all_gather(second_gain, ("dp", "seq"), axis=0, tiled=True),
        lax.all_gather(second_shift, ("dp", "seq"), axis=0, tiled=True),
    )
    stored_list = []
    later_list = []
    for micro_step in range(micros):
        stored = upper_back(
            tokens[micro_step],
            cotangent[micro_step].astype(jnp.float32),
            feature_matrix,
            back_params,
            carries[micro_step],
        )
        stored_list.append(stored)
        later_list.append(
            prefix_2(
                (stored["state_grad"], stored["sum_grad"]),
                "seq",
                add_pair,
                (jnp.zeros_like(stored["state_grad"]), jnp.zeros_like(stored["sum_grad"])),
            )
        )
    upper_names = ["out", "out_bias", "up", "up_bias", "down", "down_bias", "gain_two", "shift_two"]
    upper_totals = [stored_list[0][name] for name in upper_names]
    micro_step = 1
    upper_totals = [
        total + stored_list[micro_step][name] for total, name in zip(upper_totals, upper_names)
    ]
    token_grads = []
    lower_totals = None
    for micro_step in range(micros):
        stored = stored_list[micro_step]
        tokens_part, input_part, gain_part, shift_part = lower_back(
            stored, later_list[micro_step], feature_matrix, back_params
        )
        token_grads.append(tokens_part)
        lower_parts = (input_part, gain_part, shift_part)
        if micro_step == 0:
            lower_totals = lower_parts
        else:
            lower_totals = jax.tree.map(jnp.add, lower_totals, lower_parts)
    shares = (
        lax.psum_scatter(lower_totals[0], ("dp", "seq"), scatter_dimension=0, tiled=True),
        lax.psum_scatter(upper_totals[0], ("dp", "seq"), scatter_dimension=0, tiled=True),
        lax.psum_scatter(upper_totals[1], ("dp", "seq"), scatter_dimension=0, tiled=True),
        lax.psum_scatter(upper_totals[2], ("dp", "seq"), scatter_dimension=0, tiled=True),
        lax.psum_scatter(upper_totals[3], ("dp", "seq"), scatter_dimension=0, tiled=True),
        lax.psum_scatter(upper_totals[4], ("dp", "seq"), scatter_dimension=0, tiled=True),
        lax.psum_scatter(upper_totals[5], ("dp", "seq"), scatter_dimension=0, tiled=True),
        lax.psum_scatter(lower_totals[1], ("dp", "seq"), scatter_dimension=0, tiled=True),
        lax.psum_scatter(lower_totals[2], ("dp", "seq"), scatter_dimension=0, tiled=True),
        lax.psum_scatter(upper_totals[6], ("dp", "seq"), scatter_dimension=0, tiled=True),
        lax.psum_scatter(upper_totals[7], ("dp", "seq"), scatter_dimension=0, tiled=True),
    )
    return (
        result,
        jnp.stack(token_grads),
        shares[0],
        shares[1],
        shares[2],
        shares[3],
        shares[4],
        shares[5],
        shares[6],
        shares[7],
        shares[8],
        shares[9],
        shares[10],
    )


def solution(mesh):
    in_specs = (
        P("dp", "seq", None),
        P(),
        P(("dp", "seq"), None),
        P(("dp", "seq"), None),
        P(("dp", "seq")),
        P(("dp", "seq"), None),
        P(("dp", "seq")),
        P(("dp", "seq"), None),
        P(("dp", "seq")),
        P(("dp", "seq")),
        P(("dp", "seq")),
        P(("dp", "seq")),
        P(("dp", "seq")),
        P("dp", "seq", None),
    )
    out_specs = (
        P("dp", "seq", None),
        P("dp", "seq", None),
        P(("dp", "seq"), None),
        P(("dp", "seq"), None),
        P(("dp", "seq")),
        P(("dp", "seq"), None),
        P(("dp", "seq")),
        P(("dp", "seq"), None),
        P(("dp", "seq")),
        P(("dp", "seq")),
        P(("dp", "seq")),
        P(("dp", "seq")),
        P(("dp", "seq")),
    )
    geo = Geometry(mesh)
    rows = 512 // (mesh.shape["dp"] * mesh.shape["seq"])
    if rows == 16:
        def body(*args):
            return fused(geo, args)
    else:
        body = local
    return jax.shard_map(body, mesh=mesh, in_specs=in_specs, out_specs=out_specs, check_vma=False)
```

```python
import functools
import math

import jax
import jax.numpy as jnp
from jax import lax
from jax.sharding import PartitionSpec as P

H = 8
DH = 64

from jax.experimental import pallas as pl
from jax.experimental.pallas import tpu as pltpu

MESH = pl.DeviceIdType.MESH


class Geometry:
    def __init__(self, mesh):
        dp, seq = mesh.shape["dp"], mesh.shape["seq"]
        self.C = 2
        self.Y = seq // 2
        self.X = 1 << ((dp.bit_length() - 1) // 2)
        self.Z = dp // self.X

    def me(self):
        dp, seq = lax.axis_index("dp"), lax.axis_index("seq")
        return dp // self.X, dp % self.X, seq // 2, seq % 2

    def device(self, z, x, y, c):
        return (z * self.X + x, y * 2 + c)

    def greet(self):
        z, x, y, c = self.me()
        peers = [self.device(z, x, y, 1 - c)]
        peers += [self.device((z + i) % self.Z, (x + j) % self.X, (y + k) % self.Y, c)
                  for i in range(self.Z) for j in range(self.X) for k in range(self.Y)][1:]
        semaphore = pltpu.get_barrier_semaphore()
        for peer in peers:
            pl.semaphore_signal(semaphore, inc=1, device_id=peer, device_id_type=MESH)

    def barrier(self):
        pl.semaphore_wait(pltpu.get_barrier_semaphore(), self.Z * self.X * self.Y)


class Lane:
    def __init__(self):
        self.count = 0
        self.send = self.recv = None

    def take(self, n=1):
        first = self.count
        self.count += n
        return first


def remote(lane, index, src, dst, device):
    return pltpu.make_async_remote_copy(
        src_ref=src, dst_ref=dst, send_sem=lane.send.at[index], recv_sem=lane.recv.at[index],
        device_id=device, device_id_type=MESH)


class Gather:
    def __init__(self, geo, lane, orders):
        self.geo, self.lane, self.orders = geo, lane, orders
        self.zs = lane.take()
        self.second = lane.take(max(geo.X, geo.Y) - 1)
        self.third = lane.take(max(geo.X, geo.Y) - 1)
        self.core = lane.take()

    def bind(self, own, full):
        self.own, self.full = own, full

    def z_copies(self):
        g = self.geo
        z, x, y, c = g.me()
        for k in range(1, g.Z):
            yield remote(self.lane, self.zs, self.own, self.full.at[z, x, y, c], g.device((z + k) % g.Z, x, y, c))

    def z_whole(self):
        g = self.geo
        z, x, y, c = g.me()
        slots = self.full.at[pl.ds(0, g.Z - 1), x, y, c]
        return remote(self.lane, self.zs, slots, slots, g.device((z + 1) % g.Z, x, y, c))

    def axis_copies(self, phase, order, incoming):
        g = self.geo
        z, x, y, c = g.me()
        base = self.second if phase == 2 else self.third
        along_x = (phase == 2) == (order == 0)
        size = g.X if along_x else g.Y
        for k in range(1, size):
            if along_x:
                source = (x + g.X - k) % g.X if incoming else x
                device = g.device(z, (x + k) % g.X, y, c)
                slot = self.full.at[:, source, y, c] if phase == 2 else self.full.at[:, source, :, c]
            else:
                source = (y + g.Y - k) % g.Y if incoming else y
                device = g.device(z, x, (y + k) % g.Y, c)
                slot = self.full.at[:, x, source, c] if phase == 2 else self.full.at[:, :, source, c]
            yield remote(self.lane, base + k - 1, slot, slot, device)

    def both(self, action):
        c = self.geo.me()[3]
        if self.orders[0] == self.orders[1]:
            action(self.orders[0])
            return
        for core in range(2):
            @pl.when(c == core)
            def _():
                action(self.orders[core])

    def step(self, n):
        g = self.geo
        z, x, y, c = g.me()
        if n == 0:
            for copy in self.z_copies():
                copy.start()
            self.full[z, x, y, c] = self.own[...]
        elif n == 1:
            self.z_whole().wait_recv()
            self.both(lambda order: [copy.start() for copy in self.axis_copies(2, order, False)])
        elif n == 2:
            def go(order):
                for copy in self.axis_copies(2, order, True):
                    copy.wait_recv()
                for copy in self.axis_copies(3, order, False):
                    copy.start()
            self.both(go)
        elif n == 3:
            def go(order):
                for copy in self.axis_copies(3, order, True):
                    copy.wait_recv()
            self.both(go)
            slot = self.full.at[:, :, :, c]
            remote(self.lane, self.core, slot, slot, g.device(z, x, y, 1 - c)).start()
        else:
            slot = self.full.at[:, :, :, 1 - c]
            remote(self.lane, self.core, slot, slot, g.device(z, x, y, 1 - c)).wait_recv()

    def drain(self):
        g = self.geo
        z, x, y, c = g.me()
        self.z_whole().wait_send()

        def go(order):
            for phase in (2, 3):
                for copy in self.axis_copies(phase, order, False):
                    copy.wait_send()
        self.both(go)
        slot = self.full.at[:, :, :, c]
        remote(self.lane, self.core, slot, slot, g.device(z, x, y, 1 - c)).wait_send()


class Scatter:
    def __init__(self, geo, lane, orders):
        self.geo, self.lane, self.orders = geo, lane, orders
        self.core = lane.take()
        self.first = lane.take(max(geo.X, geo.Y) - 1)
        self.second = lane.take(max(geo.X, geo.Y) - 1)
        self.zs = lane.take()

    @staticmethod
    def scratch(geo, rows, width):
        wide = max(geo.X, geo.Y)
        kind = jnp.bfloat16
        return [
            pltpu.VMEM((geo.Z, geo.X, geo.Y, rows, width), kind),
            pltpu.VMEM((wide - 1, geo.Z, wide, rows, width), kind),
            pltpu.VMEM((wide - 1, geo.Z, rows, width), kind),
            pltpu.VMEM((geo.Z - 1, rows, width), kind),
        ]

    def bind(self, part, out, buffers):
        self.part, self.out = part, out
        self.rc, self.ra, self.rb, self.rz = buffers

    def both(self, action):
        c = self.geo.me()[3]
        if self.orders[0] == self.orders[1]:
            action(self.orders[0])
            return
        for core in range(2):
            @pl.when(c == core)
            def _():
                action(self.orders[core])

    def core_copy(self):
        z, x, y, c = self.geo.me()
        return remote(self.lane, self.core, self.part.at[:, :, :, 1 - c], self.rc,
                      self.geo.device(z, x, y, 1 - c))

    def axis_copies(self, phase, order):
        g = self.geo
        z, x, y, c = g.me()
        base = self.first if phase == 1 else self.second
        along_x = (phase == 1) == (order == 1)
        for k in range(1, g.X if along_x else g.Y):
            if along_x:
                far = (x + k) % g.X
                device = g.device(z, far, y, c)
                src = self.part.at[:, far, :, c] if phase == 1 else self.part.at[:, far, y, c]
                dst = self.ra.at[k - 1, :, pl.ds(0, g.Y)] if phase == 1 else self.rb.at[k - 1]
            else:
                far = (y + k) % g.Y
                device = g.device(z, x, far, c)
                src = self.part.at[:, :, far, c] if phase == 1 else self.part.at[:, x, far, c]
                dst = self.ra.at[k - 1, :, pl.ds(0, g.X)] if phase == 1 else self.rb.at[k - 1]
            yield remote(self.lane, base + k - 1, src, dst, device)

    def z_copies(self):
        g = self.geo
        z, x, y, c = g.me()
        for k in range(1, g.Z):
            far = (z + k) % g.Z
            yield remote(self.lane, self.zs, self.part.at[far, x, y, c], self.rz.at[k - 1], g.device(far, x, y, c))

    def z_whole(self):
        g = self.geo
        z, x, y, c = g.me()
        return remote(self.lane, self.zs, self.rz, self.rz, g.device((z + 1) % g.Z, x, y, c))

    def step(self, n):
        g = self.geo
        z, x, y, c = g.me()
        wide = lambda ref: ref.astype(jnp.float32)
        if n == 0:
            self.core_copy().start()
        elif n == 1:
            self.core_copy().wait_recv()

            def add(i, _):
                total = wide(self.part[i, :, :, c]) + wide(self.rc[i])
                self.part[i, :, :, c] = total.astype(jnp.bfloat16)
                return 0
            lax.fori_loop(0, g.Z, add, 0)
            self.both(lambda order: [copy.start() for copy in self.axis_copies(1, order)])
        elif n == 2:
            def go(order):
                copies = list(self.axis_copies(1, order))
                for copy in copies:
                    copy.wait_recv()
                count = len(copies)
                if order == 0:
                    def add(i, _):
                        total = wide(self.part[i, :, y, c])
                        for k in range(count):
                            total += wide(self.ra[k, i, : g.X])
                        self.part[i, :, y, c] = total.astype(jnp.bfloat16)
                        return 0
                else:
                    def add(i, _):
                        total = wide(self.part[i, x, :, c])
                        for k in range(count):
                            total += wide(self.ra[k, i, : g.Y])
                        self.part[i, x, :, c] = total.astype(jnp.bfloat16)
                        return 0
                lax.fori_loop(0, g.Z, add, 0)
                for copy in self.axis_copies(2, order):
                    copy.start()
            self.both(go)
        elif n == 3:
            def go(order):
                copies = list(self.axis_copies(2, order))
                for copy in copies:
                    copy.wait_recv()

                def add(i, _):
                    total = wide(self.part[i, x, y, c])
                    for k in range(len(copies)):
                        total += wide(self.rb[k, i])
                    self.part[i, x, y, c] = total.astype(jnp.bfloat16)
                    return 0
                lax.fori_loop(0, g.Z, add, 0)
            self.both(go)
            for copy in self.z_copies():
                copy.start()
        else:
            total = wide(self.part[z, x, y, c])
            self.z_whole().wait_recv()
            for k in range(g.Z - 1):
                total += wide(self.rz[k])
            self.out[...] = total

    def drain(self):
        self.core_copy().wait_send()

        def go(order):
            for phase in (1, 2):
                for copy in self.axis_copies(phase, order):
                    copy.wait_send()
        self.both(go)
        self.z_whole().wait_send()


epsilon = 1e-05
finest_precision = lax.Precision.HIGHEST


def prefix(array, axis, combine, identity):
    count, here = (lax.axis_size(axis), lax.axis_index(axis))
    everything = jax.tree.map(
        lambda part, kind: lax.all_gather(part.astype(kind), axis),
        array,
        (jnp.bfloat16, jnp.bfloat16),
    )
    start = jax.tree.map(
        lambda part, zero: jnp.broadcast_to(jnp.asarray(zero, part.dtype), part.shape),
        array,
        identity,
    )

    def hop(k, before):
        reached = k < here
        new = combine(
            before, jax.tree.map(lambda part, own: part[k].astype(own.dtype), everything, array)
        )
        return jax.tree.map(lambda a, b: jnp.where(reached, a, b), new, before)

    return lax.fori_loop(0, count, hop, start)


def prefix_2(array, axis, join, neutral):
    count = lax.axis_size(axis)
    place = lax.axis_index(axis)
    ahead = count - 1 - place
    gathered = jax.tree.map(
        lambda a, kind: lax.all_gather(a.astype(kind), axis),
        array,
        jax.tree.map(lambda a: jnp.bfloat16 if a.dtype == jnp.float32 else a.dtype, array),
    )
    state = jax.tree.map(lambda a, e: jnp.zeros_like(a) + jnp.asarray(e, a.dtype), array, neutral)

    def one(hop, state):
        source = count - 1 - hop
        return join(
            state,
            jax.tree.map(
                lambda a, own: lax.dynamic_index_in_dim(a, source, 0, False).astype(own.dtype),
                gathered,
                array,
            ),
        )

    return lax.fori_loop(0, ahead, one, state)


def layer_norm(value_rows, norm_gain, norm_shift):
    center = jnp.mean(value_rows, axis=-1, keepdims=True)
    centred = value_rows - center
    spread = jnp.mean(centred * centred, axis=-1, keepdims=True)
    return centred * lax.rsqrt(spread + epsilon) * norm_gain + norm_shift


def gelu_tanh(value_rows):
    return jax.nn.gelu(value_rows, approximate=True)


def add_pair(earlier, later_term):
    return (earlier[0] + later_term[0], earlier[1] + later_term[1])


def causal_mask(length):
    positions = jnp.arange(length)
    return (positions[:, None] >= positions[None, :]).astype(jnp.float32)


def favor_map(proj_low, matrix, feature_scale):
    raw_proj = jnp.einsum("rhd,dm->rhm", proj_low, matrix, preferred_element_type=jnp.float32)
    projection = proj_low.astype(jnp.float32)
    half_norm = (
        0.5
        * feature_scale
        * feature_scale
        * jnp.sum(projection * projection, axis=-1, keepdims=True)
    )
    return jnp.exp(feature_scale * raw_proj - half_norm) / math.sqrt(matrix.shape[1])


def favor_back(map_grad, favor_value, proj_low, matrix, feature_scale):
    log_grad = map_grad * favor_value
    raw_grad = (feature_scale * log_grad).astype(jnp.bfloat16)
    projection = proj_low.astype(jnp.float32)
    through = jnp.einsum("rhm,dm->rhd", raw_grad, matrix, preferred_element_type=jnp.float32)
    return (
        through
        - feature_scale * feature_scale * jnp.sum(log_grad, axis=-1, keepdims=True) * projection
    )


def front(token_block, matrix, params):
    inputs = token_block.astype(jnp.float32)
    length = inputs.shape[0]
    normed = layer_norm(
        inputs, params[7].astype(jnp.float32), params[8].astype(jnp.float32)
    ).astype(jnp.bfloat16)
    mixed = jnp.dot(normed, params[0], preferred_element_type=jnp.float32).astype(jnp.bfloat16)
    head_parts = mixed.reshape(length, 3, H, DH)
    feature_scale = DH ** (-0.25)
    query_features = favor_map(head_parts[:, 0], matrix, feature_scale)
    key_features = favor_map(head_parts[:, 1], matrix, feature_scale)
    query_reduced = query_features.astype(jnp.bfloat16)
    key_reduced = key_features.astype(jnp.bfloat16)
    value_rows = head_parts[:, 2]
    block_local_state = jnp.einsum(
        "nqo,nqi->qoi", key_reduced, value_rows, preferred_element_type=jnp.float32
    )
    local_sum = jnp.sum(key_reduced.astype(jnp.float32), axis=0)
    return (
        inputs,
        normed,
        head_parts,
        query_features,
        key_features,
        query_reduced,
        key_reduced,
        value_rows,
        block_local_state,
        local_sum,
    )


def attend(query_reduced, key_reduced, value_rows, running_prefix_state, norm_sum):
    causal = causal_mask(query_reduced.shape[0])
    scores = (
        jnp.einsum("ihm,jhm->hij", query_reduced, key_reduced, preferred_element_type=jnp.float32)
        * causal[None]
    )
    denominator = jnp.sum(scores, axis=-1).T + jnp.einsum(
        "ihm,hm->ih", query_reduced.astype(jnp.float32), norm_sum, precision=finest_precision
    )
    attention_numerator = jnp.einsum(
        "hij,jhd->ihd", scores.astype(jnp.bfloat16), value_rows, preferred_element_type=jnp.float32
    )
    attention_numerator = attention_numerator + jnp.einsum(
        "plq,lqu->plu",
        query_reduced,
        running_prefix_state.astype(jnp.bfloat16),
        preferred_element_type=jnp.float32,
    )
    return (attention_numerator / denominator[:, :, None], attention_numerator, denominator)


def upper(inputs, output, params):
    length = output.shape[0]
    attended = output.reshape(length, -1).astype(jnp.bfloat16)
    middle = (
        inputs
        + jnp.dot(attended, params[1], preferred_element_type=jnp.float32)
        + params[2].astype(jnp.float32)
    )
    return (attended, middle)


def feed(middle, params):
    normed_two = layer_norm(
        middle, params[9].astype(jnp.float32), params[10].astype(jnp.float32)
    ).astype(jnp.bfloat16)
    hidden = jnp.dot(normed_two, params[3], preferred_element_type=jnp.float32) + params[4].astype(
        jnp.float32
    )
    active = gelu_tanh(hidden).astype(jnp.bfloat16)
    return (
        middle
        + jnp.dot(active, params[5], preferred_element_type=jnp.float32)
        + params[6].astype(jnp.float32)
    )


def upper_back(token_block, upstream, matrix, params, block_carry):
    pieces = front(token_block, matrix, params)
    (
        inputs,
        normed,
        head_parts,
        query_features,
        key_features,
        query_reduced,
        key_reduced,
        value_rows,
        block_local_state,
        local_sum,
    ) = pieces
    running_prefix_state, norm_sum = block_carry
    output, attention_numerator, denominator = attend(
        query_reduced, key_reduced, value_rows, running_prefix_state, norm_sum
    )
    attended, middle = upper(inputs, output, params)
    normed_float, second_pull = jax.vjp(
        layer_norm, middle, params[9].astype(jnp.float32), params[10].astype(jnp.float32)
    )
    normed_two = normed_float.astype(jnp.bfloat16)
    hidden = jnp.dot(normed_two, params[3], preferred_element_type=jnp.float32) + params[4].astype(
        jnp.float32
    )
    active_float, gelu_pull = jax.vjp(gelu_tanh, hidden)
    active = active_float.astype(jnp.bfloat16)
    stored = {"front": pieces, "carry": block_carry}
    down_term = upstream.astype(jnp.bfloat16)
    stored["down"] = jnp.einsum("rf,rd->fd", active, down_term, preferred_element_type=jnp.float32)
    stored["down_bias"] = jnp.sum(upstream, axis=0)
    active_grad = jnp.einsum("rd,fd->rf", down_term, params[5], preferred_element_type=jnp.float32)
    (hidden_grad,) = gelu_pull(active_grad)
    up_term = hidden_grad.astype(jnp.bfloat16)
    stored["up"] = jnp.einsum("rd,rf->df", normed_two, up_term, preferred_element_type=jnp.float32)
    stored["up_bias"] = jnp.sum(hidden_grad, axis=0)
    normed_two_grad = jnp.einsum(
        "rf,df->rd", up_term, params[3], preferred_element_type=jnp.float32
    )
    middle_part, gain_two_grad, shift_two_grad = second_pull(normed_two_grad)
    stored["gain_two"] = gain_two_grad
    stored["shift_two"] = shift_two_grad
    middle_grad = upstream + middle_part
    stored["middle_grad"] = middle_grad
    out_term = middle_grad.astype(jnp.bfloat16)
    stored["out"] = jnp.einsum("re,rd->ed", attended, out_term, preferred_element_type=jnp.float32)
    stored["out_bias"] = jnp.sum(middle_grad, axis=0)
    attended_grad = jnp.einsum(
        "rd,ed->re", out_term, params[1], preferred_element_type=jnp.float32
    ).reshape(output.shape)
    numerator_grad = (attended_grad / denominator[:, :, None]).astype(jnp.bfloat16)
    denom_grad = -jnp.sum(attended_grad * attention_numerator, axis=-1) / (
        denominator * denominator
    )
    stored["numer_grad"] = numerator_grad
    stored["denom_grad"] = denom_grad
    stored["state_grad"] = jnp.einsum(
        "jfp,jfl->fpl", query_reduced, numerator_grad, preferred_element_type=jnp.float32
    )
    stored["sum_grad"] = jnp.einsum(
        "ih,ihm->hm", denom_grad, query_reduced.astype(jnp.float32), precision=finest_precision
    )
    return stored


def lower_back(stored, later_part, matrix, params):
    (
        inputs,
        normed,
        head_parts,
        query_features,
        key_features,
        query_reduced,
        key_reduced,
        value_rows,
        block_local_state,
        local_sum,
    ) = stored["front"]
    running_prefix_state, norm_sum = stored["carry"]
    state_later, sum_later = later_part
    numerator_grad = stored["numer_grad"]
    denom_grad = stored["denom_grad"]
    length = inputs.shape[0]
    causal = causal_mask(length)
    scores = (
        jnp.einsum("ihm,jhm->hij", query_reduced, key_reduced, preferred_element_type=jnp.float32)
        * causal[None]
    )
    scores_grad = jnp.einsum(
        "ihd,jhd->hij", numerator_grad, value_rows, preferred_element_type=jnp.float32
    )
    score_term = ((scores_grad + denom_grad.T[:, :, None]) * causal[None]).astype(jnp.bfloat16)
    later_reduced = state_later.astype(jnp.bfloat16)
    query_grad = jnp.einsum(
        "hij,jhm->ihm", score_term, key_reduced, preferred_element_type=jnp.float32
    )
    query_grad = query_grad + jnp.einsum(
        "gvw,vcw->gvc",
        numerator_grad,
        running_prefix_state.astype(jnp.bfloat16),
        preferred_element_type=jnp.float32,
    )
    query_grad = query_grad + denom_grad[:, :, None] * norm_sum[None]
    key_grad = jnp.einsum(
        "hij,ihm->jhm", score_term, query_reduced, preferred_element_type=jnp.float32
    )
    key_grad = key_grad + jnp.einsum(
        "prc,rqc->prq", value_rows, later_reduced, preferred_element_type=jnp.float32
    )
    key_grad = key_grad + sum_later[None]
    value_grad = jnp.einsum(
        "hij,ihd->jhd",
        scores.astype(jnp.bfloat16),
        numerator_grad,
        preferred_element_type=jnp.float32,
    )
    value_grad = value_grad + jnp.einsum(
        "qsa,saw->qsw", key_reduced, later_reduced, preferred_element_type=jnp.float32
    )
    feature_scale = DH ** (-0.25)
    query_proj = favor_back(query_grad, query_features, head_parts[:, 0], matrix, feature_scale)
    key_proj = favor_back(key_grad, key_features, head_parts[:, 1], matrix, feature_scale)
    mixed_grad = (
        jnp.stack([query_proj, key_proj, value_grad], axis=1)
        .reshape(length, -1)
        .astype(jnp.bfloat16)
    )
    input_part = jnp.einsum("rd,re->de", normed, mixed_grad, preferred_element_type=jnp.float32)
    normed_grad = jnp.einsum("re,de->rd", mixed_grad, params[0], preferred_element_type=jnp.float32)
    _, first_pull = jax.vjp(
        layer_norm, inputs, params[7].astype(jnp.float32), params[8].astype(jnp.float32)
    )
    inputs_part, gain_one_grad, shift_one_grad = first_pull(normed_grad)
    return (stored["middle_grad"] + inputs_part, input_part, gain_one_grad, shift_one_grad)


BF = jnp.bfloat16
F32 = jnp.float32
M = 256
SCALE = DH ** (-0.25)
LOG2E = math.log2(math.e)
PAIRS = H // 2
STATE_ROWS = 144


def dot(a, b):
    return jnp.dot(a, b, preferred_element_type=F32)


def dot_nt(a, b):
    return lax.dot_general(a, b, (((1,), (1,)), ((), ())), preferred_element_type=F32)


class States:
    def __init__(self, geo, lane, earlier):
        self.geo, self.lane, self.earlier = geo, lane, earlier
        self.per = geo.Y + 1
        self.first = lane.take(self.per * PAIRS)

    @staticmethod
    def scratch(geo):
        one = (PAIRS, STATE_ROWS, M)
        two = (PAIRS, 2, STATE_ROWS, M)
        return [pltpu.VMEM(two, BF), pltpu.VMEM(two, BF), pltpu.VMEM(one, BF),
                pltpu.VMEM((PAIRS, max(geo.Y - 1, 1), STATE_ROWS, M), BF), pltpu.VMEM(one, BF),
                pltpu.VMEM(one, BF), pltpu.VMEM(two, BF)]

    def bind(self, buffers):
        self.own, self.sibling, self.chip, self.chips, self.base, self.base_sibling, self.total = buffers

    def copies(self, p, phase):
        g = self.geo
        z, x, y, c = g.me()
        index = self.first + p * self.per
        other = g.device(z, x, y, 1 - c)
        if phase == 0:
            return [remote(self.lane, index, self.own.at[p], self.sibling.at[p], other)]
        if phase == 1:
            return [remote(self.lane, index + k, self.chip.at[p], self.chips.at[p, k - 1],
                           g.device(z, x, (y + k) % g.Y, c)) for k in range(1, g.Y)]
        return [remote(self.lane, index + g.Y, self.base.at[p], self.base_sibling.at[p], other)]

    def step(self, n, p):
        g = self.geo
        z, x, y, c = g.me()
        if n > 0:
            for copy in self.copies(p, n - 1):
                copy.wait_recv()
        if n == 1:
            self.chip[p] = (self.own[p, c].astype(F32) + self.sibling[p, c].astype(F32)).astype(BF)
        elif n == 2:
            total = jnp.zeros((STATE_ROWS, M), F32)
            for k in range(1, g.Y):
                source = (y + g.Y - k) % g.Y
                counts = source < y if self.earlier else source > y
                total += jnp.where(counts, 1.0, 0.0) * self.chips[p, k - 1].astype(F32)
            self.base[p] = total.astype(BF)
        elif n == 3:
            near = jnp.where(c == (1 if self.earlier else 0), 1.0, 0.0)
            self.total[p, c] = (self.base[p].astype(F32) + near * self.sibling[p, c].astype(F32)).astype(BF)
            self.total[p, 1 - c] = (self.base_sibling[p].astype(F32)
                                    + near * self.sibling[p, 1 - c].astype(F32)).astype(BF)
        if n < 3:
            for copy in self.copies(p, n):
                copy.start()

    def drain(self):
        for p in range(PAIRS):
            for phase in range(3):
                for copy in self.copies(p, phase):
                    copy.wait_send()


class GatherPlane(Gather):
    def __init__(self, geo, lane):
        self.geo, self.lane = geo, lane
        self.far = [(j, k) for j in range(geo.X) for k in range(geo.Y)][1:]
        self.zs, self.plane, self.core = lane.take(), lane.take(len(self.far)), lane.take()

    def plane_copies(self, incoming):
        g = self.geo
        z, x, y, c = g.me()
        for n, (j, k) in enumerate(self.far):
            slot = self.full.at[:, (x + g.X - j) % g.X, (y + g.Y - k) % g.Y, c] if incoming else self.full.at[:, x, y, c]
            yield remote(self.lane, self.plane + n, slot, slot, g.device(z, (x + j) % g.X, (y + k) % g.Y, c))

    def core_copy(self, own):
        z, x, y, c = self.geo.me()
        slot = self.full.at[:, :, :, c if own else 1 - c]
        return remote(self.lane, self.core, slot, slot, self.geo.device(z, x, y, 1 - c))

    def step(self, n):
        if n == 0:
            super().step(0)
        elif n == 1:
            self.z_whole().wait_recv()
            for copy in self.plane_copies(False):
                copy.start()
        elif n == 2:
            for copy in self.plane_copies(True):
                copy.wait_recv()
            self.core_copy(True).start()
        else:
            self.core_copy(False).wait_recv()

    def drain(self):
        self.z_whole().wait_send()
        for copy in self.plane_copies(False):
            copy.wait_send()
        self.core_copy(True).wait_send()


class PairStates:
    def __init__(self, states, p):
        self.states, self.p = states, p

    def step(self, n):
        self.states.step(n, self.p)


class ScatterDirect:
    def __init__(self, geo, lane):
        self.geo, self.lane = geo, lane
        self.far = [(i, j, k) for i in range(geo.Z) for j in range(geo.X) for k in range(geo.Y)][1:]
        self.core = lane.take()
        self.first = lane.take()

    @staticmethod
    def scratch(geo, rows, width):
        return [pltpu.VMEM((geo.Z, geo.X, geo.Y, rows, width), jnp.bfloat16),
                pltpu.VMEM((geo.Z * geo.X * geo.Y - 1, rows, width), jnp.bfloat16)]

    def bind(self, part, out, buffers):
        self.part, self.out = part, out
        self.rc, self.rz = buffers

    def core_copy(self):
        z, x, y, c = self.geo.me()
        return remote(self.lane, self.core, self.part.at[:, :, :, 1 - c], self.rc, self.geo.device(z, x, y, 1 - c))

    def copies(self):
        g = self.geo
        z, x, y, c = g.me()
        for n, (i, j, k) in enumerate(self.far):
            to = ((z + i) % g.Z, (x + j) % g.X, (y + k) % g.Y, c)
            yield remote(self.lane, self.first, self.part.at[to], self.rz.at[n], g.device(*to))

    def whole(self):
        z, x, y, c = self.geo.me()
        return remote(self.lane, self.first, self.rz, self.rz, self.geo.device((z + 1) % self.geo.Z, x, y, c))

    def step(self, n):
        g = self.geo
        z, x, y, c = g.me()
        if n == 0:
            self.core_copy().start()
        elif n == 1:
            self.core_copy().wait_recv()

            def add(i, _):
                total = self.part[i, :, :, c].astype(F32) + self.rc[i].astype(F32)
                self.part[i, :, :, c] = total.astype(BF)
                return 0
            lax.fori_loop(0, g.Z, add, 0)
            for copy in self.copies():
                copy.start()
        else:
            total = self.part[z, x, y, c].astype(F32)
            self.whole().wait_recv()
            for n in range(len(self.far)):
                total += self.rz[n].astype(F32)
            self.out[...] = total

    def drain(self):
        self.core_copy().wait_send()
        self.whole().wait_send()


DIRECT = ("rG",)
PLANE = ()
ORDERS = {"I3": (1, 1), "F0": (1, 1), "I1": (1, 1), "rF0": (0, 0), "rF3": (1, 1)}
PLAN = {
    "start": (("S", 0), ("I0", 0), ("I1", 0), ("I2", 0), ("I3", 0),),
    "first": (("O", 0), ("F0", 0), ("F1", 0), ("F2", 0), ("S", 1), ("I0", 1), ("I1", 1), ("S", 2), ("I2", 1),
        ("I0", 2), ("I3", 1), ("I1", 2), ("O", 1), ("S", 3), ("I2", 2), ("S", 4),),
    "norm0": (("I0", 3),),
    "proj.pre0": (("F0", 1), ("I3", 2), ("I0", 4),),
    "proj0": (("f0", 0),),
    "proj.pre1": (("F3", 0), ("I1", 3), ("O", 2), ("F1", 1), ("I2", 3), ("f0", 1), ("I1", 4),),
    "proj1": (("f1", 0), ("I2", 4), ("I3", 3), ("F0", 2), ("F2", 1),),
    "proj2": (("f2", 0), ("O", 3),),
    "proj.pre3": (("f1", 1), ("I3", 4),),
    "proj3": (("f3", 0), ("F3", 1),),
    "block0": (("f2", 1), ("O", 4),),
    "block1": (("f3", 1),),
    "block2": (("F1", 2),),
    "block3": (("f1", 2),),
    "att.pre0": (("f0", 2), ("F0", 3), ("f0", 3),),
    "att.pre1": (("f1", 3),),
    "att1": (("f2", 2), ("F2", 2),),
    "att.pre2": (("F0", 4), ("F3", 2), ("f3", 2), ("f2", 3),),
    "att.pre3": (("f3", 3),),
    "mid": (("F1", 3),),
    "feed0": (("rF0", 0), ("F1", 4), ("F2", 3),),
    "feed1": (("rF1", 0), ("rF0", 1), ("F2", 4), ("F3", 3),),
    "feed2": (("rF2", 0), ("rF1", 1), ("F3", 4),),
    "feed3": (("rF3", 0), ("rF2", 1),),
    "out": (("rF0", 2),),
    "st0": (("b0", 0),),
    "st1": (("b1", 0),),
    "st2": (("b2", 0), ("rF1", 2), ("rO", 0),),
    "st3": (("b3", 0), ("rF3", 1), ("b0", 1),),
    "q0": (("b1", 1), ("b2", 1), ("b3", 1), ("rO", 1),),
    "q1": (("rF2", 2), ("rF0", 3),),
    "q2": (("rF1", 3), ("b0", 2),),
    "q.end": (("b1", 2), ("b0", 3), ("rQ", 0),),
    "k0": (("b2", 2), ("rF0", 4),),
    "k.pre1": (("b1", 3),),
    "k1": (("b3", 2), ("rQ", 1), ("rF3", 2),),
    "k.pre2": (("b2", 3),),
    "k2": (("b3", 3), ("rF1", 4), ("rO", 2),),
    "k3": (("rF2", 3),),
    "k.end": (("rK", 0), ("rQ", 2),),
    "v0": (("rV0", 0), ("rK", 1), ("rF3", 3),),
    "v1": (("rV1", 0), ("rV0", 1), ("rQ", 3), ("rF2", 4),),
    "fb0": (("rV1", 1),),
    "fb1": (("rG", 0), ("rK", 2), ("rO", 3),),
    "end0": (("rF3", 4), ("rV0", 2), ("rQ", 4), ("rG", 1), ("rV1", 2), ("rK", 3), ("rV0", 3), ("rO", 4),),
    "end": (("rV1", 3), ("rG", 2), ("rK", 4), ("rV0", 4), ("rV1", 4),),
}


def layer_kernel(geo, lane, plan, *refs):
    (tokens_hbm, cot_hbm, feat_hbm, out_bias_hbm, down_bias_hbm, first_gain_hbm, first_shift_hbm, second_gain_hbm,
     second_shift_hbm, up_bias_hbm, wi_hbm, wo_hbm, wu_hbm, wd_hbm,
     result_hbm, tokens_grad_hbm, inp_hbm, out_hbm, up_hbm, down_hbm, vec_hbm,
     feat, out_bias_in, down_bias_in, first_gain_in, first_shift_in, second_gain_in, second_shift_in, up_bias_in,
     wi_in, wu_in, wd_in, inp_out, out_out, up_out, down_out, vec_out,
     tokens, cot, result, tokens_grad, small_own, small, wi_own, wi, wo_own, wo_all, wf_own, wf,
     normed, normed_t, mixed, pq, pk, den, attended, middle, n2_t,
     act, hg, vecs, grads, fa, ft, perm, part_q, part_k, part_v, part_o, part_f, part_g, up_parts, vec_sum) = refs[:73]
    rest = list(refs[73:])
    fwd, bwd, tasks = plan
    take = lambda n: [rest.pop(0) for _ in range(n)]
    fwd.bind(take(7))
    bwd.bind(take(7))
    scatter_buffers = {name: take(2 if type(task) is ScatterDirect else 4)
                       for name, task in tasks.items() if name[0] == "r"}
    lane.send, lane.recv = take(2)
    local_sem = rest.pop(0)
    tasks["S"].bind(small_own, small)
    tasks["O"].bind(wo_own, wo_all)
    tasks["rO"].bind(part_o, out_out, scatter_buffers["rO"])
    tasks["rG"].bind(part_g, vec_sum, scatter_buffers["rG"])
    wide = tokens.shape[-1]
    tasks["rQ"].bind(part_q, inp_out.at[:, pl.ds(0, wide)], scatter_buffers["rQ"])
    tasks["rK"].bind(part_k, inp_out.at[:, pl.ds(wide, wide)], scatter_buffers["rK"])
    for n in range(2):
        tasks[f"rV{n}"].bind(part_v.at[n], inp_out.at[:, pl.ds(2 * wide + 256 * n, 256)], scatter_buffers[f"rV{n}"])
    for p in range(PAIRS):
        tasks[f"I{p}"].bind(wi_own.at[p], wi.at[p])
    for t in range(wf.shape[0]):
        tasks[f"F{t}"].bind(wf_own.at[t], wf.at[t])
        tasks[f"rF{t}"].bind(part_f.at[t], up_parts.at[t], scatter_buffers[f"rF{t}"])
    n2 = normed
    D = tokens.shape[-1]
    L = tokens.shape[1]
    TILES = wf.shape[0]
    HALF = L // 2
    lead = (geo.Z, geo.X, geo.Y, 2)
    z, x, y, c = geo.me()
    place = (((z * geo.X + x) * geo.Y + y) * 2 + c) % 8

    def loop(n, body):
        def step(i, _):
            body(i)
            return 0
        lax.fori_loop(0, n, step, 0)

    def pairs(body, before, after):
        def step(p):
            if before:
                pump_at(p, [before + f"{n}" for n in range(PAIRS)])
            body(p, 0)
            body(p, 1)
            pump_at(p, [after + f"{n}" for n in range(PAIRS)])
        loop(PAIRS, step)

    def pump(point):
        for name, n in PLAN.get(point, ()):
            tasks[name].step(n)

    def pump_at(now, points):
        for when, point in enumerate(points):
            if point in PLAN:
                @pl.when(now == when)
                def _():
                    pump(point)

    def local(i, src, dst):
        return pltpu.make_async_copy(src, dst, local_sem.at[i])

    entry = ((feat_hbm, feat), (out_bias_hbm, out_bias_in), (down_bias_hbm, down_bias_in),
             (first_gain_hbm, first_gain_in), (first_shift_hbm, first_shift_in), (second_gain_hbm, second_gain_in),
             (second_shift_hbm, second_shift_in), (up_bias_hbm, up_bias_in), (wi_hbm, wi_in), (wo_hbm, wo_own),
             (wu_hbm, wu_in), (wd_hbm, wd_in))
    entry = [local(9 + i, a, b) for i, (a, b) in enumerate(entry)]
    for copy in entry[1:9] + entry[:1] + entry[9:]:
        copy.start()
    local(0, tokens_hbm, tokens).start()
    local(1, cot_hbm, cot).start()
    geo.greet()
    for copy in entry[1:9]:
        copy.wait()
    vec_sum[...] = jnp.zeros((16, 128), F32)
    for v, ref in enumerate((out_bias_in, down_bias_in, first_gain_in, first_shift_in, second_gain_in,
                             second_shift_in)):
        vec_sum[v, :16] = ref[...].astype(F32)
    up_bias_row = up_bias_in[...].astype(F32)
    for t in range(TILES):
        vec_sum[6 + t, :16] = up_bias_row[t * 16:(t + 1) * 16]
    small_own[...] = pltpu.roll(vec_sum[...], place * 16, 1).astype(BF)
    for p in range(PAIRS):
        wi_own[p] = jnp.concatenate([wi_in[:, k * D + p * 128: k * D + (p + 1) * 128] for k in range(3)], axis=1)
    geo.barrier()
    pump("start")
    for copy in entry[:1] + entry[9:]:
        copy.wait()
    source = lax.broadcasted_iota(jnp.int32, (512, 1), 0)
    target = (source % 64) // 16 * 128 + source // 64 * 16 + source % 16
    perm[...] = jnp.where(lax.broadcasted_iota(jnp.int32, (512, 512), 1) == target, 1.0, 0.0).astype(BF)
    stacked = jnp.concatenate([wu_in[:, g * 512:(g + 1) * 512] for g in range(TILES)], axis=0)
    stacked = dot(stacked, perm[...]).astype(BF)
    for t in range(TILES):
        for g in range(TILES):
            wf_own[t, :, g * 128:(g + 1) * 128] = stacked[g * 16:(g + 1) * 16, t * 128:(t + 1) * 128]
        wf_own[t, :, D:] = wd_in[t * 16:(t + 1) * 16]

    f = feat[...]
    zero = jnp.zeros((DH, M), BF)
    one = jnp.ones((DH, M), BF)
    fa[0] = jnp.concatenate([f, zero, -one, zero], axis=0)
    fa[1] = jnp.concatenate([zero, f, zero, -one], axis=0)
    ft[...] = jnp.concatenate([jnp.concatenate([f, zero], axis=1), jnp.concatenate([zero, f], axis=1),
                               jnp.concatenate([one, zero], axis=1), jnp.concatenate([zero, one], axis=1)], axis=0)
    low_lane = lax.broadcasted_iota(jnp.int32, (1, 128), 1) < DH
    m0f = jnp.where(low_lane, 1.0, 0.0)
    m0 = m0f.astype(BF)
    m1 = (1.0 - m0f).astype(BF)
    tri_r = lax.broadcasted_iota(jnp.int32, (HALF, HALF), 0)
    tri_c = lax.broadcasted_iota(jnp.int32, (HALF, HALF), 1)

    pump("first")

    flat = lambda v: v.reshape(-1, v.shape[-1])
    sums = jnp.sum(small[...].astype(F32).reshape(-1, 8, 16, 128), axis=1)
    vecs[...] = jnp.concatenate([sums[g] for g in range(D // 128)], axis=1)
    out_bias, down_bias = lambda: vecs[0:1], lambda: vecs[1:2]

    def norm_parts(rows):
        center = jnp.mean(rows, axis=-1, keepdims=True)
        centred = rows - center
        spread = jnp.mean(centred * centred, axis=-1, keepdims=True)
        inv = lax.rsqrt(spread + epsilon)
        return centred * inv, inv

    def first_norm(s):
        hat, _ = norm_parts(tokens[s].astype(F32))
        value = (hat * vecs[2:3] + vecs[3:4]).astype(BF)
        normed[s] = value
        normed_t[s] = value.T
    pump("vec")
    local(0, tokens_hbm, tokens).wait()
    first_norm(0)
    pump("norm0")
    first_norm(1)
    pump("norm1")

    def vx(s, p):
        v = mixed[s, p, :, 2 * 128:]
        ones = jnp.ones(v.shape, BF)
        return (jnp.concatenate([v * m0, ones * m0], axis=1), jnp.concatenate([v * m1, ones * m1], axis=1))

    def project(p, s):
        mixed[s, p] = dot(normed[s], flat(wi[p])).astype(BF)
        for part, target in ((0, pq), (1, pk)):
            rows = mixed[s, p, :, part * 128:(part + 1) * 128]
            wide = rows.astype(F32)
            lhs = jnp.concatenate([rows, (wide * wide * (0.5 * SCALE)).astype(BF)], axis=1)
            for h in range(2):
                power = dot(lhs, fa[h]) * (SCALE * LOG2E) - 0.5 * math.log2(M)
                target[s, 2 * p + h] = jnp.exp2(power).astype(BF)
        v = mixed[s, p, :, 2 * 128:]
        lhs = jnp.concatenate([v.T, jnp.ones((16, L), BF)], axis=0)
        r0 = dot(lhs, pk[s, 2 * p])
        r1 = dot(lhs, pk[s, 2 * p + 1])
        fwd.own[p, s] = jnp.concatenate([r0[:64], r1[64:128], r0[128:136], r1[136:]], axis=0).astype(BF)
    pairs(project, "proj.pre", "proj")

    def state_cols(total, p, s, h, copies):
        state = total[p, s, h * 64:(h + 1) * 64]
        extra = total[p, s, 128:144].astype(F32)[8 * h:8 * h + 8]
        zeros = jnp.zeros((DH, M), BF)
        if copies:
            extra = jnp.concatenate([extra] * 8, axis=0).astype(BF)
        else:
            extra = jnp.concatenate([extra, jnp.zeros((56, M), F32)], axis=0).astype(BF)
        parts = [state, zeros, extra, zeros] if h == 0 else [zeros, state, zeros, extra]
        return jnp.concatenate(parts, axis=0)

    lower = tri_r >= tri_c
    upper = tri_r <= tri_c

    def attend_block(p, s):
        v0, v1 = vx(s, p)
        lanes = pl.ds(pl.multiple_of(p * 128, 128), 128)
        for b in range(2):
            rows = slice(b * HALF, (b + 1) * HALF)
            scores = []
            for h in range(2):
                q = pq[s, 2 * p + h, rows]
                if b == 1:
                    scores.append(dot_nt(q, pk[s, 2 * p + h, :HALF]).astype(BF))
                scores.append(jnp.where(lower, dot_nt(q, pk[s, 2 * p + h, rows]), 0.0).astype(BF))
            rhs = jnp.concatenate([v0[:(b + 1) * HALF], v1[:(b + 1) * HALF]], axis=0)
            ext = dot(jnp.concatenate(scores, axis=1), rhs)
            result[s, rows, lanes] = ext[:, :128]
            den[s, rows, lanes] = ext[:, 128:]
    pairs(attend_block, None, "block")

    def attend_earlier(p, s):
        lanes = pl.ds(pl.multiple_of(p * 128, 128), 128)
        states = jnp.concatenate([state_cols(fwd.total, p, s, h, True) for h in range(2)], axis=1)
        ext = dot_nt(jnp.concatenate([pq[s, 2 * p], pq[s, 2 * p + 1]], axis=1), states)
        inv = 1.0 / (ext[:, 128:] + den[s, :, lanes])
        den[s, :, lanes] = inv
        attended[s, :, lanes] = ((ext[:, :128] + result[s, :, lanes]) * inv).astype(BF)
    pairs(attend_earlier, "att.pre", "att")
    pump("mid.pre")
    local(1, cot_hbm, cot).wait()

    def wo():
        return flat(wo_all[...])

    def to_middle(s):
        value = tokens[s].astype(F32) + dot(attended[s], wo()) + out_bias()
        middle[s] = value
        hat, _ = norm_parts(value)
        low = (hat * vecs[4:5] + vecs[5:6]).astype(BF)
        n2[s] = low
        n2_t[s] = low.T
        result[s] = value + down_bias()
        tokens_grad[s] = jnp.zeros((L, D), F32)
    to_middle(0)
    to_middle(1)
    pump("mid")
    grads[...] = jnp.zeros(grads.shape, F32)

    k0 = math.sqrt(2.0 / math.pi)

    def feed_tile(t):
        pump_at(t, [f"feed.pre{n}" for n in range(TILES)])
        bias = vecs[pl.ds(6 + t, 1)]
        wut = lambda: flat(wf[t, :, :, :, :, :, :D])
        wdt = lambda: flat(wf[t, :, :, :, :, :, D:])

        def seq(s):
            for b in range(2):
                rows = slice(b * HALF, (b + 1) * HALF)
                u = (dot(n2[s, rows], wut()) + bias).astype(BF)
                uu = u * u
                th = jnp.tanh(u * (BF(k0) + BF(k0 * 0.044715) * uu))
                half = BF(0.5) + BF(0.5) * th
                a = u * half
                act[s, rows] = a
                slope = half + a * (BF(1.0) - half) * (BF(2.0 * k0) + BF(6.0 * 0.044715 * k0) * uu)
                back = dot_nt(cot[s, rows], wdt()) * slope.astype(F32)
                grads[pl.ds(6 + t, 1)] += jnp.sum(back, axis=0, keepdims=True)
                low = back.astype(BF)
                hg[s, rows] = low
                result[s, rows] += dot(a, wdt())
                tokens_grad[s, rows] += dot_nt(low, wut())
        seq(0)
        seq(1)
        dwd = dot(act[0].T, cot[0]) + dot(act[1].T, cot[1])
        part_f[t, :, :, :, :, :, D:] = dwd.astype(BF).reshape(lead + (-1, D))
        dwu = dot(n2_t[0], hg[0]) + dot(n2_t[1], hg[1])
        part_f[t, :, :, :, :, :, :D] = dwu.astype(BF).reshape(lead + (-1, 512))
        pump_at(t, [f"feed{n}" for n in range(TILES)])
    loop(TILES, feed_tile)
    local(2, result, result_hbm).start()

    ones_block = jnp.concatenate([jnp.concatenate([jnp.ones((64, 64), F32), jnp.zeros((64, 64), F32)], axis=1),
                                  jnp.concatenate([jnp.zeros((64, 64), F32), jnp.ones((64, 64), F32)], axis=1)],
                                 axis=0).astype(BF)
    ones_two = jnp.concatenate([ones_block, ones_block], axis=0)
    lane_id = lax.broadcasted_iota(jnp.int32, (1, 128), 1)
    hi_lane = jnp.where((lane_id % DH) == 0, 1.0, 0.0)
    lo_lane = jnp.where((lane_id % DH) == 1, 1.0, 0.0)

    def norm_back(rows, dy, gain):
        hat, inv = norm_parts(rows)
        dg = dy * gain
        m_a = jnp.mean(dg, axis=-1, keepdims=True)
        m_b = jnp.mean(dg * hat, axis=-1, keepdims=True)
        return (inv * (dg - m_a - hat * m_b), jnp.sum(dy * hat, axis=0, keepdims=True),
                jnp.sum(dy, axis=0, keepdims=True))

    def out_back(s):
        dx, dgain, dshift = norm_back(middle[s], tokens_grad[s], vecs[4:5])
        up = cot[s].astype(F32)
        mg = up + dx
        middle[s] = mg
        low = mg.astype(BF)
        act[s] = low
        grads[0:1] += jnp.sum(mg, axis=0, keepdims=True)
        grads[1:2] += jnp.sum(up, axis=0, keepdims=True)
        grads[4:5] += dgain
        grads[5:6] += dshift
        ag = dot_nt(low, wo())
        inv = den[s]
        ng = ag * inv
        prod = ng * attended[s].astype(F32)
        n2[s] = ng.astype(BF)
        for p in range(PAIRS):
            cols = slice(p * 128, (p + 1) * 128)
            pr = prod[:, cols]
            hi = pr.astype(BF)
            lo = (pr - hi.astype(F32)).astype(BF)
            dgr = -dot(jnp.concatenate([hi, lo], axis=1), ones_two)
            dhi = dgr.astype(BF).astype(F32)
            dlo = dgr - dhi
            hg[s, :, cols] = (dhi * hi_lane + dlo * lo_lane).astype(BF)
    out_back(0)
    out_back(1)
    dwo = dot(attended[0].T, act[0]) + dot(attended[1].T, act[1])
    part_o[...] = dwo.astype(BF).reshape(lead + (-1, D))
    pump("out")

    def ngx(s, p):
        lanes = pl.ds(pl.multiple_of(p * 128, 128), 128)
        return jnp.concatenate([n2[s, :, lanes], hg[s, :, lanes]], axis=1)

    def state_back(p):
        def seq(s):
            lhs = ngx(s, p).T
            r0 = dot(lhs, pq[s, 2 * p])
            r1 = dot(lhs, pq[s, 2 * p + 1])
            bwd.own[p, s] = jnp.concatenate([r0[:64], r1[64:128], r0[128:136], r1[192:200]], axis=0).astype(BF)
        seq(0)
        seq(1)
        pump_at(p, [f"st{n}" for n in range(PAIRS)])
    loop(PAIRS, state_back)

    lo, hi = slice(0, HALF), slice(HALF, L)

    def masked(keep, value):
        return jnp.where(keep, value, 0.0).astype(BF)

    def through_features(s, p, part, logs):
        through = dot_nt(jnp.concatenate(logs, axis=1), ft[...])
        cols = slice(part * 128, (part + 1) * 128)
        rows = mixed[s, p, :, cols].astype(F32)
        mixed[s, p, :, cols] = (SCALE * through[:, :128] - SCALE * SCALE * through[:, 128:] * rows).astype(BF)

    def input_part(part, chosen):
        cols = slice(part * 128, (part + 1) * 128)
        total = sum(dot(normed_t[s], jnp.concatenate([mixed[s, p, :, cols] for p in chosen], axis=1))
                    for s in range(2))
        return total.astype(BF).reshape(lead + (-1, 128 * len(chosen)))

    def query_back(p, s):
        x = ngx(s, p)
        logs = []
        for h, v in enumerate(vx(s, p)):
            q, k = pq[s, 2 * p + h], pk[s, 2 * p + h]
            sx = state_cols(fwd.total, p, s, h, True)
            g00 = masked(lower, dot_nt(x[lo], v[lo]))
            g10 = dot_nt(x[hi], v[lo]).astype(BF)
            g11 = masked(lower, dot_nt(x[hi], v[hi]))
            qg0 = dot(jnp.concatenate([g00, x[lo]], axis=1), jnp.concatenate([k[lo], sx], axis=0))
            qg1 = dot(jnp.concatenate([g10, g11, x[hi]], axis=1), jnp.concatenate([k, sx], axis=0))
            logs.append(jnp.concatenate([qg0, qg1], axis=0).astype(BF) * q)
        through_features(s, p, 0, logs)
    pairs(query_back, None, "q")
    part_q[...] = input_part(0, range(PAIRS))
    pump("q.end")

    def key_back(p, s):
        x = ngx(s, p)
        logs = []
        for h, v in enumerate(vx(s, p)):
            q, k = pq[s, 2 * p + h], pk[s, 2 * p + h]
            sg = state_cols(bwd.total, p, s, h, False)
            t00 = masked(upper, dot_nt(v[lo], x[lo]))
            t01 = dot_nt(v[lo], x[hi]).astype(BF)
            t11 = masked(upper, dot_nt(v[hi], x[hi]))
            kg0 = dot(jnp.concatenate([t00, t01, v[lo]], axis=1), jnp.concatenate([q, sg], axis=0))
            kg1 = dot(jnp.concatenate([t11, v[hi]], axis=1), jnp.concatenate([q[hi], sg], axis=0))
            logs.append(jnp.concatenate([kg0, kg1], axis=0).astype(BF) * k)
        through_features(s, p, 1, logs)
    pairs(key_back, "k.pre", "k")
    part_k[...] = input_part(1, range(PAIRS))
    pump("k.end")

    def value_back(p, s):
        lanes = pl.ds(pl.multiple_of(p * 128, 128), 128)
        ng = n2[s, :, lanes]
        parts = []
        for h in range(2):
            q, k = pq[s, 2 * p + h], pk[s, 2 * p + h]
            parts.append((masked(upper, dot_nt(k[lo], q[lo])), dot_nt(k[lo], q[hi]).astype(BF),
                          masked(upper, dot_nt(k[hi], q[hi]))))
        n0, n1 = ng * m0, ng * m1
        vg0 = dot(jnp.concatenate([parts[0][0], parts[0][1], parts[1][0], parts[1][1]], axis=1),
                  jnp.concatenate([n0, n1], axis=0))
        vg1 = dot(jnp.concatenate([parts[0][2], parts[1][2]], axis=1), jnp.concatenate([n0[hi], n1[hi]], axis=0))
        zeros = jnp.zeros((DH, M), BF)
        sgt = jnp.concatenate([jnp.concatenate([bwd.total[p, s, :64], zeros], axis=0),
                               jnp.concatenate([zeros, bwd.total[p, s, 64:128]], axis=0)], axis=1)
        vg = jnp.concatenate([vg0, vg1], axis=0)
        vg += dot_nt(jnp.concatenate([pk[s, 2 * p], pk[s, 2 * p + 1]], axis=1), sgt)
        mixed[s, p, :, 256:] = vg.astype(BF)
    for n in range(2):
        def step(i):
            value_back(2 * n + i, 0)
            value_back(2 * n + i, 1)
        loop(2, step)
        part_v[n] = input_part(2, range(2 * n, 2 * n + 2))
        pump(f"v{n}")

    def normed_back(s):
        for b in range(2):
            rows = slice(b * HALF, (b + 1) * HALF)
            back = dot_nt(mixed[s, 0, rows], flat(wi[0]))
            for p in range(1, PAIRS):
                back += dot_nt(mixed[s, p, rows], flat(wi[p]))
            tokens_grad[s, rows] = back
    normed_back(0)
    pump("nb0")
    normed_back(1)
    pump("nb1")

    def first_back(s):
        dx, dgain, dshift = norm_back(tokens[s].astype(F32), tokens_grad[s], vecs[2:3])
        tokens_grad[s] = middle[s] + dx
        grads[2:3] += dgain
        grads[3:4] += dshift
    first_back(0)
    pump("fb0")
    first_back(1)
    for g in range(D // 128):
        tile = grads[:, g * 128:(g + 1) * 128].astype(BF)
        for k in range(8):
            chip, core = (8 * g + k) // 2, k % 2
            part_g[chip // (geo.X * geo.Y), chip // geo.Y % geo.X, chip % geo.Y, core] = tile
    local(3, tokens_grad, tokens_grad_hbm).start()
    pump("fb1")
    pump("end0")
    local(5, out_out, out_hbm).start()
    stacked = jnp.concatenate([jnp.concatenate([up_parts[t, :, g * 128:(g + 1) * 128] for t in range(TILES)], axis=1)
                               for g in range(TILES)], axis=0)
    high = stacked.astype(BF)
    low = (stacked - high.astype(F32)).astype(BF)
    stacked = dot_nt(high, perm[...]) + dot_nt(low, perm[...])
    for g in range(TILES):
        up_out[:, g * 512:(g + 1) * 512] = stacked[g * 16:(g + 1) * 16]
    for t in range(TILES):
        down_out[t * 16:(t + 1) * 16] = up_parts[t, :, D:]
    local(6, up_out, up_hbm).start()
    local(7, down_out, down_hbm).start()
    late = {name for name, n in PLAN["end"]}
    drains = [fwd, bwd] + [task for name, task in tasks.items() if name not in late and hasattr(task, "drain")]
    for task in drains:
        task.drain()
    pump("end")
    vec_out[...] = pltpu.roll(vec_sum[...], lax.rem(8 - place, 8) * 16, 1)
    local(8, vec_out, vec_hbm).start()
    local(4, inp_out, inp_hbm).start()
    for i, (a, b) in enumerate(((result, result_hbm), (tokens_grad, tokens_grad_hbm), (inp_out, inp_hbm),
                                (out_out, out_hbm), (up_out, up_hbm), (down_out, down_hbm), (vec_out, vec_hbm))):
        local(2 + i, a, b).wait()
    for name in sorted(late):
        if hasattr(tasks[name], "drain"):
            tasks[name].drain()


def finish_kernel(*refs):
    ins, outs = refs[:7], refs[7:20]
    held, (inp, out, up, down, vec), vec_rows = refs[20], refs[21:26], refs[26:33]
    in_sems, out_sems = refs[33:]
    waits = []

    def copy(src, dst, sems, i):
        return pltpu.make_async_copy(src, dst, sems.at[i])
    small_in = [copy(a, b, in_sems, i) for i, (a, b) in enumerate(zip(ins[2:], (inp, out, up, down, vec)))]
    for one in small_in[:1] + small_in[4:]:
        one.start()
    cuts = []
    for n in range(2):
        for m in range(ins[n].shape[0]):
            for k in range(2):
                rows = pl.ds(k * (ins[n].shape[1] // 2), ins[n].shape[1] // 2)
                slot = held.at[n, m, rows]
                cuts.append((copy(ins[n].at[m, rows], slot, in_sems, 5 + len(cuts)),
                             copy(slot, outs[n].at[m, rows], out_sems, 11 + len(cuts))))
    for first, _ in cuts[:4]:
        first.start()
    for one in small_in[1:4]:
        one.start()
    for first, _ in cuts[4:]:
        first.start()
    small_in[0].wait()
    small_in[4].wait()
    n = vec_rows[0].shape[-1]
    for v in range(6):
        vec_rows[v][...] = vec[v, :n]
    for t in range(up.shape[-1] // 512):
        vec_rows[6][pl.ds(t * n, n)] = vec[6 + t, :n]
    final = {2: inp, 4: vec_rows[0], 8: vec_rows[1], 9: vec_rows[2], 10: vec_rows[3], 11: vec_rows[4],
             12: vec_rows[5], 6: vec_rows[6]}
    for i, (place, ref) in enumerate(final.items()):
        waits.append(copy(ref, outs[place], out_sems, i))
        waits[-1].start()
    for first, second in cuts[:4]:
        first.wait()
        second.start()
        waits.append(second)
    for i, (one, ref, place) in enumerate(zip(small_in[1:4], (out, up, down), (3, 5, 7))):
        one.wait()
        waits.append(copy(ref, outs[place], out_sems, 8 + i))
        waits[-1].start()
    for first, second in cuts[4:]:
        first.wait()
        second.start()
        waits.append(second)
    for one in waits:
        one.wait()


def fused(geo, args):
    (tokens, feature_matrix, input_weight, output_weight, output_bias, up_weight, up_bias, down_weight,
     down_bias, first_gain, first_shift, second_gain, second_shift, cotangent) = args
    rows, D = input_weight.shape[0], tokens.shape[-1]
    L = tokens.shape[1]
    FF = up_weight.shape[1]
    tiles = FF // 512
    lane = Lane()
    fwd, bwd = States(geo, lane, True), States(geo, lane, False)
    names = ["S", "O"] + [f"I{p}" for p in range(PAIRS)] + [f"F{t}" for t in range(tiles)]
    tasks = {name: GatherPlane(geo, lane) if name in PLANE else Gather(geo, lane, ORDERS.get(name, (0, 1)))
             for name in names}
    scatters = {"rO": D, "rQ": D, "rK": D, "rV0": 256, "rV1": 256, "rG": 128}
    scatters.update({f"rF{t}": 2 * D for t in range(tiles)})
    for name in scatters:
        tasks[name] = ScatterDirect(geo, lane) if name in DIRECT else Scatter(geo, lane, ORDERS.get(name, (0, 1)))
    for p in range(PAIRS):
        tasks[f"f{p}"], tasks[f"b{p}"] = PairStates(fwd, p), PairStates(bwd, p)
    plan = (fwd, bwd, tasks)
    lead = (geo.Z, geo.X, geo.Y, 2)
    V = pltpu.VMEM
    shape = jax.ShapeDtypeStruct
    outs = [shape(tokens.shape, F32), shape(tokens.shape, F32), shape(input_weight.shape, F32),
            shape((rows, D), F32), shape((rows, FF), F32), shape(down_weight.shape, F32), shape((rows, 128), F32)]
    arrays = (tokens, cotangent, feature_matrix, output_bias, down_bias, first_gain, first_shift, second_gain,
              second_shift, up_bias, input_weight, output_weight, up_weight, down_weight)
    scratch = [V(a.shape, BF) for a in arrays[2:11] + arrays[12:]] + [V(o.shape, F32) for o in outs[2:]]
    scratch += [
        V((2, L, D), BF), V((2, L, D), BF), V((2, L, D), F32), V((2, L, D), F32),
        V((rows, 128), BF), V(lead + (rows, 128), BF), V((PAIRS, rows, 384), BF), V((PAIRS,) + lead + (rows, 384), BF),
        V((rows, D), BF), V(lead + (rows, D), BF), V((tiles, rows, 2 * D), BF),
        V((tiles,) + lead + (rows, 2 * D), BF),
        V((2, L, D), BF), V((2, D, L), BF), V((2, PAIRS, L, 384), BF), V((2, H, L, M), BF), V((2, H, L, M), BF),
        V((2, L, D), F32), V((2, L, D), BF), V((2, L, D), F32), V((2, D, L), BF),
        V((2, L, 512), BF), V((2, L, 512), BF), V((16, D), F32), V((16, D), F32),
        V((2, M, M), BF), V((M, 2 * M), BF), V((512, 512), BF),
        V(lead + (rows, D), BF), V(lead + (rows, D), BF), V((2,) + lead + (rows, 256), BF), V(lead + (rows, D), BF),
        V((tiles,) + lead + (rows, 2 * D), BF), V(lead + (rows, 128), BF), V((tiles, rows, 2 * D), F32), V((rows, 128), F32),
    ]
    scratch += States.scratch(geo) + States.scratch(geo)
    for name, width in scatters.items():
        scratch += type(tasks[name]).scratch(geo, rows, width)
    scratch += [pltpu.SemaphoreType.DMA((lane.count,)), pltpu.SemaphoreType.DMA((lane.count,)),
                pltpu.SemaphoreType.DMA((21,))]
    hbm = pl.BlockSpec(memory_space=pl.ANY)
    parts = pl.pallas_call(
        functools.partial(layer_kernel, geo, lane, plan),
        out_shape=outs, in_specs=[hbm] * 14, out_specs=[hbm] * 7, scratch_shapes=scratch,
        compiler_params=pltpu.CompilerParams(collective_id=0, has_side_effects=True, vmem_limit_bytes=60 << 20),
    )(*arrays)
    vector = shape((rows,), F32)
    final = [outs[0], outs[1], shape(input_weight.shape, F32), outs[3], vector, outs[4],
             shape(up_bias.shape, F32), outs[5]] + [vector] * 5
    return pl.pallas_call(
        finish_kernel,
        out_shape=final, in_specs=[hbm] * 7, out_specs=[hbm] * 13,
        scratch_shapes=[V((2,) + tokens.shape, F32)] + [V(o.shape, F32) for o in outs[2:]]
        + [V((rows,), F32)] * 6 + [V(up_bias.shape, F32)]
        + [pltpu.SemaphoreType.DMA((13,)), pltpu.SemaphoreType.DMA((19,))],
        compiler_params=pltpu.CompilerParams(vmem_limit_bytes=60 << 20),
    )(*parts)

def local(
    tokens,
    feature_matrix,
    input_weight,
    output_weight,
    output_bias,
    up_weight,
    up_bias,
    down_weight,
    down_bias,
    first_gain,
    first_shift,
    second_gain,
    second_shift,
    cotangent,
):
    params = (
        lax.all_gather(input_weight, ("dp", "seq"), axis=0, tiled=True),
        lax.all_gather(output_weight, ("dp", "seq"), axis=0, tiled=True),
        lax.all_gather(output_bias, ("dp", "seq"), axis=0, tiled=True),
        lax.all_gather(up_weight, ("dp", "seq"), axis=0, tiled=True),
        lax.all_gather(up_bias, ("dp", "seq"), axis=0, tiled=True),
        lax.all_gather(down_weight, ("dp", "seq"), axis=0, tiled=True),
        lax.all_gather(down_bias, ("dp", "seq"), axis=0, tiled=True),
        lax.all_gather(first_gain, ("dp", "seq"), axis=0, tiled=True),
        lax.all_gather(first_shift, ("dp", "seq"), axis=0, tiled=True),
        lax.all_gather(second_gain, ("dp", "seq"), axis=0, tiled=True),
        lax.all_gather(second_shift, ("dp", "seq"), axis=0, tiled=True),
    )
    micros = tokens.shape[0]
    fronts = []
    carries = []
    for micro_step in range(micros):
        pieces = front(tokens[micro_step], feature_matrix, params)
        fronts.append(pieces)
        carries.append(
            prefix(
                (pieces[8], pieces[9]),
                "seq",
                add_pair,
                (jnp.zeros_like(pieces[8]), jnp.zeros_like(pieces[9])),
            )
        )
    results = []
    for micro_step in range(micros):
        pieces = fronts[micro_step]
        running_prefix_state, norm_sum = carries[micro_step]
        output = attend(pieces[5], pieces[6], pieces[7], running_prefix_state, norm_sum)[0]
        attended, middle = upper(pieces[0], output, params)
        results.append(feed(middle, params))
    result = jnp.stack(results)
    back_params = (
        lax.all_gather(input_weight, ("dp", "seq"), axis=0, tiled=True),
        lax.all_gather(output_weight, ("dp", "seq"), axis=0, tiled=True),
        lax.all_gather(output_bias, ("dp", "seq"), axis=0, tiled=True),
        lax.all_gather(up_weight, ("dp", "seq"), axis=0, tiled=True),
        lax.all_gather(up_bias, ("dp", "seq"), axis=0, tiled=True),
        lax.all_gather(down_weight, ("dp", "seq"), axis=0, tiled=True),
        lax.all_gather(down_bias, ("dp", "seq"), axis=0, tiled=True),
        lax.all_gather(first_gain, ("dp", "seq"), axis=0, tiled=True),
        lax.all_gather(first_shift, ("dp", "seq"), axis=0, tiled=True),
        lax.all_gather(second_gain, ("dp", "seq"), axis=0, tiled=True),
        lax.all_gather(second_shift, ("dp", "seq"), axis=0, tiled=True),
    )
    stored_list = []
    later_list = []
    for micro_step in range(micros):
        stored = upper_back(
            tokens[micro_step],
            cotangent[micro_step].astype(jnp.float32),
            feature_matrix,
            back_params,
            carries[micro_step],
        )
        stored_list.append(stored)
        later_list.append(
            prefix_2(
                (stored["state_grad"], stored["sum_grad"]),
                "seq",
                add_pair,
                (jnp.zeros_like(stored["state_grad"]), jnp.zeros_like(stored["sum_grad"])),
            )
        )
    upper_names = ["out", "out_bias", "up", "up_bias", "down", "down_bias", "gain_two", "shift_two"]
    upper_totals = [stored_list[0][name] for name in upper_names]
    micro_step = 1
    upper_totals = [
        total + stored_list[micro_step][name] for total, name in zip(upper_totals, upper_names)
    ]
    token_grads = []
    lower_totals = None
    for micro_step in range(micros):
        stored = stored_list[micro_step]
        tokens_part, input_part, gain_part, shift_part = lower_back(
            stored, later_list[micro_step], feature_matrix, back_params
        )
        token_grads.append(tokens_part)
        lower_parts = (input_part, gain_part, shift_part)
        if micro_step == 0:
            lower_totals = lower_parts
        else:
            lower_totals = jax.tree.map(jnp.add, lower_totals, lower_parts)
    shares = (
        lax.psum_scatter(lower_totals[0], ("dp", "seq"), scatter_dimension=0, tiled=True),
        lax.psum_scatter(upper_totals[0], ("dp", "seq"), scatter_dimension=0, tiled=True),
        lax.psum_scatter(upper_totals[1], ("dp", "seq"), scatter_dimension=0, tiled=True),
        lax.psum_scatter(upper_totals[2], ("dp", "seq"), scatter_dimension=0, tiled=True),
        lax.psum_scatter(upper_totals[3], ("dp", "seq"), scatter_dimension=0, tiled=True),
        lax.psum_scatter(upper_totals[4], ("dp", "seq"), scatter_dimension=0, tiled=True),
        lax.psum_scatter(upper_totals[5], ("dp", "seq"), scatter_dimension=0, tiled=True),
        lax.psum_scatter(lower_totals[1], ("dp", "seq"), scatter_dimension=0, tiled=True),
        lax.psum_scatter(lower_totals[2], ("dp", "seq"), scatter_dimension=0, tiled=True),
        lax.psum_scatter(upper_totals[6], ("dp", "seq"), scatter_dimension=0, tiled=True),
        lax.psum_scatter(upper_totals[7], ("dp", "seq"), scatter_dimension=0, tiled=True),
    )
    return (
        result,
        jnp.stack(token_grads),
        shares[0],
        shares[1],
        shares[2],
        shares[3],
        shares[4],
        shares[5],
        shares[6],
        shares[7],
        shares[8],
        shares[9],
        shares[10],
    )


def solution(mesh):
    in_specs = (
        P("dp", "seq", None),
        P(),
        P(("dp", "seq"), None),
        P(("dp", "seq"), None),
        P(("dp", "seq")),
        P(("dp", "seq"), None),
        P(("dp", "seq")),
        P(("dp", "seq"), None),
        P(("dp", "seq")),
        P(("dp", "seq")),
        P(("dp", "seq")),
        P(("dp", "seq")),
        P(("dp", "seq")),
        P("dp", "seq", None),
    )
    out_specs = (
        P("dp", "seq", None),
        P("dp", "seq", None),
        P(("dp", "seq"), None),
        P(("dp", "seq"), None),
        P(("dp", "seq")),
        P(("dp", "seq"), None),
        P(("dp", "seq")),
        P(("dp", "seq"), None),
        P(("dp", "seq")),
        P(("dp", "seq")),
        P(("dp", "seq")),
        P(("dp", "seq")),
        P(("dp", "seq")),
    )
    geo = Geometry(mesh)
    rows = 512 // (mesh.shape["dp"] * mesh.shape["seq"])
    if rows == 16:
        def body(*args):
            return fused(geo, args)
    else:
        body = local
    return jax.shard_map(body, mesh=mesh, in_specs=in_specs, out_specs=out_specs, check_vma=False)
```

```python
import functools
import math

import jax
import jax.numpy as jnp
from jax import lax
from jax.sharding import PartitionSpec as P

H = 8
DH = 64

from jax.experimental import pallas as pl
from jax.experimental.pallas import tpu as pltpu

MESH = pl.DeviceIdType.MESH


class Geometry:
    def __init__(self, mesh):
        dp, seq = mesh.shape["dp"], mesh.shape["seq"]
        self.C = 2
        self.Y = seq // 2
        self.X = 1 << ((dp.bit_length() - 1) // 2)
        self.Z = dp // self.X

    def me(self):
        dp, seq = lax.axis_index("dp"), lax.axis_index("seq")
        return dp // self.X, dp % self.X, seq // 2, seq % 2

    def device(self, z, x, y, c):
        return (z * self.X + x, y * 2 + c)

    def greet(self):
        z, x, y, c = self.me()
        peers = [self.device(z, x, y, 1 - c)]
        peers += [self.device((z + i) % self.Z, (x + j) % self.X, (y + k) % self.Y, c)
                  for i in range(self.Z) for j in range(self.X) for k in range(self.Y)][1:]
        semaphore = pltpu.get_barrier_semaphore()
        for peer in peers:
            pl.semaphore_signal(semaphore, inc=1, device_id=peer, device_id_type=MESH)

    def barrier(self):
        pl.semaphore_wait(pltpu.get_barrier_semaphore(), self.Z * self.X * self.Y)


class Lane:
    def __init__(self):
        self.count = 0
        self.send = self.recv = None

    def take(self, n=1):
        first = self.count
        self.count += n
        return first


def remote(lane, index, src, dst, device):
    return pltpu.make_async_remote_copy(
        src_ref=src, dst_ref=dst, send_sem=lane.send.at[index], recv_sem=lane.recv.at[index],
        device_id=device, device_id_type=MESH)


class Gather:
    def __init__(self, geo, lane, orders):
        self.geo, self.lane, self.orders = geo, lane, orders
        self.zs = lane.take()
        self.second = lane.take(max(geo.X, geo.Y) - 1)
        self.third = lane.take(max(geo.X, geo.Y) - 1)
        self.core = lane.take()

    def bind(self, own, full):
        self.own, self.full = own, full

    def z_copies(self):
        g = self.geo
        z, x, y, c = g.me()
        for k in range(1, g.Z):
            yield remote(self.lane, self.zs, self.own, self.full.at[z, x, y, c], g.device((z + k) % g.Z, x, y, c))

    def z_whole(self):
        g = self.geo
        z, x, y, c = g.me()
        slots = self.full.at[pl.ds(0, g.Z - 1), x, y, c]
        return remote(self.lane, self.zs, slots, slots, g.device((z + 1) % g.Z, x, y, c))

    def axis_copies(self, phase, order, incoming):
        g = self.geo
        z, x, y, c = g.me()
        base = self.second if phase == 2 else self.third
        along_x = (phase == 2) == (order == 0)
        size = g.X if along_x else g.Y
        for k in range(1, size):
            if along_x:
                source = (x + g.X - k) % g.X if incoming else x
                device = g.device(z, (x + k) % g.X, y, c)
                slot = self.full.at[:, source, y, c] if phase == 2 else self.full.at[:, source, :, c]
            else:
                source = (y + g.Y - k) % g.Y if incoming else y
                device = g.device(z, x, (y + k) % g.Y, c)
                slot = self.full.at[:, x, source, c] if phase == 2 else self.full.at[:, :, source, c]
            yield remote(self.lane, base + k - 1, slot, slot, device)

    def both(self, action):
        c = self.geo.me()[3]
        if self.orders[0] == self.orders[1]:
            action(self.orders[0])
            return
        for core in range(2):
            @pl.when(c == core)
            def _():
                action(self.orders[core])

    def step(self, n):
        g = self.geo
        z, x, y, c = g.me()
        if n == 0:
            for copy in self.z_copies():
                copy.start()
            self.full[z, x, y, c] = self.own[...]
        elif n == 1:
            self.z_whole().wait_recv()
            self.both(lambda order: [copy.start() for copy in self.axis_copies(2, order, False)])
        elif n == 2:
            def go(order):
                for copy in self.axis_copies(2, order, True):
                    copy.wait_recv()
                for copy in self.axis_copies(3, order, False):
                    copy.start()
            self.both(go)
        elif n == 3:
            def go(order):
                for copy in self.axis_copies(3, order, True):
                    copy.wait_recv()
            self.both(go)
            slot = self.full.at[:, :, :, c]
            remote(self.lane, self.core, slot, slot, g.device(z, x, y, 1 - c)).start()
        else:
            slot = self.full.at[:, :, :, 1 - c]
            remote(self.lane, self.core, slot, slot, g.device(z, x, y, 1 - c)).wait_recv()

    def drain(self):
        g = self.geo
        z, x, y, c = g.me()
        self.z_whole().wait_send()

        def go(order):
            for phase in (2, 3):
                for copy in self.axis_copies(phase, order, False):
                    copy.wait_send()
        self.both(go)
        slot = self.full.at[:, :, :, c]
        remote(self.lane, self.core, slot, slot, g.device(z, x, y, 1 - c)).wait_send()


class Scatter:
    def __init__(self, geo, lane, orders):
        self.geo, self.lane, self.orders = geo, lane, orders
        self.core = lane.take()
        self.first = lane.take(max(geo.X, geo.Y) - 1)
        self.second = lane.take(max(geo.X, geo.Y) - 1)
        self.zs = lane.take()

    @staticmethod
    def scratch(geo, rows, width):
        wide = max(geo.X, geo.Y)
        kind = jnp.bfloat16
        return [
            pltpu.VMEM((geo.Z, geo.X, geo.Y, rows, width), kind),
            pltpu.VMEM((wide - 1, geo.Z, wide, rows, width), kind),
            pltpu.VMEM((wide - 1, geo.Z, rows, width), kind),
            pltpu.VMEM((geo.Z - 1, rows, width), kind),
        ]

    def bind(self, part, out, buffers):
        self.part, self.out = part, out
        self.rc, self.ra, self.rb, self.rz = buffers

    def both(self, action):
        c = self.geo.me()[3]
        if self.orders[0] == self.orders[1]:
            action(self.orders[0])
            return
        for core in range(2):
            @pl.when(c == core)
            def _():
                action(self.orders[core])

    def core_copy(self):
        z, x, y, c = self.geo.me()
        return remote(self.lane, self.core, self.part.at[:, :, :, 1 - c], self.rc,
                      self.geo.device(z, x, y, 1 - c))

    def axis_copies(self, phase, order):
        g = self.geo
        z, x, y, c = g.me()
        base = self.first if phase == 1 else self.second
        along_x = (phase == 1) == (order == 1)
        for k in range(1, g.X if along_x else g.Y):
            if along_x:
                far = (x + k) % g.X
                device = g.device(z, far, y, c)
                src = self.part.at[:, far, :, c] if phase == 1 else self.part.at[:, far, y, c]
                dst = self.ra.at[k - 1, :, pl.ds(0, g.Y)] if phase == 1 else self.rb.at[k - 1]
            else:
                far = (y + k) % g.Y
                device = g.device(z, x, far, c)
                src = self.part.at[:, :, far, c] if phase == 1 else self.part.at[:, x, far, c]
                dst = self.ra.at[k - 1, :, pl.ds(0, g.X)] if phase == 1 else self.rb.at[k - 1]
            yield remote(self.lane, base + k - 1, src, dst, device)

    def z_copies(self):
        g = self.geo
        z, x, y, c = g.me()
        for k in range(1, g.Z):
            far = (z + k) % g.Z
            yield remote(self.lane, self.zs, self.part.at[far, x, y, c], self.rz.at[k - 1], g.device(far, x, y, c))

    def z_whole(self):
        g = self.geo
        z, x, y, c = g.me()
        return remote(self.lane, self.zs, self.rz, self.rz, g.device((z + 1) % g.Z, x, y, c))

    def step(self, n):
        g = self.geo
        z, x, y, c = g.me()
        wide = lambda ref: ref.astype(jnp.float32)
        if n == 0:
            self.core_copy().start()
        elif n == 1:
            self.core_copy().wait_recv()

            def add(i, _):
                total = wide(self.part[i, :, :, c]) + wide(self.rc[i])
                self.part[i, :, :, c] = total.astype(jnp.bfloat16)
                return 0
            lax.fori_loop(0, g.Z, add, 0)
            self.both(lambda order: [copy.start() for copy in self.axis_copies(1, order)])
        elif n == 2:
            def go(order):
                copies = list(self.axis_copies(1, order))
                for copy in copies:
                    copy.wait_recv()
                count = len(copies)
                if order == 0:
                    def add(i, _):
                        total = wide(self.part[i, :, y, c])
                        for k in range(count):
                            total += wide(self.ra[k, i, : g.X])
                        self.part[i, :, y, c] = total.astype(jnp.bfloat16)
                        return 0
                else:
                    def add(i, _):
                        total = wide(self.part[i, x, :, c])
                        for k in range(count):
                            total += wide(self.ra[k, i, : g.Y])
                        self.part[i, x, :, c] = total.astype(jnp.bfloat16)
                        return 0
                lax.fori_loop(0, g.Z, add, 0)
                for copy in self.axis_copies(2, order):
                    copy.start()
            self.both(go)
        elif n == 3:
            def go(order):
                copies = list(self.axis_copies(2, order))
                for copy in copies:
                    copy.wait_recv()

                def add(i, _):
                    total = wide(self.part[i, x, y, c])
                    for k in range(len(copies)):
                        total += wide(self.rb[k, i])
                    self.part[i, x, y, c] = total.astype(jnp.bfloat16)
                    return 0
                lax.fori_loop(0, g.Z, add, 0)
            self.both(go)
            for copy in self.z_copies():
                copy.start()
        else:
            total = wide(self.part[z, x, y, c])
            self.z_whole().wait_recv()
            for k in range(g.Z - 1):
                total += wide(self.rz[k])
            self.out[...] = total

    def drain(self):
        self.core_copy().wait_send()

        def go(order):
            for phase in (1, 2):
                for copy in self.axis_copies(phase, order):
                    copy.wait_send()
        self.both(go)
        self.z_whole().wait_send()


epsilon = 1e-05
finest_precision = lax.Precision.HIGHEST


def prefix(array, axis, combine, identity):
    count, here = (lax.axis_size(axis), lax.axis_index(axis))
    everything = jax.tree.map(
        lambda part, kind: lax.all_gather(part.astype(kind), axis),
        array,
        (jnp.bfloat16, jnp.bfloat16),
    )
    start = jax.tree.map(
        lambda part, zero: jnp.broadcast_to(jnp.asarray(zero, part.dtype), part.shape),
        array,
        identity,
    )

    def hop(k, before):
        reached = k < here
        new = combine(
            before, jax.tree.map(lambda part, own: part[k].astype(own.dtype), everything, array)
        )
        return jax.tree.map(lambda a, b: jnp.where(reached, a, b), new, before)

    return lax.fori_loop(0, count, hop, start)


def prefix_2(array, axis, join, neutral):
    count = lax.axis_size(axis)
    place = lax.axis_index(axis)
    ahead = count - 1 - place
    gathered = jax.tree.map(
        lambda a, kind: lax.all_gather(a.astype(kind), axis),
        array,
        jax.tree.map(lambda a: jnp.bfloat16 if a.dtype == jnp.float32 else a.dtype, array),
    )
    state = jax.tree.map(lambda a, e: jnp.zeros_like(a) + jnp.asarray(e, a.dtype), array, neutral)

    def one(hop, state):
        source = count - 1 - hop
        return join(
            state,
            jax.tree.map(
                lambda a, own: lax.dynamic_index_in_dim(a, source, 0, False).astype(own.dtype),
                gathered,
                array,
            ),
        )

    return lax.fori_loop(0, ahead, one, state)


def layer_norm(value_rows, norm_gain, norm_shift):
    center = jnp.mean(value_rows, axis=-1, keepdims=True)
    centred = value_rows - center
    spread = jnp.mean(centred * centred, axis=-1, keepdims=True)
    return centred * lax.rsqrt(spread + epsilon) * norm_gain + norm_shift


def gelu_tanh(value_rows):
    return jax.nn.gelu(value_rows, approximate=True)


def add_pair(earlier, later_term):
    return (earlier[0] + later_term[0], earlier[1] + later_term[1])


def causal_mask(length):
    positions = jnp.arange(length)
    return (positions[:, None] >= positions[None, :]).astype(jnp.float32)


def favor_map(proj_low, matrix, feature_scale):
    raw_proj = jnp.einsum("rhd,dm->rhm", proj_low, matrix, preferred_element_type=jnp.float32)
    projection = proj_low.astype(jnp.float32)
    half_norm = (
        0.5
        * feature_scale
        * feature_scale
        * jnp.sum(projection * projection, axis=-1, keepdims=True)
    )
    return jnp.exp(feature_scale * raw_proj - half_norm) / math.sqrt(matrix.shape[1])


def favor_back(map_grad, favor_value, proj_low, matrix, feature_scale):
    log_grad = map_grad * favor_value
    raw_grad = (feature_scale * log_grad).astype(jnp.bfloat16)
    projection = proj_low.astype(jnp.float32)
    through = jnp.einsum("rhm,dm->rhd", raw_grad, matrix, preferred_element_type=jnp.float32)
    return (
        through
        - feature_scale * feature_scale * jnp.sum(log_grad, axis=-1, keepdims=True) * projection
    )


def front(token_block, matrix, params):
    inputs = token_block.astype(jnp.float32)
    length = inputs.shape[0]
    normed = layer_norm(
        inputs, params[7].astype(jnp.float32), params[8].astype(jnp.float32)
    ).astype(jnp.bfloat16)
    mixed = jnp.dot(normed, params[0], preferred_element_type=jnp.float32).astype(jnp.bfloat16)
    head_parts = mixed.reshape(length, 3, H, DH)
    feature_scale = DH ** (-0.25)
    query_features = favor_map(head_parts[:, 0], matrix, feature_scale)
    key_features = favor_map(head_parts[:, 1], matrix, feature_scale)
    query_reduced = query_features.astype(jnp.bfloat16)
    key_reduced = key_features.astype(jnp.bfloat16)
    value_rows = head_parts[:, 2]
    block_local_state = jnp.einsum(
        "nqo,nqi->qoi", key_reduced, value_rows, preferred_element_type=jnp.float32
    )
    local_sum = jnp.sum(key_reduced.astype(jnp.float32), axis=0)
    return (
        inputs,
        normed,
        head_parts,
        query_features,
        key_features,
        query_reduced,
        key_reduced,
        value_rows,
        block_local_state,
        local_sum,
    )


def attend(query_reduced, key_reduced, value_rows, running_prefix_state, norm_sum):
    causal = causal_mask(query_reduced.shape[0])
    scores = (
        jnp.einsum("ihm,jhm->hij", query_reduced, key_reduced, preferred_element_type=jnp.float32)
        * causal[None]
    )
    denominator = jnp.sum(scores, axis=-1).T + jnp.einsum(
        "ihm,hm->ih", query_reduced.astype(jnp.float32), norm_sum, precision=finest_precision
    )
    attention_numerator = jnp.einsum(
        "hij,jhd->ihd", scores.astype(jnp.bfloat16), value_rows, preferred_element_type=jnp.float32
    )
    attention_numerator = attention_numerator + jnp.einsum(
        "plq,lqu->plu",
        query_reduced,
        running_prefix_state.astype(jnp.bfloat16),
        preferred_element_type=jnp.float32,
    )
    return (attention_numerator / denominator[:, :, None], attention_numerator, denominator)


def upper(inputs, output, params):
    length = output.shape[0]
    attended = output.reshape(length, -1).astype(jnp.bfloat16)
    middle = (
        inputs
        + jnp.dot(attended, params[1], preferred_element_type=jnp.float32)
        + params[2].astype(jnp.float32)
    )
    return (attended, middle)


def feed(middle, params):
    normed_two = layer_norm(
        middle, params[9].astype(jnp.float32), params[10].astype(jnp.float32)
    ).astype(jnp.bfloat16)
    hidden = jnp.dot(normed_two, params[3], preferred_element_type=jnp.float32) + params[4].astype(
        jnp.float32
    )
    active = gelu_tanh(hidden).astype(jnp.bfloat16)
    return (
        middle
        + jnp.dot(active, params[5], preferred_element_type=jnp.float32)
        + params[6].astype(jnp.float32)
    )


def upper_back(token_block, upstream, matrix, params, block_carry):
    pieces = front(token_block, matrix, params)
    (
        inputs,
        normed,
        head_parts,
        query_features,
        key_features,
        query_reduced,
        key_reduced,
        value_rows,
        block_local_state,
        local_sum,
    ) = pieces
    running_prefix_state, norm_sum = block_carry
    output, attention_numerator, denominator = attend(
        query_reduced, key_reduced, value_rows, running_prefix_state, norm_sum
    )
    attended, middle = upper(inputs, output, params)
    normed_float, second_pull = jax.vjp(
        layer_norm, middle, params[9].astype(jnp.float32), params[10].astype(jnp.float32)
    )
    normed_two = normed_float.astype(jnp.bfloat16)
    hidden = jnp.dot(normed_two, params[3], preferred_element_type=jnp.float32) + params[4].astype(
        jnp.float32
    )
    active_float, gelu_pull = jax.vjp(gelu_tanh, hidden)
    active = active_float.astype(jnp.bfloat16)
    stored = {"front": pieces, "carry": block_carry}
    down_term = upstream.astype(jnp.bfloat16)
    stored["down"] = jnp.einsum("rf,rd->fd", active, down_term, preferred_element_type=jnp.float32)
    stored["down_bias"] = jnp.sum(upstream, axis=0)
    active_grad = jnp.einsum("rd,fd->rf", down_term, params[5], preferred_element_type=jnp.float32)
    (hidden_grad,) = gelu_pull(active_grad)
    up_term = hidden_grad.astype(jnp.bfloat16)
    stored["up"] = jnp.einsum("rd,rf->df", normed_two, up_term, preferred_element_type=jnp.float32)
    stored["up_bias"] = jnp.sum(hidden_grad, axis=0)
    normed_two_grad = jnp.einsum(
        "rf,df->rd", up_term, params[3], preferred_element_type=jnp.float32
    )
    middle_part, gain_two_grad, shift_two_grad = second_pull(normed_two_grad)
    stored["gain_two"] = gain_two_grad
    stored["shift_two"] = shift_two_grad
    middle_grad = upstream + middle_part
    stored["middle_grad"] = middle_grad
    out_term = middle_grad.astype(jnp.bfloat16)
    stored["out"] = jnp.einsum("re,rd->ed", attended, out_term, preferred_element_type=jnp.float32)
    stored["out_bias"] = jnp.sum(middle_grad, axis=0)
    attended_grad = jnp.einsum(
        "rd,ed->re", out_term, params[1], preferred_element_type=jnp.float32
    ).reshape(output.shape)
    numerator_grad = (attended_grad / denominator[:, :, None]).astype(jnp.bfloat16)
    denom_grad = -jnp.sum(attended_grad * attention_numerator, axis=-1) / (
        denominator * denominator
    )
    stored["numer_grad"] = numerator_grad
    stored["denom_grad"] = denom_grad
    stored["state_grad"] = jnp.einsum(
        "jfp,jfl->fpl", query_reduced, numerator_grad, preferred_element_type=jnp.float32
    )
    stored["sum_grad"] = jnp.einsum(
        "ih,ihm->hm", denom_grad, query_reduced.astype(jnp.float32), precision=finest_precision
    )
    return stored


def lower_back(stored, later_part, matrix, params):
    (
        inputs,
        normed,
        head_parts,
        query_features,
        key_features,
        query_reduced,
        key_reduced,
        value_rows,
        block_local_state,
        local_sum,
    ) = stored["front"]
    running_prefix_state, norm_sum = stored["carry"]
    state_later, sum_later = later_part
    numerator_grad = stored["numer_grad"]
    denom_grad = stored["denom_grad"]
    length = inputs.shape[0]
    causal = causal_mask(length)
    scores = (
        jnp.einsum("ihm,jhm->hij", query_reduced, key_reduced, preferred_element_type=jnp.float32)
        * causal[None]
    )
    scores_grad = jnp.einsum(
        "ihd,jhd->hij", numerator_grad, value_rows, preferred_element_type=jnp.float32
    )
    score_term = ((scores_grad + denom_grad.T[:, :, None]) * causal[None]).astype(jnp.bfloat16)
    later_reduced = state_later.astype(jnp.bfloat16)
    query_grad = jnp.einsum(
        "hij,jhm->ihm", score_term, key_reduced, preferred_element_type=jnp.float32
    )
    query_grad = query_grad + jnp.einsum(
        "gvw,vcw->gvc",
        numerator_grad,
        running_prefix_state.astype(jnp.bfloat16),
        preferred_element_type=jnp.float32,
    )
    query_grad = query_grad + denom_grad[:, :, None] * norm_sum[None]
    key_grad = jnp.einsum(
        "hij,ihm->jhm", score_term, query_reduced, preferred_element_type=jnp.float32
    )
    key_grad = key_grad + jnp.einsum(
        "prc,rqc->prq", value_rows, later_reduced, preferred_element_type=jnp.float32
    )
    key_grad = key_grad + sum_later[None]
    value_grad = jnp.einsum(
        "hij,ihd->jhd",
        scores.astype(jnp.bfloat16),
        numerator_grad,
        preferred_element_type=jnp.float32,
    )
    value_grad = value_grad + jnp.einsum(
        "qsa,saw->qsw", key_reduced, later_reduced, preferred_element_type=jnp.float32
    )
    feature_scale = DH ** (-0.25)
    query_proj = favor_back(query_grad, query_features, head_parts[:, 0], matrix, feature_scale)
    key_proj = favor_back(key_grad, key_features, head_parts[:, 1], matrix, feature_scale)
    mixed_grad = (
        jnp.stack([query_proj, key_proj, value_grad], axis=1)
        .reshape(length, -1)
        .astype(jnp.bfloat16)
    )
    input_part = jnp.einsum("rd,re->de", normed, mixed_grad, preferred_element_type=jnp.float32)
    normed_grad = jnp.einsum("re,de->rd", mixed_grad, params[0], preferred_element_type=jnp.float32)
    _, first_pull = jax.vjp(
        layer_norm, inputs, params[7].astype(jnp.float32), params[8].astype(jnp.float32)
    )
    inputs_part, gain_one_grad, shift_one_grad = first_pull(normed_grad)
    return (stored["middle_grad"] + inputs_part, input_part, gain_one_grad, shift_one_grad)


BF = jnp.bfloat16
F32 = jnp.float32
M = 256
SCALE = DH ** (-0.25)
LOG2E = math.log2(math.e)
PAIRS = H // 2
STATE_ROWS = 144


def dot(a, b):
    return jnp.dot(a, b, preferred_element_type=F32)


def dot_nt(a, b):
    return lax.dot_general(a, b, (((1,), (1,)), ((), ())), preferred_element_type=F32)


class States:
    def __init__(self, geo, lane, earlier):
        self.geo, self.lane, self.earlier = geo, lane, earlier
        self.per = geo.Y + 1
        self.first = lane.take(self.per * PAIRS)

    @staticmethod
    def scratch(geo):
        one = (PAIRS, STATE_ROWS, M)
        two = (PAIRS, 2, STATE_ROWS, M)
        return [pltpu.VMEM(two, BF), pltpu.VMEM(two, BF), pltpu.VMEM(one, BF),
                pltpu.VMEM((PAIRS, max(geo.Y - 1, 1), STATE_ROWS, M), BF), pltpu.VMEM(one, BF),
                pltpu.VMEM(one, BF), pltpu.VMEM(two, BF)]

    def bind(self, buffers):
        self.own, self.sibling, self.chip, self.chips, self.base, self.base_sibling, self.total = buffers

    def copies(self, p, phase):
        g = self.geo
        z, x, y, c = g.me()
        index = self.first + p * self.per
        other = g.device(z, x, y, 1 - c)
        if phase == 0:
            return [remote(self.lane, index, self.own.at[p], self.sibling.at[p], other)]
        if phase == 1:
            return [remote(self.lane, index + k, self.chip.at[p], self.chips.at[p, k - 1],
                           g.device(z, x, (y + k) % g.Y, c)) for k in range(1, g.Y)]
        return [remote(self.lane, index + g.Y, self.base.at[p], self.base_sibling.at[p], other)]

    def step(self, n, p):
        g = self.geo
        z, x, y, c = g.me()
        if n > 0:
            for copy in self.copies(p, n - 1):
                copy.wait_recv()
        if n == 1:
            self.chip[p] = (self.own[p, c].astype(F32) + self.sibling[p, c].astype(F32)).astype(BF)
        elif n == 2:
            total = jnp.zeros((STATE_ROWS, M), F32)
            for k in range(1, g.Y):
                source = (y + g.Y - k) % g.Y
                counts = source < y if self.earlier else source > y
                total += jnp.where(counts, 1.0, 0.0) * self.chips[p, k - 1].astype(F32)
            self.base[p] = total.astype(BF)
        elif n == 3:
            near = jnp.where(c == (1 if self.earlier else 0), 1.0, 0.0)
            self.total[p, c] = (self.base[p].astype(F32) + near * self.sibling[p, c].astype(F32)).astype(BF)
            self.total[p, 1 - c] = (self.base_sibling[p].astype(F32)
                                    + near * self.sibling[p, 1 - c].astype(F32)).astype(BF)
        if n < 3:
            for copy in self.copies(p, n):
                copy.start()

    def drain(self):
        for p in range(PAIRS):
            for phase in range(3):
                for copy in self.copies(p, phase):
                    copy.wait_send()


class GatherPlane(Gather):
    def __init__(self, geo, lane):
        self.geo, self.lane = geo, lane
        self.far = [(j, k) for j in range(geo.X) for k in range(geo.Y)][1:]
        self.zs, self.plane, self.core = lane.take(), lane.take(len(self.far)), lane.take()

    def plane_copies(self, incoming):
        g = self.geo
        z, x, y, c = g.me()
        for n, (j, k) in enumerate(self.far):
            slot = self.full.at[:, (x + g.X - j) % g.X, (y + g.Y - k) % g.Y, c] if incoming else self.full.at[:, x, y, c]
            yield remote(self.lane, self.plane + n, slot, slot, g.device(z, (x + j) % g.X, (y + k) % g.Y, c))

    def core_copy(self, own):
        z, x, y, c = self.geo.me()
        slot = self.full.at[:, :, :, c if own else 1 - c]
        return remote(self.lane, self.core, slot, slot, self.geo.device(z, x, y, 1 - c))

    def step(self, n):
        if n == 0:
            super().step(0)
        elif n == 1:
            self.z_whole().wait_recv()
            for copy in self.plane_copies(False):
                copy.start()
        elif n == 2:
            for copy in self.plane_copies(True):
                copy.wait_recv()
            self.core_copy(True).start()
        else:
            self.core_copy(False).wait_recv()

    def drain(self):
        self.z_whole().wait_send()
        for copy in self.plane_copies(False):
            copy.wait_send()
        self.core_copy(True).wait_send()


class PairStates:
    def __init__(self, states, p):
        self.states, self.p = states, p

    def step(self, n):
        self.states.step(n, self.p)


class ScatterDirect:
    def __init__(self, geo, lane):
        self.geo, self.lane = geo, lane
        self.far = [(i, j, k) for i in range(geo.Z) for j in range(geo.X) for k in range(geo.Y)][1:]
        self.core = lane.take()
        self.first = lane.take()

    @staticmethod
    def scratch(geo, rows, width):
        return [pltpu.VMEM((geo.Z, geo.X, geo.Y, rows, width), jnp.bfloat16),
                pltpu.VMEM((geo.Z * geo.X * geo.Y - 1, rows, width), jnp.bfloat16)]

    def bind(self, part, out, buffers):
        self.part, self.out = part, out
        self.rc, self.rz = buffers

    def core_copy(self):
        z, x, y, c = self.geo.me()
        return remote(self.lane, self.core, self.part.at[:, :, :, 1 - c], self.rc, self.geo.device(z, x, y, 1 - c))

    def copies(self):
        g = self.geo
        z, x, y, c = g.me()
        for n, (i, j, k) in enumerate(self.far):
            to = ((z + i) % g.Z, (x + j) % g.X, (y + k) % g.Y, c)
            yield remote(self.lane, self.first, self.part.at[to], self.rz.at[n], g.device(*to))

    def whole(self):
        z, x, y, c = self.geo.me()
        return remote(self.lane, self.first, self.rz, self.rz, self.geo.device((z + 1) % self.geo.Z, x, y, c))

    def step(self, n):
        g = self.geo
        z, x, y, c = g.me()
        if n == 0:
            self.core_copy().start()
        elif n == 1:
            self.core_copy().wait_recv()

            def add(i, _):
                total = self.part[i, :, :, c].astype(F32) + self.rc[i].astype(F32)
                self.part[i, :, :, c] = total.astype(BF)
                return 0
            lax.fori_loop(0, g.Z, add, 0)
            for copy in self.copies():
                copy.start()
        else:
            total = self.part[z, x, y, c].astype(F32)
            self.whole().wait_recv()
            for n in range(len(self.far)):
                total += self.rz[n].astype(F32)
            self.out[...] = total

    def drain(self):
        self.core_copy().wait_send()
        self.whole().wait_send()


DIRECT = ("rG", "rV1",)
PLANE = ()
ORDERS = {"I3": (1, 1), "F0": (1, 1), "I1": (1, 1), "rF3": (1, 1)}
PLAN = {
    "start": (("S", 0), ("I0", 0), ("I1", 0), ("I2", 0), ("I3", 0),),
    "first": (("O", 0), ("F0", 0), ("F1", 0), ("F2", 0), ("F3", 0), ("S", 1), ("I0", 1), ("I1", 1), ("S", 2),
        ("I2", 1), ("I0", 2), ("I3", 1), ("I1", 2), ("O", 1), ("S", 3), ("I2", 2), ("S", 4),),
    "norm0": (("I0", 3),),
    "proj.pre0": (("F0", 1), ("I3", 2), ("I0", 4),),
    "proj0": (("f0", 0),),
    "proj.pre1": (("I1", 3), ("O", 2), ("F1", 1), ("I2", 3), ("f0", 1), ("I1", 4),),
    "proj1": (("f1", 0), ("I3", 3), ("F0", 2), ("F2", 1),),
    "proj.pre2": (("I2", 4),),
    "proj2": (("f2", 0),),
    "proj.pre3": (("f1", 1), ("I3", 4),),
    "proj3": (("f3", 0), ("F3", 1),),
    "block0": (("f2", 1),),
    "block1": (("f3", 1),),
    "block3": (("f1", 2),),
    "att.pre0": (("O", 3), ("F1", 2), ("f0", 2), ("F0", 3), ("f1", 3), ("O", 4), ("F2", 2), ("f0", 3),),
    "att0": (("f2", 2),),
    "att.pre2": (("F0", 4), ("f3", 2), ("f2", 3),),
    "att2": (("F3", 2),),
    "att.pre3": (("f3", 3),),
    "mid": (("F1", 3),),
    "feed0": (("rF0", 0), ("F2", 3),),
    "feed.pre1": (("F1", 4),),
    "feed1": (("rF1", 0), ("rF0", 1), ("F2", 4), ("F3", 3),),
    "feed2": (("rF2", 0), ("rF1", 1), ("F3", 4),),
    "feed3": (("rF0", 2), ("rF2", 1),),
    "out": (("rF1", 2), ("rO", 0),),
    "st0": (("b0", 0), ("rF3", 0),),
    "st1": (("b1", 0),),
    "st2": (("b2", 0),),
    "st3": (("b3", 0), ("rO", 1),),
    "q0": (("b0", 1), ("b1", 1), ("b2", 1), ("rF3", 1),),
    "q2": (("b3", 1), ("rO", 2),),
    "q3": (("b0", 2), ("rF1", 3),),
    "q.end": (("rQ", 0), ("rF0", 3),),
    "k.pre0": (("rF2", 2), ("b1", 2), ("b0", 3),),
    "k0": (("b1", 3), ("b2", 2), ("rQ", 1),),
    "k1": (("b3", 2), ("b2", 3), ("rF3", 2),),
    "k2": (("b3", 3), ("rF2", 3), ("rO", 3),),
    "k3": (("rQ", 2),),
    "k.end": (("rK", 0),),
    "v0": (("rV0", 0), ("rK", 1), ("rF3", 3),),
    "v1": (("rV1", 0), ("rV0", 1), ("rQ", 3), ("rF2", 4), ("rO", 4),),
    "nb1": (("rK", 2), ("rF0", 4), ("rV1", 1),),
    "fb1": (("rG", 0), ("rF1", 4), ("rF3", 4),),
    "end": (("rV0", 2), ("rQ", 4), ("rG", 1), ("rK", 3), ("rV0", 3), ("rV1", 2), ("rG", 2), ("rK", 4), ("rV0", 4),),
}


def layer_kernel(geo, lane, plan, *refs):
    (tokens_hbm, cot_hbm, feat_hbm, out_bias_hbm, down_bias_hbm, first_gain_hbm, first_shift_hbm, second_gain_hbm,
     second_shift_hbm, up_bias_hbm, wi_hbm, wo_hbm, wu_hbm, wd_hbm,
     result_hbm, tokens_grad_hbm, inp_hbm, out_hbm, up_hbm, down_hbm, vec_hbm,
     feat, out_bias_in, down_bias_in, first_gain_in, first_shift_in, second_gain_in, second_shift_in, up_bias_in,
     wi_in, wu_in, wd_in, inp_out, out_out, up_out, down_out, vec_out,
     tokens, cot, result, tokens_grad, small_own, small, wi_own, wi, wo_own, wo_all, wf_own, wf,
     normed, normed_t, mixed, pq, pk, den, attended, middle, n2_t,
     act, hg, vecs, grads, fa, ft, perm, part_q, part_k, part_v, part_o, part_f, part_g, up_parts, vec_sum) = refs[:73]
    rest = list(refs[73:])
    fwd, bwd, tasks = plan
    take = lambda n: [rest.pop(0) for _ in range(n)]
    fwd.bind(take(7))
    bwd.bind(take(7))
    scatter_buffers = {name: take(2 if type(task) is ScatterDirect else 4)
                       for name, task in tasks.items() if name[0] == "r"}
    lane.send, lane.recv = take(2)
    local_sem = rest.pop(0)
    tasks["S"].bind(small_own, small)
    tasks["O"].bind(wo_own, wo_all)
    tasks["rO"].bind(part_o, out_out, scatter_buffers["rO"])
    tasks["rG"].bind(part_g, vec_sum, scatter_buffers["rG"])
    wide = tokens.shape[-1]
    tasks["rQ"].bind(part_q, inp_out.at[:, pl.ds(0, wide)], scatter_buffers["rQ"])
    tasks["rK"].bind(part_k, inp_out.at[:, pl.ds(wide, wide)], scatter_buffers["rK"])
    for n in range(2):
        tasks[f"rV{n}"].bind(part_v.at[n], inp_out.at[:, pl.ds(2 * wide + 256 * n, 256)], scatter_buffers[f"rV{n}"])
    for p in range(PAIRS):
        tasks[f"I{p}"].bind(wi_own.at[p], wi.at[p])
    for t in range(wf.shape[0]):
        tasks[f"F{t}"].bind(wf_own.at[t], wf.at[t])
        tasks[f"rF{t}"].bind(part_f.at[t], up_parts.at[t], scatter_buffers[f"rF{t}"])
    n2 = normed
    D = tokens.shape[-1]
    L = tokens.shape[1]
    TILES = wf.shape[0]
    HALF = L // 2
    lead = (geo.Z, geo.X, geo.Y, 2)
    z, x, y, c = geo.me()
    place = (((z * geo.X + x) * geo.Y + y) * 2 + c) % 8

    def loop(n, body):
        def step(i, _):
            body(i)
            return 0
        lax.fori_loop(0, n, step, 0)

    def pairs(body, before, after):
        def step(p):
            if before:
                pump_at(p, [before + f"{n}" for n in range(PAIRS)])
            body(p, 0)
            body(p, 1)
            pump_at(p, [after + f"{n}" for n in range(PAIRS)])
        loop(PAIRS, step)

    def pump(point):
        for name, n in PLAN.get(point, ()):
            tasks[name].step(n)

    def pump_at(now, points):
        for when, point in enumerate(points):
            if point in PLAN:
                @pl.when(now == when)
                def _():
                    pump(point)

    def local(i, src, dst):
        return pltpu.make_async_copy(src, dst, local_sem.at[i])

    entry = ((feat_hbm, feat), (out_bias_hbm, out_bias_in), (down_bias_hbm, down_bias_in),
             (first_gain_hbm, first_gain_in), (first_shift_hbm, first_shift_in), (second_gain_hbm, second_gain_in),
             (second_shift_hbm, second_shift_in), (up_bias_hbm, up_bias_in), (wi_hbm, wi_in), (wo_hbm, wo_own),
             (wu_hbm, wu_in), (wd_hbm, wd_in))
    entry = [local(9 + i, a, b) for i, (a, b) in enumerate(entry)]
    for copy in entry[1:9] + entry[:1] + entry[9:]:
        copy.start()
    local(0, tokens_hbm, tokens).start()
    local(1, cot_hbm, cot).start()
    geo.greet()
    for copy in entry[1:9]:
        copy.wait()
    vec_sum[...] = jnp.zeros((16, 128), F32)
    for v, ref in enumerate((out_bias_in, down_bias_in, first_gain_in, first_shift_in, second_gain_in,
                             second_shift_in)):
        vec_sum[v, :16] = ref[...].astype(F32)
    up_bias_row = up_bias_in[...].astype(F32)
    for t in range(TILES):
        vec_sum[6 + t, :16] = up_bias_row[t * 16:(t + 1) * 16]
    small_own[...] = pltpu.roll(vec_sum[...], place * 16, 1).astype(BF)
    for p in range(PAIRS):
        wi_own[p] = jnp.concatenate([wi_in[:, k * D + p * 128: k * D + (p + 1) * 128] for k in range(3)], axis=1)
    geo.barrier()
    pump("start")
    for copy in entry[:1] + entry[9:]:
        copy.wait()
    source = lax.broadcasted_iota(jnp.int32, (512, 1), 0)
    target = (source % 64) // 16 * 128 + source // 64 * 16 + source % 16
    perm[...] = jnp.where(lax.broadcasted_iota(jnp.int32, (512, 512), 1) == target, 1.0, 0.0).astype(BF)
    stacked = jnp.concatenate([wu_in[:, g * 512:(g + 1) * 512] for g in range(TILES)], axis=0)
    stacked = dot(stacked, perm[...]).astype(BF)
    for t in range(TILES):
        for g in range(TILES):
            wf_own[t, :, g * 128:(g + 1) * 128] = stacked[g * 16:(g + 1) * 16, t * 128:(t + 1) * 128]
        wf_own[t, :, D:] = wd_in[t * 16:(t + 1) * 16]

    f = feat[...]
    zero = jnp.zeros((DH, M), BF)
    one = jnp.ones((DH, M), BF)
    fa[0] = jnp.concatenate([f, zero, -one, zero], axis=0)
    fa[1] = jnp.concatenate([zero, f, zero, -one], axis=0)
    ft[...] = jnp.concatenate([jnp.concatenate([f, zero], axis=1), jnp.concatenate([zero, f], axis=1),
                               jnp.concatenate([one, zero], axis=1), jnp.concatenate([zero, one], axis=1)], axis=0)
    low_lane = lax.broadcasted_iota(jnp.int32, (1, 128), 1) < DH
    m0f = jnp.where(low_lane, 1.0, 0.0)
    m0 = m0f.astype(BF)
    m1 = (1.0 - m0f).astype(BF)
    tri_r = lax.broadcasted_iota(jnp.int32, (HALF, HALF), 0)
    tri_c = lax.broadcasted_iota(jnp.int32, (HALF, HALF), 1)

    pump("first")

    flat = lambda v: v.reshape(-1, v.shape[-1])
    sums = jnp.sum(small[...].astype(F32).reshape(-1, 8, 16, 128), axis=1)
    vecs[...] = jnp.concatenate([sums[g] for g in range(D // 128)], axis=1)
    out_bias, down_bias = lambda: vecs[0:1], lambda: vecs[1:2]

    def norm_parts(rows):
        center = jnp.mean(rows, axis=-1, keepdims=True)
        centred = rows - center
        spread = jnp.mean(centred * centred, axis=-1, keepdims=True)
        inv = lax.rsqrt(spread + epsilon)
        return centred * inv, inv

    def first_norm(s):
        hat, _ = norm_parts(tokens[s].astype(F32))
        value = (hat * vecs[2:3] + vecs[3:4]).astype(BF)
        normed[s] = value
        normed_t[s] = value.T
    pump("vec")
    local(0, tokens_hbm, tokens).wait()
    first_norm(0)
    pump("norm0")
    first_norm(1)
    pump("norm1")

    def vx(s, p):
        v = mixed[s, p, :, 2 * 128:]
        ones = jnp.ones(v.shape, BF)
        return (jnp.concatenate([v * m0, ones * m0], axis=1), jnp.concatenate([v * m1, ones * m1], axis=1))

    def project(p, s):
        mixed[s, p] = dot(normed[s], flat(wi[p])).astype(BF)
        for part, target in ((0, pq), (1, pk)):
            rows = mixed[s, p, :, part * 128:(part + 1) * 128]
            wide = rows.astype(F32)
            lhs = jnp.concatenate([rows, (wide * wide * (0.5 * SCALE)).astype(BF)], axis=1)
            for h in range(2):
                power = dot(lhs, fa[h]) * (SCALE * LOG2E) - 0.5 * math.log2(M)
                target[s, 2 * p + h] = jnp.exp2(power).astype(BF)
        v = mixed[s, p, :, 2 * 128:]
        lhs = jnp.concatenate([v.T, jnp.ones((16, L), BF)], axis=0)
        r0 = dot(lhs, pk[s, 2 * p])
        r1 = dot(lhs, pk[s, 2 * p + 1])
        fwd.own[p, s] = jnp.concatenate([r0[:64], r1[64:128], r0[128:136], r1[136:]], axis=0).astype(BF)
    pairs(project, "proj.pre", "proj")

    def state_cols(total, p, s, h, copies):
        state = total[p, s, h * 64:(h + 1) * 64]
        extra = total[p, s, 128:144].astype(F32)[8 * h:8 * h + 8]
        zeros = jnp.zeros((DH, M), BF)
        if copies:
            extra = jnp.concatenate([extra] * 8, axis=0).astype(BF)
        else:
            extra = jnp.concatenate([extra, jnp.zeros((56, M), F32)], axis=0).astype(BF)
        parts = [state, zeros, extra, zeros] if h == 0 else [zeros, state, zeros, extra]
        return jnp.concatenate(parts, axis=0)

    lower = tri_r >= tri_c
    upper = tri_r <= tri_c

    def attend_block(p, s):
        v0, v1 = vx(s, p)
        lanes = pl.ds(pl.multiple_of(p * 128, 128), 128)
        for b in range(2):
            rows = slice(b * HALF, (b + 1) * HALF)
            scores = []
            for h in range(2):
                q = pq[s, 2 * p + h, rows]
                if b == 1:
                    scores.append(dot_nt(q, pk[s, 2 * p + h, :HALF]).astype(BF))
                scores.append(jnp.where(lower, dot_nt(q, pk[s, 2 * p + h, rows]), 0.0).astype(BF))
            rhs = jnp.concatenate([v0[:(b + 1) * HALF], v1[:(b + 1) * HALF]], axis=0)
            ext = dot(jnp.concatenate(scores, axis=1), rhs)
            result[s, rows, lanes] = ext[:, :128]
            den[s, rows, lanes] = ext[:, 128:]
    pairs(attend_block, None, "block")

    def attend_earlier(p, s):
        lanes = pl.ds(pl.multiple_of(p * 128, 128), 128)
        states = jnp.concatenate([state_cols(fwd.total, p, s, h, True) for h in range(2)], axis=1)
        ext = dot_nt(jnp.concatenate([pq[s, 2 * p], pq[s, 2 * p + 1]], axis=1), states)
        inv = 1.0 / (ext[:, 128:] + den[s, :, lanes])
        den[s, :, lanes] = inv
        attended[s, :, lanes] = ((ext[:, :128] + result[s, :, lanes]) * inv).astype(BF)
    pairs(attend_earlier, "att.pre", "att")
    pump("mid.pre")
    local(1, cot_hbm, cot).wait()

    def wo():
        return flat(wo_all[...])

    def to_middle(s):
        value = tokens[s].astype(F32) + dot(attended[s], wo()) + out_bias()
        middle[s] = value
        hat, _ = norm_parts(value)
        low = (hat * vecs[4:5] + vecs[5:6]).astype(BF)
        n2[s] = low
        n2_t[s] = low.T
        result[s] = value + down_bias()
        tokens_grad[s] = jnp.zeros((L, D), F32)
    to_middle(0)
    to_middle(1)
    pump("mid")
    grads[...] = jnp.zeros(grads.shape, F32)

    k0 = math.sqrt(2.0 / math.pi)

    def feed_tile(t):
        pump_at(t, [f"feed.pre{n}" for n in range(TILES)])
        bias = vecs[pl.ds(6 + t, 1)]
        wut = lambda: flat(wf[t, :, :, :, :, :, :D])
        wdt = lambda: flat(wf[t, :, :, :, :, :, D:])

        def seq(s):
            for b in range(2):
                rows = slice(b * HALF, (b + 1) * HALF)
                u = (dot(n2[s, rows], wut()) + bias).astype(BF)
                uu = u * u
                th = jnp.tanh(u * (BF(k0) + BF(k0 * 0.044715) * uu))
                half = BF(0.5) + BF(0.5) * th
                a = u * half
                act[s, rows] = a
                slope = half + a * (BF(1.0) - half) * (BF(2.0 * k0) + BF(6.0 * 0.044715 * k0) * uu)
                back = dot_nt(cot[s, rows], wdt()) * slope.astype(F32)
                grads[pl.ds(6 + t, 1)] += jnp.sum(back, axis=0, keepdims=True)
                low = back.astype(BF)
                hg[s, rows] = low
                result[s, rows] += dot(a, wdt())
                tokens_grad[s, rows] += dot_nt(low, wut())
        seq(0)
        seq(1)
        dwd = dot(act[0].T, cot[0]) + dot(act[1].T, cot[1])
        part_f[t, :, :, :, :, :, D:] = dwd.astype(BF).reshape(lead + (-1, D))
        dwu = dot(n2_t[0], hg[0]) + dot(n2_t[1], hg[1])
        part_f[t, :, :, :, :, :, :D] = dwu.astype(BF).reshape(lead + (-1, 512))
        pump_at(t, [f"feed{n}" for n in range(TILES)])
    loop(TILES, feed_tile)
    local(2, result, result_hbm).start()

    ones_block = jnp.concatenate([jnp.concatenate([jnp.ones((64, 64), F32), jnp.zeros((64, 64), F32)], axis=1),
                                  jnp.concatenate([jnp.zeros((64, 64), F32), jnp.ones((64, 64), F32)], axis=1)],
                                 axis=0).astype(BF)
    ones_two = jnp.concatenate([ones_block, ones_block], axis=0)
    lane_id = lax.broadcasted_iota(jnp.int32, (1, 128), 1)
    hi_lane = jnp.where((lane_id % DH) == 0, 1.0, 0.0)
    lo_lane = jnp.where((lane_id % DH) == 1, 1.0, 0.0)

    def norm_back(rows, dy, gain):
        hat, inv = norm_parts(rows)
        dg = dy * gain
        m_a = jnp.mean(dg, axis=-1, keepdims=True)
        m_b = jnp.mean(dg * hat, axis=-1, keepdims=True)
        return (inv * (dg - m_a - hat * m_b), jnp.sum(dy * hat, axis=0, keepdims=True),
                jnp.sum(dy, axis=0, keepdims=True))

    def out_back(s):
        dx, dgain, dshift = norm_back(middle[s], tokens_grad[s], vecs[4:5])
        up = cot[s].astype(F32)
        mg = up + dx
        middle[s] = mg
        low = mg.astype(BF)
        act[s] = low
        grads[0:1] += jnp.sum(mg, axis=0, keepdims=True)
        grads[1:2] += jnp.sum(up, axis=0, keepdims=True)
        grads[4:5] += dgain
        grads[5:6] += dshift
        ag = dot_nt(low, wo())
        inv = den[s]
        ng = ag * inv
        prod = ng * attended[s].astype(F32)
        n2[s] = ng.astype(BF)
        for p in range(PAIRS):
            cols = slice(p * 128, (p + 1) * 128)
            pr = prod[:, cols]
            hi = pr.astype(BF)
            lo = (pr - hi.astype(F32)).astype(BF)
            dgr = -dot(jnp.concatenate([hi, lo], axis=1), ones_two)
            dhi = dgr.astype(BF).astype(F32)
            dlo = dgr - dhi
            hg[s, :, cols] = (dhi * hi_lane + dlo * lo_lane).astype(BF)
    out_back(0)
    out_back(1)
    dwo = dot(attended[0].T, act[0]) + dot(attended[1].T, act[1])
    part_o[...] = dwo.astype(BF).reshape(lead + (-1, D))
    pump("out")

    def ngx(s, p):
        lanes = pl.ds(pl.multiple_of(p * 128, 128), 128)
        return jnp.concatenate([n2[s, :, lanes], hg[s, :, lanes]], axis=1)

    def state_back(p):
        def seq(s):
            lhs = ngx(s, p).T
            r0 = dot(lhs, pq[s, 2 * p])
            r1 = dot(lhs, pq[s, 2 * p + 1])
            bwd.own[p, s] = jnp.concatenate([r0[:64], r1[64:128], r0[128:136], r1[192:200]], axis=0).astype(BF)
        seq(0)
        seq(1)
        pump_at(p, [f"st{n}" for n in range(PAIRS)])
    loop(PAIRS, state_back)

    lo, hi = slice(0, HALF), slice(HALF, L)

    def masked(keep, value):
        return jnp.where(keep, value, 0.0).astype(BF)

    def through_features(s, p, part, logs):
        through = dot_nt(jnp.concatenate(logs, axis=1), ft[...])
        cols = slice(part * 128, (part + 1) * 128)
        rows = mixed[s, p, :, cols].astype(F32)
        mixed[s, p, :, cols] = (SCALE * through[:, :128] - SCALE * SCALE * through[:, 128:] * rows).astype(BF)

    def input_part(part, chosen):
        cols = slice(part * 128, (part + 1) * 128)
        total = sum(dot(normed_t[s], jnp.concatenate([mixed[s, p, :, cols] for p in chosen], axis=1))
                    for s in range(2))
        return total.astype(BF).reshape(lead + (-1, 128 * len(chosen)))

    def query_back(p, s):
        x = ngx(s, p)
        logs = []
        for h, v in enumerate(vx(s, p)):
            q, k = pq[s, 2 * p + h], pk[s, 2 * p + h]
            sx = state_cols(fwd.total, p, s, h, True)
            g00 = masked(lower, dot_nt(x[lo], v[lo]))
            g10 = dot_nt(x[hi], v[lo]).astype(BF)
            g11 = masked(lower, dot_nt(x[hi], v[hi]))
            qg0 = dot(jnp.concatenate([g00, x[lo]], axis=1), jnp.concatenate([k[lo], sx], axis=0))
            qg1 = dot(jnp.concatenate([g10, g11, x[hi]], axis=1), jnp.concatenate([k, sx], axis=0))
            logs.append(jnp.concatenate([qg0, qg1], axis=0).astype(BF) * q)
        through_features(s, p, 0, logs)
    pairs(query_back, None, "q")
    part_q[...] = input_part(0, range(PAIRS))
    pump("q.end")

    def key_back(p, s):
        x = ngx(s, p)
        logs = []
        for h, v in enumerate(vx(s, p)):
            q, k = pq[s, 2 * p + h], pk[s, 2 * p + h]
            sg = state_cols(bwd.total, p, s, h, False)
            t00 = masked(upper, dot_nt(v[lo], x[lo]))
            t01 = dot_nt(v[lo], x[hi]).astype(BF)
            t11 = masked(upper, dot_nt(v[hi], x[hi]))
            kg0 = dot(jnp.concatenate([t00, t01, v[lo]], axis=1), jnp.concatenate([q, sg], axis=0))
            kg1 = dot(jnp.concatenate([t11, v[hi]], axis=1), jnp.concatenate([q[hi], sg], axis=0))
            logs.append(jnp.concatenate([kg0, kg1], axis=0).astype(BF) * k)
        through_features(s, p, 1, logs)
    pairs(key_back, "k.pre", "k")
    part_k[...] = input_part(1, range(PAIRS))
    pump("k.end")

    def value_back(p, s):
        lanes = pl.ds(pl.multiple_of(p * 128, 128), 128)
        ng = n2[s, :, lanes]
        parts = []
        for h in range(2):
            q, k = pq[s, 2 * p + h], pk[s, 2 * p + h]
            parts.append((masked(upper, dot_nt(k[lo], q[lo])), dot_nt(k[lo], q[hi]).astype(BF),
                          masked(upper, dot_nt(k[hi], q[hi]))))
        n0, n1 = ng * m0, ng * m1
        vg0 = dot(jnp.concatenate([parts[0][0], parts[0][1], parts[1][0], parts[1][1]], axis=1),
                  jnp.concatenate([n0, n1], axis=0))
        vg1 = dot(jnp.concatenate([parts[0][2], parts[1][2]], axis=1), jnp.concatenate([n0[hi], n1[hi]], axis=0))
        zeros = jnp.zeros((DH, M), BF)
        sgt = jnp.concatenate([jnp.concatenate([bwd.total[p, s, :64], zeros], axis=0),
                               jnp.concatenate([zeros, bwd.total[p, s, 64:128]], axis=0)], axis=1)
        vg = jnp.concatenate([vg0, vg1], axis=0)
        vg += dot_nt(jnp.concatenate([pk[s, 2 * p], pk[s, 2 * p + 1]], axis=1), sgt)
        mixed[s, p, :, 256:] = vg.astype(BF)
    for n in range(2):
        def step(i):
            value_back(2 * n + i, 0)
            value_back(2 * n + i, 1)
        loop(2, step)
        part_v[n] = input_part(2, range(2 * n, 2 * n + 2))
        pump(f"v{n}")

    def normed_back(s):
        for b in range(2):
            rows = slice(b * HALF, (b + 1) * HALF)
            back = dot_nt(mixed[s, 0, rows], flat(wi[0]))
            for p in range(1, PAIRS):
                back += dot_nt(mixed[s, p, rows], flat(wi[p]))
            tokens_grad[s, rows] = back
    normed_back(0)
    pump("nb0")
    normed_back(1)
    pump("nb1")

    def first_back(s):
        dx, dgain, dshift = norm_back(tokens[s].astype(F32), tokens_grad[s], vecs[2:3])
        tokens_grad[s] = middle[s] + dx
        grads[2:3] += dgain
        grads[3:4] += dshift
    first_back(0)
    pump("fb0")
    first_back(1)
    for g in range(D // 128):
        tile = grads[:, g * 128:(g + 1) * 128].astype(BF)
        for k in range(8):
            chip, core = (8 * g + k) // 2, k % 2
            part_g[chip // (geo.X * geo.Y), chip // geo.Y % geo.X, chip % geo.Y, core] = tile
    local(3, tokens_grad, tokens_grad_hbm).start()
    pump("fb1")
    pump("end0")
    local(5, out_out, out_hbm).start()
    stacked = jnp.concatenate([jnp.concatenate([up_parts[t, :, g * 128:(g + 1) * 128] for t in range(TILES)], axis=1)
                               for g in range(TILES)], axis=0)
    high = stacked.astype(BF)
    low = (stacked - high.astype(F32)).astype(BF)
    stacked = dot_nt(high, perm[...]) + dot_nt(low, perm[...])
    for g in range(TILES):
        up_out[:, g * 512:(g + 1) * 512] = stacked[g * 16:(g + 1) * 16]
    for t in range(TILES):
        down_out[t * 16:(t + 1) * 16] = up_parts[t, :, D:]
    local(6, up_out, up_hbm).start()
    local(7, down_out, down_hbm).start()
    late = {name for name, n in PLAN["end"]}
    drains = [fwd, bwd] + [task for name, task in tasks.items() if name not in late and hasattr(task, "drain")]
    for task in drains:
        task.drain()
    pump("end")
    vec_out[...] = pltpu.roll(vec_sum[...], lax.rem(8 - place, 8) * 16, 1)
    local(8, vec_out, vec_hbm).start()
    local(4, inp_out, inp_hbm).start()
    for i, (a, b) in enumerate(((result, result_hbm), (tokens_grad, tokens_grad_hbm), (inp_out, inp_hbm),
                                (out_out, out_hbm), (up_out, up_hbm), (down_out, down_hbm), (vec_out, vec_hbm))):
        local(2 + i, a, b).wait()
    for name in sorted(late):
        if hasattr(tasks[name], "drain"):
            tasks[name].drain()


def finish_kernel(*refs):
    ins, outs = refs[:7], refs[7:20]
    held, (inp, out, up, down, vec), vec_rows = refs[20], refs[21:26], refs[26:33]
    in_sems, out_sems = refs[33:]
    waits = []

    def copy(src, dst, sems, i):
        return pltpu.make_async_copy(src, dst, sems.at[i])
    small_in = [copy(a, b, in_sems, i) for i, (a, b) in enumerate(zip(ins[2:], (inp, out, up, down, vec)))]
    for one in small_in[:1] + small_in[4:]:
        one.start()
    cuts = []
    for n in range(2):
        for m in range(ins[n].shape[0]):
            for k in range(2):
                rows = pl.ds(k * (ins[n].shape[1] // 2), ins[n].shape[1] // 2)
                slot = held.at[n, m, rows]
                cuts.append((copy(ins[n].at[m, rows], slot, in_sems, 5 + len(cuts)),
                             copy(slot, outs[n].at[m, rows], out_sems, 11 + len(cuts))))
    for first, _ in cuts[:4]:
        first.start()
    for one in small_in[1:4]:
        one.start()
    for first, _ in cuts[4:]:
        first.start()
    small_in[0].wait()
    small_in[4].wait()
    n = vec_rows[0].shape[-1]
    for v in range(6):
        vec_rows[v][...] = vec[v, :n]
    for t in range(up.shape[-1] // 512):
        vec_rows[6][pl.ds(t * n, n)] = vec[6 + t, :n]
    final = {2: inp, 4: vec_rows[0], 8: vec_rows[1], 9: vec_rows[2], 10: vec_rows[3], 11: vec_rows[4],
             12: vec_rows[5], 6: vec_rows[6]}
    for i, (place, ref) in enumerate(final.items()):
        waits.append(copy(ref, outs[place], out_sems, i))
        waits[-1].start()
    for first, second in cuts[:4]:
        first.wait()
        second.start()
        waits.append(second)
    for i, (one, ref, place) in enumerate(zip(small_in[1:4], (out, up, down), (3, 5, 7))):
        one.wait()
        waits.append(copy(ref, outs[place], out_sems, 8 + i))
        waits[-1].start()
    for first, second in cuts[4:]:
        first.wait()
        second.start()
        waits.append(second)
    for one in waits:
        one.wait()


def fused(geo, args):
    (tokens, feature_matrix, input_weight, output_weight, output_bias, up_weight, up_bias, down_weight,
     down_bias, first_gain, first_shift, second_gain, second_shift, cotangent) = args
    rows, D = input_weight.shape[0], tokens.shape[-1]
    L = tokens.shape[1]
    FF = up_weight.shape[1]
    tiles = FF // 512
    lane = Lane()
    fwd, bwd = States(geo, lane, True), States(geo, lane, False)
    names = ["S", "O"] + [f"I{p}" for p in range(PAIRS)] + [f"F{t}" for t in range(tiles)]
    tasks = {name: GatherPlane(geo, lane) if name in PLANE else Gather(geo, lane, ORDERS.get(name, (0, 1)))
             for name in names}
    scatters = {"rO": D, "rQ": D, "rK": D, "rV0": 256, "rV1": 256, "rG": 128}
    scatters.update({f"rF{t}": 2 * D for t in range(tiles)})
    for name in scatters:
        tasks[name] = ScatterDirect(geo, lane) if name in DIRECT else Scatter(geo, lane, ORDERS.get(name, (0, 1)))
    for p in range(PAIRS):
        tasks[f"f{p}"], tasks[f"b{p}"] = PairStates(fwd, p), PairStates(bwd, p)
    plan = (fwd, bwd, tasks)
    lead = (geo.Z, geo.X, geo.Y, 2)
    V = pltpu.VMEM
    shape = jax.ShapeDtypeStruct
    outs = [shape(tokens.shape, F32), shape(tokens.shape, F32), shape(input_weight.shape, F32),
            shape((rows, D), F32), shape((rows, FF), F32), shape(down_weight.shape, F32), shape((rows, 128), F32)]
    arrays = (tokens, cotangent, feature_matrix, output_bias, down_bias, first_gain, first_shift, second_gain,
              second_shift, up_bias, input_weight, output_weight, up_weight, down_weight)
    scratch = [V(a.shape, BF) for a in arrays[2:11] + arrays[12:]] + [V(o.shape, F32) for o in outs[2:]]
    scratch += [
        V((2, L, D), BF), V((2, L, D), BF), V((2, L, D), F32), V((2, L, D), F32),
        V((rows, 128), BF), V(lead + (rows, 128), BF), V((PAIRS, rows, 384), BF), V((PAIRS,) + lead + (rows, 384), BF),
        V((rows, D), BF), V(lead + (rows, D), BF), V((tiles, rows, 2 * D), BF),
        V((tiles,) + lead + (rows, 2 * D), BF),
        V((2, L, D), BF), V((2, D, L), BF), V((2, PAIRS, L, 384), BF), V((2, H, L, M), BF), V((2, H, L, M), BF),
        V((2, L, D), F32), V((2, L, D), BF), V((2, L, D), F32), V((2, D, L), BF),
        V((2, L, 512), BF), V((2, L, 512), BF), V((16, D), F32), V((16, D), F32),
        V((2, M, M), BF), V((M, 2 * M), BF), V((512, 512), BF),
        V(lead + (rows, D), BF), V(lead + (rows, D), BF), V((2,) + lead + (rows, 256), BF), V(lead + (rows, D), BF),
        V((tiles,) + lead + (rows, 2 * D), BF), V(lead + (rows, 128), BF), V((tiles, rows, 2 * D), F32), V((rows, 128), F32),
    ]
    scratch += States.scratch(geo) + States.scratch(geo)
    for name, width in scatters.items():
        scratch += type(tasks[name]).scratch(geo, rows, width)
    scratch += [pltpu.SemaphoreType.DMA((lane.count,)), pltpu.SemaphoreType.DMA((lane.count,)),
                pltpu.SemaphoreType.DMA((21,))]
    hbm = pl.BlockSpec(memory_space=pl.ANY)
    parts = pl.pallas_call(
        functools.partial(layer_kernel, geo, lane, plan),
        out_shape=outs, in_specs=[hbm] * 14, out_specs=[hbm] * 7, scratch_shapes=scratch,
        compiler_params=pltpu.CompilerParams(collective_id=0, has_side_effects=True, vmem_limit_bytes=60 << 20),
    )(*arrays)
    vector = shape((rows,), F32)
    final = [outs[0], outs[1], shape(input_weight.shape, F32), outs[3], vector, outs[4],
             shape(up_bias.shape, F32), outs[5]] + [vector] * 5
    return pl.pallas_call(
        finish_kernel,
        out_shape=final, in_specs=[hbm] * 7, out_specs=[hbm] * 13,
        scratch_shapes=[V((2,) + tokens.shape, F32)] + [V(o.shape, F32) for o in outs[2:]]
        + [V((rows,), F32)] * 6 + [V(up_bias.shape, F32)]
        + [pltpu.SemaphoreType.DMA((13,)), pltpu.SemaphoreType.DMA((19,))],
        compiler_params=pltpu.CompilerParams(vmem_limit_bytes=60 << 20),
    )(*parts)

def local(
    tokens,
    feature_matrix,
    input_weight,
    output_weight,
    output_bias,
    up_weight,
    up_bias,
    down_weight,
    down_bias,
    first_gain,
    first_shift,
    second_gain,
    second_shift,
    cotangent,
):
    params = (
        lax.all_gather(input_weight, ("dp", "seq"), axis=0, tiled=True),
        lax.all_gather(output_weight, ("dp", "seq"), axis=0, tiled=True),
        lax.all_gather(output_bias, ("dp", "seq"), axis=0, tiled=True),
        lax.all_gather(up_weight, ("dp", "seq"), axis=0, tiled=True),
        lax.all_gather(up_bias, ("dp", "seq"), axis=0, tiled=True),
        lax.all_gather(down_weight, ("dp", "seq"), axis=0, tiled=True),
        lax.all_gather(down_bias, ("dp", "seq"), axis=0, tiled=True),
        lax.all_gather(first_gain, ("dp", "seq"), axis=0, tiled=True),
        lax.all_gather(first_shift, ("dp", "seq"), axis=0, tiled=True),
        lax.all_gather(second_gain, ("dp", "seq"), axis=0, tiled=True),
        lax.all_gather(second_shift, ("dp", "seq"), axis=0, tiled=True),
    )
    micros = tokens.shape[0]
    fronts = []
    carries = []
    for micro_step in range(micros):
        pieces = front(tokens[micro_step], feature_matrix, params)
        fronts.append(pieces)
        carries.append(
            prefix(
                (pieces[8], pieces[9]),
                "seq",
                add_pair,
                (jnp.zeros_like(pieces[8]), jnp.zeros_like(pieces[9])),
            )
        )
    results = []
    for micro_step in range(micros):
        pieces = fronts[micro_step]
        running_prefix_state, norm_sum = carries[micro_step]
        output = attend(pieces[5], pieces[6], pieces[7], running_prefix_state, norm_sum)[0]
        attended, middle = upper(pieces[0], output, params)
        results.append(feed(middle, params))
    result = jnp.stack(results)
    back_params = (
        lax.all_gather(input_weight, ("dp", "seq"), axis=0, tiled=True),
        lax.all_gather(output_weight, ("dp", "seq"), axis=0, tiled=True),
        lax.all_gather(output_bias, ("dp", "seq"), axis=0, tiled=True),
        lax.all_gather(up_weight, ("dp", "seq"), axis=0, tiled=True),
        lax.all_gather(up_bias, ("dp", "seq"), axis=0, tiled=True),
        lax.all_gather(down_weight, ("dp", "seq"), axis=0, tiled=True),
        lax.all_gather(down_bias, ("dp", "seq"), axis=0, tiled=True),
        lax.all_gather(first_gain, ("dp", "seq"), axis=0, tiled=True),
        lax.all_gather(first_shift, ("dp", "seq"), axis=0, tiled=True),
        lax.all_gather(second_gain, ("dp", "seq"), axis=0, tiled=True),
        lax.all_gather(second_shift, ("dp", "seq"), axis=0, tiled=True),
    )
    stored_list = []
    later_list = []
    for micro_step in range(micros):
        stored = upper_back(
            tokens[micro_step],
            cotangent[micro_step].astype(jnp.float32),
            feature_matrix,
            back_params,
            carries[micro_step],
        )
        stored_list.append(stored)
        later_list.append(
            prefix_2(
                (stored["state_grad"], stored["sum_grad"]),
                "seq",
                add_pair,
                (jnp.zeros_like(stored["state_grad"]), jnp.zeros_like(stored["sum_grad"])),
            )
        )
    upper_names = ["out", "out_bias", "up", "up_bias", "down", "down_bias", "gain_two", "shift_two"]
    upper_totals = [stored_list[0][name] for name in upper_names]
    micro_step = 1
    upper_totals = [
        total + stored_list[micro_step][name] for total, name in zip(upper_totals, upper_names)
    ]
    token_grads = []
    lower_totals = None
    for micro_step in range(micros):
        stored = stored_list[micro_step]
        tokens_part, input_part, gain_part, shift_part = lower_back(
            stored, later_list[micro_step], feature_matrix, back_params
        )
        token_grads.append(tokens_part)
        lower_parts = (input_part, gain_part, shift_part)
        if micro_step == 0:
            lower_totals = lower_parts
        else:
            lower_totals = jax.tree.map(jnp.add, lower_totals, lower_parts)
    shares = (
        lax.psum_scatter(lower_totals[0], ("dp", "seq"), scatter_dimension=0, tiled=True),
        lax.psum_scatter(upper_totals[0], ("dp", "seq"), scatter_dimension=0, tiled=True),
        lax.psum_scatter(upper_totals[1], ("dp", "seq"), scatter_dimension=0, tiled=True),
        lax.psum_scatter(upper_totals[2], ("dp", "seq"), scatter_dimension=0, tiled=True),
        lax.psum_scatter(upper_totals[3], ("dp", "seq"), scatter_dimension=0, tiled=True),
        lax.psum_scatter(upper_totals[4], ("dp", "seq"), scatter_dimension=0, tiled=True),
        lax.psum_scatter(upper_totals[5], ("dp", "seq"), scatter_dimension=0, tiled=True),
        lax.psum_scatter(lower_totals[1], ("dp", "seq"), scatter_dimension=0, tiled=True),
        lax.psum_scatter(lower_totals[2], ("dp", "seq"), scatter_dimension=0, tiled=True),
        lax.psum_scatter(upper_totals[6], ("dp", "seq"), scatter_dimension=0, tiled=True),
        lax.psum_scatter(upper_totals[7], ("dp", "seq"), scatter_dimension=0, tiled=True),
    )
    return (
        result,
        jnp.stack(token_grads),
        shares[0],
        shares[1],
        shares[2],
        shares[3],
        shares[4],
        shares[5],
        shares[6],
        shares[7],
        shares[8],
        shares[9],
        shares[10],
    )


def solution(mesh):
    in_specs = (
        P("dp", "seq", None),
        P(),
        P(("dp", "seq"), None),
        P(("dp", "seq"), None),
        P(("dp", "seq")),
        P(("dp", "seq"), None),
        P(("dp", "seq")),
        P(("dp", "seq"), None),
        P(("dp", "seq")),
        P(("dp", "seq")),
        P(("dp", "seq")),
        P(("dp", "seq")),
        P(("dp", "seq")),
        P("dp", "seq", None),
    )
    out_specs = (
        P("dp", "seq", None),
        P("dp", "seq", None),
        P(("dp", "seq"), None),
        P(("dp", "seq"), None),
        P(("dp", "seq")),
        P(("dp", "seq"), None),
        P(("dp", "seq")),
        P(("dp", "seq"), None),
        P(("dp", "seq")),
        P(("dp", "seq")),
        P(("dp", "seq")),
        P(("dp", "seq")),
        P(("dp", "seq")),
    )
    geo = Geometry(mesh)
    rows = 512 // (mesh.shape["dp"] * mesh.shape["seq"])
    if rows == 16:
        def body(*args):
            return fused(geo, args)
    else:
        body = local
    return jax.shard_map(body, mesh=mesh, in_specs=in_specs, out_specs=out_specs, check_vma=False)
```

```python
import functools
import math

import jax
import jax.numpy as jnp
from jax import lax
from jax.sharding import PartitionSpec as P

H = 8
DH = 64

from jax.experimental import pallas as pl
from jax.experimental.pallas import tpu as pltpu

MESH = pl.DeviceIdType.MESH


class Geometry:
    def __init__(self, mesh):
        dp, seq = mesh.shape["dp"], mesh.shape["seq"]
        self.C = 2
        self.Y = seq // 2
        self.X = 1 << ((dp.bit_length() - 1) // 2)
        self.Z = dp // self.X

    def me(self):
        dp, seq = lax.axis_index("dp"), lax.axis_index("seq")
        return dp // self.X, dp % self.X, seq // 2, seq % 2

    def device(self, z, x, y, c):
        return (z * self.X + x, y * 2 + c)

    def greet(self):
        z, x, y, c = self.me()
        peers = [self.device(z, x, y, 1 - c)]
        peers += [self.device((z + i) % self.Z, (x + j) % self.X, (y + k) % self.Y, c)
                  for i in range(self.Z) for j in range(self.X) for k in range(self.Y)][1:]
        semaphore = pltpu.get_barrier_semaphore()
        for peer in peers:
            pl.semaphore_signal(semaphore, inc=1, device_id=peer, device_id_type=MESH)

    def barrier(self):
        pl.semaphore_wait(pltpu.get_barrier_semaphore(), self.Z * self.X * self.Y)


class Lane:
    def __init__(self):
        self.count = 0
        self.send = self.recv = None

    def take(self, n=1):
        first = self.count
        self.count += n
        return first


def remote(lane, index, src, dst, device):
    return pltpu.make_async_remote_copy(
        src_ref=src, dst_ref=dst, send_sem=lane.send.at[index], recv_sem=lane.recv.at[index],
        device_id=device, device_id_type=MESH)


class Gather:
    def __init__(self, geo, lane, orders):
        self.geo, self.lane, self.orders = geo, lane, orders
        self.zs = lane.take()
        self.second = lane.take(max(geo.X, geo.Y) - 1)
        self.third = lane.take(max(geo.X, geo.Y) - 1)
        self.core = lane.take()

    def bind(self, own, full):
        self.own, self.full = own, full

    def z_copies(self):
        g = self.geo
        z, x, y, c = g.me()
        for k in range(1, g.Z):
            yield remote(self.lane, self.zs, self.own, self.full.at[z, x, y, c], g.device((z + k) % g.Z, x, y, c))

    def z_whole(self):
        g = self.geo
        z, x, y, c = g.me()
        slots = self.full.at[pl.ds(0, g.Z - 1), x, y, c]
        return remote(self.lane, self.zs, slots, slots, g.device((z + 1) % g.Z, x, y, c))

    def axis_copies(self, phase, order, incoming):
        g = self.geo
        z, x, y, c = g.me()
        base = self.second if phase == 2 else self.third
        along_x = (phase == 2) == (order == 0)
        size = g.X if along_x else g.Y
        for k in range(1, size):
            if along_x:
                source = (x + g.X - k) % g.X if incoming else x
                device = g.device(z, (x + k) % g.X, y, c)
                slot = self.full.at[:, source, y, c] if phase == 2 else self.full.at[:, source, :, c]
            else:
                source = (y + g.Y - k) % g.Y if incoming else y
                device = g.device(z, x, (y + k) % g.Y, c)
                slot = self.full.at[:, x, source, c] if phase == 2 else self.full.at[:, :, source, c]
            yield remote(self.lane, base + k - 1, slot, slot, device)

    def both(self, action):
        c = self.geo.me()[3]
        if self.orders[0] == self.orders[1]:
            action(self.orders[0])
            return
        for core in range(2):
            @pl.when(c == core)
            def _():
                action(self.orders[core])

    def step(self, n):
        g = self.geo
        z, x, y, c = g.me()
        if n == 0:
            for copy in self.z_copies():
                copy.start()
            self.full[z, x, y, c] = self.own[...]
        elif n == 1:
            self.z_whole().wait_recv()
            self.both(lambda order: [copy.start() for copy in self.axis_copies(2, order, False)])
        elif n == 2:
            def go(order):
                for copy in self.axis_copies(2, order, True):
                    copy.wait_recv()
                for copy in self.axis_copies(3, order, False):
                    copy.start()
            self.both(go)
        elif n == 3:
            def go(order):
                for copy in self.axis_copies(3, order, True):
                    copy.wait_recv()
            self.both(go)
            slot = self.full.at[:, :, :, c]
            remote(self.lane, self.core, slot, slot, g.device(z, x, y, 1 - c)).start()
        else:
            slot = self.full.at[:, :, :, 1 - c]
            remote(self.lane, self.core, slot, slot, g.device(z, x, y, 1 - c)).wait_recv()

    def drain(self):
        g = self.geo
        z, x, y, c = g.me()
        self.z_whole().wait_send()

        def go(order):
            for phase in (2, 3):
                for copy in self.axis_copies(phase, order, False):
                    copy.wait_send()
        self.both(go)
        slot = self.full.at[:, :, :, c]
        remote(self.lane, self.core, slot, slot, g.device(z, x, y, 1 - c)).wait_send()


class Scatter:
    def __init__(self, geo, lane, orders):
        self.geo, self.lane, self.orders = geo, lane, orders
        self.core = lane.take()
        self.first = lane.take(max(geo.X, geo.Y) - 1)
        self.second = lane.take(max(geo.X, geo.Y) - 1)
        self.zs = lane.take()

    @staticmethod
    def scratch(geo, rows, width):
        wide = max(geo.X, geo.Y)
        kind = jnp.bfloat16
        return [
            pltpu.VMEM((geo.Z, geo.X, geo.Y, rows, width), kind),
            pltpu.VMEM((wide - 1, geo.Z, wide, rows, width), kind),
            pltpu.VMEM((wide - 1, geo.Z, rows, width), kind),
            pltpu.VMEM((geo.Z - 1, rows, width), kind),
        ]

    def bind(self, part, out, buffers):
        self.part, self.out = part, out
        self.rc, self.ra, self.rb, self.rz = buffers

    def both(self, action):
        c = self.geo.me()[3]
        if self.orders[0] == self.orders[1]:
            action(self.orders[0])
            return
        for core in range(2):
            @pl.when(c == core)
            def _():
                action(self.orders[core])

    def core_copy(self):
        z, x, y, c = self.geo.me()
        return remote(self.lane, self.core, self.part.at[:, :, :, 1 - c], self.rc,
                      self.geo.device(z, x, y, 1 - c))

    def axis_copies(self, phase, order):
        g = self.geo
        z, x, y, c = g.me()
        base = self.first if phase == 1 else self.second
        along_x = (phase == 1) == (order == 1)
        for k in range(1, g.X if along_x else g.Y):
            if along_x:
                far = (x + k) % g.X
                device = g.device(z, far, y, c)
                src = self.part.at[:, far, :, c] if phase == 1 else self.part.at[:, far, y, c]
                dst = self.ra.at[k - 1, :, pl.ds(0, g.Y)] if phase == 1 else self.rb.at[k - 1]
            else:
                far = (y + k) % g.Y
                device = g.device(z, x, far, c)
                src = self.part.at[:, :, far, c] if phase == 1 else self.part.at[:, x, far, c]
                dst = self.ra.at[k - 1, :, pl.ds(0, g.X)] if phase == 1 else self.rb.at[k - 1]
            yield remote(self.lane, base + k - 1, src, dst, device)

    def z_copies(self):
        g = self.geo
        z, x, y, c = g.me()
        for k in range(1, g.Z):
            far = (z + k) % g.Z
            yield remote(self.lane, self.zs, self.part.at[far, x, y, c], self.rz.at[k - 1], g.device(far, x, y, c))

    def z_whole(self):
        g = self.geo
        z, x, y, c = g.me()
        return remote(self.lane, self.zs, self.rz, self.rz, g.device((z + 1) % g.Z, x, y, c))

    def step(self, n):
        g = self.geo
        z, x, y, c = g.me()
        wide = lambda ref: ref.astype(jnp.float32)
        if n == 0:
            self.core_copy().start()
        elif n == 1:
            self.core_copy().wait_recv()

            def add(i, _):
                total = wide(self.part[i, :, :, c]) + wide(self.rc[i])
                self.part[i, :, :, c] = total.astype(jnp.bfloat16)
                return 0
            lax.fori_loop(0, g.Z, add, 0)
            self.both(lambda order: [copy.start() for copy in self.axis_copies(1, order)])
        elif n == 2:
            def go(order):
                copies = list(self.axis_copies(1, order))
                for copy in copies:
                    copy.wait_recv()
                count = len(copies)
                if order == 0:
                    def add(i, _):
                        total = wide(self.part[i, :, y, c])
                        for k in range(count):
                            total += wide(self.ra[k, i, : g.X])
                        self.part[i, :, y, c] = total.astype(jnp.bfloat16)
                        return 0
                else:
                    def add(i, _):
                        total = wide(self.part[i, x, :, c])
                        for k in range(count):
                            total += wide(self.ra[k, i, : g.Y])
                        self.part[i, x, :, c] = total.astype(jnp.bfloat16)
                        return 0
                lax.fori_loop(0, g.Z, add, 0)
                for copy in self.axis_copies(2, order):
                    copy.start()
            self.both(go)
        elif n == 3:
            def go(order):
                copies = list(self.axis_copies(2, order))
                for copy in copies:
                    copy.wait_recv()

                def add(i, _):
                    total = wide(self.part[i, x, y, c])
                    for k in range(len(copies)):
                        total += wide(self.rb[k, i])
                    self.part[i, x, y, c] = total.astype(jnp.bfloat16)
                    return 0
                lax.fori_loop(0, g.Z, add, 0)
            self.both(go)
            for copy in self.z_copies():
                copy.start()
        else:
            total = wide(self.part[z, x, y, c])
            self.z_whole().wait_recv()
            for k in range(g.Z - 1):
                total += wide(self.rz[k])
            self.out[...] = total

    def drain(self):
        self.core_copy().wait_send()

        def go(order):
            for phase in (1, 2):
                for copy in self.axis_copies(phase, order):
                    copy.wait_send()
        self.both(go)
        self.z_whole().wait_send()


epsilon = 1e-05
finest_precision = lax.Precision.HIGHEST


def prefix(array, axis, combine, identity):
    count, here = (lax.axis_size(axis), lax.axis_index(axis))
    everything = jax.tree.map(
        lambda part, kind: lax.all_gather(part.astype(kind), axis),
        array,
        (jnp.bfloat16, jnp.bfloat16),
    )
    start = jax.tree.map(
        lambda part, zero: jnp.broadcast_to(jnp.asarray(zero, part.dtype), part.shape),
        array,
        identity,
    )

    def hop(k, before):
        reached = k < here
        new = combine(
            before, jax.tree.map(lambda part, own: part[k].astype(own.dtype), everything, array)
        )
        return jax.tree.map(lambda a, b: jnp.where(reached, a, b), new, before)

    return lax.fori_loop(0, count, hop, start)


def prefix_2(array, axis, join, neutral):
    count = lax.axis_size(axis)
    place = lax.axis_index(axis)
    ahead = count - 1 - place
    gathered = jax.tree.map(
        lambda a, kind: lax.all_gather(a.astype(kind), axis),
        array,
        jax.tree.map(lambda a: jnp.bfloat16 if a.dtype == jnp.float32 else a.dtype, array),
    )
    state = jax.tree.map(lambda a, e: jnp.zeros_like(a) + jnp.asarray(e, a.dtype), array, neutral)

    def one(hop, state):
        source = count - 1 - hop
        return join(
            state,
            jax.tree.map(
                lambda a, own: lax.dynamic_index_in_dim(a, source, 0, False).astype(own.dtype),
                gathered,
                array,
            ),
        )

    return lax.fori_loop(0, ahead, one, state)


def layer_norm(value_rows, norm_gain, norm_shift):
    center = jnp.mean(value_rows, axis=-1, keepdims=True)
    centred = value_rows - center
    spread = jnp.mean(centred * centred, axis=-1, keepdims=True)
    return centred * lax.rsqrt(spread + epsilon) * norm_gain + norm_shift


def gelu_tanh(value_rows):
    return jax.nn.gelu(value_rows, approximate=True)


def add_pair(earlier, later_term):
    return (earlier[0] + later_term[0], earlier[1] + later_term[1])


def causal_mask(length):
    positions = jnp.arange(length)
    return (positions[:, None] >= positions[None, :]).astype(jnp.float32)


def favor_map(proj_low, matrix, feature_scale):
    raw_proj = jnp.einsum("rhd,dm->rhm", proj_low, matrix, preferred_element_type=jnp.float32)
    projection = proj_low.astype(jnp.float32)
    half_norm = (
        0.5
        * feature_scale
        * feature_scale
        * jnp.sum(projection * projection, axis=-1, keepdims=True)
    )
    return jnp.exp(feature_scale * raw_proj - half_norm) / math.sqrt(matrix.shape[1])


def favor_back(map_grad, favor_value, proj_low, matrix, feature_scale):
    log_grad = map_grad * favor_value
    raw_grad = (feature_scale * log_grad).astype(jnp.bfloat16)
    projection = proj_low.astype(jnp.float32)
    through = jnp.einsum("rhm,dm->rhd", raw_grad, matrix, preferred_element_type=jnp.float32)
    return (
        through
        - feature_scale * feature_scale * jnp.sum(log_grad, axis=-1, keepdims=True) * projection
    )


def front(token_block, matrix, params):
    inputs = token_block.astype(jnp.float32)
    length = inputs.shape[0]
    normed = layer_norm(
        inputs, params[7].astype(jnp.float32), params[8].astype(jnp.float32)
    ).astype(jnp.bfloat16)
    mixed = jnp.dot(normed, params[0], preferred_element_type=jnp.float32).astype(jnp.bfloat16)
    head_parts = mixed.reshape(length, 3, H, DH)
    feature_scale = DH ** (-0.25)
    query_features = favor_map(head_parts[:, 0], matrix, feature_scale)
    key_features = favor_map(head_parts[:, 1], matrix, feature_scale)
    query_reduced = query_features.astype(jnp.bfloat16)
    key_reduced = key_features.astype(jnp.bfloat16)
    value_rows = head_parts[:, 2]
    block_local_state = jnp.einsum(
        "nqo,nqi->qoi", key_reduced, value_rows, preferred_element_type=jnp.float32
    )
    local_sum = jnp.sum(key_reduced.astype(jnp.float32), axis=0)
    return (
        inputs,
        normed,
        head_parts,
        query_features,
        key_features,
        query_reduced,
        key_reduced,
        value_rows,
        block_local_state,
        local_sum,
    )


def attend(query_reduced, key_reduced, value_rows, running_prefix_state, norm_sum):
    causal = causal_mask(query_reduced.shape[0])
    scores = (
        jnp.einsum("ihm,jhm->hij", query_reduced, key_reduced, preferred_element_type=jnp.float32)
        * causal[None]
    )
    denominator = jnp.sum(scores, axis=-1).T + jnp.einsum(
        "ihm,hm->ih", query_reduced.astype(jnp.float32), norm_sum, precision=finest_precision
    )
    attention_numerator = jnp.einsum(
        "hij,jhd->ihd", scores.astype(jnp.bfloat16), value_rows, preferred_element_type=jnp.float32
    )
    attention_numerator = attention_numerator + jnp.einsum(
        "plq,lqu->plu",
        query_reduced,
        running_prefix_state.astype(jnp.bfloat16),
        preferred_element_type=jnp.float32,
    )
    return (attention_numerator / denominator[:, :, None], attention_numerator, denominator)


def upper(inputs, output, params):
    length = output.shape[0]
    attended = output.reshape(length, -1).astype(jnp.bfloat16)
    middle = (
        inputs
        + jnp.dot(attended, params[1], preferred_element_type=jnp.float32)
        + params[2].astype(jnp.float32)
    )
    return (attended, middle)


def feed(middle, params):
    normed_two = layer_norm(
        middle, params[9].astype(jnp.float32), params[10].astype(jnp.float32)
    ).astype(jnp.bfloat16)
    hidden = jnp.dot(normed_two, params[3], preferred_element_type=jnp.float32) + params[4].astype(
        jnp.float32
    )
    active = gelu_tanh(hidden).astype(jnp.bfloat16)
    return (
        middle
        + jnp.dot(active, params[5], preferred_element_type=jnp.float32)
        + params[6].astype(jnp.float32)
    )


def upper_back(token_block, upstream, matrix, params, block_carry):
    pieces = front(token_block, matrix, params)
    (
        inputs,
        normed,
        head_parts,
        query_features,
        key_features,
        query_reduced,
        key_reduced,
        value_rows,
        block_local_state,
        local_sum,
    ) = pieces
    running_prefix_state, norm_sum = block_carry
    output, attention_numerator, denominator = attend(
        query_reduced, key_reduced, value_rows, running_prefix_state, norm_sum
    )
    attended, middle = upper(inputs, output, params)
    normed_float, second_pull = jax.vjp(
        layer_norm, middle, params[9].astype(jnp.float32), params[10].astype(jnp.float32)
    )
    normed_two = normed_float.astype(jnp.bfloat16)
    hidden = jnp.dot(normed_two, params[3], preferred_element_type=jnp.float32) + params[4].astype(
        jnp.float32
    )
    active_float, gelu_pull = jax.vjp(gelu_tanh, hidden)
    active = active_float.astype(jnp.bfloat16)
    stored = {"front": pieces, "carry": block_carry}
    down_term = upstream.astype(jnp.bfloat16)
    stored["down"] = jnp.einsum("rf,rd->fd", active, down_term, preferred_element_type=jnp.float32)
    stored["down_bias"] = jnp.sum(upstream, axis=0)
    active_grad = jnp.einsum("rd,fd->rf", down_term, params[5], preferred_element_type=jnp.float32)
    (hidden_grad,) = gelu_pull(active_grad)
    up_term = hidden_grad.astype(jnp.bfloat16)
    stored["up"] = jnp.einsum("rd,rf->df", normed_two, up_term, preferred_element_type=jnp.float32)
    stored["up_bias"] = jnp.sum(hidden_grad, axis=0)
    normed_two_grad = jnp.einsum(
        "rf,df->rd", up_term, params[3], preferred_element_type=jnp.float32
    )
    middle_part, gain_two_grad, shift_two_grad = second_pull(normed_two_grad)
    stored["gain_two"] = gain_two_grad
    stored["shift_two"] = shift_two_grad
    middle_grad = upstream + middle_part
    stored["middle_grad"] = middle_grad
    out_term = middle_grad.astype(jnp.bfloat16)
    stored["out"] = jnp.einsum("re,rd->ed", attended, out_term, preferred_element_type=jnp.float32)
    stored["out_bias"] = jnp.sum(middle_grad, axis=0)
    attended_grad = jnp.einsum(
        "rd,ed->re", out_term, params[1], preferred_element_type=jnp.float32
    ).reshape(output.shape)
    numerator_grad = (attended_grad / denominator[:, :, None]).astype(jnp.bfloat16)
    denom_grad = -jnp.sum(attended_grad * attention_numerator, axis=-1) / (
        denominator * denominator
    )
    stored["numer_grad"] = numerator_grad
    stored["denom_grad"] = denom_grad
    stored["state_grad"] = jnp.einsum(
        "jfp,jfl->fpl", query_reduced, numerator_grad, preferred_element_type=jnp.float32
    )
    stored["sum_grad"] = jnp.einsum(
        "ih,ihm->hm", denom_grad, query_reduced.astype(jnp.float32), precision=finest_precision
    )
    return stored


def lower_back(stored, later_part, matrix, params):
    (
        inputs,
        normed,
        head_parts,
        query_features,
        key_features,
        query_reduced,
        key_reduced,
        value_rows,
        block_local_state,
        local_sum,
    ) = stored["front"]
    running_prefix_state, norm_sum = stored["carry"]
    state_later, sum_later = later_part
    numerator_grad = stored["numer_grad"]
    denom_grad = stored["denom_grad"]
    length = inputs.shape[0]
    causal = causal_mask(length)
    scores = (
        jnp.einsum("ihm,jhm->hij", query_reduced, key_reduced, preferred_element_type=jnp.float32)
        * causal[None]
    )
    scores_grad = jnp.einsum(
        "ihd,jhd->hij", numerator_grad, value_rows, preferred_element_type=jnp.float32
    )
    score_term = ((scores_grad + denom_grad.T[:, :, None]) * causal[None]).astype(jnp.bfloat16)
    later_reduced = state_later.astype(jnp.bfloat16)
    query_grad = jnp.einsum(
        "hij,jhm->ihm", score_term, key_reduced, preferred_element_type=jnp.float32
    )
    query_grad = query_grad + jnp.einsum(
        "gvw,vcw->gvc",
        numerator_grad,
        running_prefix_state.astype(jnp.bfloat16),
        preferred_element_type=jnp.float32,
    )
    query_grad = query_grad + denom_grad[:, :, None] * norm_sum[None]
    key_grad = jnp.einsum(
        "hij,ihm->jhm", score_term, query_reduced, preferred_element_type=jnp.float32
    )
    key_grad = key_grad + jnp.einsum(
        "prc,rqc->prq", value_rows, later_reduced, preferred_element_type=jnp.float32
    )
    key_grad = key_grad + sum_later[None]
    value_grad = jnp.einsum(
        "hij,ihd->jhd",
        scores.astype(jnp.bfloat16),
        numerator_grad,
        preferred_element_type=jnp.float32,
    )
    value_grad = value_grad + jnp.einsum(
        "qsa,saw->qsw", key_reduced, later_reduced, preferred_element_type=jnp.float32
    )
    feature_scale = DH ** (-0.25)
    query_proj = favor_back(query_grad, query_features, head_parts[:, 0], matrix, feature_scale)
    key_proj = favor_back(key_grad, key_features, head_parts[:, 1], matrix, feature_scale)
    mixed_grad = (
        jnp.stack([query_proj, key_proj, value_grad], axis=1)
        .reshape(length, -1)
        .astype(jnp.bfloat16)
    )
    input_part = jnp.einsum("rd,re->de", normed, mixed_grad, preferred_element_type=jnp.float32)
    normed_grad = jnp.einsum("re,de->rd", mixed_grad, params[0], preferred_element_type=jnp.float32)
    _, first_pull = jax.vjp(
        layer_norm, inputs, params[7].astype(jnp.float32), params[8].astype(jnp.float32)
    )
    inputs_part, gain_one_grad, shift_one_grad = first_pull(normed_grad)
    return (stored["middle_grad"] + inputs_part, input_part, gain_one_grad, shift_one_grad)


BF = jnp.bfloat16
F32 = jnp.float32
M = 256
SCALE = DH ** (-0.25)
LOG2E = math.log2(math.e)
PAIRS = H // 2
STATE_ROWS = 144


def dot(a, b):
    return jnp.dot(a, b, preferred_element_type=F32)


def dot_nt(a, b):
    return lax.dot_general(a, b, (((1,), (1,)), ((), ())), preferred_element_type=F32)


class States:
    def __init__(self, geo, lane, earlier):
        self.geo, self.lane, self.earlier = geo, lane, earlier
        self.per = geo.Y + 1
        self.first = lane.take(self.per * PAIRS)

    @staticmethod
    def scratch(geo):
        one = (PAIRS, STATE_ROWS, M)
        two = (PAIRS, 2, STATE_ROWS, M)
        return [pltpu.VMEM(two, BF), pltpu.VMEM(two, BF), pltpu.VMEM(one, BF),
                pltpu.VMEM((PAIRS, max(geo.Y - 1, 1), STATE_ROWS, M), BF), pltpu.VMEM(one, BF),
                pltpu.VMEM(one, BF), pltpu.VMEM(two, BF)]

    def bind(self, buffers):
        self.own, self.sibling, self.chip, self.chips, self.base, self.base_sibling, self.total = buffers

    def copies(self, p, phase):
        g = self.geo
        z, x, y, c = g.me()
        index = self.first + p * self.per
        other = g.device(z, x, y, 1 - c)
        if phase == 0:
            return [remote(self.lane, index, self.own.at[p], self.sibling.at[p], other)]
        if phase == 1:
            return [remote(self.lane, index + k, self.chip.at[p], self.chips.at[p, k - 1],
                           g.device(z, x, (y + k) % g.Y, c)) for k in range(1, g.Y)]
        return [remote(self.lane, index + g.Y, self.base.at[p], self.base_sibling.at[p], other)]

    def step(self, n, p):
        g = self.geo
        z, x, y, c = g.me()
        if n > 0:
            for copy in self.copies(p, n - 1):
                copy.wait_recv()
        if n == 1:
            self.chip[p] = (self.own[p, c].astype(F32) + self.sibling[p, c].astype(F32)).astype(BF)
        elif n == 2:
            total = jnp.zeros((STATE_ROWS, M), F32)
            for k in range(1, g.Y):
                source = (y + g.Y - k) % g.Y
                counts = source < y if self.earlier else source > y
                total += jnp.where(counts, 1.0, 0.0) * self.chips[p, k - 1].astype(F32)
            self.base[p] = total.astype(BF)
        elif n == 3:
            near = jnp.where(c == (1 if self.earlier else 0), 1.0, 0.0)
            self.total[p, c] = (self.base[p].astype(F32) + near * self.sibling[p, c].astype(F32)).astype(BF)
            self.total[p, 1 - c] = (self.base_sibling[p].astype(F32)
                                    + near * self.sibling[p, 1 - c].astype(F32)).astype(BF)
        if n < 3:
            for copy in self.copies(p, n):
                copy.start()

    def drain(self):
        for p in range(PAIRS):
            for phase in range(3):
                for copy in self.copies(p, phase):
                    copy.wait_send()


class GatherPlane(Gather):
    def __init__(self, geo, lane):
        self.geo, self.lane = geo, lane
        self.far = [(j, k) for j in range(geo.X) for k in range(geo.Y)][1:]
        self.zs, self.plane, self.core = lane.take(), lane.take(len(self.far)), lane.take()

    def plane_copies(self, incoming):
        g = self.geo
        z, x, y, c = g.me()
        for n, (j, k) in enumerate(self.far):
            slot = self.full.at[:, (x + g.X - j) % g.X, (y + g.Y - k) % g.Y, c] if incoming else self.full.at[:, x, y, c]
            yield remote(self.lane, self.plane + n, slot, slot, g.device(z, (x + j) % g.X, (y + k) % g.Y, c))

    def core_copy(self, own):
        z, x, y, c = self.geo.me()
        slot = self.full.at[:, :, :, c if own else 1 - c]
        return remote(self.lane, self.core, slot, slot, self.geo.device(z, x, y, 1 - c))

    def step(self, n):
        if n == 0:
            super().step(0)
        elif n == 1:
            self.z_whole().wait_recv()
            for copy in self.plane_copies(False):
                copy.start()
        elif n == 2:
            for copy in self.plane_copies(True):
                copy.wait_recv()
            self.core_copy(True).start()
        else:
            self.core_copy(False).wait_recv()

    def drain(self):
        self.z_whole().wait_send()
        for copy in self.plane_copies(False):
            copy.wait_send()
        self.core_copy(True).wait_send()


class PairStates:
    def __init__(self, states, p):
        self.states, self.p = states, p

    def step(self, n):
        self.states.step(n, self.p)


class ScatterDirect:
    def __init__(self, geo, lane):
        self.geo, self.lane = geo, lane
        self.far = [(i, j, k) for i in range(geo.Z) for j in range(geo.X) for k in range(geo.Y)][1:]
        self.core = lane.take()
        self.first = lane.take()

    @staticmethod
    def scratch(geo, rows, width):
        return [pltpu.VMEM((geo.Z, geo.X, geo.Y, rows, width), jnp.bfloat16),
                pltpu.VMEM((geo.Z * geo.X * geo.Y - 1, rows, width), jnp.bfloat16)]

    def bind(self, part, out, buffers):
        self.part, self.out = part, out
        self.rc, self.rz = buffers

    def core_copy(self):
        z, x, y, c = self.geo.me()
        return remote(self.lane, self.core, self.part.at[:, :, :, 1 - c], self.rc, self.geo.device(z, x, y, 1 - c))

    def copies(self):
        g = self.geo
        z, x, y, c = g.me()
        for n, (i, j, k) in enumerate(self.far):
            to = ((z + i) % g.Z, (x + j) % g.X, (y + k) % g.Y, c)
            yield remote(self.lane, self.first, self.part.at[to], self.rz.at[n], g.device(*to))

    def whole(self):
        z, x, y, c = self.geo.me()
        return remote(self.lane, self.first, self.rz, self.rz, self.geo.device((z + 1) % self.geo.Z, x, y, c))

    def step(self, n):
        g = self.geo
        z, x, y, c = g.me()
        if n == 0:
            self.core_copy().start()
        elif n == 1:
            self.core_copy().wait_recv()

            def add(i, _):
                total = self.part[i, :, :, c].astype(F32) + self.rc[i].astype(F32)
                self.part[i, :, :, c] = total.astype(BF)
                return 0
            lax.fori_loop(0, g.Z, add, 0)
            for copy in self.copies():
                copy.start()
        else:
            total = self.part[z, x, y, c].astype(F32)
            self.whole().wait_recv()
            for n in range(len(self.far)):
                total += self.rz[n].astype(F32)
            self.out[...] = total

    def drain(self):
        self.core_copy().wait_send()
        self.whole().wait_send()


DIRECT = ("rG", "rV1",)
PLANE = ()
ORDERS = {"I3": (1, 1), "F0": (1, 1), "I1": (1, 1), "rF3": (1, 1)}
PLAN = {
    "start": (("S", 0), ("I0", 0), ("I1", 0), ("I2", 0), ("I3", 0),),
    "first": (("O", 0), ("F0", 0), ("F1", 0), ("F2", 0), ("F3", 0), ("S", 1), ("I0", 1), ("I1", 1), ("S", 2),
        ("I2", 1), ("I0", 2), ("I3", 1), ("I1", 2), ("O", 1), ("S", 3), ("I2", 2), ("S", 4),),
    "norm0": (("I0", 3),),
    "proj.pre0": (("F0", 1), ("I3", 2), ("I0", 4),),
    "proj0": (("f0", 0),),
    "proj.pre1": (("I1", 3), ("O", 2), ("F1", 1), ("I2", 3), ("f0", 1), ("I1", 4),),
    "proj1": (("f1", 0), ("I3", 3), ("F0", 2), ("F2", 1),),
    "proj.pre2": (("I2", 4),),
    "proj2": (("f2", 0),),
    "proj.pre3": (("f1", 1), ("I3", 4),),
    "proj3": (("f3", 0), ("F3", 1),),
    "block0": (("f2", 1),),
    "block1": (("f3", 1),),
    "block3": (("f1", 2),),
    "att.pre0": (("O", 3), ("F1", 2), ("f0", 2), ("F0", 3), ("f1", 3), ("O", 4), ("F2", 2), ("f0", 3),),
    "att0": (("f2", 2),),
    "att.pre2": (("F0", 4), ("f3", 2), ("f2", 3),),
    "att2": (("F3", 2),),
    "att.pre3": (("f3", 3),),
    "mid": (("F1", 3),),
    "feed0": (("rF0", 0), ("F2", 3),),
    "feed.pre1": (("F1", 4),),
    "feed1": (("rF1", 0), ("rF0", 1), ("F2", 4), ("F3", 3),),
    "feed2": (("rF2", 0), ("rF1", 1), ("F3", 4),),
    "feed3": (("rF0", 2), ("rF2", 1),),
    "out": (("rF1", 2), ("rO", 0),),
    "st0": (("b0", 0), ("rF3", 0),),
    "st1": (("b1", 0),),
    "st2": (("b2", 0),),
    "st3": (("b3", 0), ("rO", 1),),
    "q0": (("b0", 1), ("b1", 1), ("b2", 1), ("rF3", 1),),
    "q2": (("b3", 1), ("rO", 2),),
    "q3": (("b0", 2), ("rF1", 3),),
    "q.end": (("rQ", 0), ("rF0", 3),),
    "k.pre0": (("rF2", 2), ("b1", 2), ("b0", 3),),
    "k0": (("b1", 3), ("b2", 2), ("rQ", 1),),
    "k1": (("b3", 2), ("b2", 3), ("rF3", 2),),
    "k2": (("b3", 3), ("rF2", 3), ("rO", 3),),
    "k3": (("rQ", 2),),
    "k.end": (("rK", 0),),
    "v0": (("rV0", 0), ("rK", 1), ("rF3", 3),),
    "v1": (("rV1", 0), ("rV0", 1), ("rQ", 3), ("rF2", 4), ("rO", 4),),
    "nb1": (("rK", 2), ("rF0", 4), ("rV1", 1),),
    "fb1": (("rG", 0), ("rF1", 4), ("rF3", 4),),
    "end": (("rV0", 2), ("rQ", 4), ("rG", 1), ("rK", 3), ("rV0", 3), ("rV1", 2), ("rG", 2), ("rK", 4), ("rV0", 4),),
}


def layer_kernel(geo, lane, plan, *refs):
    (tokens_hbm, cot_hbm, feat_hbm, out_bias_hbm, down_bias_hbm, first_gain_hbm, first_shift_hbm, second_gain_hbm,
     second_shift_hbm, up_bias_hbm, wi_hbm, wo_hbm, wu_hbm, wd_hbm,
     result_hbm, tokens_grad_hbm, inp_hbm, out_hbm, up_hbm, down_hbm, vec_hbm,
     feat, out_bias_in, down_bias_in, first_gain_in, first_shift_in, second_gain_in, second_shift_in, up_bias_in,
     wi_in, wu_in, wd_in, inp_out, out_out, up_out, down_out, vec_out,
     tokens, cot, result, tokens_grad, small_own, small, wi_own, wi, wo_own, wo_all, wf_own, wf,
     normed, normed_t, mixed, pq, pk, den, attended, middle, n2_t,
     act, hg, vecs, grads, fa, ft, perm, part_q, part_k, part_v, part_o, part_f, part_g, up_parts, vec_sum) = refs[:73]
    rest = list(refs[73:])
    fwd, bwd, tasks = plan
    take = lambda n: [rest.pop(0) for _ in range(n)]
    fwd.bind(take(7))
    bwd.bind(take(7))
    scatter_buffers = {name: take(2 if type(task) is ScatterDirect else 4)
                       for name, task in tasks.items() if name[0] == "r"}
    lane.send, lane.recv = take(2)
    local_sem = rest.pop(0)
    tasks["S"].bind(small_own, small)
    tasks["O"].bind(wo_own, wo_all)
    tasks["rO"].bind(part_o, out_out, scatter_buffers["rO"])
    tasks["rG"].bind(part_g, vec_sum, scatter_buffers["rG"])
    wide = tokens.shape[-1]
    tasks["rQ"].bind(part_q, inp_out.at[:, pl.ds(0, wide)], scatter_buffers["rQ"])
    tasks["rK"].bind(part_k, inp_out.at[:, pl.ds(wide, wide)], scatter_buffers["rK"])
    for n in range(2):
        tasks[f"rV{n}"].bind(part_v.at[n], inp_out.at[:, pl.ds(2 * wide + 256 * n, 256)], scatter_buffers[f"rV{n}"])
    for p in range(PAIRS):
        tasks[f"I{p}"].bind(wi_own.at[p], wi.at[p])
    for t in range(wf.shape[0]):
        tasks[f"F{t}"].bind(wf_own.at[t], wf.at[t])
        tasks[f"rF{t}"].bind(part_f.at[t], up_parts.at[t], scatter_buffers[f"rF{t}"])
    n2 = normed
    D = tokens.shape[-1]
    L = tokens.shape[1]
    TILES = wf.shape[0]
    HALF = L // 2
    lead = (geo.Z, geo.X, geo.Y, 2)
    z, x, y, c = geo.me()
    place = (((z * geo.X + x) * geo.Y + y) * 2 + c) % 8

    def loop(n, body):
        def step(i, _):
            body(i)
            return 0
        lax.fori_loop(0, n, step, 0)

    def pairs(body, before, after):
        def step(p):
            if before:
                pump_at(p, [before + f"{n}" for n in range(PAIRS)])
            body(p, 0)
            body(p, 1)
            pump_at(p, [after + f"{n}" for n in range(PAIRS)])
        loop(PAIRS, step)

    def pump(point):
        for name, n in PLAN.get(point, ()):
            tasks[name].step(n)

    def pump_at(now, points):
        for when, point in enumerate(points):
            if point in PLAN:
                @pl.when(now == when)
                def _():
                    pump(point)

    def local(i, src, dst):
        return pltpu.make_async_copy(src, dst, local_sem.at[i])

    entry = ((feat_hbm, feat), (out_bias_hbm, out_bias_in), (down_bias_hbm, down_bias_in),
             (first_gain_hbm, first_gain_in), (first_shift_hbm, first_shift_in), (second_gain_hbm, second_gain_in),
             (second_shift_hbm, second_shift_in), (up_bias_hbm, up_bias_in), (wi_hbm, wi_in), (wo_hbm, wo_own),
             (wu_hbm, wu_in), (wd_hbm, wd_in))
    entry = [local(9 + i, a, b) for i, (a, b) in enumerate(entry)]
    for copy in entry[1:9] + entry[:1] + entry[9:]:
        copy.start()
    local(0, tokens_hbm, tokens).start()
    local(1, cot_hbm, cot).start()
    geo.greet()
    for copy in entry[1:9]:
        copy.wait()
    vec_sum[...] = jnp.zeros((16, 128), F32)
    for v, ref in enumerate((out_bias_in, down_bias_in, first_gain_in, first_shift_in, second_gain_in,
                             second_shift_in)):
        vec_sum[v, :16] = ref[...].astype(F32)
    up_bias_row = up_bias_in[...].astype(F32)
    for t in range(TILES):
        vec_sum[6 + t, :16] = up_bias_row[t * 16:(t + 1) * 16]
    small_own[...] = pltpu.roll(vec_sum[...], place * 16, 1).astype(BF)
    for p in range(PAIRS):
        wi_own[p] = jnp.concatenate([wi_in[:, k * D + p * 128: k * D + (p + 1) * 128] for k in range(3)], axis=1)
    geo.barrier()
    pump("start")
    for copy in entry[:1] + entry[9:]:
        copy.wait()
    source = lax.broadcasted_iota(jnp.int32, (512, 1), 0)
    target = (source % 64) // 16 * 128 + source // 64 * 16 + source % 16
    perm[...] = jnp.where(lax.broadcasted_iota(jnp.int32, (512, 512), 1) == target, 1.0, 0.0).astype(BF)
    stacked = jnp.concatenate([wu_in[:, g * 512:(g + 1) * 512] for g in range(TILES)], axis=0)
    stacked = dot(stacked, perm[...]).astype(BF)
    for t in range(TILES):
        for g in range(TILES):
            wf_own[t, :, g * 128:(g + 1) * 128] = stacked[g * 16:(g + 1) * 16, t * 128:(t + 1) * 128]
        wf_own[t, :, D:] = wd_in[t * 16:(t + 1) * 16]

    f = feat[...]
    zero = jnp.zeros((DH, M), BF)
    one = jnp.ones((DH, M), BF)
    fa[0] = jnp.concatenate([f, zero, -one, zero], axis=0)
    fa[1] = jnp.concatenate([zero, f, zero, -one], axis=0)
    ft[...] = jnp.concatenate([jnp.concatenate([f, zero], axis=1), jnp.concatenate([zero, f], axis=1),
                               jnp.concatenate([one, zero], axis=1), jnp.concatenate([zero, one], axis=1)], axis=0)
    low_lane = lax.broadcasted_iota(jnp.int32, (1, 128), 1) < DH
    m0f = jnp.where(low_lane, 1.0, 0.0)
    m0 = m0f.astype(BF)
    m1 = (1.0 - m0f).astype(BF)
    tri_r = lax.broadcasted_iota(jnp.int32, (HALF, HALF), 0)
    tri_c = lax.broadcasted_iota(jnp.int32, (HALF, HALF), 1)

    pump("first")

    flat = lambda v: v.reshape(-1, v.shape[-1])
    sums = jnp.sum(small[...].astype(F32).reshape(-1, 8, 16, 128), axis=1)
    vecs[...] = jnp.concatenate([sums[g] for g in range(D // 128)], axis=1)
    out_bias, down_bias = lambda: vecs[0:1], lambda: vecs[1:2]

    def norm_parts(rows):
        center = jnp.mean(rows, axis=-1, keepdims=True)
        centred = rows - center
        spread = jnp.mean(centred * centred, axis=-1, keepdims=True)
        inv = lax.rsqrt(spread + epsilon)
        return centred * inv, inv

    def first_norm(s):
        hat, _ = norm_parts(tokens[s].astype(F32))
        value = (hat * vecs[2:3] + vecs[3:4]).astype(BF)
        normed[s] = value
        normed_t[s] = value.T
    pump("vec")
    local(0, tokens_hbm, tokens).wait()
    first_norm(0)
    pump("norm0")
    first_norm(1)
    pump("norm1")

    def vx(s, p):
        v = mixed[s, p, :, 2 * 128:]
        ones = jnp.ones(v.shape, BF)
        return (jnp.concatenate([v * m0, ones * m0], axis=1), jnp.concatenate([v * m1, ones * m1], axis=1))

    def project(p, s):
        mixed[s, p] = dot(normed[s], flat(wi[p])).astype(BF)
        for part, target in ((0, pq), (1, pk)):
            rows = mixed[s, p, :, part * 128:(part + 1) * 128]
            wide = rows.astype(F32)
            lhs = jnp.concatenate([rows, (wide * wide * (0.5 * SCALE)).astype(BF)], axis=1)
            for h in range(2):
                power = dot(lhs, fa[h]) * (SCALE * LOG2E) - 0.5 * math.log2(M)
                target[s, 2 * p + h] = jnp.exp2(power).astype(BF)
        v = mixed[s, p, :, 2 * 128:]
        lhs = jnp.concatenate([v.T, jnp.ones((16, L), BF)], axis=0)
        r0 = dot(lhs, pk[s, 2 * p])
        r1 = dot(lhs, pk[s, 2 * p + 1])
        fwd.own[p, s] = jnp.concatenate([r0[:64], r1[64:128], r0[128:136], r1[136:]], axis=0).astype(BF)
    pairs(project, "proj.pre", "proj")

    def state_cols(total, p, s, h, copies):
        state = total[p, s, h * 64:(h + 1) * 64]
        extra = total[p, s, 128:144].astype(F32)[8 * h:8 * h + 8]
        zeros = jnp.zeros((DH, M), BF)
        if copies:
            extra = jnp.concatenate([extra] * 8, axis=0).astype(BF)
        else:
            extra = jnp.concatenate([extra, jnp.zeros((56, M), F32)], axis=0).astype(BF)
        parts = [state, zeros, extra, zeros] if h == 0 else [zeros, state, zeros, extra]
        return jnp.concatenate(parts, axis=0)

    lower = tri_r >= tri_c
    upper = tri_r <= tri_c

    def attend_block(p, s):
        v0, v1 = vx(s, p)
        lanes = pl.ds(pl.multiple_of(p * 128, 128), 128)
        for b in range(2):
            rows = slice(b * HALF, (b + 1) * HALF)
            scores = []
            for h in range(2):
                q = pq[s, 2 * p + h, rows]
                if b == 1:
                    scores.append(dot_nt(q, pk[s, 2 * p + h, :HALF]).astype(BF))
                scores.append(jnp.where(lower, dot_nt(q, pk[s, 2 * p + h, rows]), 0.0).astype(BF))
            rhs = jnp.concatenate([v0[:(b + 1) * HALF], v1[:(b + 1) * HALF]], axis=0)
            ext = dot(jnp.concatenate(scores, axis=1), rhs)
            result[s, rows, lanes] = ext[:, :128]
            den[s, rows, lanes] = ext[:, 128:]
    pairs(attend_block, None, "block")

    def attend_earlier(p, s):
        lanes = pl.ds(pl.multiple_of(p * 128, 128), 128)
        states = jnp.concatenate([state_cols(fwd.total, p, s, h, True) for h in range(2)], axis=1)
        ext = dot_nt(jnp.concatenate([pq[s, 2 * p], pq[s, 2 * p + 1]], axis=1), states)
        inv = 1.0 / (ext[:, 128:] + den[s, :, lanes])
        den[s, :, lanes] = inv
        attended[s, :, lanes] = ((ext[:, :128] + result[s, :, lanes]) * inv).astype(BF)
    pairs(attend_earlier, "att.pre", "att")
    pump("mid.pre")
    local(1, cot_hbm, cot).wait()

    def wo():
        return flat(wo_all[...])

    def to_middle(s):
        value = tokens[s].astype(F32) + dot(attended[s], wo()) + out_bias()
        middle[s] = value
        hat, _ = norm_parts(value)
        low = (hat * vecs[4:5] + vecs[5:6]).astype(BF)
        n2[s] = low
        n2_t[s] = low.T
        result[s] = value + down_bias()
        tokens_grad[s] = jnp.zeros((L, D), F32)
    to_middle(0)
    to_middle(1)
    pump("mid")
    grads[...] = jnp.zeros(grads.shape, F32)

    k0 = math.sqrt(2.0 / math.pi)

    def feed_tile(t):
        pump_at(t, [f"feed.pre{n}" for n in range(TILES)])
        bias = vecs[pl.ds(6 + t, 1)]
        wut = lambda: flat(wf[t, :, :, :, :, :, :D])
        wdt = lambda: flat(wf[t, :, :, :, :, :, D:])

        def seq(s):
            for b in range(2):
                rows = slice(b * HALF, (b + 1) * HALF)
                u = (dot(n2[s, rows], wut()) + bias).astype(BF)
                uu = u * u
                th = jnp.tanh(u * (BF(k0) + BF(k0 * 0.044715) * uu))
                half = BF(0.5) + BF(0.5) * th
                a = u * half
                act[s, rows] = a
                slope = half + a * (BF(1.0) - half) * (BF(2.0 * k0) + BF(6.0 * 0.044715 * k0) * uu)
                back = dot_nt(cot[s, rows], wdt()) * slope.astype(F32)
                grads[pl.ds(6 + t, 1)] += jnp.sum(back, axis=0, keepdims=True)
                low = back.astype(BF)
                hg[s, rows] = low
                result[s, rows] += dot(a, wdt())
                tokens_grad[s, rows] += dot_nt(low, wut())
        seq(0)
        seq(1)
        dwd = dot(act[0].T, cot[0]) + dot(act[1].T, cot[1])
        part_f[t, :, :, :, :, :, D:] = dwd.astype(BF).reshape(lead + (-1, D))
        dwu = dot(n2_t[0], hg[0]) + dot(n2_t[1], hg[1])
        part_f[t, :, :, :, :, :, :D] = dwu.astype(BF).reshape(lead + (-1, 512))
        pump_at(t, [f"feed{n}" for n in range(TILES)])
    loop(TILES, feed_tile)
    local(2, result, result_hbm).start()

    ones_block = jnp.concatenate([jnp.concatenate([jnp.ones((64, 64), F32), jnp.zeros((64, 64), F32)], axis=1),
                                  jnp.concatenate([jnp.zeros((64, 64), F32), jnp.ones((64, 64), F32)], axis=1)],
                                 axis=0).astype(BF)
    ones_two = jnp.concatenate([ones_block, ones_block], axis=0)
    lane_id = lax.broadcasted_iota(jnp.int32, (1, 128), 1)
    hi_lane = jnp.where((lane_id % DH) == 0, 1.0, 0.0)
    lo_lane = jnp.where((lane_id % DH) == 1, 1.0, 0.0)

    def norm_back(rows, dy, gain):
        hat, inv = norm_parts(rows)
        dg = dy * gain
        m_a = jnp.mean(dg, axis=-1, keepdims=True)
        m_b = jnp.mean(dg * hat, axis=-1, keepdims=True)
        return (inv * (dg - m_a - hat * m_b), jnp.sum(dy * hat, axis=0, keepdims=True),
                jnp.sum(dy, axis=0, keepdims=True))

    def out_back(s):
        dx, dgain, dshift = norm_back(middle[s], tokens_grad[s], vecs[4:5])
        up = cot[s].astype(F32)
        mg = up + dx
        middle[s] = mg
        low = mg.astype(BF)
        act[s] = low
        grads[0:1] += jnp.sum(mg, axis=0, keepdims=True)
        grads[1:2] += jnp.sum(up, axis=0, keepdims=True)
        grads[4:5] += dgain
        grads[5:6] += dshift
        ag = dot_nt(low, wo())
        inv = den[s]
        ng = ag * inv
        prod = ng * attended[s].astype(F32)
        n2[s] = ng.astype(BF)
        for p in range(PAIRS):
            cols = slice(p * 128, (p + 1) * 128)
            pr = prod[:, cols]
            hi = pr.astype(BF)
            lo = (pr - hi.astype(F32)).astype(BF)
            dgr = -dot(jnp.concatenate([hi, lo], axis=1), ones_two)
            dhi = dgr.astype(BF).astype(F32)
            dlo = dgr - dhi
            hg[s, :, cols] = (dhi * hi_lane + dlo * lo_lane).astype(BF)
    out_back(0)
    out_back(1)
    dwo = dot(attended[0].T, act[0]) + dot(attended[1].T, act[1])
    part_o[...] = dwo.astype(BF).reshape(lead + (-1, D))
    pump("out")

    def ngx(s, p):
        lanes = pl.ds(pl.multiple_of(p * 128, 128), 128)
        return jnp.concatenate([n2[s, :, lanes], hg[s, :, lanes]], axis=1)

    def state_back(p):
        def seq(s):
            lhs = ngx(s, p).T
            r0 = dot(lhs, pq[s, 2 * p])
            r1 = dot(lhs, pq[s, 2 * p + 1])
            bwd.own[p, s] = jnp.concatenate([r0[:64], r1[64:128], r0[128:136], r1[192:200]], axis=0).astype(BF)
        seq(0)
        seq(1)
        pump_at(p, [f"st{n}" for n in range(PAIRS)])
    loop(PAIRS, state_back)

    lo, hi = slice(0, HALF), slice(HALF, L)

    def masked(keep, value):
        return jnp.where(keep, value, 0.0).astype(BF)

    def through_features(s, p, part, logs):
        through = dot_nt(jnp.concatenate(logs, axis=1), ft[...])
        cols = slice(part * 128, (part + 1) * 128)
        rows = mixed[s, p, :, cols].astype(F32)
        mixed[s, p, :, cols] = (SCALE * through[:, :128] - SCALE * SCALE * through[:, 128:] * rows).astype(BF)

    def input_part(part, chosen):
        cols = slice(part * 128, (part + 1) * 128)
        total = sum(dot(normed_t[s], jnp.concatenate([mixed[s, p, :, cols] for p in chosen], axis=1))
                    for s in range(2))
        return total.astype(BF).reshape(lead + (-1, 128 * len(chosen)))

    def query_back(p, s):
        x = ngx(s, p)
        logs = []
        for h, v in enumerate(vx(s, p)):
            q, k = pq[s, 2 * p + h], pk[s, 2 * p + h]
            sx = state_cols(fwd.total, p, s, h, True)
            g00 = masked(lower, dot_nt(x[lo], v[lo]))
            g10 = dot_nt(x[hi], v[lo]).astype(BF)
            g11 = masked(lower, dot_nt(x[hi], v[hi]))
            qg0 = dot(jnp.concatenate([g00, x[lo]], axis=1), jnp.concatenate([k[lo], sx], axis=0))
            qg1 = dot(jnp.concatenate([g10, g11, x[hi]], axis=1), jnp.concatenate([k, sx], axis=0))
            logs.append(jnp.concatenate([qg0, qg1], axis=0).astype(BF) * q)
        through_features(s, p, 0, logs)
    pairs(query_back, None, "q")
    part_q[...] = input_part(0, range(PAIRS))
    pump("q.end")

    def key_back(p, s):
        x = ngx(s, p)
        logs = []
        for h, v in enumerate(vx(s, p)):
            q, k = pq[s, 2 * p + h], pk[s, 2 * p + h]
            sg = state_cols(bwd.total, p, s, h, False)
            t00 = masked(upper, dot_nt(v[lo], x[lo]))
            t01 = dot_nt(v[lo], x[hi]).astype(BF)
            t11 = masked(upper, dot_nt(v[hi], x[hi]))
            kg0 = dot(jnp.concatenate([t00, t01, v[lo]], axis=1), jnp.concatenate([q, sg], axis=0))
            kg1 = dot(jnp.concatenate([t11, v[hi]], axis=1), jnp.concatenate([q[hi], sg], axis=0))
            logs.append(jnp.concatenate([kg0, kg1], axis=0).astype(BF) * k)
        through_features(s, p, 1, logs)
    pairs(key_back, "k.pre", "k")
    part_k[...] = input_part(1, range(PAIRS))
    pump("k.end")

    def value_back(p, s):
        lanes = pl.ds(pl.multiple_of(p * 128, 128), 128)
        ng = n2[s, :, lanes]
        parts = []
        for h in range(2):
            q, k = pq[s, 2 * p + h], pk[s, 2 * p + h]
            parts.append((masked(upper, dot_nt(k[lo], q[lo])), dot_nt(k[lo], q[hi]).astype(BF),
                          masked(upper, dot_nt(k[hi], q[hi]))))
        n0, n1 = ng * m0, ng * m1
        vg0 = dot(jnp.concatenate([parts[0][0], parts[0][1], parts[1][0], parts[1][1]], axis=1),
                  jnp.concatenate([n0, n1], axis=0))
        vg1 = dot(jnp.concatenate([parts[0][2], parts[1][2]], axis=1), jnp.concatenate([n0[hi], n1[hi]], axis=0))
        zeros = jnp.zeros((DH, M), BF)
        sgt = jnp.concatenate([jnp.concatenate([bwd.total[p, s, :64], zeros], axis=0),
                               jnp.concatenate([zeros, bwd.total[p, s, 64:128]], axis=0)], axis=1)
        vg = jnp.concatenate([vg0, vg1], axis=0)
        vg += dot_nt(jnp.concatenate([pk[s, 2 * p], pk[s, 2 * p + 1]], axis=1), sgt)
        mixed[s, p, :, 256:] = vg.astype(BF)
    for n in range(2):
        def step(i):
            value_back(2 * n + i, 0)
            value_back(2 * n + i, 1)
        loop(2, step)
        part_v[n] = input_part(2, range(2 * n, 2 * n + 2))
        pump(f"v{n}")

    def normed_back(s):
        for b in range(2):
            rows = slice(b * HALF, (b + 1) * HALF)
            back = dot_nt(mixed[s, 0, rows], flat(wi[0]))
            for p in range(1, PAIRS):
                back += dot_nt(mixed[s, p, rows], flat(wi[p]))
            tokens_grad[s, rows] = back
    normed_back(0)
    pump("nb0")
    normed_back(1)
    pump("nb1")

    def first_back(s):
        dx, dgain, dshift = norm_back(tokens[s].astype(F32), tokens_grad[s], vecs[2:3])
        tokens_grad[s] = middle[s] + dx
        grads[2:3] += dgain
        grads[3:4] += dshift
    first_back(0)
    pump("fb0")
    first_back(1)
    for g in range(D // 128):
        tile = grads[:, g * 128:(g + 1) * 128].astype(BF)
        for k in range(8):
            chip, core = (8 * g + k) // 2, k % 2
            part_g[chip // (geo.X * geo.Y), chip // geo.Y % geo.X, chip % geo.Y, core] = tile
    local(3, tokens_grad, tokens_grad_hbm).start()
    pump("fb1")
    pump("end0")
    local(5, out_out, out_hbm).start()
    stacked = jnp.concatenate([jnp.concatenate([up_parts[t, :, g * 128:(g + 1) * 128] for t in range(TILES)], axis=1)
                               for g in range(TILES)], axis=0)
    high = stacked.astype(BF)
    low = (stacked - high.astype(F32)).astype(BF)
    stacked = dot_nt(high, perm[...]) + dot_nt(low, perm[...])
    for g in range(TILES):
        up_out[:, g * 512:(g + 1) * 512] = stacked[g * 16:(g + 1) * 16]
    for t in range(TILES):
        down_out[t * 16:(t + 1) * 16] = up_parts[t, :, D:]
    local(6, up_out, up_hbm).start()
    local(7, down_out, down_hbm).start()
    late = {name for name, n in PLAN["end"]}
    drains = [fwd, bwd] + [task for name, task in tasks.items() if name not in late and hasattr(task, "drain")]
    for task in drains:
        task.drain()
    pump("end")
    vec_out[...] = pltpu.roll(vec_sum[...], lax.rem(8 - place, 8) * 16, 1)
    local(8, vec_out, vec_hbm).start()
    local(4, inp_out, inp_hbm).start()
    for i, (a, b) in enumerate(((result, result_hbm), (tokens_grad, tokens_grad_hbm), (inp_out, inp_hbm),
                                (out_out, out_hbm), (up_out, up_hbm), (down_out, down_hbm), (vec_out, vec_hbm))):
        local(2 + i, a, b).wait()
    for name in sorted(late):
        if hasattr(tasks[name], "drain"):
            tasks[name].drain()


def finish_kernel(*refs):
    ins, outs = refs[:7], refs[7:20]
    held, (inp, out, up, down, vec), vec_rows = refs[20], refs[21:26], refs[26:33]
    in_sems, out_sems = refs[33:]
    waits = []

    def copy(src, dst, sems, i):
        return pltpu.make_async_copy(src, dst, sems.at[i])
    small_in = [copy(a, b, in_sems, i) for i, (a, b) in enumerate(zip(ins[2:], (inp, out, up, down, vec)))]
    for one in small_in[:1] + small_in[4:]:
        one.start()
    cuts = []
    for n in range(2):
        for m in range(ins[n].shape[0]):
            for k in range(4):
                rows = pl.ds(k * (ins[n].shape[1] // 4), ins[n].shape[1] // 4)
                slot = held.at[n, m, rows]
                cuts.append((copy(ins[n].at[m, rows], slot, in_sems, 5 + len(cuts)),
                             copy(slot, outs[n].at[m, rows], out_sems, 11 + len(cuts))))
    for first, _ in cuts[:4]:
        first.start()
    for one in small_in[1:4]:
        one.start()
    for first, _ in cuts[4:]:
        first.start()
    small_in[0].wait()
    small_in[4].wait()
    n = vec_rows[0].shape[-1]
    for v in range(6):
        vec_rows[v][...] = vec[v, :n]
    for t in range(up.shape[-1] // 512):
        vec_rows[6][pl.ds(t * n, n)] = vec[6 + t, :n]
    final = {2: inp, 4: vec_rows[0], 8: vec_rows[1], 9: vec_rows[2], 10: vec_rows[3], 11: vec_rows[4],
             12: vec_rows[5], 6: vec_rows[6]}
    for i, (place, ref) in enumerate(final.items()):
        waits.append(copy(ref, outs[place], out_sems, i))
        waits[-1].start()
    for first, second in cuts[:4]:
        first.wait()
        second.start()
        waits.append(second)
    for i, (one, ref, place) in enumerate(zip(small_in[1:4], (out, up, down), (3, 5, 7))):
        one.wait()
        waits.append(copy(ref, outs[place], out_sems, 8 + i))
        waits[-1].start()
    for first, second in cuts[4:]:
        first.wait()
        second.start()
        waits.append(second)
    for one in waits:
        one.wait()


def fused(geo, args):
    (tokens, feature_matrix, input_weight, output_weight, output_bias, up_weight, up_bias, down_weight,
     down_bias, first_gain, first_shift, second_gain, second_shift, cotangent) = args
    rows, D = input_weight.shape[0], tokens.shape[-1]
    L = tokens.shape[1]
    FF = up_weight.shape[1]
    tiles = FF // 512
    lane = Lane()
    fwd, bwd = States(geo, lane, True), States(geo, lane, False)
    names = ["S", "O"] + [f"I{p}" for p in range(PAIRS)] + [f"F{t}" for t in range(tiles)]
    tasks = {name: GatherPlane(geo, lane) if name in PLANE else Gather(geo, lane, ORDERS.get(name, (0, 1)))
             for name in names}
    scatters = {"rO": D, "rQ": D, "rK": D, "rV0": 256, "rV1": 256, "rG": 128}
    scatters.update({f"rF{t}": 2 * D for t in range(tiles)})
    for name in scatters:
        tasks[name] = ScatterDirect(geo, lane) if name in DIRECT else Scatter(geo, lane, ORDERS.get(name, (0, 1)))
    for p in range(PAIRS):
        tasks[f"f{p}"], tasks[f"b{p}"] = PairStates(fwd, p), PairStates(bwd, p)
    plan = (fwd, bwd, tasks)
    lead = (geo.Z, geo.X, geo.Y, 2)
    V = pltpu.VMEM
    shape = jax.ShapeDtypeStruct
    outs = [shape(tokens.shape, F32), shape(tokens.shape, F32), shape(input_weight.shape, F32),
            shape((rows, D), F32), shape((rows, FF), F32), shape(down_weight.shape, F32), shape((rows, 128), F32)]
    arrays = (tokens, cotangent, feature_matrix, output_bias, down_bias, first_gain, first_shift, second_gain,
              second_shift, up_bias, input_weight, output_weight, up_weight, down_weight)
    scratch = [V(a.shape, BF) for a in arrays[2:11] + arrays[12:]] + [V(o.shape, F32) for o in outs[2:]]
    scratch += [
        V((2, L, D), BF), V((2, L, D), BF), V((2, L, D), F32), V((2, L, D), F32),
        V((rows, 128), BF), V(lead + (rows, 128), BF), V((PAIRS, rows, 384), BF), V((PAIRS,) + lead + (rows, 384), BF),
        V((rows, D), BF), V(lead + (rows, D), BF), V((tiles, rows, 2 * D), BF),
        V((tiles,) + lead + (rows, 2 * D), BF),
        V((2, L, D), BF), V((2, D, L), BF), V((2, PAIRS, L, 384), BF), V((2, H, L, M), BF), V((2, H, L, M), BF),
        V((2, L, D), F32), V((2, L, D), BF), V((2, L, D), F32), V((2, D, L), BF),
        V((2, L, 512), BF), V((2, L, 512), BF), V((16, D), F32), V((16, D), F32),
        V((2, M, M), BF), V((M, 2 * M), BF), V((512, 512), BF),
        V(lead + (rows, D), BF), V(lead + (rows, D), BF), V((2,) + lead + (rows, 256), BF), V(lead + (rows, D), BF),
        V((tiles,) + lead + (rows, 2 * D), BF), V(lead + (rows, 128), BF), V((tiles, rows, 2 * D), F32), V((rows, 128), F32),
    ]
    scratch += States.scratch(geo) + States.scratch(geo)
    for name, width in scatters.items():
        scratch += type(tasks[name]).scratch(geo, rows, width)
    scratch += [pltpu.SemaphoreType.DMA((lane.count,)), pltpu.SemaphoreType.DMA((lane.count,)),
                pltpu.SemaphoreType.DMA((21,))]
    hbm = pl.BlockSpec(memory_space=pl.ANY)
    parts = pl.pallas_call(
        functools.partial(layer_kernel, geo, lane, plan),
        out_shape=outs, in_specs=[hbm] * 14, out_specs=[hbm] * 7, scratch_shapes=scratch,
        compiler_params=pltpu.CompilerParams(collective_id=0, has_side_effects=True, vmem_limit_bytes=60 << 20),
    )(*arrays)
    vector = shape((rows,), F32)
    final = [outs[0], outs[1], shape(input_weight.shape, F32), outs[3], vector, outs[4],
             shape(up_bias.shape, F32), outs[5]] + [vector] * 5
    return pl.pallas_call(
        finish_kernel,
        out_shape=final, in_specs=[hbm] * 7, out_specs=[hbm] * 13,
        scratch_shapes=[V((2,) + tokens.shape, F32)] + [V(o.shape, F32) for o in outs[2:]]
        + [V((rows,), F32)] * 6 + [V(up_bias.shape, F32)]
        + [pltpu.SemaphoreType.DMA((21,)), pltpu.SemaphoreType.DMA((27,))],
        compiler_params=pltpu.CompilerParams(vmem_limit_bytes=60 << 20),
    )(*parts)

def local(
    tokens,
    feature_matrix,
    input_weight,
    output_weight,
    output_bias,
    up_weight,
    up_bias,
    down_weight,
    down_bias,
    first_gain,
    first_shift,
    second_gain,
    second_shift,
    cotangent,
):
    params = (
        lax.all_gather(input_weight, ("dp", "seq"), axis=0, tiled=True),
        lax.all_gather(output_weight, ("dp", "seq"), axis=0, tiled=True),
        lax.all_gather(output_bias, ("dp", "seq"), axis=0, tiled=True),
        lax.all_gather(up_weight, ("dp", "seq"), axis=0, tiled=True),
        lax.all_gather(up_bias, ("dp", "seq"), axis=0, tiled=True),
        lax.all_gather(down_weight, ("dp", "seq"), axis=0, tiled=True),
        lax.all_gather(down_bias, ("dp", "seq"), axis=0, tiled=True),
        lax.all_gather(first_gain, ("dp", "seq"), axis=0, tiled=True),
        lax.all_gather(first_shift, ("dp", "seq"), axis=0, tiled=True),
        lax.all_gather(second_gain, ("dp", "seq"), axis=0, tiled=True),
        lax.all_gather(second_shift, ("dp", "seq"), axis=0, tiled=True),
    )
    micros = tokens.shape[0]
    fronts = []
    carries = []
    for micro_step in range(micros):
        pieces = front(tokens[micro_step], feature_matrix, params)
        fronts.append(pieces)
        carries.append(
            prefix(
                (pieces[8], pieces[9]),
                "seq",
                add_pair,
                (jnp.zeros_like(pieces[8]), jnp.zeros_like(pieces[9])),
            )
        )
    results = []
    for micro_step in range(micros):
        pieces = fronts[micro_step]
        running_prefix_state, norm_sum = carries[micro_step]
        output = attend(pieces[5], pieces[6], pieces[7], running_prefix_state, norm_sum)[0]
        attended, middle = upper(pieces[0], output, params)
        results.append(feed(middle, params))
    result = jnp.stack(results)
    back_params = (
        lax.all_gather(input_weight, ("dp", "seq"), axis=0, tiled=True),
        lax.all_gather(output_weight, ("dp", "seq"), axis=0, tiled=True),
        lax.all_gather(output_bias, ("dp", "seq"), axis=0, tiled=True),
        lax.all_gather(up_weight, ("dp", "seq"), axis=0, tiled=True),
        lax.all_gather(up_bias, ("dp", "seq"), axis=0, tiled=True),
        lax.all_gather(down_weight, ("dp", "seq"), axis=0, tiled=True),
        lax.all_gather(down_bias, ("dp", "seq"), axis=0, tiled=True),
        lax.all_gather(first_gain, ("dp", "seq"), axis=0, tiled=True),
        lax.all_gather(first_shift, ("dp", "seq"), axis=0, tiled=True),
        lax.all_gather(second_gain, ("dp", "seq"), axis=0, tiled=True),
        lax.all_gather(second_shift, ("dp", "seq"), axis=0, tiled=True),
    )
    stored_list = []
    later_list = []
    for micro_step in range(micros):
        stored = upper_back(
            tokens[micro_step],
            cotangent[micro_step].astype(jnp.float32),
            feature_matrix,
            back_params,
            carries[micro_step],
        )
        stored_list.append(stored)
        later_list.append(
            prefix_2(
                (stored["state_grad"], stored["sum_grad"]),
                "seq",
                add_pair,
                (jnp.zeros_like(stored["state_grad"]), jnp.zeros_like(stored["sum_grad"])),
            )
        )
    upper_names = ["out", "out_bias", "up", "up_bias", "down", "down_bias", "gain_two", "shift_two"]
    upper_totals = [stored_list[0][name] for name in upper_names]
    micro_step = 1
    upper_totals = [
        total + stored_list[micro_step][name] for total, name in zip(upper_totals, upper_names)
    ]
    token_grads = []
    lower_totals = None
    for micro_step in range(micros):
        stored = stored_list[micro_step]
        tokens_part, input_part, gain_part, shift_part = lower_back(
            stored, later_list[micro_step], feature_matrix, back_params
        )
        token_grads.append(tokens_part)
        lower_parts = (input_part, gain_part, shift_part)
        if micro_step == 0:
            lower_totals = lower_parts
        else:
            lower_totals = jax.tree.map(jnp.add, lower_totals, lower_parts)
    shares = (
        lax.psum_scatter(lower_totals[0], ("dp", "seq"), scatter_dimension=0, tiled=True),
        lax.psum_scatter(upper_totals[0], ("dp", "seq"), scatter_dimension=0, tiled=True),
        lax.psum_scatter(upper_totals[1], ("dp", "seq"), scatter_dimension=0, tiled=True),
        lax.psum_scatter(upper_totals[2], ("dp", "seq"), scatter_dimension=0, tiled=True),
        lax.psum_scatter(upper_totals[3], ("dp", "seq"), scatter_dimension=0, tiled=True),
        lax.psum_scatter(upper_totals[4], ("dp", "seq"), scatter_dimension=0, tiled=True),
        lax.psum_scatter(upper_totals[5], ("dp", "seq"), scatter_dimension=0, tiled=True),
        lax.psum_scatter(lower_totals[1], ("dp", "seq"), scatter_dimension=0, tiled=True),
        lax.psum_scatter(lower_totals[2], ("dp", "seq"), scatter_dimension=0, tiled=True),
        lax.psum_scatter(upper_totals[6], ("dp", "seq"), scatter_dimension=0, tiled=True),
        lax.psum_scatter(upper_totals[7], ("dp", "seq"), scatter_dimension=0, tiled=True),
    )
    return (
        result,
        jnp.stack(token_grads),
        shares[0],
        shares[1],
        shares[2],
        shares[3],
        shares[4],
        shares[5],
        shares[6],
        shares[7],
        shares[8],
        shares[9],
        shares[10],
    )


def solution(mesh):
    in_specs = (
        P("dp", "seq", None),
        P(),
        P(("dp", "seq"), None),
        P(("dp", "seq"), None),
        P(("dp", "seq")),
        P(("dp", "seq"), None),
        P(("dp", "seq")),
        P(("dp", "seq"), None),
        P(("dp", "seq")),
        P(("dp", "seq")),
        P(("dp", "seq")),
        P(("dp", "seq")),
        P(("dp", "seq")),
        P("dp", "seq", None),
    )
    out_specs = (
        P("dp", "seq", None),
        P("dp", "seq", None),
        P(("dp", "seq"), None),
        P(("dp", "seq"), None),
        P(("dp", "seq")),
        P(("dp", "seq"), None),
        P(("dp", "seq")),
        P(("dp", "seq"), None),
        P(("dp", "seq")),
        P(("dp", "seq")),
        P(("dp", "seq")),
        P(("dp", "seq")),
        P(("dp", "seq")),
    )
    geo = Geometry(mesh)
    rows = 512 // (mesh.shape["dp"] * mesh.shape["seq"])
    if rows == 16:
        def body(*args):
            return fused(geo, args)
    else:
        body = local
    return jax.shard_map(body, mesh=mesh, in_specs=in_specs, out_specs=out_specs, check_vma=False)
```
